32 devices in a mesh: pipe: 2 (over y), dp: 16 (over z, x, core).
Axes of the slice: x: 2, y: 2, z: 4, core: 2. Of those that a mesh axis runs over, the one named last changes fastest.
Arguments:
- embeddings: bfloat16 [32, 256, 768], P('dp'), may hold values from -6 to 6
- cotangent: bfloat16 [32, 256, 768], P('dp'), may hold values from -6 to 6
- seg_ids: int32 [32, 256], P('dp'), may hold values from 0 to 1, as said below
- thought_pos: int32 [32, 12], P('dp'), may hold values from 1 to 254, as said below
- w_qkv: bfloat16 [2, 768, 2304], P('pipe'), may hold values from -0.21875 to 0.21875
- w_out: bfloat16 [2, 768, 768], P('pipe'), may hold values from -0.875 to 0.875
- w_up: bfloat16 [2, 768, 3072], P('pipe'), may hold values from -0.21875 to 0.21875
- w_down: bfloat16 [2, 3072, 768], P('pipe'), may hold values from -0.109375 to 0.109375
- small_params: float32 [2, 9216], P('pipe'), may hold values from -1 to 1.6, as said below
Outputs:
- section_out: float32 [2, 32, 256, 768], P('pipe', 'dp')
- grad_qkv: float32 [2, 768, 2304], P('pipe', 'dp')
- grad_out: float32 [2, 768, 768], P('pipe', 'dp')
- grad_up: float32 [2, 768, 3072], P('pipe', 'dp')
- grad_down: float32 [2, 3072, 768], P('pipe', 'dp')
- grad_small: float32 [2, 9216], P('pipe', 'dp')
The draws below stay inside these ranges and needn't reach their ends.
Inputs may be any that keep to these rules, and one draw needn't show every extreme that they name: `seg_ids`: each row packs two examples: 0 on its first positions, 1 on the rest, each example at least 64 long. `thought_pos`: per row, 6 consecutive positions inside the first example, then 6 consecutive inside the second, increasing; never an example's first position. `small_params`: the layer norms' gains are positive.
All inputs are finite; a program needn't handle non-finite values.
Results may differ from the reference program's by a relative error of at most 0.02.
Values sent between devices are 32-bit elements; how exact they have to be, the bound alone decides.
A program may use at most 576 MiB of HBM per device.

```python
import math
import jax
import jax.numpy as jnp
from jax import lax

D = 768
HEADS = 12
FF = 3072
ROW_LEN = 256
TPE = 6
LAYERS = 2
PACK = 9216
ROWS = 32


def layout(key):
    first_len = jax.random.randint(jax.random.fold_in(key, 101), (ROWS,), ROW_LEN // 4, 3 * ROW_LEN // 4 + 1)
    second_len = ROW_LEN - first_len
    raw_one = jax.random.randint(jax.random.fold_in(key, 102), (ROWS,), 0, 1 << 20)
    raw_two = jax.random.randint(jax.random.fold_in(key, 103), (ROWS,), 0, 1 << 20)
    row_number = jnp.arange(ROWS, dtype=jnp.int32)
    start_one = jnp.where(row_number == 0, 1, 1 + raw_one % (first_len - TPE - 1))
    start_two = jnp.where(row_number == 0, second_len - TPE - 1, 1 + raw_two % (second_len - TPE - 1))
    return (first_len, start_one, start_two)


def draw_seg_ids(key, part):
    first_len, start_one, start_two = layout(key)
    places = jnp.arange(ROW_LEN, dtype=jnp.int32)
    return (places[None, :] >= first_len[:, None]).astype(jnp.int32)


def draw_thought_pos(key, part):
    first_len, start_one, start_two = layout(key)
    offsets = jnp.arange(TPE, dtype=jnp.int32)
    first_run = start_one[:, None] + offsets[None, :]
    second_run = first_len[:, None] + start_two[:, None] + offsets[None, :]
    return jnp.concatenate([first_run, second_run], axis=1).astype(jnp.int32)


def draw_small_params(key, part):
    key = jax.random.fold_in(key, 7)
    columns = jnp.arange(PACK, dtype=jnp.int32)[None, :] + jnp.zeros((LAYERS, 1), jnp.int32)
    is_gain = (columns < D) | (columns >= 5 * D) & (columns < 6 * D)
    gain_key, bias_key = jax.random.split(key)
    gains = jnp.exp(jax.random.uniform(gain_key, (LAYERS, PACK), jnp.float32, math.log(0.6), math.log(1.6)))
    biases = jnp.clip(0.3 * jax.random.normal(bias_key, (LAYERS, PACK), jnp.float32), -1.0, 1.0)
    return jnp.where(is_gain, gains, biases).astype(jnp.float32)


def shard_levels(rng, dims, cuts, least, largest):
    def one(dim, parts):
        heights = jax.random.uniform(jax.random.fold_in(jax.random.fold_in(rng, 6), dim), (parts,), jnp.float32, least / len(cuts), largest / len(cuts))
        return jnp.repeat(jnp.exp(heights), dims[dim] // parts).reshape((-1,) + (1,) * (len(dims) - dim - 1))

    factor_of = one(*cuts[0])
    for cut in cuts[1:]:
        factor_of = factor_of * one(*cut)
    return factor_of


def normal_values(key, shape, width, most, cuts=(), kind=jnp.bfloat16):
    values = jax.random.normal(key, shape, jnp.float32) * width
    if len(cuts) > 0:
        values = shard_levels(key, shape, cuts, -0.22, 0.18) * values
    return jnp.clip(values, min=-most, max=most).astype(kind)


def setup_inputs(seed: int = 0) -> dict:
    splits = jax.random.split(jax.random.key(seed), 10)
    embeddings = normal_values(splits[0], (ROWS, ROW_LEN, D), 1.0, 6.0, ((0, 16),))
    cotangent = normal_values(splits[1], (ROWS, ROW_LEN, D), 1.0, 6.0, ((0, 16),))
    seg_ids = draw_seg_ids(jax.random.fold_in(splits[9], 71), 0)
    thought_pos = draw_thought_pos(jax.random.fold_in(splits[9], 71), 0)
    w_qkv = normal_values(splits[4], (LAYERS, D, 3 * D), D ** -0.5, 0.21875, ((0, 2),))
    w_out = normal_values(splits[5], (LAYERS, D, D), (D // 16) ** -0.5, 0.875, ((0, 2),))
    w_up = normal_values(splits[6], (LAYERS, D, FF), D ** -0.5, 0.21875, ((0, 2),))
    w_down = normal_values(splits[7], (LAYERS, FF, D), FF ** -0.5, 0.109375, ((0, 2),))
    small_params = draw_small_params(jax.random.fold_in(splits[9], 71), 0)
    return {"embeddings": embeddings, "cotangent": cotangent, "seg_ids": seg_ids, "thought_pos": thought_pos, "w_qkv": w_qkv, "w_out": w_out, "w_up": w_up, "w_down": w_down, "small_params": small_params}


epsilon = 1e-05
masked_score = -1000000000.0
highest = lax.Precision.HIGHEST

@jax.custom_vjp
def low(v):
    return lax.optimization_barrier(v.astype(jnp.bfloat16)).astype(jnp.float32)

@jax.custom_vjp
def low_back(v):
    return v

def low_keep(v):
    return (low(v), None)

def low_pass(kept, grad):
    return (grad,)

def back_keep(v):
    return (v, None)

def back_low(kept, grad):
    return (low(grad),)
low.defvjp(low_keep, low_pass)
low_back.defvjp(back_keep, back_low)

def unpack_small(packed):
    pieces = [packed[number * D:(number + 1) * D] for number in range(7)]
    return pieces + [packed[7 * D:7 * D + FF], packed[7 * D + FF:8 * D + FF]]

def layer_norm(values, scaling, offset):
    center = lax.optimization_barrier(jnp.mean(values, -1, keepdims=True))
    centred = values - center
    spread = lax.optimization_barrier(jnp.mean(centred * centred, -1, keepdims=True))
    return centred * lax.rsqrt(spread + epsilon) * scaling + offset

def attend(row_pair):
    joined, segment = row_pair
    length = joined.shape[0]
    split_parts = joined.reshape(length, 3, HEADS, D // HEADS)
    queries = split_parts[:, 0]
    key_heads = split_parts[:, 1]
    value_heads = split_parts[:, 2]
    scores = jnp.einsum('qhe,khe->hqk', queries, key_heads, precision=highest) * (D // HEADS) ** (-0.5)
    scores = low_back(scores)
    places = jnp.arange(length, dtype=jnp.int32)
    allowed = (segment[:, None] == segment[None, :]) & (places[None, :] <= places[:, None])
    scores = jnp.where(allowed[None], scores, masked_score)
    probabilities = low(jax.nn.softmax(scores, -1))
    attended = jnp.einsum('hqk,khe->qhe', probabilities, value_heads, precision=highest)
    return attended.reshape(length, D)

def layer(hidden_in, w_qkv, w_out, w_up, w_down, packed, seg_ids):
    gain_one, shift_one, bias_query, bias_value, bias_out, gain_two, shift_two, bias_up, bias_down = unpack_small(packed)
    normed = low(layer_norm(hidden_in, gain_one, shift_one))
    bias_joint = jnp.concatenate([bias_query, jnp.zeros_like(bias_query), bias_value])
    joined = low(low_back(jnp.dot(normed, w_qkv, precision=highest) + bias_joint))
    attended = lax.map(jax.checkpoint(attend), (joined, seg_ids))
    attended = low(low_back(attended))
    middle = hidden_in + low_back(jnp.dot(attended, w_out, precision=highest) + bias_out)
    normed_two = low(layer_norm(middle, gain_two, shift_two))
    raised = low_back(jnp.dot(normed_two, w_up, precision=highest) + bias_up)
    activated = low(jax.nn.gelu(raised, approximate=True))
    return middle + low_back(jnp.dot(activated, w_down, precision=highest) + bias_down)

def stack_layers(hidden_in, weights, seg_ids):
    for layer_number in range(LAYERS):
        hidden_in = layer(hidden_in, *[weight[layer_number] for weight in weights], seg_ids)
    return hidden_in

def reference(embeddings, cotangent, seg_ids, thought_pos, w_qkv, w_out, w_up, w_down, small_params):
    inputs = embeddings.astype(jnp.float32)
    weights = (w_qkv.astype(jnp.float32), w_out.astype(jnp.float32), w_up.astype(jnp.float32), w_down.astype(jnp.float32), small_params.astype(jnp.float32))
    places = jnp.arange(ROW_LEN, dtype=jnp.int32)
    chosen = places[None, :, None] == thought_pos[:, None, :]
    marked = jnp.any(chosen, -1)[:, :, None]
    selector = chosen.astype(jnp.float32)

    def model(start, *params):
        latent = stack_layers(start, params, seg_ids)
        carried = jnp.take_along_axis(latent, (thought_pos - 1)[:, :, None], axis=1)
        placed = jnp.einsum('rlt,rtd->rld', selector, carried, precision=highest)
        return stack_layers(jnp.where(marked, placed, start), params, seg_ids)
    output, pullback = jax.vjp(model, inputs, *weights)
    grads = pullback(cotangent.astype(jnp.float32))
    section_out = jnp.stack([grads[0], output])
    return (section_out, grads[1], grads[2], grads[3], grads[4], grads[5])
```

```python
import functools

import jax
import jax.numpy as jnp
from jax import lax
from jax.experimental import pallas as pl
from jax.experimental.pallas import tpu as pltpu
from jax.sharding import PartitionSpec as P

HEADS = 12
BF = jnp.bfloat16
F32 = jnp.float32
MESH = pl.DeviceIdType.MESH
EPSILON = 1e-05
MASKED = -1000000000.0
NO_CAP = 3e38
LAT = 16
CHUNK = 64
G1, B1, BQ, BV, BO, G2, B2, BU = 0, 1, 2, 3, 4, 5, 6, 7


def dot(a, b):
    return lax.dot_general(a, b, (((1,), (0,)), ((), ())), preferred_element_type=F32)


def dot_nt(a, b):
    return lax.dot_general(a, b, (((1,), (1,)), ((), ())), preferred_element_type=F32)


def dot_tn(a, b):
    return lax.dot_general(a, b, (((0,), (0,)), ((), ())), preferred_element_type=F32)


def exact_dot(a, b):
    return lax.dot_general(
        a,
        b,
        (((1,), (0,)), ((), ())),
        precision=lax.Precision.HIGHEST,
        preferred_element_type=F32,
    )


def exact_dot_tn(a, b):
    return lax.dot_general(
        a,
        b,
        (((0,), (0,)), ((), ())),
        precision=lax.Precision.HIGHEST,
        preferred_element_type=F32,
    )


def normalized(values):
    centred = values - jnp.mean(values, -1, keepdims=True)
    spread = jnp.mean(centred * centred, -1, keepdims=True)
    scale = lax.rsqrt(spread + EPSILON)
    return centred * scale, scale


def norm_back(hat, scale, grad):
    along = jnp.mean(grad * hat, -1, keepdims=True)
    return scale * (grad - jnp.mean(grad, -1, keepdims=True) - hat * along)


def gelu_both(u):
    c = 0.7978845608028654
    square = u * u
    t = jnp.tanh(c * u * (1.0 + 0.044715 * square))
    half = 0.5 + 0.5 * t
    slope = half + (0.5 * c) * u * (1.0 - t * t) * (1.0 + (3 * 0.044715) * square)
    return u * half, slope


def column_sum(values):
    return jnp.sum(values.astype(F32), 0, keepdims=True)


def softmax(scores):
    e = jnp.exp(scores - jnp.max(scores, -1, keepdims=True))
    return (e * (1.0 / jnp.sum(e, -1, keepdims=True))).astype(BF)


def layers_kernel(
    sizes,
    emb,
    cot,
    seg,
    tpos,
    wqkv_h,
    wout_h,
    wup_h,
    wdown_h,
    small,
    sec,
    fa1,
    fdj,
    fo,
    fdhr,
    fa2,
    fdu,
    fg,
    fdm,
    sg,
    wqkv,
    wout,
    wup,
    wdown,
    xin,
    yb,
    dyb,
    jn,
    pr,
    hm,
    slope,
    a1,
    ob,
    a2,
    gb,
    dm,
    dub,
    dhr,
    djb,
    da,
    dob,
    cap,
    lat,
    thg,
    lx,
    lq,
    lp,
    lh,
    la2,
    lo,
    lg,
    lslope,
    wsem,
    osem,
    ysend,
    yrecv,
    gsend,
    grecv,
    lsend,
    lrecv,
    tsend,
    trecv,
):
    rows, length, width, inner, thoughts = sizes
    blocks = inner // width
    bd = BU + blocks
    pairs = HEADS // 2
    me = lax.axis_index("pipe")
    other = 1 - me

    weights = [
        pltpu.make_async_copy(source.at[0], target, wsem.at[number])
        for number, (source, target) in enumerate(
            ((wqkv_h, wqkv), (wout_h, wout), (wup_h, wup), (wdown_h, wdown))
        )
    ]
    for copy in weights:
        copy.start()
    barrier = pltpu.get_barrier_semaphore()
    pl.semaphore_signal(barrier, inc=1, device_id={"pipe": other}, device_id_type=MESH)
    pl.semaphore_wait(barrier, 1)
    sg[...] = jnp.zeros_like(sg)

    def remote(source, target, send, recv):
        return pltpu.make_async_remote_copy(
            src_ref=source,
            dst_ref=target,
            send_sem=send,
            recv_sem=recv,
            device_id={"pipe": other},
            device_id_type=MESH,
        )

    def send_y(k):
        return remote(yb.at[k], xin.at[k], ysend.at[k], yrecv.at[k])

    def send_grad(k):
        return remote(yb.at[k], dyb.at[k], gsend.at[k], grecv.at[k])

    def send_lat(r):
        return remote(lat.at[r], lat.at[r], lsend.at[r], lrecv.at[r])

    def send_thoughts(r):
        return remote(thg.at[r], thg.at[r], tsend.at[r], trecv.at[r])

    def started(source, target, number):
        copy = pltpu.make_async_copy(source, target, osem.at[number])
        copy.start()
        return copy

    def finish(copies):
        for copy in copies:
            copy.wait()

    def each_chunk(step):
        def body(i, carry):
            step(pl.ds(pl.multiple_of(i * CHUNK, CHUNK), CHUNK), i * CHUNK)
            return carry

        lax.fori_loop(0, length // CHUNK, body, 0)

    def row(number):
        return small[number : number + 1, :]

    def group(number):
        return slice(number * width, (number + 1) * width)

    lane = lax.broadcasted_iota(jnp.int32, (1, 128), 1)
    low = lane < 64
    halves = (jnp.where(low, 1.0, 0.0).astype(BF), jnp.where(low, 0.0, 1.0).astype(BF))

    def first_length(r):
        segment = seg[pl.ds(r, 1), :]
        return jnp.sum(jnp.where(segment == 0, 1.0, 0.0), -1, keepdims=True).astype(jnp.int32)

    def set_cap(r):
        first = first_length(r)
        query = lax.broadcasted_iota(jnp.int32, (length, length), 0)
        key = lax.broadcasted_iota(jnp.int32, (length, length), 1)
        lowest = jnp.where(query >= first, first, 0)
        cap[...] = jnp.where((key <= query) & (key >= lowest), NO_CAP, MASKED)

    def positions(r, shift):
        number = lax.broadcasted_iota(jnp.int32, (LAT, 1), 0)
        result = jnp.full((LAT, 1), -1, jnp.int32)
        for j in range(thoughts):
            result = jnp.where(number == j, tpos[r, j] - shift, result)
        return result

    def selector(place):
        return jnp.where(lax.broadcasted_iota(jnp.int32, (LAT, length), 1) == place, 1.0, 0.0)

    def unmarked(r, start):
        place = lax.broadcasted_iota(jnp.int32, (CHUNK, 1), 0) + start
        keep = jnp.ones((CHUNK, 1), F32)
        for j in range(thoughts):
            keep = jnp.where(place == tpos[r, j], 0.0, keep)
        return keep

    def head_lanes(part, hp):
        return pl.ds(pl.multiple_of(part * width + hp * 128, 128), 128)

    def norm_one(x):
        def step(part, _):
            hat, _ = normalized(x[part, :])
            a1[part, :] = (hat * row(G1) + row(B1)).astype(BF)

        each_chunk(step)

    def forward(k, x, y, first=None):
        def need(number):
            if first is not None:

                @pl.when(first)
                def _():
                    weights[number].wait()

        norm_one(x)
        copies = [started(a1, fa1.at[k], 0)]
        need(0)
        for part, bias in ((0, BQ), (1, None), (2, BV)):
            joined = dot(a1[...], wqkv[:, group(part)])
            if bias is not None:
                joined = joined + row(bias)
            jn[k, :, group(part)] = joined.astype(BF)

        def heads(hp, carry):
            q = jn[k, :, head_lanes(0, hp)]
            key = jn[k, :, head_lanes(1, hp)]
            value = jn[k, :, head_lanes(2, hp)]
            out = []
            for h in range(2):
                scores = dot_nt(q * (halves[h] * 0.125), key)
                chance = softmax(jnp.minimum(scores, cap[...]))
                pr[k, 2 * hp + h] = chance
                out.append(dot(chance, value))
            ob[:, head_lanes(0, hp)] = jnp.where(low, out[0], out[1]).astype(BF)
            return carry

        lax.fori_loop(0, pairs, heads, 0)
        copies.append(started(ob, fo.at[k], 1))
        need(1)
        hm[k] = x[...] + dot(ob[...], wout[...]) + row(BO)

        def step(part, _):
            hat, _ = normalized(hm[k, part, :])
            a2[part, :] = (hat * row(G2) + row(B2)).astype(BF)
            y[part, :] = hm[k, part, :] + row(bd)

        each_chunk(step)
        copies.append(started(a2, fa2.at[k], 2))
        need(2)
        need(3)

        def mlp(c, carry):
            part = pl.ds(pl.multiple_of(c * width, width), width)
            u = dot(a2[...], wup[:, part]) + small[pl.ds(BU + c, 1), :]
            g, d = gelu_both(u)
            gb[:, part] = g.astype(BF)
            slope[k, :, part] = d.astype(BF)
            y[...] += dot(gb[:, part], wdown[part, :])
            return carry

        lax.fori_loop(0, blocks, mlp, 0)
        copies.append(started(gb, fg.at[k], 3))
        return copies

    def backward(k, x, dy, dx):
        def step(part, _):
            branch = dy[part, :].astype(BF)
            dm[part, :] = branch
            sg[bd : bd + 1, :] += column_sum(branch)

        each_chunk(step)
        copies = [started(dm, fdm.at[k], 4)]
        da[...] = jnp.zeros_like(da)

        def mlp(c, carry):
            part = pl.ds(pl.multiple_of(c * width, width), width)
            grad = (dot_nt(dm[...], wdown[part, :]) * slope[k, :, part]).astype(BF)
            dub[:, part] = grad
            sg[pl.ds(BU + c, 1), :] += column_sum(grad)
            da[...] += dot_nt(grad, wup[:, part])
            return carry

        lax.fori_loop(0, blocks, mlp, 0)
        copies.append(started(dub, fdu.at[k], 5))

        def step_two(part, _):
            hat, scale = normalized(hm[k, part, :])
            grad = da[part, :]
            sg[G2 : G2 + 1, :] += column_sum(grad * hat)
            sg[B2 : B2 + 1, :] += column_sum(grad)
            middle = dy[part, :] + norm_back(hat, scale, grad * row(G2))
            dy[part, :] = middle
            branch = middle.astype(BF)
            dhr[part, :] = branch
            sg[BO : BO + 1, :] += column_sum(branch)

        each_chunk(step_two)
        copies.append(started(dhr, fdhr.at[k], 6))
        dob[...] = dot_nt(dhr[...], wout[...]).astype(BF)

        def heads(hp, carry):
            q = jn[k, :, head_lanes(0, hp)]
            key = jn[k, :, head_lanes(1, hp)]
            value = jn[k, :, head_lanes(2, hp)]
            grad_out = dob[:, head_lanes(0, hp)]
            dq, dk, dv = [], [], []
            for h in range(2):
                chance = pr[k, 2 * hp + h]
                grad_chance = dot_nt(grad_out * halves[h], value)
                chance_full = chance.astype(F32)
                inner_part = chance_full * grad_chance
                total = jnp.sum(inner_part, -1, keepdims=True)
                grad_scores = (inner_part - chance_full * total).astype(BF)
                dq.append(dot(grad_scores, key))
                dk.append(dot_tn(grad_scores, q))
                dv.append(dot_tn(chance, grad_out))
            djb[:, head_lanes(0, hp)] = (jnp.where(low, dq[0], dq[1]) * 0.125).astype(BF)
            djb[:, head_lanes(1, hp)] = (jnp.where(low, dk[0], dk[1]) * 0.125).astype(BF)
            djb[:, head_lanes(2, hp)] = jnp.where(low, dv[0], dv[1]).astype(BF)
            return carry

        lax.fori_loop(0, pairs, heads, 0)
        copies.append(started(djb, fdj.at[k], 7))
        into_input(x, dy, dx)
        return copies

    def into_input(x, middle, dx):
        sg[BQ : BQ + 1, :] += column_sum(djb[:, group(0)])
        sg[BV : BV + 1, :] += column_sum(djb[:, group(2)])
        da[...] = dot_nt(djb[...], wqkv[...])

        def step(part, _):
            hat, scale = normalized(x[part, :])
            grad = da[part, :]
            sg[G1 : G1 + 1, :] += column_sum(grad * hat)
            sg[B1 : B1 + 1, :] += column_sum(grad)
            dx[part, :] = middle[part, :] + norm_back(hat, scale, grad * row(G1))

        each_chunk(step)

    def forward_latent(r):
        x = xin.at[r]
        norm_one(x)
        copies = [started(a1, fa1.at[r], 0)]
        jn[r, :, group(1)] = dot(a1[...], wqkv[:, group(1)]).astype(BF)
        jn[r, :, group(2)] = (dot(a1[...], wqkv[:, group(2)]) + row(BV)).astype(BF)
        place = positions(r, 1)
        chosen = exact_dot(selector(place), x[...])
        lx[r] = chosen
        hat, _ = normalized(chosen)
        normed = (hat * row(G1) + row(B1)).astype(BF)
        lq[r] = (dot(normed, wqkv[:, group(0)]) + row(BQ)).astype(BF)
        first = first_length(r)
        key_place = lax.broadcasted_iota(jnp.int32, (LAT, length), 1)
        lowest = jnp.where(place >= first, first, 0)
        limit = jnp.where((key_place <= place) & (key_place >= lowest), NO_CAP, MASKED)

        def heads(hp, carry):
            q = lq[r, :, head_lanes(0, hp)]
            key = jn[r, :, head_lanes(1, hp)]
            value = jn[r, :, head_lanes(2, hp)]
            out = []
            for h in range(2):
                scores = dot_nt(q * (halves[h] * 0.125), key)
                chance = softmax(jnp.minimum(scores, limit))
                lp[r, 2 * hp + h] = chance
                out.append(dot(chance, value))
            lo[r, :, head_lanes(0, hp)] = jnp.where(low, out[0], out[1]).astype(BF)
            return carry

        lax.fori_loop(0, pairs, heads, 0)
        middle = chosen + dot(lo[r], wout[...]) + row(BO)
        lh[r] = middle
        hat, _ = normalized(middle)
        la2[r] = (hat * row(G2) + row(B2)).astype(BF)
        lat[r] = middle + row(bd)

        def mlp(c, carry):
            part = pl.ds(pl.multiple_of(c * width, width), width)
            u = dot(la2[r], wup[:, part]) + small[pl.ds(BU + c, 1), :]
            g, d = gelu_both(u)
            lg[r, :, part] = g.astype(BF)
            lslope[r, :, part] = d.astype(BF)
            lat[r] += dot(lg[r, :, part], wdown[part, :])
            return carry

        lax.fori_loop(0, blocks, mlp, 0)
        return copies

    def backward_latent(r, dx):
        grad_result = thg[r]
        branch = grad_result.astype(BF)
        top = slice(0, LAT)
        sg[bd : bd + 1, :] += column_sum(branch)
        dm[top, :] = branch
        a2[top, :] = la2[r]
        ob[top, :] = lo[r]
        gb[top, :] = lg[r]
        copies = [
            started(dm, fdm.at[r], 4),
            started(a2, fa2.at[r], 2),
            started(ob, fo.at[r], 1),
            started(gb, fg.at[r], 3),
        ]
        da[top, :] = jnp.zeros((LAT, width), F32)

        def mlp(c, carry):
            part = pl.ds(pl.multiple_of(c * width, width), width)
            grad = (dot_nt(dm[top, :], wdown[part, :]) * lslope[r, :, part]).astype(BF)
            dub[top, part] = grad
            sg[pl.ds(BU + c, 1), :] += column_sum(grad)
            da[top, :] += dot_nt(grad, wup[:, part])
            return carry

        lax.fori_loop(0, blocks, mlp, 0)
        copies.append(started(dub, fdu.at[r], 5))
        hat, scale = normalized(lh[r])
        grad = da[top, :]
        sg[G2 : G2 + 1, :] += column_sum(grad * hat)
        sg[B2 : B2 + 1, :] += column_sum(grad)
        middle = grad_result + norm_back(hat, scale, grad * row(G2))
        rounded = middle.astype(BF)
        dhr[top, :] = rounded
        sg[BO : BO + 1, :] += column_sum(rounded)
        copies.append(started(dhr, fdhr.at[r], 6))
        place = positions(r, 1)
        chosen = selector(place)
        dyb[r] = exact_dot_tn(chosen, middle)
        dob[top, :] = dot_nt(rounded, wout[...]).astype(BF)

        def heads(hp, carry):
            q = lq[r, :, head_lanes(0, hp)]
            key = jn[r, :, head_lanes(1, hp)]
            value = jn[r, :, head_lanes(2, hp)]
            grad_out = dob[top, head_lanes(0, hp)]
            dq, dk, dv = [], [], []
            for h in range(2):
                chance = lp[r, 2 * hp + h]
                grad_chance = dot_nt(grad_out * halves[h], value)
                chance_full = chance.astype(F32)
                inner_part = chance_full * grad_chance
                total = jnp.sum(inner_part, -1, keepdims=True)
                grad_scores = (inner_part - chance_full * total).astype(BF)
                dq.append(dot(grad_scores, key))
                dk.append(dot_tn(grad_scores, q))
                dv.append(dot_tn(chance, grad_out))
            grad_q = (jnp.where(low, dq[0], dq[1]) * 0.125).astype(BF)
            djb[:, head_lanes(0, hp)] = dot_tn(chosen.astype(BF), grad_q).astype(BF)
            djb[:, head_lanes(1, hp)] = (jnp.where(low, dk[0], dk[1]) * 0.125).astype(BF)
            djb[:, head_lanes(2, hp)] = jnp.where(low, dv[0], dv[1]).astype(BF)
            return carry

        lax.fori_loop(0, pairs, heads, 0)
        copies.append(started(djb, fdj.at[r], 7))
        into_input(xin.at[r], dyb.at[r], dx)
        return copies

    @pl.when(me == 0)
    def _():
        def forward_step(k, carry):
            r = lax.rem(k, rows)
            set_cap(r)

            @pl.when(k < rows)
            def _():
                xin[k] = emb[r].astype(F32)

            @pl.when(k >= rows)
            def _():
                send_lat(r).wait_recv()
                placed = exact_dot_tn(selector(positions(r, 0)), lat[r])
                xin[k] = placed

                def step(part, start):
                    xin[k, part, :] += emb[r, part, :].astype(F32) * unmarked(r, start)

                each_chunk(step)

            copies = forward(k, xin.at[k], yb.at[k], first=k == 0)
            send_y(k).start()
            finish(copies)
            return carry

        lax.fori_loop(0, 2 * rows, forward_step, 0)

        def backward_step(i, carry):
            k = lax.rem(i + rows, 2 * rows)
            r = lax.rem(i, rows)
            send_y(k).wait_send()
            send_grad(k).wait_recv()
            copies = backward(k, xin.at[k], dyb.at[k], yb.at[k])

            @pl.when(i < rows)
            def _():
                thg[r] = exact_dot(selector(positions(r, 0)), yb[k])
                send_thoughts(r).start()

            @pl.when(i >= rows)
            def _():
                def step(part, start):
                    yb[k, part, :] += yb[rows + r, part, :] * unmarked(r, start)

                each_chunk(step)
                started(yb.at[k], sec.at[0, r], 8).wait()

            finish(copies)
            return carry

        lax.fori_loop(0, 2 * rows, backward_step, 0)

        def drain(r, carry):
            send_thoughts(r).wait_send()
            return carry

        lax.fori_loop(0, rows, drain, 0)

    @pl.when(me == 1)
    def _():
        finish(weights)

        def latent_step(r, carry):
            send_y(r).wait_recv()
            copies = forward_latent(r)
            send_lat(r).start()
            finish(copies)
            return carry

        lax.fori_loop(0, rows, latent_step, 0)

        def language_step(r, carry):
            k = rows + r
            set_cap(r)
            send_y(k).wait_recv()
            copies = forward(k, xin.at[k], dyb.at[k])
            copies.append(started(dyb.at[k], sec.at[0, r], 8))
            dyb[r] = cot[r].astype(F32)
            copies += backward(k, xin.at[k], dyb.at[r], yb.at[k])
            send_grad(k).start()
            finish(copies)
            return carry

        lax.fori_loop(0, rows, language_step, 0)
        for staged in (dm, a2, ob, gb, dub, dhr):
            staged[...] = jnp.zeros_like(staged)

        def latent_back_step(r, carry):
            send_thoughts(r).wait_recv()
            copies = backward_latent(r, yb.at[r])
            send_grad(r).start()
            finish(copies)
            return carry

        lax.fori_loop(0, rows, latent_back_step, 0)

        def drain(r, carry):
            send_lat(r).wait_send()
            send_grad(r).wait_send()
            send_grad(rows + r).wait_send()
            return carry

        lax.fori_loop(0, rows, drain, 0)


def layers(emb, cot, seg, tpos, w_qkv, w_out, w_up, w_down, small):
    rows, length, width = emb.shape
    inner = w_up.shape[2]
    thoughts = tpos.shape[1]
    slots = 2 * rows
    packed = small.shape[0]
    vmem = pl.BlockSpec(memory_space=pltpu.VMEM)
    anywhere = pl.BlockSpec(memory_space=pl.ANY)
    smem = pl.BlockSpec(memory_space=pltpu.SMEM)

    def factor(columns):
        return jax.ShapeDtypeStruct((slots, length, columns), BF)

    def block(columns, kind=BF):
        return pltpu.VMEM((length, columns), kind)

    def few(columns, kind=BF):
        return pltpu.VMEM((rows, LAT, columns), kind)

    sizes = (rows, length, width, inner, thoughts)
    return pl.pallas_call(
        functools.partial(layers_kernel, sizes),
        out_shape=(
            jax.ShapeDtypeStruct((1, rows, length, width), F32),
            factor(width),
            factor(3 * width),
            factor(width),
            factor(width),
            factor(width),
            factor(inner),
            factor(inner),
            factor(width),
            jax.ShapeDtypeStruct((packed, width), F32),
        ),
        in_specs=[vmem, vmem, vmem, smem] + [anywhere] * 4 + [vmem],
        out_specs=(anywhere,) * 9 + (vmem,),
        scratch_shapes=[
            pltpu.VMEM((width, 3 * width), BF),
            pltpu.VMEM((width, width), BF),
            pltpu.VMEM((width, inner), BF),
            pltpu.VMEM((inner, width), BF),
            pltpu.VMEM((slots, length, width), F32),
            pltpu.VMEM((slots, length, width), F32),
            pltpu.VMEM((slots, length, width), F32),
            pltpu.VMEM((slots, length, 3 * width), BF),
            pltpu.VMEM((slots, HEADS, length, length), BF),
            pltpu.VMEM((slots, length, width), F32),
            pltpu.VMEM((slots, length, inner), BF),
            block(width),
            block(width),
            block(width),
            block(inner),
            block(width),
            block(inner),
            block(width),
            block(3 * width),
            block(width, F32),
            block(width),
            block(length, F32),
            few(width, F32),
            few(width, F32),
            few(width, F32),
            few(width),
            pltpu.VMEM((rows, HEADS, LAT, length), BF),
            few(width, F32),
            few(width),
            few(width),
            few(inner),
            few(inner),
            pltpu.SemaphoreType.DMA((4,)),
            pltpu.SemaphoreType.DMA((9,)),
        ]
        + [pltpu.SemaphoreType.DMA((slots,))] * 4
        + [pltpu.SemaphoreType.DMA((rows,))] * 4,
        compiler_params=pltpu.CompilerParams(
            collective_id=0, has_side_effects=True, vmem_limit_bytes=62 << 20
        ),
    )(emb, cot, seg, tpos, w_qkv, w_out, w_up, w_down, small)


def summed_by_parts(factors, small_grads):
    fa1, fdj, fo, fdhr, fa2, fdu, fg, fdm = factors

    def product(left, right):
        whole = jnp.einsum("ktm,ktn->mn", left, right, preferred_element_type=F32)
        return lax.psum_scatter(whole[None], "dp", scatter_dimension=1, tiled=True)

    small = lax.psum_scatter(
        small_grads.reshape(1, -1), "dp", scatter_dimension=1, tiled=True
    )
    return product(fa1, fdj), product(fo, fdhr), product(fa2, fdu), product(fg, fdm), small


def per_device(
    embeddings, cotangent, seg_ids, thought_pos, w_qkv, w_out, w_up, w_down, small_params
):
    width = embeddings.shape[2]
    small = small_params.reshape(-1, width)
    section_out, *factors, small_grads = layers(
        embeddings, cotangent, seg_ids, thought_pos, w_qkv, w_out, w_up, w_down, small
    )
    return (section_out,) + tuple(summed_by_parts(factors, small_grads))


def solution(mesh):
    return jax.shard_map(
        per_device,
        mesh=mesh,
        in_specs=(
            P("dp", None, None),
            P("dp", None, None),
            P("dp", None),
            P("dp", None),
            P("pipe", None, None),
            P("pipe", None, None),
            P("pipe", None, None),
            P("pipe", None, None),
            P("pipe", None),
        ),
        out_specs=(
            P("pipe", "dp", None, None),
            P("pipe", "dp", None),
            P("pipe", "dp", None),
            P("pipe", "dp", None),
            P("pipe", "dp", None),
            P("pipe", "dp"),
        ),
        check_vma=False,
    )
```

```python
import functools

import jax
import jax.numpy as jnp
from jax import lax
from jax.experimental import pallas as pl
from jax.experimental.pallas import tpu as pltpu
from jax.sharding import PartitionSpec as P

HEADS = 12
BF = jnp.bfloat16
F32 = jnp.float32
MESH = pl.DeviceIdType.MESH
EPSILON = 1e-05
MASKED = -1000000000.0
NO_CAP = 3e38
LAT = 16
CHUNK = 64
G1, B1, BQ, BV, BO, G2, B2, BU = 0, 1, 2, 3, 4, 5, 6, 7


def dot(a, b):
    return lax.dot_general(a, b, (((1,), (0,)), ((), ())), preferred_element_type=F32)


def dot_nt(a, b):
    return lax.dot_general(a, b, (((1,), (1,)), ((), ())), preferred_element_type=F32)


def dot_tn(a, b):
    return lax.dot_general(a, b, (((0,), (0,)), ((), ())), preferred_element_type=F32)


def exact_dot(a, b):
    return lax.dot_general(
        a,
        b,
        (((1,), (0,)), ((), ())),
        precision=lax.Precision.HIGHEST,
        preferred_element_type=F32,
    )


def exact_dot_tn(a, b):
    return lax.dot_general(
        a,
        b,
        (((0,), (0,)), ((), ())),
        precision=lax.Precision.HIGHEST,
        preferred_element_type=F32,
    )


def normalized(values):
    centred = values - jnp.mean(values, -1, keepdims=True)
    spread = jnp.mean(centred * centred, -1, keepdims=True)
    scale = lax.rsqrt(spread + EPSILON)
    return centred * scale, scale


def norm_back(hat, scale, grad):
    along = jnp.mean(grad * hat, -1, keepdims=True)
    return scale * (grad - jnp.mean(grad, -1, keepdims=True) - hat * along)


def gelu_both(u):
    c = 0.7978845608028654
    square = u * u
    t = jnp.tanh(c * u * (1.0 + 0.044715 * square))
    half = 0.5 + 0.5 * t
    slope = half + (0.5 * c) * u * (1.0 - t * t) * (1.0 + (3 * 0.044715) * square)
    return u * half, slope


def column_sum(values):
    return jnp.sum(values.astype(F32), 0, keepdims=True)


def softmax(scores):
    e = jnp.exp(scores - jnp.max(scores, -1, keepdims=True))
    return (e * (1.0 / jnp.sum(e, -1, keepdims=True))).astype(BF)


def layers_kernel(
    sizes,
    emb,
    cot,
    seg,
    tpos,
    wqkv_h,
    wout_h,
    wup_h,
    wdown_h,
    small,
    sec,
    fa1,
    fdj,
    fo,
    fdhr,
    fa2,
    fdu,
    fg,
    fdm,
    sg,
    wqkv,
    wout,
    wup,
    wdown,
    xin,
    yb,
    dyb,
    jn,
    pr,
    hm,
    slope,
    a1,
    ob,
    a2,
    gb,
    dm,
    dub,
    dhr,
    djb,
    da,
    dob,
    cap,
    lat,
    thg,
    lx,
    lq,
    lp,
    lh,
    la2,
    lo,
    lg,
    lslope,
    wsem,
    osem,
    ysend,
    yrecv,
    gsend,
    grecv,
    lsend,
    lrecv,
    tsend,
    trecv,
):
    rows, length, width, inner, thoughts = sizes
    blocks = inner // width
    bd = BU + blocks
    pairs = HEADS // 2
    me = lax.axis_index("pipe")
    other = 1 - me

    weights = [
        pltpu.make_async_copy(source.at[0], target, wsem.at[number])
        for number, (source, target) in enumerate(
            ((wqkv_h, wqkv), (wout_h, wout), (wup_h, wup), (wdown_h, wdown))
        )
    ]
    for copy in weights:
        copy.start()
    barrier = pltpu.get_barrier_semaphore()
    pl.semaphore_signal(barrier, inc=1, device_id={"pipe": other}, device_id_type=MESH)
    pl.semaphore_wait(barrier, 1)
    sg[...] = jnp.zeros_like(sg)

    def remote(source, target, send, recv):
        return pltpu.make_async_remote_copy(
            src_ref=source,
            dst_ref=target,
            send_sem=send,
            recv_sem=recv,
            device_id={"pipe": other},
            device_id_type=MESH,
        )

    def send_y(k):
        return remote(yb.at[k], xin.at[k], ysend.at[k], yrecv.at[k])

    def send_grad(k):
        return remote(yb.at[k], dyb.at[k], gsend.at[k], grecv.at[k])

    def send_lat(r):
        return remote(lat.at[r], lat.at[r], lsend.at[r], lrecv.at[r])

    def send_thoughts(r):
        return remote(thg.at[r], thg.at[r], tsend.at[r], trecv.at[r])

    def started(source, target, number):
        copy = pltpu.make_async_copy(source, target, osem.at[number])
        copy.start()
        return copy

    def finish(copies):
        for copy in copies:
            copy.wait()

    def each_chunk(step):
        def body(i, carry):
            step(pl.ds(pl.multiple_of(i * CHUNK, CHUNK), CHUNK), i * CHUNK)
            return carry

        lax.fori_loop(0, length // CHUNK, body, 0)

    def row(number):
        return small[number : number + 1, :]

    def group(number):
        return slice(number * width, (number + 1) * width)

    lane = lax.broadcasted_iota(jnp.int32, (1, 128), 1)
    low = lane < 64
    halves = (jnp.where(low, 1.0, 0.0).astype(BF), jnp.where(low, 0.0, 1.0).astype(BF))

    def first_length(r):
        segment = seg[pl.ds(r, 1), :]
        return jnp.sum(jnp.where(segment == 0, 1.0, 0.0), -1, keepdims=True).astype(jnp.int32)

    def set_cap(r):
        first = first_length(r)
        query = lax.broadcasted_iota(jnp.int32, (length, length), 0)
        key = lax.broadcasted_iota(jnp.int32, (length, length), 1)
        lowest = jnp.where(query >= first, first, 0)
        cap[...] = jnp.where((key <= query) & (key >= lowest), NO_CAP, MASKED)

    def positions(r, shift):
        number = lax.broadcasted_iota(jnp.int32, (LAT, 1), 0)
        result = jnp.full((LAT, 1), -1, jnp.int32)
        for j in range(thoughts):
            result = jnp.where(number == j, tpos[r, j] - shift, result)
        return result

    def selector(place):
        return jnp.where(lax.broadcasted_iota(jnp.int32, (LAT, length), 1) == place, 1.0, 0.0)

    def unmarked(r, start):
        place = lax.broadcasted_iota(jnp.int32, (CHUNK, 1), 0) + start
        keep = jnp.ones((CHUNK, 1), F32)
        for j in range(thoughts):
            keep = jnp.where(place == tpos[r, j], 0.0, keep)
        return keep

    def head_lanes(part, hp):
        return pl.ds(pl.multiple_of(part * width + hp * 128, 128), 128)

    def norm_one(x):
        def step(part, _):
            hat, _ = normalized(x[part, :])
            a1[part, :] = (hat * row(G1) + row(B1)).astype(BF)

        each_chunk(step)

    def forward(k, x, y, first=None):
        def need(number):
            if first is not None:

                @pl.when(first)
                def _():
                    weights[number].wait()

        norm_one(x)
        copies = [started(a1, fa1.at[k], 0)]
        need(0)
        for part, bias in ((0, BQ), (1, None), (2, BV)):
            joined = dot(a1[...], wqkv[:, group(part)])
            if bias is not None:
                joined = joined + row(bias)
            jn[k, :, group(part)] = joined.astype(BF)

        def heads(hp, carry):
            q = jn[k, :, head_lanes(0, hp)]
            key = jn[k, :, head_lanes(1, hp)]
            value = jn[k, :, head_lanes(2, hp)]
            out = []
            for h in range(2):
                scores = dot_nt(q * (halves[h] * 0.125), key)
                chance = softmax(jnp.minimum(scores, cap[...]))
                pr[k, 2 * hp + h] = chance
                out.append(dot(chance, value))
            ob[:, head_lanes(0, hp)] = jnp.where(low, out[0], out[1]).astype(BF)
            return carry

        lax.fori_loop(0, pairs, heads, 0)
        copies.append(started(ob, fo.at[k], 1))
        need(1)
        hm[k] = x[...] + dot(ob[...], wout[...]) + row(BO)

        def step(part, _):
            hat, _ = normalized(hm[k, part, :])
            a2[part, :] = (hat * row(G2) + row(B2)).astype(BF)
            y[part, :] = hm[k, part, :] + row(bd)

        each_chunk(step)
        copies.append(started(a2, fa2.at[k], 2))
        need(2)
        need(3)

        def mlp(c, carry):
            part = pl.ds(pl.multiple_of(c * width, width), width)
            u = dot(a2[...], wup[:, part]) + small[pl.ds(BU + c, 1), :]
            g, d = gelu_both(u)
            gb[:, part] = g.astype(BF)
            slope[k, :, part] = d.astype(BF)
            y[...] += dot(gb[:, part], wdown[part, :])
            return carry

        lax.fori_loop(0, blocks, mlp, 0)
        copies.append(started(gb, fg.at[k], 3))
        return copies

    def backward(k, x, dy, dx):
        def step(part, _):
            branch = dy[part, :].astype(BF)
            dm[part, :] = branch
            sg[bd : bd + 1, :] += column_sum(branch)

        each_chunk(step)
        copies = [started(dm, fdm.at[k], 4)]
        da[...] = jnp.zeros_like(da)

        def mlp(c, carry):
            part = pl.ds(pl.multiple_of(c * width, width), width)
            grad = (dot_nt(dm[...], wdown[part, :]) * slope[k, :, part]).astype(BF)
            dub[:, part] = grad
            sg[pl.ds(BU + c, 1), :] += column_sum(grad)
            da[...] += dot_nt(grad, wup[:, part])
            return carry

        lax.fori_loop(0, blocks, mlp, 0)
        copies.append(started(dub, fdu.at[k], 5))

        def step_two(part, _):
            hat, scale = normalized(hm[k, part, :])
            grad = da[part, :]
            sg[G2 : G2 + 1, :] += column_sum(grad * hat)
            sg[B2 : B2 + 1, :] += column_sum(grad)
            middle = dy[part, :] + norm_back(hat, scale, grad * row(G2))
            dy[part, :] = middle
            branch = middle.astype(BF)
            dhr[part, :] = branch
            sg[BO : BO + 1, :] += column_sum(branch)

        each_chunk(step_two)
        copies.append(started(dhr, fdhr.at[k], 6))
        dob[...] = dot_nt(dhr[...], wout[...]).astype(BF)

        def heads(hp, carry):
            q = jn[k, :, head_lanes(0, hp)]
            key = jn[k, :, head_lanes(1, hp)]
            value = jn[k, :, head_lanes(2, hp)]
            grad_out = dob[:, head_lanes(0, hp)]
            dq, dk, dv = [], [], []
            for h in range(2):
                chance = pr[k, 2 * hp + h]
                grad_chance = dot_nt(grad_out * halves[h], value)
                chance_full = chance.astype(F32)
                inner_part = chance_full * grad_chance
                total = jnp.sum(inner_part, -1, keepdims=True)
                grad_scores = (inner_part - chance_full * total).astype(BF)
                dq.append(dot(grad_scores, key))
                dk.append(dot_tn(grad_scores, q))
                dv.append(dot_tn(chance, grad_out))
            djb[:, head_lanes(0, hp)] = (jnp.where(low, dq[0], dq[1]) * 0.125).astype(BF)
            djb[:, head_lanes(1, hp)] = (jnp.where(low, dk[0], dk[1]) * 0.125).astype(BF)
            djb[:, head_lanes(2, hp)] = jnp.where(low, dv[0], dv[1]).astype(BF)
            return carry

        lax.fori_loop(0, pairs, heads, 0)
        copies.append(started(djb, fdj.at[k], 7))
        into_input(x, dy, dx)
        return copies

    def into_input(x, middle, dx):
        sg[BQ : BQ + 1, :] += column_sum(djb[:, group(0)])
        sg[BV : BV + 1, :] += column_sum(djb[:, group(2)])
        da[...] = dot_nt(djb[...], wqkv[...])

        def step(part, _):
            hat, scale = normalized(x[part, :])
            grad = da[part, :]
            sg[G1 : G1 + 1, :] += column_sum(grad * hat)
            sg[B1 : B1 + 1, :] += column_sum(grad)
            dx[part, :] = middle[part, :] + norm_back(hat, scale, grad * row(G1))

        each_chunk(step)

    def forward_latent(r):
        x = xin.at[r]
        norm_one(x)
        copies = [started(a1, fa1.at[r], 0)]
        jn[r, :, group(1)] = dot(a1[...], wqkv[:, group(1)]).astype(BF)
        jn[r, :, group(2)] = (dot(a1[...], wqkv[:, group(2)]) + row(BV)).astype(BF)
        place = positions(r, 1)
        chosen = exact_dot(selector(place), x[...])
        lx[r] = chosen
        hat, _ = normalized(chosen)
        normed = (hat * row(G1) + row(B1)).astype(BF)
        lq[r] = (dot(normed, wqkv[:, group(0)]) + row(BQ)).astype(BF)
        first = first_length(r)
        key_place = lax.broadcasted_iota(jnp.int32, (LAT, length), 1)
        lowest = jnp.where(place >= first, first, 0)
        limit = jnp.where((key_place <= place) & (key_place >= lowest), NO_CAP, MASKED)

        def heads(hp, carry):
            q = lq[r, :, head_lanes(0, hp)]
            key = jn[r, :, head_lanes(1, hp)]
            value = jn[r, :, head_lanes(2, hp)]
            out = []
            for h in range(2):
                scores = dot_nt(q * (halves[h] * 0.125), key)
                chance = softmax(jnp.minimum(scores, limit))
                lp[r, 2 * hp + h] = chance
                out.append(dot(chance, value))
            lo[r, :, head_lanes(0, hp)] = jnp.where(low, out[0], out[1]).astype(BF)
            return carry

        lax.fori_loop(0, pairs, heads, 0)
        middle = chosen + dot(lo[r], wout[...]) + row(BO)
        lh[r] = middle
        hat, _ = normalized(middle)
        la2[r] = (hat * row(G2) + row(B2)).astype(BF)
        lat[r] = middle + row(bd)

        def mlp(c, carry):
            part = pl.ds(pl.multiple_of(c * width, width), width)
            u = dot(la2[r], wup[:, part]) + small[pl.ds(BU + c, 1), :]
            g, d = gelu_both(u)
            lg[r, :, part] = g.astype(BF)
            lslope[r, :, part] = d.astype(BF)
            lat[r] += dot(lg[r, :, part], wdown[part, :])
            return carry

        lax.fori_loop(0, blocks, mlp, 0)
        return copies

    def backward_latent(r, dx):
        grad_result = thg[r]
        branch = grad_result.astype(BF)
        top = slice(0, LAT)
        sg[bd : bd + 1, :] += column_sum(branch)
        dm[top, :] = branch
        a2[top, :] = la2[r]
        ob[top, :] = lo[r]
        gb[top, :] = lg[r]
        copies = [
            started(dm, fdm.at[r], 4),
            started(a2, fa2.at[r], 2),
            started(ob, fo.at[r], 1),
            started(gb, fg.at[r], 3),
        ]
        da[top, :] = jnp.zeros((LAT, width), F32)

        def mlp(c, carry):
            part = pl.ds(pl.multiple_of(c * width, width), width)
            grad = (dot_nt(dm[top, :], wdown[part, :]) * lslope[r, :, part]).astype(BF)
            dub[top, part] = grad
            sg[pl.ds(BU + c, 1), :] += column_sum(grad)
            da[top, :] += dot_nt(grad, wup[:, part])
            return carry

        lax.fori_loop(0, blocks, mlp, 0)
        copies.append(started(dub, fdu.at[r], 5))
        hat, scale = normalized(lh[r])
        grad = da[top, :]
        sg[G2 : G2 + 1, :] += column_sum(grad * hat)
        sg[B2 : B2 + 1, :] += column_sum(grad)
        middle = grad_result + norm_back(hat, scale, grad * row(G2))
        rounded = middle.astype(BF)
        dhr[top, :] = rounded
        sg[BO : BO + 1, :] += column_sum(rounded)
        copies.append(started(dhr, fdhr.at[r], 6))
        place = positions(r, 1)
        chosen = selector(place)
        dyb[r] = exact_dot_tn(chosen, middle)
        dob[top, :] = dot_nt(rounded, wout[...]).astype(BF)

        def heads(hp, carry):
            q = lq[r, :, head_lanes(0, hp)]
            key = jn[r, :, head_lanes(1, hp)]
            value = jn[r, :, head_lanes(2, hp)]
            grad_out = dob[top, head_lanes(0, hp)]
            dq, dk, dv = [], [], []
            for h in range(2):
                chance = lp[r, 2 * hp + h]
                grad_chance = dot_nt(grad_out * halves[h], value)
                chance_full = chance.astype(F32)
                inner_part = chance_full * grad_chance
                total = jnp.sum(inner_part, -1, keepdims=True)
                grad_scores = (inner_part - chance_full * total).astype(BF)
                dq.append(dot(grad_scores, key))
                dk.append(dot_tn(grad_scores, q))
                dv.append(dot_tn(chance, grad_out))
            grad_q = (jnp.where(low, dq[0], dq[1]) * 0.125).astype(BF)
            djb[:, head_lanes(0, hp)] = dot_tn(chosen.astype(BF), grad_q).astype(BF)
            djb[:, head_lanes(1, hp)] = (jnp.where(low, dk[0], dk[1]) * 0.125).astype(BF)
            djb[:, head_lanes(2, hp)] = jnp.where(low, dv[0], dv[1]).astype(BF)
            return carry

        lax.fori_loop(0, pairs, heads, 0)
        copies.append(started(djb, fdj.at[r], 7))
        into_input(xin.at[r], dyb.at[r], dx)
        return copies

    @pl.when(me == 0)
    def _():
        def forward_step(k, carry):
            r = lax.rem(k, rows)
            set_cap(r)

            @pl.when(k < rows)
            def _():
                xin[k] = emb[r].astype(F32)

            @pl.when(k >= rows)
            def _():
                send_lat(r).wait_recv()
                placed = exact_dot_tn(selector(positions(r, 0)), lat[r])
                xin[k] = placed

                def step(part, start):
                    xin[k, part, :] += emb[r, part, :].astype(F32) * unmarked(r, start)

                each_chunk(step)

            copies = forward(k, xin.at[k], yb.at[k], first=k == 0)
            send_y(k).start()
            finish(copies)
            return carry

        lax.fori_loop(0, 2 * rows, forward_step, 0)

        def backward_step(i, carry):
            k = lax.rem(i + rows, 2 * rows)
            r = lax.rem(i, rows)
            send_y(k).wait_send()
            send_grad(k).wait_recv()
            copies = backward(k, xin.at[k], dyb.at[k], yb.at[k])

            @pl.when(i < rows)
            def _():
                thg[r] = exact_dot(selector(positions(r, 0)), yb[k])
                send_thoughts(r).start()

            @pl.when(i >= rows)
            def _():
                def step(part, start):
                    yb[k, part, :] += yb[rows + r, part, :] * unmarked(r, start)

                each_chunk(step)
                started(yb.at[k], sec.at[0, r], 8).wait()

            finish(copies)
            return carry

        lax.fori_loop(0, 2 * rows, backward_step, 0)

        def drain(r, carry):
            send_thoughts(r).wait_send()
            return carry

        lax.fori_loop(0, rows, drain, 0)

    @pl.when(me == 1)
    def _():
        finish(weights)

        def latent_step(r, carry):
            send_y(r).wait_recv()
            copies = forward_latent(r)
            send_lat(r).start()
            finish(copies)
            return carry

        lax.fori_loop(0, rows, latent_step, 0)

        def language_step(r, carry):
            k = rows + r
            set_cap(r)
            send_y(k).wait_recv()
            copies = forward(k, xin.at[k], dyb.at[k])
            copies.append(started(dyb.at[k], sec.at[0, r], 8))
            dyb[r] = cot[r].astype(F32)
            copies += backward(k, xin.at[k], dyb.at[r], yb.at[k])
            send_grad(k).start()
            finish(copies)
            return carry

        lax.fori_loop(0, rows, language_step, 0)
        for staged in (dm, a2, ob, gb, dub, dhr):
            staged[...] = jnp.zeros_like(staged)

        def latent_back_step(r, carry):
            send_thoughts(r).wait_recv()
            copies = backward_latent(r, yb.at[r])
            send_grad(r).start()
            finish(copies)
            return carry

        lax.fori_loop(0, rows, latent_back_step, 0)

        def drain(r, carry):
            send_lat(r).wait_send()
            send_grad(r).wait_send()
            send_grad(rows + r).wait_send()
            return carry

        lax.fori_loop(0, rows, drain, 0)


def layers(emb, cot, seg, tpos, w_qkv, w_out, w_up, w_down, small):
    rows, length, width = emb.shape
    inner = w_up.shape[2]
    thoughts = tpos.shape[1]
    slots = 2 * rows
    packed = small.shape[0]
    vmem = pl.BlockSpec(memory_space=pltpu.VMEM)
    anywhere = pl.BlockSpec(memory_space=pl.ANY)
    smem = pl.BlockSpec(memory_space=pltpu.SMEM)

    def factor(columns):
        return jax.ShapeDtypeStruct((slots, length, columns), BF)

    def block(columns, kind=BF):
        return pltpu.VMEM((length, columns), kind)

    def few(columns, kind=BF):
        return pltpu.VMEM((rows, LAT, columns), kind)

    sizes = (rows, length, width, inner, thoughts)
    return pl.pallas_call(
        functools.partial(layers_kernel, sizes),
        out_shape=(
            jax.ShapeDtypeStruct((1, rows, length, width), F32),
            factor(width),
            factor(3 * width),
            factor(width),
            factor(width),
            factor(width),
            factor(inner),
            factor(inner),
            factor(width),
            jax.ShapeDtypeStruct((packed, width), F32),
        ),
        in_specs=[vmem, vmem, vmem, smem] + [anywhere] * 4 + [vmem],
        out_specs=(anywhere,) * 9 + (vmem,),
        scratch_shapes=[
            pltpu.VMEM((width, 3 * width), BF),
            pltpu.VMEM((width, width), BF),
            pltpu.VMEM((width, inner), BF),
            pltpu.VMEM((inner, width), BF),
            pltpu.VMEM((slots, length, width), F32),
            pltpu.VMEM((slots, length, width), F32),
            pltpu.VMEM((slots, length, width), F32),
            pltpu.VMEM((slots, length, 3 * width), BF),
            pltpu.VMEM((slots, HEADS, length, length), BF),
            pltpu.VMEM((slots, length, width), F32),
            pltpu.VMEM((slots, length, inner), BF),
            block(width),
            block(width),
            block(width),
            block(inner),
            block(width),
            block(inner),
            block(width),
            block(3 * width),
            block(width, F32),
            block(width),
            block(length, F32),
            few(width, F32),
            few(width, F32),
            few(width, F32),
            few(width),
            pltpu.VMEM((rows, HEADS, LAT, length), BF),
            few(width, F32),
            few(width),
            few(width),
            few(inner),
            few(inner),
            pltpu.SemaphoreType.DMA((4,)),
            pltpu.SemaphoreType.DMA((9,)),
        ]
        + [pltpu.SemaphoreType.DMA((slots,))] * 4
        + [pltpu.SemaphoreType.DMA((rows,))] * 4,
        compiler_params=pltpu.CompilerParams(
            collective_id=0, has_side_effects=True, vmem_limit_bytes=62 << 20
        ),
    )(emb, cot, seg, tpos, w_qkv, w_out, w_up, w_down, small)


def summed_by_parts(factors, small_grads):
    fa1, fdj, fo, fdhr, fa2, fdu, fg, fdm = factors

    def product(left, right):
        whole = jnp.einsum("ktm,ktn->mn", left, right, preferred_element_type=F32)
        return lax.psum_scatter(whole[None], "dp", scatter_dimension=1, tiled=True)

    small = lax.psum_scatter(
        small_grads.reshape(1, -1), "dp", scatter_dimension=1, tiled=True
    )
    return product(fa1, fdj), product(fo, fdhr), product(fa2, fdu), product(fg, fdm), small


def gradients_kernel(
    sizes,
    plan,
    fa1,
    fdj,
    fo,
    fdhr,
    fa2,
    fdu,
    fg,
    fdm,
    small,
    gqkv,
    gout,
    gup,
    gdown,
    gsmall,
    left,
    right,
    wa,
    wb,
    ra,
    rb,
    rs,
    xa,
    xb,
    xs,
    ua,
    ub,
    us,
    na,
    nb,
    ns,
    lsem,
    pair_send,
    pair_recv,
    side_send,
    side_recv,
    up_send,
    up_recv,
    down_send,
    down_recv,
):
    width, narrow, depth = sizes
    me = lax.axis_index("dp")
    core = lax.rem(me, 2)
    side = lax.rem(me // 2, 2)
    level = me // 4
    partner = me + 1 - 2 * core
    beside = me + 2 - 4 * side
    above, below = me + 4, me - 4

    def remote(source, target, send, recv, device):
        return pltpu.make_async_remote_copy(
            src_ref=source,
            dst_ref=target,
            send_sem=send,
            recv_sem=recv,
            device_id={"dp": device},
            device_id_type=MESH,
        )

    lefts = {"qkv": fa1, "out": fo, "up": fa2, "down": fg}
    rights = {"qkv": fdj, "out": fdhr, "up": fdu, "down": fdm}
    steps = []
    for number, (name, part) in enumerate(plan):
        if name == "down":
            steps += [(number, name, block, part, narrow) for block in range(depth)]
        elif name != "small":
            steps.append((number, name, 0, part, width))

    def loads(index):
        _, name, block, part, columns = steps[index]
        slot = index % 2
        return (
            pltpu.make_async_copy(
                lefts[name].at[:, :, block * width : (block + 1) * width],
                left.at[slot],
                lsem.at[slot, 0],
            ),
            pltpu.make_async_copy(
                rights[name].at[:, :, part * columns : (part + 1) * columns],
                right.at[slot, :, :, 0:columns],
                lsem.at[slot, 1],
            ),
        )

    def start_loads(index):
        if index < len(steps):
            for copy in loads(index):
                copy.start()

    start_loads(0)

    barrier = pltpu.get_barrier_semaphore()

    def greet(device):
        pl.semaphore_signal(barrier, inc=1, device_id={"dp": device}, device_id_type=MESH)

    greet(partner)
    greet(beside)

    @pl.when(level < 3)
    def _():
        greet(above)

    @pl.when(level > 0)
    def _():
        greet(below)

    pl.semaphore_wait(barrier, 2 + (level + 2) // 3 + (5 - level) // 3)

    views = []
    counts = {"a": 0, "b": 0}
    for number, (name, part) in enumerate(plan):
        if name == "small":
            views.append((small, rs, xs, us, ns, gsmall))
            continue
        kind = "b" if name == "down" else "a"
        index = counts[kind]
        counts[kind] += 1
        if kind == "a":
            target = {"qkv": gqkv, "out": gout, "up": gup}[name]
            place = target.at[0, :, part * width : (part + 1) * width]
            views.append(
                (wa.at[index % 2], ra.at[index], xa.at[index], ua.at[index], na.at[index], place)
            )
        else:
            place = gdown.at[0, :, part * narrow : (part + 1) * narrow]
            views.append((wb, rb.at[index], xb.at[index], ub.at[index], nb.at[index], place))
    total = len(plan)
    previous = {}
    last_of = {}
    for number, (name, part) in enumerate(plan):
        kind = "s" if name == "small" else "b" if name == "down" else "a"
        mine = [n for n in range(number) if ("b" if plan[n][0] == "down" else "a") == kind]
        mine = [n for n in mine if plan[n][0] != "small"]
        back = 1 if kind == "b" else 2
        previous[number] = mine[-back] if kind != "s" and len(mine) >= back else None
        last_of[number] = True
        if previous[number] is not None:
            last_of[previous[number]] = False

    def pair_copy(number):
        w, r = views[number][:2]
        return remote(
            w.at[:, :, 1 - core], r, pair_send.at[number], pair_recv.at[number], partner
        )

    def side_copy(number):
        r, x = views[number][1:3]
        return remote(
            r.at[:, 1 - side], x, side_send.at[number], side_recv.at[number], beside
        )

    def up_copy(number, goal, source=None):
        x, u = views[number][2:4]
        return remote(
            u.at[goal - 1] if source is None else source,
            u.at[goal - 1],
            up_send.at[number, goal - 1],
            up_recv.at[number, goal - 1],
            above,
        )

    def down_copy(number, goal, source=None):
        n = views[number][4]
        return remote(
            n.at[goal] if source is None else source,
            n.at[goal],
            down_send.at[number, goal],
            down_recv.at[number, goal],
            below,
        )

    position = {"step": 0}

    def produce(number):
        name, part = plan[number]
        if name != "small":
            if previous[number] is not None:
                pair_copy(previous[number]).wait_send()
            w = views[number][0]
            while position["step"] < len(steps) and steps[position["step"]][0] == number:
                index = position["step"]
                position["step"] += 1
                _, _, block, _, columns = steps[index]
                slot = index % 2
                start_loads(index + 1)
                for copy in loads(index):
                    copy.wait()
                tokens = left.shape[1] * left.shape[2]
                if name == "down":
                    product = dot_tn(
                        left[slot].reshape(tokens, width),
                        right[slot, :, :, 0:narrow].reshape(tokens, narrow),
                    )
                    w[block] = product.reshape(w.shape[1:])
                else:

                    def tile(t, carry):
                        lanes = pl.ds(pl.multiple_of(t * narrow, narrow), narrow)
                        product = dot_tn(
                            left[slot].reshape(tokens, width),
                            right[slot, :, :, lanes].reshape(tokens, narrow),
                        )
                        w[:, :, :, :, lanes] = product.reshape(w.shape[:4] + (narrow,))
                        return carry

                    lax.fori_loop(0, width // narrow, tile, 0)
        pair_copy(number).start()

    def stage_pair(number):
        w, r = views[number][:2]
        pair_copy(number).wait_recv()

        def add(z, carry):
            for s in range(2):
                r[z, s] += w[z, s, core]
            return carry

        lax.fori_loop(0, 4, add, 0)
        side_copy(number).start()

    def stage_side(number):
        r, x = views[number][1:3]
        side_copy(number).wait_recv()

        def add(z, carry):
            x[z] += r[z, side]
            return carry

        lax.fori_loop(0, 4, add, 0)

        @pl.when(level == 0)
        def _():
            for goal in (3, 2, 1):
                up_copy(number, goal, x.at[goal]).start()

        @pl.when(level == 3)
        def _():
            for goal in (0, 1, 2):
                down_copy(number, goal, x.at[goal]).start()

    def stage_line(number):
        _, _, x, u, n, place = views[number]
        for goal in (3, 2, 1):

            @pl.when((level > 0) & (goal >= level))
            def _():
                up_copy(number, goal).wait_recv()

            @pl.when((level > 0) & (goal > level))
            def _():
                u[goal - 1] += x[goal]
                up_copy(number, goal).start()

        for goal in (0, 1, 2):

            @pl.when((level < 3) & (goal <= level))
            def _():
                down_copy(number, goal).wait_recv()

            @pl.when((level < 3) & (goal < level))
            def _():
                n[goal] += x[goal]
                down_copy(number, goal).start()

        @pl.when(level > 0)
        def _():
            x[level] += u[level - 1]

        @pl.when(level < 3)
        def _():
            x[level] += n[level]

        place[...] = x[level]

    for moment in range(total + 4):
        if moment < total:
            produce(moment)
        if 0 <= moment - 1 < total:
            stage_pair(moment - 1)
        if 0 <= moment - 2 < total:
            stage_side(moment - 2)
        if 0 <= moment - 4 < total:
            stage_line(moment - 4)
    for number in range(total):
        if last_of[number]:
            pair_copy(number).wait_send()
        side_copy(number).wait_send()
        for goal in (1, 2, 3):

            @pl.when(goal > level)
            def _():
                up_copy(number, goal).wait_send()

        for goal in (0, 1, 2):

            @pl.when(goal < level)
            def _():
                down_copy(number, goal).wait_send()


def summed_in_kernel(factors, small_grads):
    fa1, fdj, fo, fdhr, fa2, fdu, fg, fdm = factors
    slots, length, width = fa1.shape
    inner = fg.shape[2]
    owners = 16
    depth = inner // width
    narrow = 256
    a_rows, b_rows = width // owners, inner // owners
    packed = small_grads.size // owners
    lanes = 128
    s_rows = -(-packed // (8 * lanes)) * 8
    small = small_grads.reshape(owners, packed)
    small = jnp.pad(small, ((0, 0), (0, s_rows * lanes - packed)))
    small = small.reshape(4, 2, 2, s_rows, lanes)
    plan = [
        ("qkv", 0),
        ("small", 0),
        ("down", 0),
        ("qkv", 1),
        ("qkv", 2),
        ("down", 1),
        ("out", 0),
        ("up", 0),
        ("down", 2),
        ("up", 1),
        ("up", 2),
        ("up", 3),
    ]
    total = len(plan)
    a_block, b_block, s_block = (a_rows, width), (b_rows, narrow), (s_rows, lanes)
    a_count = total - 1 - width // narrow
    b_count = width // narrow
    vmem = pl.BlockSpec(memory_space=pltpu.VMEM)
    anywhere = pl.BlockSpec(memory_space=pl.ANY)

    def trio(*lead):
        return [
            pltpu.VMEM((a_count,) + lead + a_block, F32),
            pltpu.VMEM((b_count,) + lead + b_block, F32),
            pltpu.VMEM(lead + s_block, F32),
        ]

    *grads, small_grad = pl.pallas_call(
        functools.partial(gradients_kernel, (width, narrow, depth), plan),
        out_shape=(
            jax.ShapeDtypeStruct((1, a_rows, 3 * width), F32),
            jax.ShapeDtypeStruct((1, a_rows, width), F32),
            jax.ShapeDtypeStruct((1, a_rows, inner), F32),
            jax.ShapeDtypeStruct((1, b_rows, width), F32),
            jax.ShapeDtypeStruct(s_block, F32),
        ),
        in_specs=[anywhere] * 8 + [vmem],
        out_specs=(vmem,) * 5,
        scratch_shapes=[
            pltpu.VMEM((2, slots, length, width), BF),
            pltpu.VMEM((2, slots, length, width), BF),
            pltpu.VMEM((2, 4, 2, 2) + a_block, F32),
            pltpu.VMEM((4, 2, 2) + b_block, F32),
        ]
        + trio(4, 2)
        + trio(4)
        + trio(3)
        + trio(3)
        + [pltpu.SemaphoreType.DMA((2, 2))]
        + [pltpu.SemaphoreType.DMA((total,))] * 4
        + [pltpu.SemaphoreType.DMA((total, 3))] * 4,
        compiler_params=pltpu.CompilerParams(
            collective_id=1, has_side_effects=True, vmem_limit_bytes=62 << 20
        ),
    )(*factors, small)
    small_grad = small_grad.reshape(1, -1)[:, :packed]
    return tuple(grads) + (small_grad,)


def reduced(factors, small_grads):
    if lax.axis_size("dp") == 16:
        return summed_in_kernel(factors, small_grads)
    return summed_by_parts(factors, small_grads)


def per_device(
    embeddings, cotangent, seg_ids, thought_pos, w_qkv, w_out, w_up, w_down, small_params
):
    width = embeddings.shape[2]
    small = small_params.reshape(-1, width)
    section_out, *factors, small_grads = layers(
        embeddings, cotangent, seg_ids, thought_pos, w_qkv, w_out, w_up, w_down, small
    )
    return (section_out,) + tuple(reduced(factors, small_grads))


def solution(mesh):
    return jax.shard_map(
        per_device,
        mesh=mesh,
        in_specs=(
            P("dp", None, None),
            P("dp", None, None),
            P("dp", None),
            P("dp", None),
            P("pipe", None, None),
            P("pipe", None, None),
            P("pipe", None, None),
            P("pipe", None, None),
            P("pipe", None),
        ),
        out_specs=(
            P("pipe", "dp", None, None),
            P("pipe", "dp", None),
            P("pipe", "dp", None),
            P("pipe", "dp", None),
            P("pipe", "dp", None),
            P("pipe", "dp"),
        ),
        check_vma=False,
    )
```

```python
import functools

import jax
import jax.numpy as jnp
from jax import lax
from jax.experimental import pallas as pl
from jax.experimental.pallas import tpu as pltpu
from jax.sharding import PartitionSpec as P

HEADS = 12
BF = jnp.bfloat16
F32 = jnp.float32
MESH = pl.DeviceIdType.MESH
EPSILON = 1e-05
MASKED = -1000000000.0
NO_CAP = 3e38
LAT = 16
CHUNK = 128
G1, B1, BQ, BV, BO, G2, B2, BU = 0, 1, 2, 3, 4, 5, 6, 7


def dot(a, b):
    return lax.dot_general(a, b, (((1,), (0,)), ((), ())), preferred_element_type=F32)


def dot_nt(a, b):
    return lax.dot_general(a, b, (((1,), (1,)), ((), ())), preferred_element_type=F32)


def dot_tn(a, b):
    return lax.dot_general(a, b, (((0,), (0,)), ((), ())), preferred_element_type=F32)


def exact_dot(a, b):
    return lax.dot_general(
        a,
        b,
        (((1,), (0,)), ((), ())),
        precision=lax.Precision.HIGHEST,
        preferred_element_type=F32,
    )


def exact_dot_tn(a, b):
    return lax.dot_general(
        a,
        b,
        (((0,), (0,)), ((), ())),
        precision=lax.Precision.HIGHEST,
        preferred_element_type=F32,
    )


def normalized(values):
    centred = values - jnp.mean(values, -1, keepdims=True)
    spread = jnp.mean(centred * centred, -1, keepdims=True)
    scale = lax.rsqrt(spread + EPSILON)
    return centred * scale, scale


def norm_back(hat, scale, grad):
    along = jnp.mean(grad * hat, -1, keepdims=True)
    return scale * (grad - jnp.mean(grad, -1, keepdims=True) - hat * along)


def gelu_both(u):
    c = 0.7978845608028654
    square = u * u
    t = jnp.tanh(c * u * (1.0 + 0.044715 * square))
    half = 0.5 + 0.5 * t
    slope = half + (0.5 * c) * u * (1.0 - t * t) * (1.0 + (3 * 0.044715) * square)
    return u * half, slope


def column_sum(values):
    return jnp.sum(values.astype(F32), 0, keepdims=True)


def softmax(scores):
    e = jnp.exp(scores - jnp.max(scores, -1, keepdims=True))
    return (e * (1.0 / jnp.sum(e, -1, keepdims=True))).astype(BF)


def layers_kernel(
    sizes,
    emb,
    cot,
    seg,
    tpos,
    wqkv_h,
    wout_h,
    wup_h,
    wdown_h,
    small,
    sec,
    fa1,
    fdj,
    fo,
    fdhr,
    fa2,
    fdu,
    fg,
    fdm,
    sg,
    wqkv,
    wout,
    wup,
    wdown,
    xin,
    yb,
    dyb,
    jn,
    pr,
    hm,
    slope,
    a1,
    ob,
    a2,
    gb,
    dm,
    dub,
    dhr,
    djb,
    da,
    dob,
    cap,
    lat,
    thg,
    lx,
    lq,
    lp,
    lh,
    la2,
    lo,
    lg,
    lslope,
    wsem,
    osem,
    ysend,
    yrecv,
    gsend,
    grecv,
    lsend,
    lrecv,
    tsend,
    trecv,
):
    rows, length, width, inner, thoughts = sizes
    blocks = inner // width
    bd = BU + blocks
    pairs = HEADS // 2
    me = lax.axis_index("pipe")
    other = 1 - me

    weights = [
        pltpu.make_async_copy(source.at[0], target, wsem.at[number])
        for number, (source, target) in enumerate(
            ((wqkv_h, wqkv), (wout_h, wout), (wup_h, wup), (wdown_h, wdown))
        )
    ]
    for copy in weights:
        copy.start()
    barrier = pltpu.get_barrier_semaphore()
    pl.semaphore_signal(barrier, inc=1, device_id={"pipe": other}, device_id_type=MESH)
    pl.semaphore_wait(barrier, 1)
    sg[...] = jnp.zeros_like(sg)

    def remote(source, target, send, recv):
        return pltpu.make_async_remote_copy(
            src_ref=source,
            dst_ref=target,
            send_sem=send,
            recv_sem=recv,
            device_id={"pipe": other},
            device_id_type=MESH,
        )

    def send_y(k):
        return remote(yb.at[k], xin.at[k], ysend.at[k], yrecv.at[k])

    def send_grad(k):
        return remote(yb.at[k], dyb.at[k], gsend.at[k], grecv.at[k])

    def send_lat(r):
        return remote(lat.at[r], lat.at[r], lsend.at[r], lrecv.at[r])

    def send_thoughts(r):
        return remote(thg.at[r], thg.at[r], tsend.at[r], trecv.at[r])

    def started(source, target, number):
        copy = pltpu.make_async_copy(source, target, osem.at[number])
        copy.start()
        return copy

    def finish(copies):
        for copy in copies:
            copy.wait()

    def each_chunk(step):
        def body(i, carry):
            step(pl.ds(pl.multiple_of(i * CHUNK, CHUNK), CHUNK), i * CHUNK)
            return carry

        lax.fori_loop(0, length // CHUNK, body, 0)

    def row(number):
        return small[:, group(number)]

    def group(number):
        return slice(number * width, (number + 1) * width)

    lane = lax.broadcasted_iota(jnp.int32, (1, 128), 1)
    low = lane < 64
    halves = (jnp.where(low, 1.0, 0.0).astype(BF), jnp.where(low, 0.0, 1.0).astype(BF))

    def first_length(r):
        segment = seg[pl.ds(r, 1), :]
        return jnp.sum(jnp.where(segment == 0, 1.0, 0.0), -1, keepdims=True).astype(jnp.int32)

    def set_cap(r):
        first = first_length(r)
        query = lax.broadcasted_iota(jnp.int32, (length, length), 0)
        key = lax.broadcasted_iota(jnp.int32, (length, length), 1)
        lowest = jnp.where(query >= first, first, 0)
        cap[...] = jnp.where((key <= query) & (key >= lowest), NO_CAP, MASKED)

    def positions(r, shift):
        number = lax.broadcasted_iota(jnp.int32, (LAT, 1), 0)
        result = jnp.full((LAT, 1), -1, jnp.int32)
        for j in range(thoughts):
            result = jnp.where(number == j, tpos[r, j] - shift, result)
        return result

    def selector(place):
        return jnp.where(lax.broadcasted_iota(jnp.int32, (LAT, length), 1) == place, 1.0, 0.0)

    def unmarked(r, start):
        place = lax.broadcasted_iota(jnp.int32, (CHUNK, 1), 0) + start
        keep = jnp.ones((CHUNK, 1), F32)
        for j in range(thoughts):
            keep = jnp.where(place == tpos[r, j], 0.0, keep)
        return keep

    def head_lanes(part, hp):
        return slice(part * width + hp * 128, part * width + (hp + 1) * 128)

    def norm_one(x):
        def step(part, _):
            hat, _ = normalized(x[part, :])
            a1[part, :] = (hat * row(G1) + row(B1)).astype(BF)

        each_chunk(step)

    def forward(k, x, y, first=None):
        def need(number):
            if first is not None:

                @pl.when(first)
                def _():
                    weights[number].wait()

        norm_one(x)
        copies = [started(a1, fa1.at[k], 0)]
        need(0)
        for part, bias in ((0, BQ), (1, None), (2, BV)):
            joined = dot(a1[...], wqkv[:, group(part)])
            if bias is not None:
                joined = joined + row(bias)
            jn[k, :, group(part)] = joined.astype(BF)

        def heads(hp):
            q = jn[k, :, head_lanes(0, hp)]
            key = jn[k, :, head_lanes(1, hp)]
            value = jn[k, :, head_lanes(2, hp)]
            out = []
            for h in range(2):
                scores = dot_nt(q * (halves[h] * 0.125), key)
                chance = softmax(jnp.minimum(scores, cap[...]))
                pr[k, 2 * hp + h] = chance
                out.append(dot(chance, value))
            ob[:, head_lanes(0, hp)] = jnp.where(low, out[0], out[1]).astype(BF)

        for hp in range(pairs):
            heads(hp)
        copies.append(started(ob, fo.at[k], 1))
        need(1)
        hm[k] = x[...] + dot(ob[...], wout[...]) + row(BO)

        def step(part, _):
            hat, _ = normalized(hm[k, part, :])
            a2[part, :] = (hat * row(G2) + row(B2)).astype(BF)
            y[part, :] = hm[k, part, :] + row(bd)

        each_chunk(step)
        copies.append(started(a2, fa2.at[k], 2))
        need(2)
        need(3)

        def mlp(c):
            part = group(c)
            u = dot(a2[...], wup[:, part]) + row(BU + c)
            g, d = gelu_both(u)
            gb[:, part] = g.astype(BF)
            slope[k, :, part] = d.astype(BF)
            y[...] += dot(gb[:, part], wdown[part, :])

        for c in range(blocks):
            mlp(c)
        copies.append(started(gb, fg.at[k], 3))
        return copies

    def backward(k, x, dy, dx):
        def step(part, _):
            branch = dy[part, :].astype(BF)
            dm[part, :] = branch
            sg[bd : bd + 1, :] += column_sum(branch)

        each_chunk(step)
        copies = [started(dm, fdm.at[k], 4)]
        da[...] = jnp.zeros_like(da)

        def mlp(c):
            part = group(c)
            grad = (dot_nt(dm[...], wdown[part, :]) * slope[k, :, part]).astype(BF)
            dub[:, part] = grad
            sg[BU + c : BU + c + 1, :] += column_sum(grad)
            da[...] += dot_nt(grad, wup[:, part])

        for c in range(blocks):
            mlp(c)
        copies.append(started(dub, fdu.at[k], 5))

        def step_two(part, _):
            hat, scale = normalized(hm[k, part, :])
            grad = da[part, :]
            sg[G2 : G2 + 1, :] += column_sum(grad * hat)
            sg[B2 : B2 + 1, :] += column_sum(grad)
            middle = dy[part, :] + norm_back(hat, scale, grad * row(G2))
            dy[part, :] = middle
            branch = middle.astype(BF)
            dhr[part, :] = branch
            sg[BO : BO + 1, :] += column_sum(branch)

        each_chunk(step_two)
        copies.append(started(dhr, fdhr.at[k], 6))
        dob[...] = dot_nt(dhr[...], wout[...]).astype(BF)

        def heads(hp):
            q = jn[k, :, head_lanes(0, hp)]
            key = jn[k, :, head_lanes(1, hp)]
            value = jn[k, :, head_lanes(2, hp)]
            grad_out = dob[:, head_lanes(0, hp)]
            dq, dk, dv = [], [], []
            for h in range(2):
                chance = pr[k, 2 * hp + h]
                grad_chance = dot_nt(grad_out * halves[h], value)
                chance_full = chance.astype(F32)
                inner_part = chance_full * grad_chance
                total = jnp.sum(inner_part, -1, keepdims=True)
                grad_scores = (inner_part - chance_full * total).astype(BF)
                dq.append(dot(grad_scores, key))
                dk.append(dot_tn(grad_scores, q))
                dv.append(dot_tn(chance, grad_out))
            djb[:, head_lanes(0, hp)] = (jnp.where(low, dq[0], dq[1]) * 0.125).astype(BF)
            djb[:, head_lanes(1, hp)] = (jnp.where(low, dk[0], dk[1]) * 0.125).astype(BF)
            djb[:, head_lanes(2, hp)] = jnp.where(low, dv[0], dv[1]).astype(BF)

        for hp in range(pairs):
            heads(hp)
        copies.append(started(djb, fdj.at[k], 7))
        into_input(x, dy, dx)
        return copies

    def into_input(x, middle, dx):
        sg[BQ : BQ + 1, :] += column_sum(djb[:, group(0)])
        sg[BV : BV + 1, :] += column_sum(djb[:, group(2)])
        da[...] = dot_nt(djb[...], wqkv[...])

        def step(part, _):
            hat, scale = normalized(x[part, :])
            grad = da[part, :]
            sg[G1 : G1 + 1, :] += column_sum(grad * hat)
            sg[B1 : B1 + 1, :] += column_sum(grad)
            dx[part, :] = middle[part, :] + norm_back(hat, scale, grad * row(G1))

        each_chunk(step)

    def forward_latent(r):
        x = xin.at[r]
        norm_one(x)
        copies = [started(a1, fa1.at[r], 0)]
        jn[r, :, group(1)] = dot(a1[...], wqkv[:, group(1)]).astype(BF)
        jn[r, :, group(2)] = (dot(a1[...], wqkv[:, group(2)]) + row(BV)).astype(BF)
        place = positions(r, 1)
        chosen = exact_dot(selector(place), x[...])
        lx[r] = chosen
        hat, _ = normalized(chosen)
        normed = (hat * row(G1) + row(B1)).astype(BF)
        lq[r] = (dot(normed, wqkv[:, group(0)]) + row(BQ)).astype(BF)
        first = first_length(r)
        key_place = lax.broadcasted_iota(jnp.int32, (LAT, length), 1)
        lowest = jnp.where(place >= first, first, 0)
        limit = jnp.where((key_place <= place) & (key_place >= lowest), NO_CAP, MASKED)

        def heads(hp):
            q = lq[r, :, head_lanes(0, hp)]
            key = jn[r, :, head_lanes(1, hp)]
            value = jn[r, :, head_lanes(2, hp)]
            out = []
            for h in range(2):
                scores = dot_nt(q * (halves[h] * 0.125), key)
                chance = softmax(jnp.minimum(scores, limit))
                lp[r, 2 * hp + h] = chance
                out.append(dot(chance, value))
            lo[r, :, head_lanes(0, hp)] = jnp.where(low, out[0], out[1]).astype(BF)

        for hp in range(pairs):
            heads(hp)
        middle = chosen + dot(lo[r], wout[...]) + row(BO)
        lh[r] = middle
        hat, _ = normalized(middle)
        la2[r] = (hat * row(G2) + row(B2)).astype(BF)
        lat[r] = middle + row(bd)

        def mlp(c):
            part = group(c)
            u = dot(la2[r], wup[:, part]) + row(BU + c)
            g, d = gelu_both(u)
            lg[r, :, part] = g.astype(BF)
            lslope[r, :, part] = d.astype(BF)
            lat[r] += dot(lg[r, :, part], wdown[part, :])

        for c in range(blocks):
            mlp(c)
        return copies

    def backward_latent(r, dx):
        grad_result = thg[r]
        branch = grad_result.astype(BF)
        top = slice(0, LAT)
        sg[bd : bd + 1, :] += column_sum(branch)
        dm[top, :] = branch
        a2[top, :] = la2[r]
        ob[top, :] = lo[r]
        gb[top, :] = lg[r]
        copies = [
            started(dm, fdm.at[r], 4),
            started(a2, fa2.at[r], 2),
            started(ob, fo.at[r], 1),
            started(gb, fg.at[r], 3),
        ]
        da[top, :] = jnp.zeros((LAT, width), F32)

        def mlp(c):
            part = group(c)
            grad = (dot_nt(dm[top, :], wdown[part, :]) * lslope[r, :, part]).astype(BF)
            dub[top, part] = grad
            sg[BU + c : BU + c + 1, :] += column_sum(grad)
            da[top, :] += dot_nt(grad, wup[:, part])

        for c in range(blocks):
            mlp(c)
        copies.append(started(dub, fdu.at[r], 5))
        hat, scale = normalized(lh[r])
        grad = da[top, :]
        sg[G2 : G2 + 1, :] += column_sum(grad * hat)
        sg[B2 : B2 + 1, :] += column_sum(grad)
        middle = grad_result + norm_back(hat, scale, grad * row(G2))
        rounded = middle.astype(BF)
        dhr[top, :] = rounded
        sg[BO : BO + 1, :] += column_sum(rounded)
        copies.append(started(dhr, fdhr.at[r], 6))
        place = positions(r, 1)
        chosen = selector(place)
        dyb[r] = exact_dot_tn(chosen, middle)
        dob[top, :] = dot_nt(rounded, wout[...]).astype(BF)

        def heads(hp):
            q = lq[r, :, head_lanes(0, hp)]
            key = jn[r, :, head_lanes(1, hp)]
            value = jn[r, :, head_lanes(2, hp)]
            grad_out = dob[top, head_lanes(0, hp)]
            dq, dk, dv = [], [], []
            for h in range(2):
                chance = lp[r, 2 * hp + h]
                grad_chance = dot_nt(grad_out * halves[h], value)
                chance_full = chance.astype(F32)
                inner_part = chance_full * grad_chance
                total = jnp.sum(inner_part, -1, keepdims=True)
                grad_scores = (inner_part - chance_full * total).astype(BF)
                dq.append(dot(grad_scores, key))
                dk.append(dot_tn(grad_scores, q))
                dv.append(dot_tn(chance, grad_out))
            grad_q = (jnp.where(low, dq[0], dq[1]) * 0.125).astype(BF)
            djb[:, head_lanes(0, hp)] = dot_tn(chosen.astype(BF), grad_q).astype(BF)
            djb[:, head_lanes(1, hp)] = (jnp.where(low, dk[0], dk[1]) * 0.125).astype(BF)
            djb[:, head_lanes(2, hp)] = jnp.where(low, dv[0], dv[1]).astype(BF)

        for hp in range(pairs):
            heads(hp)
        copies.append(started(djb, fdj.at[r], 7))
        into_input(xin.at[r], dyb.at[r], dx)
        return copies

    @pl.when(me == 0)
    def _():
        def forward_step(k, carry):
            r = lax.rem(k, rows)
            set_cap(r)

            @pl.when(k < rows)
            def _():
                xin[k] = emb[r].astype(F32)

            @pl.when(k >= rows)
            def _():
                send_lat(r).wait_recv()
                placed = exact_dot_tn(selector(positions(r, 0)), lat[r])
                xin[k] = placed

                def step(part, start):
                    xin[k, part, :] += emb[r, part, :].astype(F32) * unmarked(r, start)

                each_chunk(step)

            copies = forward(k, xin.at[k], yb.at[k], first=k == 0)
            send_y(k).start()
            finish(copies)
            return carry

        lax.fori_loop(0, 2 * rows, forward_step, 0)

        def backward_step(i, carry):
            k = lax.rem(i + rows, 2 * rows)
            r = lax.rem(i, rows)
            send_y(k).wait_send()
            send_grad(k).wait_recv()
            copies = backward(k, xin.at[k], dyb.at[k], yb.at[k])

            @pl.when(i < rows)
            def _():
                thg[r] = exact_dot(selector(positions(r, 0)), yb[k])
                send_thoughts(r).start()

            @pl.when(i >= rows)
            def _():
                def step(part, start):
                    yb[k, part, :] += yb[rows + r, part, :] * unmarked(r, start)

                each_chunk(step)
                started(yb.at[k], sec.at[0, r], 8).wait()

            finish(copies)
            return carry

        lax.fori_loop(0, 2 * rows, backward_step, 0)

        def drain(r, carry):
            send_thoughts(r).wait_send()
            return carry

        lax.fori_loop(0, rows, drain, 0)

    @pl.when(me == 1)
    def _():
        finish(weights)

        def latent_step(r, carry):
            send_y(r).wait_recv()
            copies = forward_latent(r)
            send_lat(r).start()
            finish(copies)
            return carry

        lax.fori_loop(0, rows, latent_step, 0)

        def language_step(r, carry):
            k = rows + r
            set_cap(r)
            send_y(k).wait_recv()
            copies = forward(k, xin.at[k], dyb.at[k])
            copies.append(started(dyb.at[k], sec.at[0, r], 8))
            dyb[r] = cot[r].astype(F32)
            copies += backward(k, xin.at[k], dyb.at[r], yb.at[k])
            send_grad(k).start()
            finish(copies)
            return carry

        lax.fori_loop(0, rows, language_step, 0)
        for staged in (dm, a2, ob, gb, dub, dhr):
            staged[...] = jnp.zeros_like(staged)

        def latent_back_step(r, carry):
            send_thoughts(r).wait_recv()
            copies = backward_latent(r, yb.at[r])
            send_grad(r).start()
            finish(copies)
            return carry

        lax.fori_loop(0, rows, latent_back_step, 0)

        def drain(r, carry):
            send_lat(r).wait_send()
            send_grad(r).wait_send()
            send_grad(rows + r).wait_send()
            return carry

        lax.fori_loop(0, rows, drain, 0)


def layers(emb, cot, seg, tpos, w_qkv, w_out, w_up, w_down, small):
    rows, length, width = emb.shape
    inner = w_up.shape[2]
    thoughts = tpos.shape[1]
    slots = 2 * rows
    packed = small.shape[1] // width
    vmem = pl.BlockSpec(memory_space=pltpu.VMEM)
    anywhere = pl.BlockSpec(memory_space=pl.ANY)
    smem = pl.BlockSpec(memory_space=pltpu.SMEM)

    def factor(columns):
        return jax.ShapeDtypeStruct((slots, length, columns), BF)

    def block(columns, kind=BF):
        return pltpu.VMEM((length, columns), kind)

    def few(columns, kind=BF):
        return pltpu.VMEM((rows, LAT, columns), kind)

    sizes = (rows, length, width, inner, thoughts)
    return pl.pallas_call(
        functools.partial(layers_kernel, sizes),
        out_shape=(
            jax.ShapeDtypeStruct((1, rows, length, width), F32),
            factor(width),
            factor(3 * width),
            factor(width),
            factor(width),
            factor(width),
            factor(inner),
            factor(inner),
            factor(width),
            jax.ShapeDtypeStruct((packed, width), F32),
        ),
        in_specs=[vmem, vmem, vmem, smem] + [anywhere] * 4 + [vmem],
        out_specs=(anywhere,) * 9 + (vmem,),
        scratch_shapes=[
            pltpu.VMEM((width, 3 * width), BF),
            pltpu.VMEM((width, width), BF),
            pltpu.VMEM((width, inner), BF),
            pltpu.VMEM((inner, width), BF),
            pltpu.VMEM((slots, length, width), F32),
            pltpu.VMEM((slots, length, width), F32),
            pltpu.VMEM((slots, length, width), F32),
            pltpu.VMEM((slots, length, 3 * width), BF),
            pltpu.VMEM((slots, HEADS, length, length), BF),
            pltpu.VMEM((slots, length, width), F32),
            pltpu.VMEM((slots, length, inner), BF),
            block(width),
            block(width),
            block(width),
            block(inner),
            block(width),
            block(inner),
            block(width),
            block(3 * width),
            block(width, F32),
            block(width),
            block(length, F32),
            few(width, F32),
            few(width, F32),
            few(width, F32),
            few(width),
            pltpu.VMEM((rows, HEADS, LAT, length), BF),
            few(width, F32),
            few(width),
            few(width),
            few(inner),
            few(inner),
            pltpu.SemaphoreType.DMA((4,)),
            pltpu.SemaphoreType.DMA((9,)),
        ]
        + [pltpu.SemaphoreType.DMA((slots,))] * 4
        + [pltpu.SemaphoreType.DMA((rows,))] * 4,
        compiler_params=pltpu.CompilerParams(
            collective_id=0, has_side_effects=True, vmem_limit_bytes=62 << 20
        ),
    )(emb, cot, seg, tpos, w_qkv, w_out, w_up, w_down, small)


def summed_by_parts(factors, small_grads):
    fa1, fdj, fo, fdhr, fa2, fdu, fg, fdm = factors

    def product(left, right):
        whole = jnp.einsum("ktm,ktn->mn", left, right, preferred_element_type=F32)
        return lax.psum_scatter(whole[None], "dp", scatter_dimension=1, tiled=True)

    small = lax.psum_scatter(
        small_grads.reshape(1, -1), "dp", scatter_dimension=1, tiled=True
    )
    return product(fa1, fdj), product(fo, fdhr), product(fa2, fdu), product(fg, fdm), small


def gradients_kernel(
    sizes,
    plan,
    fa1,
    fdj,
    fo,
    fdhr,
    fa2,
    fdu,
    fg,
    fdm,
    small,
    gqkv,
    gout,
    gup,
    gdown,
    gsmall,
    left,
    right,
    wa,
    wb,
    ra,
    rb,
    rs,
    xa,
    xb,
    xs,
    ua,
    ub,
    us,
    na,
    nb,
    ns,
    xl,
    ul,
    nl,
    lsem,
    pair_send,
    pair_recv,
    side_send,
    side_recv,
    up_send,
    up_recv,
    down_send,
    down_recv,
):
    width, narrow, depth = sizes
    me = lax.axis_index("dp")
    core = lax.rem(me, 2)
    side = lax.rem(me // 2, 2)
    level = me // 4
    partner = me + 1 - 2 * core
    beside = me + 2 - 4 * side
    above, below = me + 4, me - 4

    def remote(source, target, send, recv, device):
        return pltpu.make_async_remote_copy(
            src_ref=source,
            dst_ref=target,
            send_sem=send,
            recv_sem=recv,
            device_id={"dp": device},
            device_id_type=MESH,
        )

    lefts = {"qkv": fa1, "out": fo, "up": fa2, "down": fg}
    rights = {"qkv": fdj, "out": fdhr, "up": fdu, "down": fdm}
    steps = []
    for number, (name, part, _) in enumerate(plan):
        if name == "down":
            steps += [(number, name, block, part, narrow) for block in range(depth)]
        elif name != "small":
            steps.append((number, name, 0, part, width))

    def loads(index):
        _, name, block, part, columns = steps[index]
        slot = index % 2
        return (
            pltpu.make_async_copy(
                lefts[name].at[:, :, block * width : (block + 1) * width],
                left.at[slot],
                lsem.at[slot, 0],
            ),
            pltpu.make_async_copy(
                rights[name].at[:, :, part * columns : (part + 1) * columns],
                right.at[slot, :, :, 0:columns],
                lsem.at[slot, 1],
            ),
        )

    def start_loads(index):
        if index < len(steps):
            for copy in loads(index):
                copy.start()

    start_loads(0)

    barrier = pltpu.get_barrier_semaphore()

    def greet(device):
        pl.semaphore_signal(barrier, inc=1, device_id={"dp": device}, device_id_type=MESH)

    greet(partner)
    greet(beside)

    @pl.when(level < 3)
    def _():
        greet(above)

    @pl.when(level > 0)
    def _():
        greet(below)

    pl.semaphore_wait(barrier, 2 + (level + 2) // 3 + (5 - level) // 3)

    views = []
    counts = {"a": 0, "b": 0, "line": 0}
    for number, (name, part, line_first) in enumerate(plan):
        if name == "small":
            views.append((small, rs, xs, us, ns, gsmall))
            continue
        kind = "b" if name == "down" else "a"
        index = counts[kind]
        counts[kind] += 1
        if kind == "a":
            target = {"qkv": gqkv, "out": gout, "up": gup}[name]
            place = target.at[0, :, part * width : (part + 1) * width]
            if line_first:
                along = counts["line"]
                counts["line"] += 1
                further = (xl.at[along], ul.at[along], nl.at[along], place)
            else:
                along = index - counts["line"]
                further = (xa.at[along], ua.at[along], na.at[along], place)
            views.append((wa.at[index % 2], ra.at[index]) + further)
        else:
            place = gdown.at[0, :, part * narrow : (part + 1) * narrow]
            views.append((wb, rb.at[index], xb.at[index], ub.at[index], nb.at[index], place))
    total = len(plan)
    previous = {}
    last_of = {}
    for number, (name, part, _) in enumerate(plan):
        kind = "s" if name == "small" else "b" if name == "down" else "a"
        mine = [n for n in range(number) if ("b" if plan[n][0] == "down" else "a") == kind]
        mine = [n for n in mine if plan[n][0] != "small"]
        back = 1 if kind == "b" else 2
        previous[number] = mine[-back] if kind != "s" and len(mine) >= back else None
        last_of[number] = True
        if previous[number] is not None:
            last_of[previous[number]] = False

    def pair_copy(number):
        w, r = views[number][:2]
        return remote(
            w.at[:, :, 1 - core], r, pair_send.at[number], pair_recv.at[number], partner
        )

    def side_copy(number):
        r, x = views[number][1:3]
        source = r.at[level, 1 - side] if plan[number][2] else r.at[:, 1 - side]
        return remote(source, x, side_send.at[number], side_recv.at[number], beside)

    def along_line(number):
        r, x = views[number][1:3]
        return r if plan[number][2] else x

    def up_copy(number, goal, source=None):
        u = views[number][3]
        return remote(
            u.at[goal - 1] if source is None else source,
            u.at[goal - 1],
            up_send.at[number, goal - 1],
            up_recv.at[number, goal - 1],
            above,
        )

    def down_copy(number, goal, source=None):
        n = views[number][4]
        return remote(
            n.at[goal] if source is None else source,
            n.at[goal],
            down_send.at[number, goal],
            down_recv.at[number, goal],
            below,
        )

    def start_line(number):
        base = along_line(number)

        @pl.when(level == 0)
        def _():
            for goal in (3, 2, 1):
                up_copy(number, goal, base.at[goal]).start()

        @pl.when(level == 3)
        def _():
            for goal in (0, 1, 2):
                down_copy(number, goal, base.at[goal]).start()

    position = {"step": 0}

    def produce(number):
        name, part, _ = plan[number]
        if name != "small":
            if previous[number] is not None:
                pair_copy(previous[number]).wait_send()
            w = views[number][0]
            while position["step"] < len(steps) and steps[position["step"]][0] == number:
                index = position["step"]
                position["step"] += 1
                _, _, block, _, columns = steps[index]
                slot = index % 2
                start_loads(index + 1)
                for copy in loads(index):
                    copy.wait()
                tokens = left.shape[1] * left.shape[2]
                if name == "down":
                    product = dot_tn(
                        left[slot].reshape(tokens, width),
                        right[slot, :, :, 0:narrow].reshape(tokens, narrow),
                    )
                    w[block] = product.reshape(w.shape[1:])
                else:

                    def tile(t, carry):
                        lanes = pl.ds(pl.multiple_of(t * narrow, narrow), narrow)
                        product = dot_tn(
                            left[slot].reshape(tokens, width),
                            right[slot, :, :, lanes].reshape(tokens, narrow),
                        )
                        w[:, :, :, :, lanes] = product.reshape(w.shape[:4] + (narrow,))
                        return carry

                    lax.fori_loop(0, width // narrow, tile, 0)
        pair_copy(number).start()

    def stage_pair(number):
        w, r = views[number][:2]
        pair_copy(number).wait_recv()

        def add(z, carry):
            for s in range(2):
                r[z, s] += w[z, s, core]
            return carry

        lax.fori_loop(0, 4, add, 0)
        if plan[number][2]:
            start_line(number)
        else:
            side_copy(number).start()

    def stage_side(number):
        if plan[number][2]:
            return
        r, x = views[number][1:3]
        side_copy(number).wait_recv()

        def add(z, carry):
            x[z] += r[z, side]
            return carry

        lax.fori_loop(0, 4, add, 0)
        start_line(number)

    def stage_up(number, height):
        u = views[number][3]
        base = along_line(number)

        @pl.when(level == height)
        def _():
            for goal in range(3, height - 1, -1):
                up_copy(number, goal).wait_recv()
                if goal > height:
                    u[goal - 1] += base[goal]
                    up_copy(number, goal).start()

    def stage_down(number, height):
        n = views[number][4]
        base = along_line(number)

        @pl.when(level == height)
        def _():
            for goal in range(0, height + 1):
                down_copy(number, goal).wait_recv()
                if goal < height:
                    n[goal] += base[goal]
                    down_copy(number, goal).start()

    def stage_sum(number):
        u, n, place = views[number][3:]
        base = along_line(number)

        @pl.when(level > 0)
        def _():
            base[level] += u[level - 1]

        @pl.when(level < 3)
        def _():
            base[level] += n[level]

        if plan[number][2]:
            side_copy(number).start()
        else:
            place[...] = base[level]

    def stage_last(number):
        if plan[number][2]:
            r, x = views[number][1:3]
            side_copy(number).wait_recv()
            views[number][5][...] = r[level, side] + x[...]

    def at(stage, number, *more):
        if 0 <= number < total:
            stage(number, *more)

    for moment in range(total + 6):
        at(produce, moment)
        at(stage_pair, moment - 1)
        at(stage_side, moment - 2)
        for height in range(4):
            if height > 0:
                at(stage_up, moment - 2 - height, height)
            if height < 3:
                at(stage_down, moment - 5 + height, height)
        at(stage_sum, moment - 5)
        at(stage_last, moment - 6)
    for number in range(total):
        if last_of[number]:
            pair_copy(number).wait_send()
        side_copy(number).wait_send()
        for goal in (1, 2, 3):

            @pl.when(goal > level)
            def _():
                up_copy(number, goal).wait_send()

        for goal in (0, 1, 2):

            @pl.when(goal < level)
            def _():
                down_copy(number, goal).wait_send()


def summed_in_kernel(factors, small_grads):
    fa1, fdj, fo, fdhr, fa2, fdu, fg, fdm = factors
    slots, length, width = fa1.shape
    inner = fg.shape[2]
    owners = 16
    depth = inner // width
    narrow = 256
    a_rows, b_rows = width // owners, inner // owners
    packed = small_grads.size // owners
    lanes = 128
    s_rows = -(-packed // (8 * lanes)) * 8
    small = small_grads.reshape(owners, packed)
    small = jnp.pad(small, ((0, 0), (0, s_rows * lanes - packed)))
    small = small.reshape(4, 2, 2, s_rows, lanes)
    plan = [
        ("qkv", 0, False),
        ("qkv", 1, True),
        ("small", 0, False),
        ("down", 0, False),
        ("qkv", 2, False),
        ("down", 1, False),
        ("out", 0, True),
        ("up", 0, False),
        ("down", 2, False),
        ("up", 1, False),
        ("up", 2, False),
        ("up", 3, False),
    ]
    total = len(plan)
    a_block, b_block, s_block = (a_rows, width), (b_rows, narrow), (s_rows, lanes)
    a_count = total - 1 - width // narrow
    b_count = width // narrow
    line_count = sum(line_first for _, _, line_first in plan)
    vmem = pl.BlockSpec(memory_space=pltpu.VMEM)
    anywhere = pl.BlockSpec(memory_space=pl.ANY)

    def trio(*lead):
        count = a_count if len(lead) == 2 else a_count - line_count
        return [
            pltpu.VMEM((count,) + lead + a_block, F32),
            pltpu.VMEM((b_count,) + lead + b_block, F32),
            pltpu.VMEM(lead + s_block, F32),
        ]

    *grads, small_grad = pl.pallas_call(
        functools.partial(gradients_kernel, (width, narrow, depth), plan),
        out_shape=(
            jax.ShapeDtypeStruct((1, a_rows, 3 * width), F32),
            jax.ShapeDtypeStruct((1, a_rows, width), F32),
            jax.ShapeDtypeStruct((1, a_rows, inner), F32),
            jax.ShapeDtypeStruct((1, b_rows, width), F32),
            jax.ShapeDtypeStruct(s_block, F32),
        ),
        in_specs=[anywhere] * 8 + [vmem],
        out_specs=(vmem,) * 5,
        scratch_shapes=[
            pltpu.VMEM((2, slots, length, width), BF),
            pltpu.VMEM((2, slots, length, width), BF),
            pltpu.VMEM((2, 4, 2, 2) + a_block, F32),
            pltpu.VMEM((4, 2, 2) + b_block, F32),
        ]
        + trio(4, 2)
        + trio(4)
        + trio(3)
        + trio(3)
        + [
            pltpu.VMEM((line_count,) + a_block, F32),
            pltpu.VMEM((line_count, 3, 2) + a_block, F32),
            pltpu.VMEM((line_count, 3, 2) + a_block, F32),
        ]
        + [pltpu.SemaphoreType.DMA((2, 2))]
        + [pltpu.SemaphoreType.DMA((total,))] * 4
        + [pltpu.SemaphoreType.DMA((total, 3))] * 4,
        compiler_params=pltpu.CompilerParams(
            collective_id=1, has_side_effects=True, vmem_limit_bytes=62 << 20
        ),
    )(*factors, small)
    small_grad = small_grad.reshape(1, -1)[:, :packed]
    return tuple(grads) + (small_grad,)


def reduced(factors, small_grads):
    if lax.axis_size("dp") == 16:
        return summed_in_kernel(factors, small_grads)
    return summed_by_parts(factors, small_grads)


def per_device(
    embeddings, cotangent, seg_ids, thought_pos, w_qkv, w_out, w_up, w_down, small_params
):
    section_out, *factors, small_grads = layers(
        embeddings, cotangent, seg_ids, thought_pos, w_qkv, w_out, w_up, w_down, small_params
    )
    return (section_out,) + tuple(reduced(factors, small_grads))


def solution(mesh):
    return jax.shard_map(
        per_device,
        mesh=mesh,
        in_specs=(
            P("dp", None, None),
            P("dp", None, None),
            P("dp", None),
            P("dp", None),
            P("pipe", None, None),
            P("pipe", None, None),
            P("pipe", None, None),
            P("pipe", None, None),
            P("pipe", None),
        ),
        out_specs=(
            P("pipe", "dp", None, None),
            P("pipe", "dp", None),
            P("pipe", "dp", None),
            P("pipe", "dp", None),
            P("pipe", "dp", None),
            P("pipe", "dp"),
        ),
        check_vma=False,
    )
```

```python
import functools

import jax
import jax.numpy as jnp
from jax import lax
from jax.experimental import pallas as pl
from jax.experimental.pallas import tpu as pltpu
from jax.sharding import PartitionSpec as P

HEADS = 12
BF = jnp.bfloat16
F32 = jnp.float32
MESH = pl.DeviceIdType.MESH
EPSILON = 1e-05
MASKED = -1000000000.0
NO_CAP = 3e38
LAT = 16
CHUNK = 128
G1, B1, BQ, BV, BO, G2, B2, BU = 0, 1, 2, 3, 4, 5, 6, 7


def dot(a, b):
    return lax.dot_general(a, b, (((1,), (0,)), ((), ())), preferred_element_type=F32)


def dot_nt(a, b):
    return lax.dot_general(a, b, (((1,), (1,)), ((), ())), preferred_element_type=F32)


def exact_dot(a, b):
    return lax.dot_general(
        a,
        b,
        (((1,), (0,)), ((), ())),
        precision=lax.Precision.HIGHEST,
        preferred_element_type=F32,
    )


def normalized(values):
    centred = values - jnp.mean(values, -1, keepdims=True)
    spread = jnp.mean(centred * centred, -1, keepdims=True)
    scale = lax.rsqrt(spread + EPSILON)
    return centred * scale, scale


def norm_back(hat, scale, grad):
    along = jnp.mean(grad * hat, -1, keepdims=True)
    return scale * (grad - jnp.mean(grad, -1, keepdims=True) - hat * along)


def gelu_both(u):
    c = 0.7978845608028654
    square = u * u
    t = jnp.tanh(c * u * (1.0 + 0.044715 * square))
    half = 0.5 + 0.5 * t
    slope = half + (0.5 * c) * u * (1.0 - t * t) * (1.0 + (3 * 0.044715) * square)
    return u * half, slope


def column_sum(values):
    return jnp.sum(values.astype(F32), 0, keepdims=True)


def softmax(scores, axis=-1):
    e = jnp.exp(scores - jnp.max(scores, axis, keepdims=True))
    return e * (1.0 / jnp.sum(e, axis, keepdims=True))


def layers_kernel(
    sizes,
    emb,
    cot,
    seg,
    tpos,
    wqkv_h,
    wout_h,
    wup_h,
    wdown_h,
    small,
    sec,
    fa1,
    fdj,
    fo,
    fdhr,
    fa2,
    fdu,
    fg,
    fdm,
    sg,
    wqkv,
    wout,
    wup,
    wdown,
    xin,
    yb,
    dyb,
    jn,
    ktb,
    dqt,
    capt,
    hm,
    slope,
    a1,
    ob,
    a2,
    gb,
    dm,
    dub,
    dhr,
    djb,
    da,
    dob,
    cap,
    lat,
    thg,
    lx,
    lq,
    lp,
    lh,
    la2,
    lo,
    lg,
    lslope,
    wsem,
    osem,
    ysend,
    yrecv,
    gsend,
    grecv,
    lsend,
    lrecv,
    tsend,
    trecv,
):
    rows, length, width, inner, thoughts = sizes
    blocks = inner // width
    bd = BU + blocks
    pairs = HEADS // 2
    me = lax.axis_index("pipe")
    other = 1 - me

    weights = [
        pltpu.make_async_copy(source.at[0], target, wsem.at[number])
        for number, (source, target) in enumerate(
            ((wqkv_h, wqkv), (wout_h, wout), (wup_h, wup), (wdown_h, wdown))
        )
    ]
    for copy in weights:
        copy.start()
    barrier = pltpu.get_barrier_semaphore()
    pl.semaphore_signal(barrier, inc=1, device_id={"pipe": other}, device_id_type=MESH)
    pl.semaphore_wait(barrier, 1)
    sg[...] = jnp.zeros_like(sg)

    def remote(source, target, send, recv):
        return pltpu.make_async_remote_copy(
            src_ref=source,
            dst_ref=target,
            send_sem=send,
            recv_sem=recv,
            device_id={"pipe": other},
            device_id_type=MESH,
        )

    def send_y(k):
        return remote(yb.at[k], xin.at[k], ysend.at[k], yrecv.at[k])

    def send_grad(k):
        return remote(yb.at[k], dyb.at[k], gsend.at[k], grecv.at[k])

    def send_lat(r):
        return remote(lat.at[r], lat.at[r], lsend.at[r], lrecv.at[r])

    def send_thoughts(r):
        return remote(thg.at[r], thg.at[r], tsend.at[r], trecv.at[r])

    def started(source, target, number):
        copy = pltpu.make_async_copy(source, target, osem.at[number])
        copy.start()
        return copy

    def finish(copies):
        for copy in copies:
            copy.wait()

    def each_chunk(step):
        def body(i, carry):
            step(pl.ds(pl.multiple_of(i * CHUNK, CHUNK), CHUNK), i * CHUNK)
            return carry

        lax.fori_loop(0, length // CHUNK, body, 0)

    def row(number):
        return small[:, group(number)]

    def group(number):
        return slice(number * width, (number + 1) * width)

    lane = lax.broadcasted_iota(jnp.int32, (1, 128), 1)
    low = lane < 64
    halves = (jnp.where(low, 1.0, 0.0).astype(BF), jnp.where(low, 0.0, 1.0).astype(BF))

    def first_length(r):
        segment = seg[pl.ds(r, 1), :]
        return jnp.sum(jnp.where(segment == 0, 1.0, 0.0), -1, keepdims=True).astype(jnp.int32)

    def set_cap(r):
        first = first_length(r)
        query = lax.broadcasted_iota(jnp.int32, (length, length), 0)
        key = lax.broadcasted_iota(jnp.int32, (length, length), 1)
        lowest = jnp.where(query >= first, first, 0)
        cap[...] = jnp.where((key <= query) & (key >= lowest), NO_CAP, MASKED)

    def set_cap_turned(r):
        first = first_length(r)
        key = lax.broadcasted_iota(jnp.int32, (length, length), 0)
        query = lax.broadcasted_iota(jnp.int32, (length, length), 1)
        lowest = jnp.where(query >= first, first, 0)
        capt[...] = jnp.where((key <= query) & (key >= lowest), NO_CAP, MASKED)

    def positions(r, shift, axis=0):
        shape = (LAT, 1) if axis == 0 else (1, LAT)
        number = lax.broadcasted_iota(jnp.int32, shape, axis)
        result = jnp.full(shape, -1, jnp.int32)
        for j in range(thoughts):
            result = jnp.where(number == j, tpos[r, j] - shift, result)
        return result

    def selector_turned(r, shift):
        place = positions(r, shift, 1)
        return jnp.where(lax.broadcasted_iota(jnp.int32, (length, LAT), 0) == place, 1.0, 0.0)

    def selector(place):
        return jnp.where(lax.broadcasted_iota(jnp.int32, (LAT, length), 1) == place, 1.0, 0.0)

    def unmarked(r, start):
        place = lax.broadcasted_iota(jnp.int32, (CHUNK, 1), 0) + start
        keep = jnp.ones((CHUNK, 1), F32)
        for j in range(thoughts):
            keep = jnp.where(place == tpos[r, j], 0.0, keep)
        return keep

    def head_lanes(part, hp):
        return slice(part * width + hp * 128, part * width + (hp + 1) * 128)

    def norm_one(x):
        def step(part, _):
            hat, _ = normalized(x[part, :])
            a1[part, :] = (hat * row(G1) + row(B1)).astype(BF)

        each_chunk(step)

    def forward(k, x, y, first=None):
        def need(number):
            if first is not None:

                @pl.when(first)
                def _():
                    weights[number].wait()

        norm_one(x)
        copies = [started(a1, fa1.at[k], 0)]
        need(0)
        for part, bias in ((0, BQ), (1, None), (2, BV)):
            joined = dot(a1[...], wqkv[:, group(part)])
            if bias is not None:
                joined = joined + row(bias)
            jn[k, :, group(part)] = joined.astype(BF)

        def heads(hp):
            q = jn[k, :, head_lanes(0, hp)]
            key = jn[k, :, head_lanes(1, hp)]
            value = jn[k, :, head_lanes(2, hp)]
            out = []
            for h in range(2):
                scores = dot_nt(q * (halves[h] * 0.125), key)
                chance = softmax(jnp.minimum(scores, cap[...])).astype(BF)
                out.append(dot(chance, value))
            ob[:, head_lanes(0, hp)] = jnp.where(low, out[0], out[1]).astype(BF)

        for hp in range(pairs):
            heads(hp)
        copies.append(started(ob, fo.at[k], 1))
        need(1)
        hm[k] = x[...] + dot(ob[...], wout[...]) + row(BO)

        def step(part, _):
            hat, _ = normalized(hm[k, part, :])
            a2[part, :] = (hat * row(G2) + row(B2)).astype(BF)
            y[part, :] = hm[k, part, :] + row(bd)

        each_chunk(step)
        copies.append(started(a2, fa2.at[k], 2))
        need(2)
        need(3)

        def mlp(c):
            part = group(c)
            u = dot(a2[...], wup[:, part]) + row(BU + c)
            g, d = gelu_both(u)
            gb[:, part] = g.astype(BF)
            slope[k, :, part] = d.astype(BF)
            y[...] += dot(gb[:, part], wdown[part, :])

        for c in range(blocks):
            mlp(c)
        copies.append(started(gb, fg.at[k], 3))
        return copies

    def backward(k, x, dy, dx):
        def step(part, _):
            branch = dy[part, :].astype(BF)
            dm[part, :] = branch
            sg[bd : bd + 1, :] += column_sum(branch)

        each_chunk(step)
        copies = [started(dm, fdm.at[k], 4)]
        da[...] = jnp.zeros_like(da)

        def mlp(c):
            part = group(c)
            grad = (dot_nt(dm[...], wdown[part, :]) * slope[k, :, part]).astype(BF)
            dub[:, part] = grad
            sg[BU + c : BU + c + 1, :] += column_sum(grad)
            da[...] += dot_nt(grad, wup[:, part])

        for c in range(blocks):
            mlp(c)
        copies.append(started(dub, fdu.at[k], 5))

        def step_two(part, _):
            hat, scale = normalized(hm[k, part, :])
            grad = da[part, :]
            sg[G2 : G2 + 1, :] += column_sum(grad * hat)
            sg[B2 : B2 + 1, :] += column_sum(grad)
            middle = dy[part, :] + norm_back(hat, scale, grad * row(G2))
            dy[part, :] = middle
            branch = middle.astype(BF)
            dhr[part, :] = branch
            sg[BO : BO + 1, :] += column_sum(branch)

        each_chunk(step_two)
        copies.append(started(dhr, fdhr.at[k], 6))
        dob[...] = dot_nt(dhr[...], wout[...]).astype(BF)

        def heads(hp):
            q = jn[k, :, head_lanes(0, hp)]
            key = jn[k, :, head_lanes(1, hp)]
            value = jn[k, :, head_lanes(2, hp)]
            grad_out = dob[:, head_lanes(0, hp)]
            dk, dv = [], []
            for h in range(2):
                scores = dot_nt(key, q * (halves[h] * 0.125))
                chance = softmax(jnp.minimum(scores, capt[...]), 0)
                inner_part = chance * dot_nt(value, grad_out * halves[h])
                total = jnp.sum(inner_part, 0, keepdims=True)
                grad_scores = (inner_part - chance * total).astype(BF)
                dv.append(dot(chance.astype(BF), grad_out))
                dk.append(dot(grad_scores, q))
                head = slice((2 * hp + h) * 64, (2 * hp + h + 1) * 64)
                dqt[head, :] = (dot(ktb[head, :], grad_scores) * 0.125).astype(BF)
            djb[:, head_lanes(1, hp)] = (jnp.where(low, dk[0], dk[1]) * 0.125).astype(BF)
            djb[:, head_lanes(2, hp)] = jnp.where(low, dv[0], dv[1]).astype(BF)

        ktb[...] = jn[k, :, group(1)].T
        for hp in range(pairs):
            heads(hp)
        djb[:, group(0)] = dqt[...].T
        copies.append(started(djb, fdj.at[k], 7))
        into_input(x, dy, dx)
        return copies

    def into_input(x, middle, dx):
        sg[BQ : BQ + 1, :] += column_sum(djb[:, group(0)])
        sg[BV : BV + 1, :] += column_sum(djb[:, group(2)])
        da[...] = dot_nt(djb[...], wqkv[...])

        def step(part, _):
            hat, scale = normalized(x[part, :])
            grad = da[part, :]
            sg[G1 : G1 + 1, :] += column_sum(grad * hat)
            sg[B1 : B1 + 1, :] += column_sum(grad)
            dx[part, :] = middle[part, :] + norm_back(hat, scale, grad * row(G1))

        each_chunk(step)

    def forward_latent(r):
        x = xin.at[r]
        norm_one(x)
        copies = [started(a1, fa1.at[r], 0)]
        jn[r, :, group(1)] = dot(a1[...], wqkv[:, group(1)]).astype(BF)
        jn[r, :, group(2)] = (dot(a1[...], wqkv[:, group(2)]) + row(BV)).astype(BF)
        place = positions(r, 1)
        chosen = exact_dot(selector(place), x[...])
        lx[r] = chosen
        hat, _ = normalized(chosen)
        normed = (hat * row(G1) + row(B1)).astype(BF)
        lq[r] = (dot(normed, wqkv[:, group(0)]) + row(BQ)).astype(BF)
        first = first_length(r)
        key_place = lax.broadcasted_iota(jnp.int32, (LAT, length), 1)
        lowest = jnp.where(place >= first, first, 0)
        limit = jnp.where((key_place <= place) & (key_place >= lowest), NO_CAP, MASKED)

        def heads(hp):
            q = lq[r, :, head_lanes(0, hp)]
            key = jn[r, :, head_lanes(1, hp)]
            value = jn[r, :, head_lanes(2, hp)]
            out = []
            for h in range(2):
                scores = dot_nt(q * (halves[h] * 0.125), key)
                chance = softmax(jnp.minimum(scores, limit)).astype(BF)
                lp[r, 2 * hp + h] = chance
                out.append(dot(chance, value))
            lo[r, :, head_lanes(0, hp)] = jnp.where(low, out[0], out[1]).astype(BF)

        for hp in range(pairs):
            heads(hp)
        middle = chosen + dot(lo[r], wout[...]) + row(BO)
        lh[r] = middle
        hat, _ = normalized(middle)
        la2[r] = (hat * row(G2) + row(B2)).astype(BF)
        lat[r] = middle + row(bd)

        def mlp(c):
            part = group(c)
            u = dot(la2[r], wup[:, part]) + row(BU + c)
            g, d = gelu_both(u)
            lg[r, :, part] = g.astype(BF)
            lslope[r, :, part] = d.astype(BF)
            lat[r] += dot(lg[r, :, part], wdown[part, :])

        for c in range(blocks):
            mlp(c)
        return copies

    def backward_latent(r, dx):
        grad_result = thg[r]
        branch = grad_result.astype(BF)
        top = slice(0, LAT)
        sg[bd : bd + 1, :] += column_sum(branch)
        dm[top, :] = branch
        a2[top, :] = la2[r]
        ob[top, :] = lo[r]
        gb[top, :] = lg[r]
        copies = [
            started(dm, fdm.at[r], 4),
            started(a2, fa2.at[r], 2),
            started(ob, fo.at[r], 1),
            started(gb, fg.at[r], 3),
        ]
        da[top, :] = jnp.zeros((LAT, width), F32)

        def mlp(c):
            part = group(c)
            grad = (dot_nt(dm[top, :], wdown[part, :]) * lslope[r, :, part]).astype(BF)
            dub[top, part] = grad
            sg[BU + c : BU + c + 1, :] += column_sum(grad)
            da[top, :] += dot_nt(grad, wup[:, part])

        for c in range(blocks):
            mlp(c)
        copies.append(started(dub, fdu.at[r], 5))
        hat, scale = normalized(lh[r])
        grad = da[top, :]
        sg[G2 : G2 + 1, :] += column_sum(grad * hat)
        sg[B2 : B2 + 1, :] += column_sum(grad)
        middle = grad_result + norm_back(hat, scale, grad * row(G2))
        rounded = middle.astype(BF)
        dhr[top, :] = rounded
        sg[BO : BO + 1, :] += column_sum(rounded)
        copies.append(started(dhr, fdhr.at[r], 6))
        spread = selector_turned(r, 1)
        dyb[r] = exact_dot(spread, middle)
        place = positions(r, 1, 1)
        first = first_length(r)
        key_place = lax.broadcasted_iota(jnp.int32, (length, LAT), 0)
        lowest = jnp.where(place >= first, first, 0)
        limit = jnp.where((key_place <= place) & (key_place >= lowest), NO_CAP, MASKED)
        dob[top, :] = dot_nt(rounded, wout[...]).astype(BF)

        def heads(hp):
            q = lq[r, :, head_lanes(0, hp)]
            key = jn[r, :, head_lanes(1, hp)]
            value = jn[r, :, head_lanes(2, hp)]
            grad_out = dob[top, head_lanes(0, hp)]
            dq, dk, dv = [], [], []
            for h in range(2):
                grad_masked = grad_out * halves[h]
                chance = lp[r, 2 * hp + h].astype(F32)
                inner_part = chance * dot_nt(grad_masked, value)
                total = jnp.sum(inner_part, -1, keepdims=True)
                dq.append(dot((inner_part - chance * total).astype(BF), key))
                scores = dot_nt(key, q * (halves[h] * 0.125))
                chance = softmax(jnp.minimum(scores, limit), 0)
                inner_part = chance * dot_nt(value, grad_masked)
                total = jnp.sum(inner_part, 0, keepdims=True)
                dk.append(dot((inner_part - chance * total).astype(BF), q))
                dv.append(dot(chance.astype(BF), grad_out))
            grad_q = (jnp.where(low, dq[0], dq[1]) * 0.125).astype(BF)
            djb[:, head_lanes(0, hp)] = dot(spread.astype(BF), grad_q).astype(BF)
            djb[:, head_lanes(1, hp)] = (jnp.where(low, dk[0], dk[1]) * 0.125).astype(BF)
            djb[:, head_lanes(2, hp)] = jnp.where(low, dv[0], dv[1]).astype(BF)

        for hp in range(pairs):
            heads(hp)
        copies.append(started(djb, fdj.at[r], 7))
        into_input(xin.at[r], dyb.at[r], dx)
        return copies

    @pl.when(me == 0)
    def _():
        def forward_step(k, carry):
            r = lax.rem(k, rows)
            set_cap(r)

            @pl.when(k < rows)
            def _():
                xin[k] = emb[r].astype(F32)

            @pl.when(k >= rows)
            def _():
                send_lat(r).wait_recv()
                xin[k] = exact_dot(selector_turned(r, 0), lat[r])

                def step(part, start):
                    xin[k, part, :] += emb[r, part, :].astype(F32) * unmarked(r, start)

                each_chunk(step)

            copies = forward(k, xin.at[k], yb.at[k], first=k == 0)
            send_y(k).start()
            finish(copies)
            return carry

        lax.fori_loop(0, 2 * rows, forward_step, 0)

        def backward_step(i, carry):
            k = lax.rem(i + rows, 2 * rows)
            r = lax.rem(i, rows)
            send_y(k).wait_send()
            send_grad(k).wait_recv()
            set_cap_turned(r)
            copies = backward(k, xin.at[k], dyb.at[k], yb.at[k])

            @pl.when(i < rows)
            def _():
                thg[r] = exact_dot(selector(positions(r, 0)), yb[k])
                send_thoughts(r).start()

            @pl.when(i >= rows)
            def _():
                def step(part, start):
                    yb[k, part, :] += yb[rows + r, part, :] * unmarked(r, start)

                each_chunk(step)
                started(yb.at[k], sec.at[0, r], 8).wait()

            finish(copies)
            return carry

        lax.fori_loop(0, 2 * rows, backward_step, 0)

        def drain(r, carry):
            send_thoughts(r).wait_send()
            return carry

        lax.fori_loop(0, rows, drain, 0)

    @pl.when(me == 1)
    def _():
        finish(weights)

        def latent_step(r, carry):
            send_y(r).wait_recv()
            copies = forward_latent(r)
            send_lat(r).start()
            finish(copies)
            return carry

        lax.fori_loop(0, rows, latent_step, 0)

        def language_step(r, carry):
            k = rows + r
            set_cap(r)
            set_cap_turned(r)
            send_y(k).wait_recv()
            copies = forward(k, xin.at[k], dyb.at[k])
            copies.append(started(dyb.at[k], sec.at[0, r], 8))
            dyb[r] = cot[r].astype(F32)
            copies += backward(k, xin.at[k], dyb.at[r], yb.at[k])
            send_grad(k).start()
            finish(copies)
            return carry

        lax.fori_loop(0, rows, language_step, 0)
        for staged in (dm, a2, ob, gb, dub, dhr):
            staged[...] = jnp.zeros_like(staged)

        def latent_back_step(r, carry):
            send_thoughts(r).wait_recv()
            copies = backward_latent(r, yb.at[r])
            send_grad(r).start()
            finish(copies)
            return carry

        lax.fori_loop(0, rows, latent_back_step, 0)

        def drain(r, carry):
            send_lat(r).wait_send()
            send_grad(r).wait_send()
            send_grad(rows + r).wait_send()
            return carry

        lax.fori_loop(0, rows, drain, 0)


def layers(emb, cot, seg, tpos, w_qkv, w_out, w_up, w_down, small):
    rows, length, width = emb.shape
    inner = w_up.shape[2]
    thoughts = tpos.shape[1]
    slots = 2 * rows
    packed = small.shape[1] // width
    vmem = pl.BlockSpec(memory_space=pltpu.VMEM)
    anywhere = pl.BlockSpec(memory_space=pl.ANY)
    smem = pl.BlockSpec(memory_space=pltpu.SMEM)

    def factor(columns):
        return jax.ShapeDtypeStruct((slots, length, columns), BF)

    def block(columns, kind=BF):
        return pltpu.VMEM((length, columns), kind)

    def few(columns, kind=BF):
        return pltpu.VMEM((rows, LAT, columns), kind)

    sizes = (rows, length, width, inner, thoughts)
    return pl.pallas_call(
        functools.partial(layers_kernel, sizes),
        out_shape=(
            jax.ShapeDtypeStruct((1, rows, length, width), F32),
            factor(width),
            factor(3 * width),
            factor(width),
            factor(width),
            factor(width),
            factor(inner),
            factor(inner),
            factor(width),
            jax.ShapeDtypeStruct((packed, width), F32),
        ),
        in_specs=[vmem, vmem, vmem, smem] + [anywhere] * 4 + [vmem],
        out_specs=(anywhere,) * 9 + (vmem,),
        scratch_shapes=[
            pltpu.VMEM((width, 3 * width), BF),
            pltpu.VMEM((width, width), BF),
            pltpu.VMEM((width, inner), BF),
            pltpu.VMEM((inner, width), BF),
            pltpu.VMEM((slots, length, width), F32),
            pltpu.VMEM((slots, length, width), F32),
            pltpu.VMEM((slots, length, width), F32),
            pltpu.VMEM((slots, length, 3 * width), BF),
            pltpu.VMEM((width, length), BF),
            pltpu.VMEM((width, length), BF),
            pltpu.VMEM((length, length), F32),
            pltpu.VMEM((slots, length, width), F32),
            pltpu.VMEM((slots, length, inner), BF),
            block(width),
            block(width),
            block(width),
            block(inner),
            block(width),
            block(inner),
            block(width),
            block(3 * width),
            block(width, F32),
            block(width),
            block(length, F32),
            few(width, F32),
            few(width, F32),
            few(width, F32),
            few(width),
            pltpu.VMEM((rows, HEADS, LAT, length), BF),
            few(width, F32),
            few(width),
            few(width),
            few(inner),
            few(inner),
            pltpu.SemaphoreType.DMA((4,)),
            pltpu.SemaphoreType.DMA((9,)),
        ]
        + [pltpu.SemaphoreType.DMA((slots,))] * 4
        + [pltpu.SemaphoreType.DMA((rows,))] * 4,
        compiler_params=pltpu.CompilerParams(
            collective_id=0, has_side_effects=True, vmem_limit_bytes=62 << 20
        ),
    )(emb, cot, seg, tpos, w_qkv, w_out, w_up, w_down, small)


def summed_by_parts(factors, small_grads):
    fa1, fdj, fo, fdhr, fa2, fdu, fg, fdm = factors

    def product(left, right):
        whole = jnp.einsum("ktm,ktn->mn", left, right, preferred_element_type=F32)
        return lax.psum_scatter(whole[None], "dp", scatter_dimension=1, tiled=True)

    small = lax.psum_scatter(
        small_grads.reshape(1, -1), "dp", scatter_dimension=1, tiled=True
    )
    return product(fa1, fdj), product(fo, fdhr), product(fa2, fdu), product(fg, fdm), small


def gradients_kernel(
    sizes,
    plan,
    fa1,
    fdj,
    fo,
    fdhr,
    fa2,
    fdu,
    fg,
    fdm,
    small,
    gqkv,
    gout,
    gup,
    gdown,
    gsmall,
    left,
    right,
    lt,
    gt,
    wa,
    wb,
    ra,
    rb,
    rs,
    xa,
    xb,
    xs,
    ua,
    ub,
    us,
    na,
    nb,
    ns,
    xl,
    ul,
    nl,
    lsem,
    pair_send,
    pair_recv,
    side_send,
    side_recv,
    up_send,
    up_recv,
    down_send,
    down_recv,
):
    width, narrow, depth = sizes
    me = lax.axis_index("dp")
    core = lax.rem(me, 2)
    side = lax.rem(me // 2, 2)
    level = me // 4
    partner = me + 1 - 2 * core
    beside = me + 2 - 4 * side
    above, below = me + 4, me - 4

    def remote(source, target, send, recv, device):
        return pltpu.make_async_remote_copy(
            src_ref=source,
            dst_ref=target,
            send_sem=send,
            recv_sem=recv,
            device_id={"dp": device},
            device_id_type=MESH,
        )

    lefts = {"qkv": fa1, "out": fo, "up": fa2, "down": fg}
    rights = {"qkv": fdj, "out": fdhr, "up": fdu, "down": fdm}
    steps = []
    turned = None
    ahead = 0
    for number, (name, part, _) in enumerate(plan):
        if name == "small":
            continue
        if name == "down":
            while ahead < depth:
                steps.append((number, name, True, ahead, None))
                ahead += 1
            steps += [(number, name, False, block, part) for block in range(depth)]
            continue
        if name != turned:
            steps.append((number, name, True, 0, None))
            turned = name
        steps.append((number, name, False, 0, part))
        for _ in range(2 if number else 1):
            if ahead < depth:
                steps.append((number, "down", True, ahead, None))
                ahead += 1

    def loads(index):
        _, name, turn, block, part = steps[index]
        slot = index % 2
        if turn:
            source = lefts[name].at[:, :, block * width : (block + 1) * width]
            return pltpu.make_async_copy(source, left.at[slot], lsem.at[slot])
        columns = narrow if name == "down" else width
        return pltpu.make_async_copy(
            rights[name].at[:, :, part * columns : (part + 1) * columns],
            right.at[slot, :, :, 0:columns],
            lsem.at[slot],
        )

    def start_loads(index):
        if index < len(steps):
            loads(index).start()

    start_loads(0)

    barrier = pltpu.get_barrier_semaphore()

    def greet(device):
        pl.semaphore_signal(barrier, inc=1, device_id={"dp": device}, device_id_type=MESH)

    greet(partner)
    greet(beside)

    @pl.when(level < 3)
    def _():
        greet(above)

    @pl.when(level > 0)
    def _():
        greet(below)

    pl.semaphore_wait(barrier, 2 + (level + 2) // 3 + (5 - level) // 3)

    views = []
    counts = {"a": 0, "b": 0, "line": 0}
    for number, (name, part, line_first) in enumerate(plan):
        if name == "small":
            views.append((small, rs, xs, us, ns, gsmall))
            continue
        kind = "b" if name == "down" else "a"
        index = counts[kind]
        counts[kind] += 1
        if kind == "a":
            target = {"qkv": gqkv, "out": gout, "up": gup}[name]
            place = target.at[0, :, part * width : (part + 1) * width]
            if line_first:
                along = counts["line"]
                counts["line"] += 1
                further = (xl.at[along], ul.at[along], nl.at[along], place)
            else:
                along = index - counts["line"]
                further = (xa.at[along], ua.at[along], na.at[along], place)
            views.append((wa.at[index % 2], ra.at[index]) + further)
        else:
            place = gdown.at[0, :, part * narrow : (part + 1) * narrow]
            views.append((wb, rb.at[index], xb.at[index], ub.at[index], nb.at[index], place))
    total = len(plan)
    previous = {}
    last_of = {}
    for number, (name, part, _) in enumerate(plan):
        kind = "s" if name == "small" else "b" if name == "down" else "a"
        mine = [n for n in range(number) if ("b" if plan[n][0] == "down" else "a") == kind]
        mine = [n for n in mine if plan[n][0] != "small"]
        back = 1 if kind == "b" else 2
        previous[number] = mine[-back] if kind != "s" and len(mine) >= back else None
        last_of[number] = True
        if previous[number] is not None:
            last_of[previous[number]] = False

    def pair_copy(number):
        w, r = views[number][:2]
        return remote(
            w.at[:, :, 1 - core], r, pair_send.at[number], pair_recv.at[number], partner
        )

    def side_copy(number):
        r, x = views[number][1:3]
        source = r.at[level, 1 - side] if plan[number][2] else r.at[:, 1 - side]
        return remote(source, x, side_send.at[number], side_recv.at[number], beside)

    def along_line(number):
        r, x = views[number][1:3]
        return r if plan[number][2] else x

    def up_copy(number, goal, source=None):
        u = views[number][3]
        return remote(
            u.at[goal - 1] if source is None else source,
            u.at[goal - 1],
            up_send.at[number, goal - 1],
            up_recv.at[number, goal - 1],
            above,
        )

    def down_copy(number, goal, source=None):
        n = views[number][4]
        return remote(
            n.at[goal] if source is None else source,
            n.at[goal],
            down_send.at[number, goal],
            down_recv.at[number, goal],
            below,
        )

    def start_line(number):
        base = along_line(number)

        @pl.when(level == 0)
        def _():
            for goal in (3, 2, 1):
                up_copy(number, goal, base.at[goal]).start()

        @pl.when(level == 3)
        def _():
            for goal in (0, 1, 2):
                down_copy(number, goal, base.at[goal]).start()

    position = {"step": 0}
    slots, length = left.shape[1:3]

    def turn_block(slot, target):
        def body(t, carry):
            tokens = pl.ds(pl.multiple_of(t * length, length), length)
            target[:, tokens] = left[slot, t].T
            return carry

        lax.fori_loop(0, slots, body, 0)

    def right_part(slot, lanes):
        part = right[slot, :, :, lanes]
        return part.reshape(slots * length, part.shape[2])

    def multiply(slot, w):
        def tile(t, carry):
            lanes = pl.ds(pl.multiple_of(t * narrow, narrow), narrow)
            product = dot(lt[...], right_part(slot, lanes))
            w[:, :, :, :, lanes] = product.reshape(w.shape[:4] + (narrow,))
            return carry

        lax.fori_loop(0, width // narrow, tile, 0)


    def produce(number):
        name, part, _ = plan[number]
        if name != "small":
            if previous[number] is not None:
                pair_copy(previous[number]).wait_send()
            w = views[number][0]
            while position["step"] < len(steps) and steps[position["step"]][0] == number:
                index = position["step"]
                position["step"] += 1
                _, source, turn, block, _ = steps[index]
                start_loads(index + 1)
                loads(index).wait()
                if turn:
                    turn_block(index % 2, gt.at[block] if source == "down" else lt)
                elif source == "down":
                    w[block] = dot(gt[block], right_part(index % 2, slice(0, narrow))).reshape(
                        w.shape[1:]
                    )
                else:
                    multiply(index % 2, w)
        pair_copy(number).start()

    def stage_pair(number):
        w, r = views[number][:2]
        pair_copy(number).wait_recv()

        def add(z, carry):
            for s in range(2):
                r[z, s] += w[z, s, core]
            return carry

        lax.fori_loop(0, 4, add, 0)
        if plan[number][2]:
            start_line(number)
        else:
            side_copy(number).start()

    def stage_side(number):
        if plan[number][2]:
            return
        r, x = views[number][1:3]
        side_copy(number).wait_recv()

        def add(z, carry):
            x[z] += r[z, side]
            return carry

        lax.fori_loop(0, 4, add, 0)
        start_line(number)

    def stage_up(number, height):
        u = views[number][3]
        base = along_line(number)

        @pl.when(level == height)
        def _():
            for goal in range(3, height - 1, -1):
                up_copy(number, goal).wait_recv()
                if goal > height:
                    u[goal - 1] += base[goal]
                    up_copy(number, goal).start()

    def stage_down(number, height):
        n = views[number][4]
        base = along_line(number)

        @pl.when(level == height)
        def _():
            for goal in range(0, height + 1):
                down_copy(number, goal).wait_recv()
                if goal < height:
                    n[goal] += base[goal]
                    down_copy(number, goal).start()

    def stage_sum(number):
        u, n, place = views[number][3:]
        base = along_line(number)

        @pl.when(level > 0)
        def _():
            base[level] += u[level - 1]

        @pl.when(level < 3)
        def _():
            base[level] += n[level]

        if plan[number][2]:
            side_copy(number).start()
        else:
            place[...] = base[level]

    def stage_last(number):
        if plan[number][2]:
            r, x = views[number][1:3]
            side_copy(number).wait_recv()
            views[number][5][...] = r[level, side] + x[...]

    def at(stage, number, *more):
        if 0 <= number < total:
            stage(number, *more)

    for moment in range(total + 6):
        at(produce, moment)
        at(stage_pair, moment - 1)
        at(stage_side, moment - 2)
        for height in range(4):
            if height > 0:
                at(stage_up, moment - 2 - height, height)
            if height < 3:
                at(stage_down, moment - 5 + height, height)
        at(stage_sum, moment - 5)
        at(stage_last, moment - 6)
    for number in range(total):
        if last_of[number]:
            pair_copy(number).wait_send()
        side_copy(number).wait_send()
        for goal in (1, 2, 3):

            @pl.when(goal > level)
            def _():
                up_copy(number, goal).wait_send()

        for goal in (0, 1, 2):

            @pl.when(goal < level)
            def _():
                down_copy(number, goal).wait_send()


def summed_in_kernel(factors, small_grads):
    fa1, fdj, fo, fdhr, fa2, fdu, fg, fdm = factors
    slots, length, width = fa1.shape
    inner = fg.shape[2]
    owners = 16
    depth = inner // width
    narrow = 256
    a_rows, b_rows = width // owners, inner // owners
    packed = small_grads.size // owners
    lanes = 128
    s_rows = -(-packed // (8 * lanes)) * 8
    small = small_grads.reshape(owners, packed)
    small = jnp.pad(small, ((0, 0), (0, s_rows * lanes - packed)))
    small = small.reshape(4, 2, 2, s_rows, lanes)
    plan = [
        ("qkv", 0, False),
        ("qkv", 1, True),
        ("small", 0, False),
        ("qkv", 2, False),
        ("down", 0, False),
        ("out", 0, True),
        ("down", 1, False),
        ("up", 0, False),
        ("down", 2, False),
        ("up", 1, False),
        ("up", 2, False),
        ("up", 3, False),
    ]
    total = len(plan)
    a_block, b_block, s_block = (a_rows, width), (b_rows, narrow), (s_rows, lanes)
    a_count = total - 1 - width // narrow
    b_count = width // narrow
    line_count = sum(line_first for _, _, line_first in plan)
    vmem = pl.BlockSpec(memory_space=pltpu.VMEM)
    anywhere = pl.BlockSpec(memory_space=pl.ANY)

    def trio(*lead):
        count = a_count if len(lead) == 2 else a_count - line_count
        return [
            pltpu.VMEM((count,) + lead + a_block, F32),
            pltpu.VMEM((b_count,) + lead + b_block, F32),
            pltpu.VMEM(lead + s_block, F32),
        ]

    *grads, small_grad = pl.pallas_call(
        functools.partial(gradients_kernel, (width, narrow, depth), plan),
        out_shape=(
            jax.ShapeDtypeStruct((1, a_rows, 3 * width), F32),
            jax.ShapeDtypeStruct((1, a_rows, width), F32),
            jax.ShapeDtypeStruct((1, a_rows, inner), F32),
            jax.ShapeDtypeStruct((1, b_rows, width), F32),
            jax.ShapeDtypeStruct(s_block, F32),
        ),
        in_specs=[anywhere] * 8 + [vmem],
        out_specs=(vmem,) * 5,
        scratch_shapes=[
            pltpu.VMEM((2, slots, length, width), BF),
            pltpu.VMEM((2, slots, length, width), BF),
            pltpu.VMEM((width, slots * length), BF),
            pltpu.VMEM((depth, width, slots * length), BF),
            pltpu.VMEM((2, 4, 2, 2) + a_block, F32),
            pltpu.VMEM((4, 2, 2) + b_block, F32),
        ]
        + trio(4, 2)
        + trio(4)
        + trio(3)
        + trio(3)
        + [
            pltpu.VMEM((line_count,) + a_block, F32),
            pltpu.VMEM((line_count, 3, 2) + a_block, F32),
            pltpu.VMEM((line_count, 3, 2) + a_block, F32),
        ]
        + [pltpu.SemaphoreType.DMA((2,))]
        + [pltpu.SemaphoreType.DMA((total,))] * 4
        + [pltpu.SemaphoreType.DMA((total, 3))] * 4,
        compiler_params=pltpu.CompilerParams(
            collective_id=1, has_side_effects=True, vmem_limit_bytes=62 << 20
        ),
    )(*factors, small)
    small_grad = small_grad.reshape(1, -1)[:, :packed]
    return tuple(grads) + (small_grad,)


def reduced(factors, small_grads):
    if lax.axis_size("dp") == 16:
        return summed_in_kernel(factors, small_grads)
    return summed_by_parts(factors, small_grads)


def per_device(
    embeddings, cotangent, seg_ids, thought_pos, w_qkv, w_out, w_up, w_down, small_params
):
    section_out, *factors, small_grads = layers(
        embeddings, cotangent, seg_ids, thought_pos, w_qkv, w_out, w_up, w_down, small_params
    )
    return (section_out,) + tuple(reduced(factors, small_grads))


def solution(mesh):
    return jax.shard_map(
        per_device,
        mesh=mesh,
        in_specs=(
            P("dp", None, None),
            P("dp", None, None),
            P("dp", None),
            P("dp", None),
            P("pipe", None, None),
            P("pipe", None, None),
            P("pipe", None, None),
            P("pipe", None, None),
            P("pipe", None),
        ),
        out_specs=(
            P("pipe", "dp", None, None),
            P("pipe", "dp", None),
            P("pipe", "dp", None),
            P("pipe", "dp", None),
            P("pipe", "dp", None),
            P("pipe", "dp"),
        ),
        check_vma=False,
    )
```

```python
import functools

import jax
import jax.numpy as jnp
from jax import lax
from jax.experimental import pallas as pl
from jax.experimental.pallas import tpu as pltpu
from jax.sharding import PartitionSpec as P

HEADS = 12
BF = jnp.bfloat16
F32 = jnp.float32
MESH = pl.DeviceIdType.MESH
EPSILON = 1e-05
MASKED = -1000000000.0
NO_CAP = 3e38
LAT = 16
CHUNK = 128
G1, B1, BQ, BV, BO, G2, B2, BU = 0, 1, 2, 3, 4, 5, 6, 7


def dot(a, b):
    return lax.dot_general(a, b, (((1,), (0,)), ((), ())), preferred_element_type=F32)


def dot_nt(a, b):
    return lax.dot_general(a, b, (((1,), (1,)), ((), ())), preferred_element_type=F32)


def exact_dot(a, b):
    return lax.dot_general(
        a,
        b,
        (((1,), (0,)), ((), ())),
        precision=lax.Precision.HIGHEST,
        preferred_element_type=F32,
    )


def normalized(values):
    centred = values - jnp.mean(values, -1, keepdims=True)
    spread = jnp.mean(centred * centred, -1, keepdims=True)
    scale = lax.rsqrt(spread + EPSILON)
    return centred * scale, scale


def norm_back(hat, scale, grad):
    along = jnp.mean(grad * hat, -1, keepdims=True)
    return scale * (grad - jnp.mean(grad, -1, keepdims=True) - hat * along)


def gelu_both(u):
    c = 0.7978845608028654
    square = u * u
    t = jnp.tanh(c * u * (1.0 + 0.044715 * square))
    half = 0.5 + 0.5 * t
    slope = half + (0.5 * c) * u * (1.0 - t * t) * (1.0 + (3 * 0.044715) * square)
    return u * half, slope


def column_sum(values):
    return jnp.sum(values.astype(F32), 0, keepdims=True)


def softmax(scores, axis=-1):
    e = jnp.exp(scores - jnp.max(scores, axis, keepdims=True))
    return e * (1.0 / jnp.sum(e, axis, keepdims=True))


def layers_kernel(
    sizes,
    emb,
    cot,
    seg,
    tpos,
    wqkv_h,
    wout_h,
    wup_h,
    wdown_h,
    small,
    sec,
    fa1,
    fdj,
    fo,
    fdhr,
    fa2,
    fdu,
    fg,
    fdm,
    hslope,
    sg,
    wqkv,
    wout,
    wup,
    wdown,
    tqkv,
    tout,
    tup,
    tdown,
    xin,
    yb,
    dyb,
    jn,
    ktb,
    dqt,
    capt,
    hm,
    slope,
    a1,
    ob,
    a2,
    gb,
    dm,
    dub,
    dhr,
    djb,
    da,
    dob,
    cap,
    lat,
    thg,
    lx,
    lq,
    lp,
    lh,
    la2,
    lo,
    lg,
    lslope,
    wsem,
    osem,
    ysend,
    yrecv,
    gsend,
    grecv,
    lsend,
    lrecv,
    tsend,
    trecv,
):
    rows, length, width, inner, thoughts = sizes
    blocks = inner // width
    bd = BU + blocks
    pairs = HEADS // 2
    me = lax.axis_index("pipe")
    other = 1 - me

    weights = [
        pltpu.make_async_copy(source.at[0], target, wsem.at[number])
        for number, (source, target) in enumerate(
            ((wqkv_h, wqkv), (wout_h, wout), (wup_h, wup), (wdown_h, wdown))
        )
    ]
    for copy in weights:
        copy.start()
    barrier = pltpu.get_barrier_semaphore()
    pl.semaphore_signal(barrier, inc=1, device_id={"pipe": other}, device_id_type=MESH)
    pl.semaphore_wait(barrier, 1)
    sg[...] = jnp.zeros_like(sg)

    def remote(source, target, send, recv):
        return pltpu.make_async_remote_copy(
            src_ref=source,
            dst_ref=target,
            send_sem=send,
            recv_sem=recv,
            device_id={"pipe": other},
            device_id_type=MESH,
        )

    def send_y(k):
        return remote(yb.at[k], xin.at[k], ysend.at[k], yrecv.at[k])

    def send_grad(k):
        return remote(yb.at[k], dyb.at[k], gsend.at[k], grecv.at[k])

    def send_lat(r):
        return remote(lat.at[r], lat.at[r], lsend.at[r], lrecv.at[r])

    def send_thoughts(r):
        return remote(thg.at[r], thg.at[r], tsend.at[r], trecv.at[r])

    def started(source, target, number):
        copy = pltpu.make_async_copy(source, target, osem.at[number])
        copy.start()
        return copy

    def finish(copies):
        for copy in copies:
            copy.wait()

    def each_chunk(step):
        def body(i, carry):
            step(pl.ds(pl.multiple_of(i * CHUNK, CHUNK), CHUNK), i * CHUNK)
            return carry

        lax.fori_loop(0, length // CHUNK, body, 0)

    def row(number):
        return small[:, group(number)]

    def group(number):
        return slice(number * width, (number + 1) * width)

    lane = lax.broadcasted_iota(jnp.int32, (1, 128), 1)
    low = lane < 64
    halves = (jnp.where(low, 1.0, 0.0).astype(BF), jnp.where(low, 0.0, 1.0).astype(BF))

    def first_length(r):
        segment = seg[pl.ds(r, 1), :]
        return jnp.sum(jnp.where(segment == 0, 1.0, 0.0), -1, keepdims=True).astype(jnp.int32)

    def set_cap(r):
        first = first_length(r)
        query = lax.broadcasted_iota(jnp.int32, (length, length), 0)
        key = lax.broadcasted_iota(jnp.int32, (length, length), 1)
        lowest = jnp.where(query >= first, first, 0)
        cap[...] = jnp.where((key <= query) & (key >= lowest), NO_CAP, MASKED)

    def set_cap_turned(r):
        first = first_length(r)
        key = lax.broadcasted_iota(jnp.int32, (length, length), 0)
        query = lax.broadcasted_iota(jnp.int32, (length, length), 1)
        lowest = jnp.where(query >= first, first, 0)
        capt[...] = jnp.where((key <= query) & (key >= lowest), NO_CAP, MASKED)

    def positions(r, shift, axis=0):
        shape = (LAT, 1) if axis == 0 else (1, LAT)
        number = lax.broadcasted_iota(jnp.int32, shape, axis)
        result = jnp.full(shape, -1, jnp.int32)
        for j in range(thoughts):
            result = jnp.where(number == j, tpos[r, j] - shift, result)
        return result

    def selector_turned(r, shift):
        place = positions(r, shift, 1)
        return jnp.where(lax.broadcasted_iota(jnp.int32, (length, LAT), 0) == place, 1.0, 0.0)

    def selector(place):
        return jnp.where(lax.broadcasted_iota(jnp.int32, (LAT, length), 1) == place, 1.0, 0.0)

    def unmarked(r, start):
        place = lax.broadcasted_iota(jnp.int32, (CHUNK, 1), 0) + start
        keep = jnp.ones((CHUNK, 1), F32)
        for j in range(thoughts):
            keep = jnp.where(place == tpos[r, j], 0.0, keep)
        return keep

    def head_lanes(part, hp):
        return slice(part * width + hp * 128, part * width + (hp + 1) * 128)

    def norm_one(x):
        def step(part, _):
            hat, _ = normalized(x[part, :])
            a1[part, :] = (hat * row(G1) + row(B1)).astype(BF)

        each_chunk(step)

    def forward(k, x, y, first=None):
        def need(number):
            if first is not None:

                @pl.when(first)
                def _():
                    weights[number].wait()

        norm_one(x)
        copies = [started(a1, fa1.at[k], 0)]
        need(0)
        for part, bias in ((0, BQ), (1, None), (2, BV)):
            joined = dot(a1[...], wqkv[:, group(part)])
            if bias is not None:
                joined = joined + row(bias)
            jn[k, :, group(part)] = joined.astype(BF)

        def heads(hp):
            q = jn[k, :, head_lanes(0, hp)]
            key = jn[k, :, head_lanes(1, hp)]
            value = jn[k, :, head_lanes(2, hp)]
            out = []
            for h in range(2):
                scores = dot_nt(q * (halves[h] * 0.125), key)
                chance = softmax(jnp.minimum(scores, cap[...])).astype(BF)
                out.append(dot(chance, value))
            ob[:, head_lanes(0, hp)] = jnp.where(low, out[0], out[1]).astype(BF)

        for hp in range(pairs):
            heads(hp)
        copies.append(started(ob, fo.at[k], 1))
        need(1)
        hm[k] = x[...] + dot(ob[...], wout[...]) + row(BO)

        def step(part, _):
            hat, _ = normalized(hm[k, part, :])
            a2[part, :] = (hat * row(G2) + row(B2)).astype(BF)
            y[part, :] = hm[k, part, :] + row(bd)

        each_chunk(step)
        copies.append(started(a2, fa2.at[k], 2))
        need(2)
        need(3)

        def mlp(c):
            part = group(c)
            u = dot(a2[...], wup[:, part]) + row(BU + c)
            g, d = gelu_both(u)
            gb[:, part] = g.astype(BF)
            slope[:, part] = d.astype(BF)
            y[...] += dot(gb[:, part], wdown[part, :])

        for c in range(blocks):
            mlp(c)
        copies.append(started(gb, fg.at[k], 3))
        if first is not None:
            copies.append(started(slope, hslope.at[k], 9))
        return copies

    def turn_weights():
        def rows_of(target, source, i):
            part = pl.ds(pl.multiple_of(i * 256, 256), 256)
            target[part, :] = source[:, part].T

        def body(i, carry):
            part = pl.ds(pl.multiple_of(i * 256, 256), 256)
            rows_of(tup, wup, i)
            tdown[:, part] = wdown[part, :].T

            @pl.when(i < 3 * width // 256)
            def _():
                rows_of(tqkv, wqkv, i)

            @pl.when(i < width // 256)
            def _():
                rows_of(tout, wout, i)

            return carry

        lax.fori_loop(0, inner // 256, body, 0)

    def backward(k, x, dy, dx, ready=None):
        def step(part, _):
            branch = dy[part, :].astype(BF)
            dm[part, :] = branch
            sg[bd : bd + 1, :] += column_sum(branch)

        each_chunk(step)
        copies = [started(dm, fdm.at[k], 4)]
        da[...] = jnp.zeros_like(da)
        if ready is not None:
            ready.wait()

        def mlp(c):
            part = group(c)
            grad = (dot(dm[...], tdown[:, part]) * slope[:, part]).astype(BF)
            dub[:, part] = grad
            sg[BU + c : BU + c + 1, :] += column_sum(grad)
            da[...] += dot(grad, tup[part, :])

        for c in range(blocks):
            mlp(c)
        copies.append(started(dub, fdu.at[k], 5))

        def step_two(part, _):
            hat, scale = normalized(hm[k, part, :])
            grad = da[part, :]
            sg[G2 : G2 + 1, :] += column_sum(grad * hat)
            sg[B2 : B2 + 1, :] += column_sum(grad)
            middle = dy[part, :] + norm_back(hat, scale, grad * row(G2))
            dy[part, :] = middle
            branch = middle.astype(BF)
            dhr[part, :] = branch
            sg[BO : BO + 1, :] += column_sum(branch)

        each_chunk(step_two)
        copies.append(started(dhr, fdhr.at[k], 6))
        dob[...] = dot(dhr[...], tout[...]).astype(BF)

        def heads(hp):
            q = jn[k, :, head_lanes(0, hp)]
            key = jn[k, :, head_lanes(1, hp)]
            value = jn[k, :, head_lanes(2, hp)]
            grad_out = dob[:, head_lanes(0, hp)]
            dk, dv = [], []
            for h in range(2):
                scores = dot_nt(key, q * (halves[h] * 0.125))
                chance = softmax(jnp.minimum(scores, capt[...]), 0)
                inner_part = chance * dot_nt(value, grad_out * halves[h])
                total = jnp.sum(inner_part, 0, keepdims=True)
                grad_scores = (inner_part - chance * total).astype(BF)
                dv.append(dot(chance.astype(BF), grad_out))
                dk.append(dot(grad_scores, q))
                head = slice((2 * hp + h) * 64, (2 * hp + h + 1) * 64)
                dqt[head, :] = (dot(ktb[head, :], grad_scores) * 0.125).astype(BF)
            djb[:, head_lanes(1, hp)] = (jnp.where(low, dk[0], dk[1]) * 0.125).astype(BF)
            djb[:, head_lanes(2, hp)] = jnp.where(low, dv[0], dv[1]).astype(BF)

        ktb[...] = jn[k, :, group(1)].T
        for hp in range(pairs):
            heads(hp)
        djb[:, group(0)] = dqt[...].T
        copies.append(started(djb, fdj.at[k], 7))
        into_input(x, dy, dx)
        return copies

    def into_input(x, middle, dx):
        sg[BQ : BQ + 1, :] += column_sum(djb[:, group(0)])
        sg[BV : BV + 1, :] += column_sum(djb[:, group(2)])
        da[...] = dot(djb[...], tqkv[...])

        def step(part, _):
            hat, scale = normalized(x[part, :])
            grad = da[part, :]
            sg[G1 : G1 + 1, :] += column_sum(grad * hat)
            sg[B1 : B1 + 1, :] += column_sum(grad)
            dx[part, :] = middle[part, :] + norm_back(hat, scale, grad * row(G1))

        each_chunk(step)

    def forward_latent(r):
        x = xin.at[r]
        norm_one(x)
        copies = [started(a1, fa1.at[r], 0)]
        jn[r, :, group(1)] = dot(a1[...], wqkv[:, group(1)]).astype(BF)
        jn[r, :, group(2)] = (dot(a1[...], wqkv[:, group(2)]) + row(BV)).astype(BF)
        place = positions(r, 1)
        chosen = exact_dot(selector(place), x[...])
        lx[r] = chosen
        hat, _ = normalized(chosen)
        normed = (hat * row(G1) + row(B1)).astype(BF)
        lq[r] = (dot(normed, wqkv[:, group(0)]) + row(BQ)).astype(BF)
        first = first_length(r)
        key_place = lax.broadcasted_iota(jnp.int32, (LAT, length), 1)
        lowest = jnp.where(place >= first, first, 0)
        limit = jnp.where((key_place <= place) & (key_place >= lowest), NO_CAP, MASKED)

        def heads(hp):
            q = lq[r, :, head_lanes(0, hp)]
            key = jn[r, :, head_lanes(1, hp)]
            value = jn[r, :, head_lanes(2, hp)]
            out = []
            for h in range(2):
                scores = dot_nt(q * (halves[h] * 0.125), key)
                chance = softmax(jnp.minimum(scores, limit)).astype(BF)
                lp[r, 2 * hp + h] = chance
                out.append(dot(chance, value))
            lo[r, :, head_lanes(0, hp)] = jnp.where(low, out[0], out[1]).astype(BF)

        for hp in range(pairs):
            heads(hp)
        middle = chosen + dot(lo[r], wout[...]) + row(BO)
        lh[r] = middle
        hat, _ = normalized(middle)
        la2[r] = (hat * row(G2) + row(B2)).astype(BF)
        lat[r] = middle + row(bd)

        def mlp(c):
            part = group(c)
            u = dot(la2[r], wup[:, part]) + row(BU + c)
            g, d = gelu_both(u)
            lg[r, :, part] = g.astype(BF)
            lslope[r, :, part] = d.astype(BF)
            lat[r] += dot(lg[r, :, part], wdown[part, :])

        for c in range(blocks):
            mlp(c)
        return copies

    def backward_latent(r, dx):
        grad_result = thg[r]
        branch = grad_result.astype(BF)
        top = slice(0, LAT)
        sg[bd : bd + 1, :] += column_sum(branch)
        dm[top, :] = branch
        a2[top, :] = la2[r]
        ob[top, :] = lo[r]
        gb[top, :] = lg[r]
        copies = [
            started(dm, fdm.at[r], 4),
            started(a2, fa2.at[r], 2),
            started(ob, fo.at[r], 1),
            started(gb, fg.at[r], 3),
        ]
        da[top, :] = jnp.zeros((LAT, width), F32)

        def mlp(c):
            part = group(c)
            grad = (dot(dm[top, :], tdown[:, part]) * lslope[r, :, part]).astype(BF)
            dub[top, part] = grad
            sg[BU + c : BU + c + 1, :] += column_sum(grad)
            da[top, :] += dot(grad, tup[part, :])

        for c in range(blocks):
            mlp(c)
        copies.append(started(dub, fdu.at[r], 5))
        hat, scale = normalized(lh[r])
        grad = da[top, :]
        sg[G2 : G2 + 1, :] += column_sum(grad * hat)
        sg[B2 : B2 + 1, :] += column_sum(grad)
        middle = grad_result + norm_back(hat, scale, grad * row(G2))
        rounded = middle.astype(BF)
        dhr[top, :] = rounded
        sg[BO : BO + 1, :] += column_sum(rounded)
        copies.append(started(dhr, fdhr.at[r], 6))
        spread = selector_turned(r, 1)
        dyb[r] = exact_dot(spread, middle)
        place = positions(r, 1, 1)
        first = first_length(r)
        key_place = lax.broadcasted_iota(jnp.int32, (length, LAT), 0)
        lowest = jnp.where(place >= first, first, 0)
        limit = jnp.where((key_place <= place) & (key_place >= lowest), NO_CAP, MASKED)
        dob[top, :] = dot(rounded, tout[...]).astype(BF)

        def heads(hp):
            q = lq[r, :, head_lanes(0, hp)]
            key = jn[r, :, head_lanes(1, hp)]
            value = jn[r, :, head_lanes(2, hp)]
            grad_out = dob[top, head_lanes(0, hp)]
            dq, dk, dv = [], [], []
            for h in range(2):
                grad_masked = grad_out * halves[h]
                chance = lp[r, 2 * hp + h].astype(F32)
                inner_part = chance * dot_nt(grad_masked, value)
                total = jnp.sum(inner_part, -1, keepdims=True)
                dq.append(dot((inner_part - chance * total).astype(BF), key))
                scores = dot_nt(key, q * (halves[h] * 0.125))
                chance = softmax(jnp.minimum(scores, limit), 0)
                inner_part = chance * dot_nt(value, grad_masked)
                total = jnp.sum(inner_part, 0, keepdims=True)
                dk.append(dot((inner_part - chance * total).astype(BF), q))
                dv.append(dot(chance.astype(BF), grad_out))
            grad_q = (jnp.where(low, dq[0], dq[1]) * 0.125).astype(BF)
            djb[:, head_lanes(0, hp)] = dot(spread.astype(BF), grad_q).astype(BF)
            djb[:, head_lanes(1, hp)] = (jnp.where(low, dk[0], dk[1]) * 0.125).astype(BF)
            djb[:, head_lanes(2, hp)] = jnp.where(low, dv[0], dv[1]).astype(BF)

        for hp in range(pairs):
            heads(hp)
        copies.append(started(djb, fdj.at[r], 7))
        into_input(xin.at[r], dyb.at[r], dx)
        return copies

    @pl.when(me == 0)
    def _():
        def forward_step(k, carry):
            r = lax.rem(k, rows)
            set_cap(r)

            @pl.when(k < rows)
            def _():
                xin[k] = emb[r].astype(F32)

            @pl.when(k >= rows)
            def _():
                send_lat(r).wait_recv()
                xin[k] = exact_dot(selector_turned(r, 0), lat[r])

                def step(part, start):
                    xin[k, part, :] += emb[r, part, :].astype(F32) * unmarked(r, start)

                each_chunk(step)

            copies = forward(k, xin.at[k], yb.at[k], first=k == 0)
            send_y(k).start()
            finish(copies)
            return carry

        lax.fori_loop(0, 2 * rows, forward_step, 0)
        turn_weights()

        def backward_step(i, carry):
            k = lax.rem(i + rows, 2 * rows)
            r = lax.rem(i, rows)
            slopes = pltpu.make_async_copy(hslope.at[k], slope, osem.at[10])
            slopes.start()
            set_cap_turned(r)
            send_y(k).wait_send()
            send_grad(k).wait_recv()
            copies = backward(k, xin.at[k], dyb.at[k], yb.at[k], slopes)

            @pl.when(i < rows)
            def _():
                thg[r] = exact_dot(selector(positions(r, 0)), yb[k])
                send_thoughts(r).start()

            @pl.when(i >= rows)
            def _():
                def step(part, start):
                    yb[k, part, :] += yb[rows + r, part, :] * unmarked(r, start)

                each_chunk(step)
                started(yb.at[k], sec.at[0, r], 8).wait()

            finish(copies)
            return carry

        lax.fori_loop(0, 2 * rows, backward_step, 0)

        def drain(r, carry):
            send_thoughts(r).wait_send()
            return carry

        lax.fori_loop(0, rows, drain, 0)

    @pl.when(me == 1)
    def _():
        finish(weights)
        turn_weights()

        def latent_step(r, carry):
            send_y(r).wait_recv()
            copies = forward_latent(r)
            send_lat(r).start()
            finish(copies)
            return carry

        lax.fori_loop(0, rows, latent_step, 0)

        def language_step(r, carry):
            k = rows + r
            set_cap(r)
            set_cap_turned(r)
            send_y(k).wait_recv()
            copies = forward(k, xin.at[k], dyb.at[k])
            copies.append(started(dyb.at[k], sec.at[0, r], 8))
            dyb[r] = cot[r].astype(F32)
            copies += backward(k, xin.at[k], dyb.at[r], yb.at[k])
            send_grad(k).start()
            finish(copies)
            return carry

        lax.fori_loop(0, rows, language_step, 0)
        for staged in (dm, a2, ob, gb, dub, dhr):
            staged[...] = jnp.zeros_like(staged)

        def latent_back_step(r, carry):
            send_thoughts(r).wait_recv()
            copies = backward_latent(r, yb.at[r])
            send_grad(r).start()
            finish(copies)
            return carry

        lax.fori_loop(0, rows, latent_back_step, 0)

        def drain(r, carry):
            send_lat(r).wait_send()
            send_grad(r).wait_send()
            send_grad(rows + r).wait_send()
            return carry

        lax.fori_loop(0, rows, drain, 0)


def layers(emb, cot, seg, tpos, w_qkv, w_out, w_up, w_down, small):
    rows, length, width = emb.shape
    inner = w_up.shape[2]
    thoughts = tpos.shape[1]
    slots = 2 * rows
    packed = small.shape[1] // width
    vmem = pl.BlockSpec(memory_space=pltpu.VMEM)
    anywhere = pl.BlockSpec(memory_space=pl.ANY)
    smem = pl.BlockSpec(memory_space=pltpu.SMEM)

    def factor(columns):
        return jax.ShapeDtypeStruct((slots, length, columns), BF)

    def block(columns, kind=BF):
        return pltpu.VMEM((length, columns), kind)

    def few(columns, kind=BF):
        return pltpu.VMEM((rows, LAT, columns), kind)

    sizes = (rows, length, width, inner, thoughts)
    return pl.pallas_call(
        functools.partial(layers_kernel, sizes),
        out_shape=(
            jax.ShapeDtypeStruct((1, rows, length, width), F32),
            factor(width),
            factor(3 * width),
            factor(width),
            factor(width),
            factor(width),
            factor(inner),
            factor(inner),
            factor(width),
            factor(inner),
            jax.ShapeDtypeStruct((packed, width), F32),
        ),
        in_specs=[vmem, vmem, vmem, smem] + [anywhere] * 4 + [vmem],
        out_specs=(anywhere,) * 10 + (vmem,),
        scratch_shapes=[
            pltpu.VMEM((width, 3 * width), BF),
            pltpu.VMEM((width, width), BF),
            pltpu.VMEM((width, inner), BF),
            pltpu.VMEM((inner, width), BF),
            pltpu.VMEM((3 * width, width), BF),
            pltpu.VMEM((width, width), BF),
            pltpu.VMEM((inner, width), BF),
            pltpu.VMEM((width, inner), BF),
            pltpu.VMEM((slots, length, width), F32),
            pltpu.VMEM((slots, length, width), F32),
            pltpu.VMEM((slots, length, width), F32),
            pltpu.VMEM((slots, length, 3 * width), BF),
            pltpu.VMEM((width, length), BF),
            pltpu.VMEM((width, length), BF),
            pltpu.VMEM((length, length), F32),
            pltpu.VMEM((slots, length, width), F32),
            block(inner),
            block(width),
            block(width),
            block(width),
            block(inner),
            block(width),
            block(inner),
            block(width),
            block(3 * width),
            block(width, F32),
            block(width),
            block(length, F32),
            few(width, F32),
            few(width, F32),
            few(width, F32),
            few(width),
            pltpu.VMEM((rows, HEADS, LAT, length), BF),
            few(width, F32),
            few(width),
            few(width),
            few(inner),
            few(inner),
            pltpu.SemaphoreType.DMA((4,)),
            pltpu.SemaphoreType.DMA((11,)),
        ]
        + [pltpu.SemaphoreType.DMA((slots,))] * 4
        + [pltpu.SemaphoreType.DMA((rows,))] * 4,
        compiler_params=pltpu.CompilerParams(
            collective_id=0, has_side_effects=True, vmem_limit_bytes=62 << 20
        ),
    )(emb, cot, seg, tpos, w_qkv, w_out, w_up, w_down, small)


def summed_by_parts(factors, small_grads):
    fa1, fdj, fo, fdhr, fa2, fdu, fg, fdm = factors

    def product(left, right):
        whole = jnp.einsum("ktm,ktn->mn", left, right, preferred_element_type=F32)
        return lax.psum_scatter(whole[None], "dp", scatter_dimension=1, tiled=True)

    small = lax.psum_scatter(
        small_grads.reshape(1, -1), "dp", scatter_dimension=1, tiled=True
    )
    return product(fa1, fdj), product(fo, fdhr), product(fa2, fdu), product(fg, fdm), small


def gradients_kernel(
    sizes,
    plan,
    fa1,
    fdj,
    fo,
    fdhr,
    fa2,
    fdu,
    fg,
    fdm,
    small,
    gqkv,
    gout,
    gup,
    gdown,
    gsmall,
    left,
    right,
    lt,
    gt,
    wa,
    wb,
    ra,
    rb,
    rs,
    xa,
    xb,
    xs,
    ua,
    ub,
    us,
    na,
    nb,
    ns,
    xl,
    ul,
    nl,
    lsem,
    pair_send,
    pair_recv,
    side_send,
    side_recv,
    up_send,
    up_recv,
    down_send,
    down_recv,
):
    width, narrow, depth = sizes
    me = lax.axis_index("dp")
    core = lax.rem(me, 2)
    side = lax.rem(me // 2, 2)
    level = me // 4
    partner = me + 1 - 2 * core
    beside = me + 2 - 4 * side
    above, below = me + 4, me - 4

    def remote(source, target, send, recv, device):
        return pltpu.make_async_remote_copy(
            src_ref=source,
            dst_ref=target,
            send_sem=send,
            recv_sem=recv,
            device_id={"dp": device},
            device_id_type=MESH,
        )

    lefts = {"qkv": fa1, "out": fo, "up": fa2, "down": fg}
    rights = {"qkv": fdj, "out": fdhr, "up": fdu, "down": fdm}
    steps = []
    turned = None
    ahead = 0
    for number, (name, part, _) in enumerate(plan):
        if name == "small":
            continue
        if name == "down":
            while ahead < depth:
                steps.append((number, name, True, ahead, None))
                ahead += 1
            steps += [(number, name, False, block, part) for block in range(depth)]
            continue
        if name != turned:
            steps.append((number, name, True, 0, None))
            turned = name
        steps.append((number, name, False, 0, part))
        for _ in range(2 if number else 1):
            if ahead < depth:
                steps.append((number, "down", True, ahead, None))
                ahead += 1

    def loads(index):
        _, name, turn, block, part = steps[index]
        slot = index % 2
        if turn:
            source = lefts[name].at[:, :, block * width : (block + 1) * width]
            return pltpu.make_async_copy(source, left.at[slot], lsem.at[slot])
        columns = narrow if name == "down" else width
        return pltpu.make_async_copy(
            rights[name].at[:, :, part * columns : (part + 1) * columns],
            right.at[slot, :, :, 0:columns],
            lsem.at[slot],
        )

    def start_loads(index):
        if index < len(steps):
            loads(index).start()

    start_loads(0)

    barrier = pltpu.get_barrier_semaphore()

    def greet(device):
        pl.semaphore_signal(barrier, inc=1, device_id={"dp": device}, device_id_type=MESH)

    greet(partner)
    greet(beside)

    @pl.when(level < 3)
    def _():
        greet(above)

    @pl.when(level > 0)
    def _():
        greet(below)

    pl.semaphore_wait(barrier, 2 + (level + 2) // 3 + (5 - level) // 3)

    views = []
    counts = {"a": 0, "b": 0, "line": 0}
    for number, (name, part, line_first) in enumerate(plan):
        if name == "small":
            views.append((small, rs, xs, us, ns, gsmall))
            continue
        kind = "b" if name == "down" else "a"
        index = counts[kind]
        counts[kind] += 1
        if kind == "a":
            target = {"qkv": gqkv, "out": gout, "up": gup}[name]
            place = target.at[0, :, part * width : (part + 1) * width]
            if line_first:
                along = counts["line"]
                counts["line"] += 1
                further = (xl.at[along], ul.at[along], nl.at[along], place)
            else:
                along = index - counts["line"]
                further = (xa.at[along], ua.at[along], na.at[along], place)
            views.append((wa.at[index % 2], ra.at[index]) + further)
        else:
            place = gdown.at[0, :, part * narrow : (part + 1) * narrow]
            views.append((wb, rb.at[index], xb.at[index], ub.at[index], nb.at[index], place))
    total = len(plan)
    previous = {}
    last_of = {}
    for number, (name, part, _) in enumerate(plan):
        kind = "s" if name == "small" else "b" if name == "down" else "a"
        mine = [n for n in range(number) if ("b" if plan[n][0] == "down" else "a") == kind]
        mine = [n for n in mine if plan[n][0] != "small"]
        back = 1 if kind == "b" else 2
        previous[number] = mine[-back] if kind != "s" and len(mine) >= back else None
        last_of[number] = True
        if previous[number] is not None:
            last_of[previous[number]] = False

    def pair_copy(number):
        w, r = views[number][:2]
        return remote(
            w.at[:, :, 1 - core], r, pair_send.at[number], pair_recv.at[number], partner
        )

    def side_copy(number):
        r, x = views[number][1:3]
        source = r.at[level, 1 - side] if plan[number][2] else r.at[:, 1 - side]
        return remote(source, x, side_send.at[number], side_recv.at[number], beside)

    def along_line(number):
        r, x = views[number][1:3]
        return r if plan[number][2] else x

    def up_copy(number, goal, source=None):
        u = views[number][3]
        return remote(
            u.at[goal - 1] if source is None else source,
            u.at[goal - 1],
            up_send.at[number, goal - 1],
            up_recv.at[number, goal - 1],
            above,
        )

    def down_copy(number, goal, source=None):
        n = views[number][4]
        return remote(
            n.at[goal] if source is None else source,
            n.at[goal],
            down_send.at[number, goal],
            down_recv.at[number, goal],
            below,
        )

    def start_line(number):
        base = along_line(number)

        @pl.when(level == 0)
        def _():
            for goal in (3, 2, 1):
                up_copy(number, goal, base.at[goal]).start()

        @pl.when(level == 3)
        def _():
            for goal in (0, 1, 2):
                down_copy(number, goal, base.at[goal]).start()

    position = {"step": 0}
    slots, length = left.shape[1:3]

    def turn_block(slot, target):
        def body(t, carry):
            tokens = pl.ds(pl.multiple_of(t * length, length), length)
            target[:, tokens] = left[slot, t].T
            return carry

        lax.fori_loop(0, slots, body, 0)

    def right_part(slot, lanes):
        part = right[slot, :, :, lanes]
        return part.reshape(slots * length, part.shape[2])

    def multiply(slot, w):
        def tile(t, carry):
            lanes = pl.ds(pl.multiple_of(t * narrow, narrow), narrow)
            product = dot(lt[...], right_part(slot, lanes))
            w[:, :, :, :, lanes] = product.reshape(w.shape[:4] + (narrow,))
            return carry

        lax.fori_loop(0, width // narrow, tile, 0)


    def produce(number):
        name, part, _ = plan[number]
        if name != "small":
            if previous[number] is not None:
                pair_copy(previous[number]).wait_send()
            w = views[number][0]
            while position["step"] < len(steps) and steps[position["step"]][0] == number:
                index = position["step"]
                position["step"] += 1
                _, source, turn, block, _ = steps[index]
                start_loads(index + 1)
                loads(index).wait()
                if turn:
                    turn_block(index % 2, gt.at[block] if source == "down" else lt)
                elif source == "down":
                    w[block] = dot(gt[block], right_part(index % 2, slice(0, narrow))).reshape(
                        w.shape[1:]
                    )
                else:
                    multiply(index % 2, w)
        pair_copy(number).start()

    def stage_pair(number):
        w, r = views[number][:2]
        pair_copy(number).wait_recv()

        def add(z, carry):
            for s in range(2):
                r[z, s] += w[z, s, core]
            return carry

        lax.fori_loop(0, 4, add, 0)
        if plan[number][2]:
            start_line(number)
        else:
            side_copy(number).start()

    def stage_side(number):
        if plan[number][2]:
            return
        r, x = views[number][1:3]
        side_copy(number).wait_recv()

        def add(z, carry):
            x[z] += r[z, side]
            return carry

        lax.fori_loop(0, 4, add, 0)
        start_line(number)

    def stage_up(number, height):
        u = views[number][3]
        base = along_line(number)

        @pl.when(level == height)
        def _():
            for goal in range(3, height - 1, -1):
                up_copy(number, goal).wait_recv()
                if goal > height:
                    u[goal - 1] += base[goal]
                    up_copy(number, goal).start()

    def stage_down(number, height):
        n = views[number][4]
        base = along_line(number)

        @pl.when(level == height)
        def _():
            for goal in range(0, height + 1):
                down_copy(number, goal).wait_recv()
                if goal < height:
                    n[goal] += base[goal]
                    down_copy(number, goal).start()

    def stage_sum(number):
        u, n, place = views[number][3:]
        base = along_line(number)

        @pl.when(level > 0)
        def _():
            base[level] += u[level - 1]

        @pl.when(level < 3)
        def _():
            base[level] += n[level]

        if plan[number][2]:
            side_copy(number).start()
        else:
            place[...] = base[level]

    def stage_last(number):
        if plan[number][2]:
            r, x = views[number][1:3]
            side_copy(number).wait_recv()
            views[number][5][...] = r[level, side] + x[...]

    def at(stage, number, *more):
        if 0 <= number < total:
            stage(number, *more)

    side_lag, hop = 3, 2
    for moment in range(total + side_lag + 3 * hop + 1):
        at(produce, moment)
        at(stage_pair, moment - 1)
        at(stage_side, moment - side_lag)
        for height in range(4):
            if height > 0:
                at(stage_up, moment - side_lag - hop * height, height)
            if height < 3:
                at(stage_down, moment - side_lag - hop * (3 - height), height)
        at(stage_sum, moment - side_lag - 3 * hop)
        at(stage_last, moment - side_lag - 3 * hop - 1)
    for number in range(total):
        if last_of[number]:
            pair_copy(number).wait_send()
        side_copy(number).wait_send()
        for goal in (1, 2, 3):

            @pl.when(goal > level)
            def _():
                up_copy(number, goal).wait_send()

        for goal in (0, 1, 2):

            @pl.when(goal < level)
            def _():
                down_copy(number, goal).wait_send()


def summed_in_kernel(factors, small_grads):
    fa1, fdj, fo, fdhr, fa2, fdu, fg, fdm = factors
    slots, length, width = fa1.shape
    inner = fg.shape[2]
    owners = 16
    depth = inner // width
    narrow = 256
    a_rows, b_rows = width // owners, inner // owners
    packed = small_grads.size // owners
    lanes = 128
    s_rows = -(-packed // (8 * lanes)) * 8
    small = small_grads.reshape(owners, packed)
    small = jnp.pad(small, ((0, 0), (0, s_rows * lanes - packed)))
    small = small.reshape(4, 2, 2, s_rows, lanes)
    plan = [
        ("qkv", 0, False),
        ("qkv", 1, True),
        ("small", 0, False),
        ("qkv", 2, False),
        ("down", 0, False),
        ("out", 0, True),
        ("down", 1, False),
        ("up", 0, False),
        ("down", 2, False),
        ("up", 1, False),
        ("up", 2, False),
        ("up", 3, False),
    ]
    total = len(plan)
    a_block, b_block, s_block = (a_rows, width), (b_rows, narrow), (s_rows, lanes)
    a_count = total - 1 - width // narrow
    b_count = width // narrow
    line_count = sum(line_first for _, _, line_first in plan)
    vmem = pl.BlockSpec(memory_space=pltpu.VMEM)
    anywhere = pl.BlockSpec(memory_space=pl.ANY)

    def trio(*lead):
        count = a_count if len(lead) == 2 else a_count - line_count
        return [
            pltpu.VMEM((count,) + lead + a_block, F32),
            pltpu.VMEM((b_count,) + lead + b_block, F32),
            pltpu.VMEM(lead + s_block, F32),
        ]

    *grads, small_grad = pl.pallas_call(
        functools.partial(gradients_kernel, (width, narrow, depth), plan),
        out_shape=(
            jax.ShapeDtypeStruct((1, a_rows, 3 * width), F32),
            jax.ShapeDtypeStruct((1, a_rows, width), F32),
            jax.ShapeDtypeStruct((1, a_rows, inner), F32),
            jax.ShapeDtypeStruct((1, b_rows, width), F32),
            jax.ShapeDtypeStruct(s_block, F32),
        ),
        in_specs=[anywhere] * 8 + [vmem],
        out_specs=(vmem,) * 5,
        scratch_shapes=[
            pltpu.VMEM((2, slots, length, width), BF),
            pltpu.VMEM((2, slots, length, width), BF),
            pltpu.VMEM((width, slots * length), BF),
            pltpu.VMEM((depth, width, slots * length), BF),
            pltpu.VMEM((2, 4, 2, 2) + a_block, F32),
            pltpu.VMEM((4, 2, 2) + b_block, F32),
        ]
        + trio(4, 2)
        + trio(4)
        + trio(3)
        + trio(3)
        + [
            pltpu.VMEM((line_count,) + a_block, F32),
            pltpu.VMEM((line_count, 3, 2) + a_block, F32),
            pltpu.VMEM((line_count, 3, 2) + a_block, F32),
        ]
        + [pltpu.SemaphoreType.DMA((2,))]
        + [pltpu.SemaphoreType.DMA((total,))] * 4
        + [pltpu.SemaphoreType.DMA((total, 3))] * 4,
        compiler_params=pltpu.CompilerParams(
            collective_id=1, has_side_effects=True, vmem_limit_bytes=62 << 20
        ),
    )(*factors, small)
    small_grad = small_grad.reshape(1, -1)[:, :packed]
    return tuple(grads) + (small_grad,)


def reduced(factors, small_grads):
    if lax.axis_size("dp") == 16:
        return summed_in_kernel(factors, small_grads)
    return summed_by_parts(factors, small_grads)


def per_device(
    embeddings, cotangent, seg_ids, thought_pos, w_qkv, w_out, w_up, w_down, small_params
):
    section_out, *factors, _, small_grads = layers(
        embeddings, cotangent, seg_ids, thought_pos, w_qkv, w_out, w_up, w_down, small_params
    )
    return (section_out,) + tuple(reduced(factors, small_grads))


def solution(mesh):
    return jax.shard_map(
        per_device,
        mesh=mesh,
        in_specs=(
            P("dp", None, None),
            P("dp", None, None),
            P("dp", None),
            P("dp", None),
            P("pipe", None, None),
            P("pipe", None, None),
            P("pipe", None, None),
            P("pipe", None, None),
            P("pipe", None),
        ),
        out_specs=(
            P("pipe", "dp", None, None),
            P("pipe", "dp", None),
            P("pipe", "dp", None),
            P("pipe", "dp", None),
            P("pipe", "dp", None),
            P("pipe", "dp"),
        ),
        check_vma=False,
    )
```

```python
import functools

import jax
import jax.numpy as jnp
from jax import lax
from jax.experimental import pallas as pl
from jax.experimental.pallas import tpu as pltpu
from jax.sharding import PartitionSpec as P

HEADS = 12
BF = jnp.bfloat16
F32 = jnp.float32
MESH = pl.DeviceIdType.MESH
EPSILON = 1e-05
MASKED = -1000000000.0
NO_CAP = 3e38
LAT = 16
BLOCK = 128
G1, B1, BQ, BV, BO, G2, B2, BU = 0, 1, 2, 3, 4, 5, 6, 7


def dot(a, b):
    return lax.dot_general(a, b, (((1,), (0,)), ((), ())), preferred_element_type=F32)


def dot_nt(a, b):
    return lax.dot_general(a, b, (((1,), (1,)), ((), ())), preferred_element_type=F32)


def exact_dot(a, b):
    return lax.dot_general(
        a,
        b,
        (((1,), (0,)), ((), ())),
        precision=lax.Precision.HIGHEST,
        preferred_element_type=F32,
    )


def normalized(values):
    centred = values - jnp.mean(values, -1, keepdims=True)
    spread = jnp.mean(centred * centred, -1, keepdims=True)
    scale = lax.rsqrt(spread + EPSILON)
    return centred * scale, scale


def norm_back(hat, scale, grad):
    along = jnp.mean(grad * hat, -1, keepdims=True)
    return scale * (grad - jnp.mean(grad, -1, keepdims=True) - hat * along)


def gelu_both(u):
    c = 0.7978845608028654
    square = u * u
    t = jnp.tanh(c * u * (1.0 + 0.044715 * square))
    half = 0.5 + 0.5 * t
    slope = half + (0.5 * c) * u * (1.0 - t * t) * (1.0 + (3 * 0.044715) * square)
    return u * half, slope


def softmax(scores, axis=-1):
    e = jnp.exp(scores - jnp.max(scores, axis, keepdims=True))
    return e * (1.0 / jnp.sum(e, axis, keepdims=True))


def layers_kernel(
    sizes,
    emb,
    cot,
    seg,
    tpos,
    wqkv_h,
    wout_h,
    wup_h,
    wdown_h,
    small,
    sec,
    fa1,
    fdj,
    fo,
    fdhr,
    fa2,
    fdu,
    fg,
    fdm,
    sg,
    sums,
    joint,
    stat,
    wide,
    wqkv,
    wout,
    wup,
    wdown,
    xin,
    yb,
    dyb,
    jn,
    ktb,
    dqt,
    capt,
    hm,
    slope,
    a1,
    ob,
    a2,
    gb,
    dm,
    dub,
    dhr,
    djb,
    da,
    dob,
    cap,
    lat,
    thg,
    lx,
    lq,
    lp,
    lh,
    la2,
    lo,
    lg,
    lslope,
    wsem,
    osem,
    ysend,
    yrecv,
    gsend,
    grecv,
    lsend,
    lrecv,
    tsend,
    trecv,
):
    rows, length, width, inner, thoughts = sizes
    blocks = inner // width
    bd = BU + blocks
    pairs = HEADS // 2
    me = lax.axis_index("pipe")
    other = 1 - me

    weights = [
        pltpu.make_async_copy(source.at[0], target, wsem.at[number])
        for number, (source, target) in enumerate(
            ((wqkv_h, wqkv), (wout_h, wout), (wup_h, wup), (wdown_h, wdown))
        )
    ]
    for copy in weights:
        copy.start()
    barrier = pltpu.get_barrier_semaphore()
    pl.semaphore_signal(barrier, inc=1, device_id={"pipe": other}, device_id_type=MESH)
    pl.semaphore_wait(barrier, 1)
    sums[...] = jnp.zeros_like(sums)
    joint[:, 0:width] = small[:, BQ * width : (BQ + 1) * width]
    joint[:, width : 2 * width] = jnp.zeros((1, width), F32)
    joint[:, 2 * width : 3 * width] = small[:, BV * width : (BV + 1) * width]

    def remote(source, target, send, recv):
        return pltpu.make_async_remote_copy(
            src_ref=source,
            dst_ref=target,
            send_sem=send,
            recv_sem=recv,
            device_id={"pipe": other},
            device_id_type=MESH,
        )

    def send_y(k):
        return remote(yb.at[k], xin.at[k], ysend.at[k], yrecv.at[k])

    def send_grad(k):
        return remote(yb.at[k], dyb.at[k], gsend.at[k], grecv.at[k])

    def send_lat(r):
        return remote(lat.at[r], lat.at[r], lsend.at[r], lrecv.at[r])

    def send_thoughts(r):
        return remote(thg.at[r], thg.at[r], tsend.at[r], trecv.at[r])

    def started(source, target, number):
        copy = pltpu.make_async_copy(source, target, osem.at[number])
        copy.start()
        return copy

    def finish(copies):
        for copy in copies:
            copy.wait()

    def each_chunk(step, count=32, unroll=2):
        def body(i, carry):
            step(pl.ds(pl.multiple_of(i * count, count), count), i * count)
            return carry

        lax.fori_loop(0, length // count, body, 0, unroll=unroll)

    def loop(count, step):
        def body(i, carry):
            step(i)
            return carry

        lax.fori_loop(0, count, body, 0)

    def add_columns(number, values):
        sums[number] += jnp.sum(values.astype(F32).reshape(-1, 8, width), 0)

    def part_lanes(c):
        return pl.ds(pl.multiple_of(c * width, width), width)

    def row_at(number):
        return small[:, part_lanes(number)]

    def row(number):
        return small[:, group(number)]

    def group(number):
        return slice(number * width, (number + 1) * width)

    lane = lax.broadcasted_iota(jnp.int32, (1, 128), 1)
    low = lane < 64
    halves = (jnp.where(low, 1.0, 0.0).astype(BF), jnp.where(low, 0.0, 1.0).astype(BF))

    def first_length(r):
        segment = seg[pl.ds(r, 1), :]
        return jnp.sum(jnp.where(segment == 0, 1.0, 0.0), -1, keepdims=True).astype(jnp.int32)

    def set_cap(r):
        first = first_length(r)
        query = lax.broadcasted_iota(jnp.int32, (length, length), 0)
        key = lax.broadcasted_iota(jnp.int32, (length, length), 1)
        lowest = jnp.where(query >= first, first, 0)
        cap[...] = jnp.where((key <= query) & (key >= lowest), NO_CAP, MASKED)

    def set_cap_turned(r):
        first = first_length(r)
        key = lax.broadcasted_iota(jnp.int32, (length, length), 0)
        query = lax.broadcasted_iota(jnp.int32, (length, length), 1)
        lowest = jnp.where(query >= first, first, 0)
        capt[...] = jnp.where((key <= query) & (key >= lowest), NO_CAP, MASKED)

    def positions(r, shift, axis=0):
        shape = (LAT, 1) if axis == 0 else (1, LAT)
        number = lax.broadcasted_iota(jnp.int32, shape, axis)
        result = jnp.full(shape, -1, jnp.int32)
        for j in range(thoughts):
            result = jnp.where(number == j, tpos[r, j] - shift, result)
        return result

    def selector_turned(r, shift):
        place = positions(r, shift, 1)
        return jnp.where(lax.broadcasted_iota(jnp.int32, (length, LAT), 0) == place, 1.0, 0.0)

    def selector(place):
        return jnp.where(lax.broadcasted_iota(jnp.int32, (LAT, length), 1) == place, 1.0, 0.0)

    def unmarked(r, start):
        place = lax.broadcasted_iota(jnp.int32, (32, 1), 0) + start
        keep = jnp.ones((32, 1), F32)
        for j in range(thoughts):
            keep = jnp.where(place == tpos[r, j], 0.0, keep)
        return keep

    def head_lanes(part, hp):
        return pl.ds(pl.multiple_of(part * width + hp * 128, 128), 128)

    def norm_rows(x, target, k, which, gain, shift, more=None):
        def step(part, _):
            values = x[part, :]
            center = jnp.mean(values, -1, keepdims=True)
            centred = values - center
            scale = lax.rsqrt(jnp.mean(centred * centred, -1, keepdims=True) + EPSILON)
            stat[k, 2 * which, part, :] = center
            stat[k, 2 * which + 1, part, :] = scale
            target[part, :] = (centred * scale * row(gain) + row(shift)).astype(BF)
            if more is not None:
                more(part, values)

        each_chunk(step)

    def norm_rows_back(x, part, k, which, gain, shift):
        scale = stat[k, 2 * which + 1, part, :]
        hat = (x[part, :] - stat[k, 2 * which, part, :]) * scale
        grad = da[part, :]
        add_columns(gain, grad * hat)
        add_columns(shift, grad)
        return norm_back(hat, scale, grad * row(gain))

    def forward(k, x, y, first=None):
        def need(number):
            if first is not None:

                @pl.when(first)
                def _():
                    weights[number].wait()

        norm_rows(x, a1, k, 0, G1, B1)
        copies = [started(a1, fa1.at[k], 0)]
        need(0)

        def project(c):
            part = part_lanes(c)
            jn[k, :, part] = (dot(a1[...], wqkv[:, part]) + joint[:, part]).astype(BF)

        loop(3, project)

        def heads(hp):
            q = jn[k, :, head_lanes(0, hp)]
            key = jn[k, :, head_lanes(1, hp)]
            value = jn[k, :, head_lanes(2, hp)]
            for start in range(0, length, BLOCK):
                end = start + BLOCK
                out = []
                for h in range(2):
                    scores = dot_nt(q[start:end] * (halves[h] * 0.125), key[:end])
                    chance = softmax(jnp.minimum(scores, cap[start:end, :end])).astype(BF)
                    out.append(dot(chance, value[:end]))
                ob[start:end, head_lanes(0, hp)] = jnp.where(low, out[0], out[1]).astype(BF)

        loop(pairs, heads)
        copies.append(started(ob, fo.at[k], 1))
        need(1)
        hm[k] = x[...] + dot(ob[...], wout[...]) + row(BO)

        def begin(part, values):
            y[part, :] = values + row(bd)

        norm_rows(hm.at[k], a2, k, 1, G2, B2, begin)
        copies.append(started(a2, fa2.at[k], 2))
        need(2)
        need(3)

        def mlp(c):
            part = part_lanes(c)
            wide[...] = dot(a2[...], wup[:, part]) + row_at(BU + c)

            def activate(rows_part, _):
                g, d = gelu_both(wide[rows_part, :])
                gb[rows_part, part] = g.astype(BF)
                slope[k, rows_part, part] = d.astype(BF)

            each_chunk(activate, 16)
            y[...] += dot(gb[:, part], wdown[part, :])

        loop(blocks, mlp)
        copies.append(started(gb, fg.at[k], 3))
        return copies

    def backward(k, x, dy, dx):
        def step(part, _):
            branch = dy[part, :].astype(BF)
            dm[part, :] = branch
            add_columns(bd, branch)

        each_chunk(step)
        copies = [started(dm, fdm.at[k], 4)]
        da[...] = jnp.zeros_like(da)

        def mlp(c):
            part = part_lanes(c)
            wide[...] = dot_nt(dm[...], wdown[part, :])

            def bend(rows_part, _):
                grad = (wide[rows_part, :] * slope[k, rows_part, part]).astype(BF)
                dub[rows_part, part] = grad
                add_columns(BU + c, grad)

            each_chunk(bend)
            da[...] += dot_nt(dub[:, part], wup[:, part])

        loop(blocks, mlp)
        copies.append(started(dub, fdu.at[k], 5))

        def step_two(part, _):
            middle = dy[part, :] + norm_rows_back(hm.at[k], part, k, 1, G2, B2)
            dy[part, :] = middle
            branch = middle.astype(BF)
            dhr[part, :] = branch
            add_columns(BO, branch)

        each_chunk(step_two)
        copies.append(started(dhr, fdhr.at[k], 6))
        dob[...] = dot_nt(dhr[...], wout[...]).astype(BF)
        ktb[...] = jn[k, :, group(1)].T

        def heads(hp):
            q = jn[k, :, head_lanes(0, hp)]
            key = jn[k, :, head_lanes(1, hp)]
            value = jn[k, :, head_lanes(2, hp)]
            grad_out = dob[:, head_lanes(0, hp)]
            dk, dv = [], []
            for h in range(2):
                head = pl.ds(pl.multiple_of(hp * 128 + h * 64, 64), 64)
                dk.append([None] * (length // BLOCK))
                dv.append([None] * (length // BLOCK))
                for start in range(0, length, BLOCK):
                    end = start + BLOCK
                    q_part, grad_part = q[start:end], grad_out[start:end]
                    scores = dot_nt(key[:end], q_part * (halves[h] * 0.125))
                    chance = softmax(jnp.minimum(scores, capt[:end, start:end]), 0)
                    inner_part = chance * dot_nt(value[:end], grad_part * halves[h])
                    total = jnp.sum(inner_part, 0, keepdims=True)
                    grad_scores = (inner_part - chance * total).astype(BF)
                    dqt[head, start:end] = (dot(ktb[head, :end], grad_scores) * 0.125).astype(BF)
                    of_value = dot(chance.astype(BF), grad_part)
                    of_key = dot(grad_scores, q_part)
                    for sums_of, piece in ((dv[h], of_value), (dk[h], of_key)):
                        for number in range(end // BLOCK):
                            block = piece[number * BLOCK : (number + 1) * BLOCK]
                            before = sums_of[number]
                            sums_of[number] = block if before is None else before + block
            for number in range(length // BLOCK):
                place = slice(number * BLOCK, (number + 1) * BLOCK)
                keys = jnp.where(low, dk[0][number], dk[1][number])
                djb[place, head_lanes(1, hp)] = (keys * 0.125).astype(BF)
                values = jnp.where(low, dv[0][number], dv[1][number])
                djb[place, head_lanes(2, hp)] = values.astype(BF)

        loop(pairs, heads)
        djb[:, group(0)] = dqt[...].T
        copies.append(started(djb, fdj.at[k], 7))
        into_input(k, x, dy, dx)
        return copies

    def into_input(k, x, middle, dx):
        da[...] = dot_nt(djb[...], wqkv[...])

        def step(part, _):
            add_columns(BQ, djb[part, group(0)])
            add_columns(BV, djb[part, group(2)])
            dx[part, :] = middle[part, :] + norm_rows_back(x, part, k, 0, G1, B1)

        each_chunk(step)

    def forward_latent(r):
        x = xin.at[r]
        norm_rows(x, a1, r, 0, G1, B1)
        copies = [started(a1, fa1.at[r], 0)]
        jn[r, :, group(1)] = dot(a1[...], wqkv[:, group(1)]).astype(BF)
        jn[r, :, group(2)] = (dot(a1[...], wqkv[:, group(2)]) + row(BV)).astype(BF)
        place = positions(r, 1)
        chosen = exact_dot(selector(place), x[...])
        lx[r] = chosen
        hat, _ = normalized(chosen)
        normed = (hat * row(G1) + row(B1)).astype(BF)
        lq[r] = (dot(normed, wqkv[:, group(0)]) + row(BQ)).astype(BF)
        first = first_length(r)
        key_place = lax.broadcasted_iota(jnp.int32, (LAT, length), 1)
        lowest = jnp.where(place >= first, first, 0)
        limit = jnp.where((key_place <= place) & (key_place >= lowest), NO_CAP, MASKED)

        def heads(hp):
            q = lq[r, :, head_lanes(0, hp)]
            key = jn[r, :, head_lanes(1, hp)]
            value = jn[r, :, head_lanes(2, hp)]
            out = []
            for h in range(2):
                scores = dot_nt(q * (halves[h] * 0.125), key)
                chance = softmax(jnp.minimum(scores, limit)).astype(BF)
                lp[r, 2 * hp + h] = chance
                out.append(dot(chance, value))
            lo[r, :, head_lanes(0, hp)] = jnp.where(low, out[0], out[1]).astype(BF)

        loop(pairs, heads)
        middle = chosen + dot(lo[r], wout[...]) + row(BO)
        lh[r] = middle
        hat, _ = normalized(middle)
        la2[r] = (hat * row(G2) + row(B2)).astype(BF)
        lat[r] = middle + row(bd)

        def mlp(c):
            part = part_lanes(c)
            u = dot(la2[r], wup[:, part]) + row_at(BU + c)
            g, d = gelu_both(u)
            lg[r, :, part] = g.astype(BF)
            lslope[r, :, part] = d.astype(BF)
            lat[r] += dot(lg[r, :, part], wdown[part, :])

        loop(blocks, mlp)
        return copies

    def backward_latent(r, dx):
        grad_result = thg[r]
        branch = grad_result.astype(BF)
        top = slice(0, LAT)
        add_columns(bd, branch)
        dm[top, :] = branch
        a2[top, :] = la2[r]
        ob[top, :] = lo[r]
        gb[top, :] = lg[r]
        copies = [
            started(dm, fdm.at[r], 4),
            started(a2, fa2.at[r], 2),
            started(ob, fo.at[r], 1),
            started(gb, fg.at[r], 3),
        ]
        da[top, :] = jnp.zeros((LAT, width), F32)

        def mlp(c):
            part = part_lanes(c)
            grad = (dot_nt(dm[top, :], wdown[part, :]) * lslope[r, :, part]).astype(BF)
            dub[top, part] = grad
            add_columns(BU + c, grad)
            da[top, :] += dot_nt(grad, wup[:, part])

        loop(blocks, mlp)
        copies.append(started(dub, fdu.at[r], 5))
        hat, scale = normalized(lh[r])
        grad = da[top, :]
        add_columns(G2, grad * hat)
        add_columns(B2, grad)
        middle = grad_result + norm_back(hat, scale, grad * row(G2))
        rounded = middle.astype(BF)
        dhr[top, :] = rounded
        add_columns(BO, rounded)
        copies.append(started(dhr, fdhr.at[r], 6))
        spread = selector_turned(r, 1)
        dyb[r] = exact_dot(spread, middle)
        place = positions(r, 1, 1)
        first = first_length(r)
        key_place = lax.broadcasted_iota(jnp.int32, (length, LAT), 0)
        lowest = jnp.where(place >= first, first, 0)
        limit = jnp.where((key_place <= place) & (key_place >= lowest), NO_CAP, MASKED)
        dob[top, :] = dot_nt(rounded, wout[...]).astype(BF)

        def heads(hp):
            q = lq[r, :, head_lanes(0, hp)]
            key = jn[r, :, head_lanes(1, hp)]
            value = jn[r, :, head_lanes(2, hp)]
            grad_out = dob[top, head_lanes(0, hp)]
            dq, dk, dv = [], [], []
            for h in range(2):
                grad_masked = grad_out * halves[h]
                chance = lp[r, 2 * hp + h].astype(F32)
                inner_part = chance * dot_nt(grad_masked, value)
                total = jnp.sum(inner_part, -1, keepdims=True)
                dq.append(dot((inner_part - chance * total).astype(BF), key))
                scores = dot_nt(key, q * (halves[h] * 0.125))
                chance = softmax(jnp.minimum(scores, limit), 0)
                inner_part = chance * dot_nt(value, grad_masked)
                total = jnp.sum(inner_part, 0, keepdims=True)
                dk.append(dot((inner_part - chance * total).astype(BF), q))
                dv.append(dot(chance.astype(BF), grad_out))
            grad_q = (jnp.where(low, dq[0], dq[1]) * 0.125).astype(BF)
            djb[:, head_lanes(0, hp)] = dot(spread.astype(BF), grad_q).astype(BF)
            djb[:, head_lanes(1, hp)] = (jnp.where(low, dk[0], dk[1]) * 0.125).astype(BF)
            djb[:, head_lanes(2, hp)] = jnp.where(low, dv[0], dv[1]).astype(BF)

        loop(pairs, heads)
        copies.append(started(djb, fdj.at[r], 7))
        into_input(r, xin.at[r], dyb.at[r], dx)
        return copies

    @pl.when(me == 0)
    def _():
        def forward_step(k, carry):
            r = lax.rem(k, rows)
            set_cap(r)

            @pl.when(k < rows)
            def _():
                xin[k] = emb[r].astype(F32)

            @pl.when(k >= rows)
            def _():
                send_lat(r).wait_recv()
                xin[k] = exact_dot(selector_turned(r, 0), lat[r])

                def step(part, start):
                    xin[k, part, :] += emb[r, part, :].astype(F32) * unmarked(r, start)

                each_chunk(step)

            copies = forward(k, xin.at[k], yb.at[k], first=k == 0)
            send_y(k).start()
            finish(copies)
            return carry

        lax.fori_loop(0, 2 * rows, forward_step, 0)

        def backward_step(i, carry):
            k = lax.rem(i + rows, 2 * rows)
            r = lax.rem(i, rows)
            send_y(k).wait_send()
            send_grad(k).wait_recv()
            set_cap_turned(r)
            copies = backward(k, xin.at[k], dyb.at[k], yb.at[k])

            @pl.when(i < rows)
            def _():
                thg[r] = exact_dot(selector(positions(r, 0)), yb[k])
                send_thoughts(r).start()

            @pl.when(i >= rows)
            def _():
                def step(part, start):
                    yb[k, part, :] += yb[rows + r, part, :] * unmarked(r, start)

                each_chunk(step)
                started(yb.at[k], sec.at[0, r], 8).wait()

            finish(copies)
            return carry

        lax.fori_loop(0, 2 * rows, backward_step, 0)

        def drain(r, carry):
            send_thoughts(r).wait_send()
            return carry

        lax.fori_loop(0, rows, drain, 0)

    @pl.when(me == 1)
    def _():
        finish(weights)

        def latent_step(r, carry):
            send_y(r).wait_recv()
            copies = forward_latent(r)
            send_lat(r).start()
            finish(copies)
            return carry

        lax.fori_loop(0, rows, latent_step, 0)

        def language_step(r, carry):
            k = rows + r
            set_cap(r)
            set_cap_turned(r)
            send_y(k).wait_recv()
            copies = forward(k, xin.at[k], dyb.at[k])
            copies.append(started(dyb.at[k], sec.at[0, r], 8))
            dyb[r] = cot[r].astype(F32)
            copies += backward(k, xin.at[k], dyb.at[r], yb.at[k])
            send_grad(k).start()
            finish(copies)
            return carry

        lax.fori_loop(0, rows, language_step, 0)
        for staged in (dm, a2, ob, gb, dub, dhr):
            staged[...] = jnp.zeros_like(staged)

        def latent_back_step(r, carry):
            send_thoughts(r).wait_recv()
            copies = backward_latent(r, yb.at[r])
            send_grad(r).start()
            finish(copies)
            return carry

        lax.fori_loop(0, rows, latent_back_step, 0)

        def drain(r, carry):
            send_lat(r).wait_send()
            send_grad(r).wait_send()
            send_grad(rows + r).wait_send()
            return carry

        lax.fori_loop(0, rows, drain, 0)

    sg[...] = jnp.sum(sums[...], 1)


def layers(emb, cot, seg, tpos, w_qkv, w_out, w_up, w_down, small):
    rows, length, width = emb.shape
    inner = w_up.shape[2]
    thoughts = tpos.shape[1]
    slots = 2 * rows
    packed = small.shape[1] // width
    vmem = pl.BlockSpec(memory_space=pltpu.VMEM)
    anywhere = pl.BlockSpec(memory_space=pl.ANY)
    smem = pl.BlockSpec(memory_space=pltpu.SMEM)

    def factor(columns):
        return jax.ShapeDtypeStruct((slots, length, columns), BF)

    def block(columns, kind=BF):
        return pltpu.VMEM((length, columns), kind)

    def few(columns, kind=BF):
        return pltpu.VMEM((rows, LAT, columns), kind)

    sizes = (rows, length, width, inner, thoughts)
    return pl.pallas_call(
        functools.partial(layers_kernel, sizes),
        out_shape=(
            jax.ShapeDtypeStruct((1, rows, length, width), F32),
            factor(width),
            factor(3 * width),
            factor(width),
            factor(width),
            factor(width),
            factor(inner),
            factor(inner),
            factor(width),
            jax.ShapeDtypeStruct((packed, width), F32),
        ),
        in_specs=[vmem, vmem, vmem, smem] + [anywhere] * 4 + [vmem],
        out_specs=(anywhere,) * 9 + (vmem,),
        scratch_shapes=[
            pltpu.VMEM((packed, 8, width), F32),
            pltpu.VMEM((1, 3 * width), F32),
            pltpu.VMEM((slots, 4, length, 1), F32),
            block(width, F32),
            pltpu.VMEM((width, 3 * width), BF),
            pltpu.VMEM((width, width), BF),
            pltpu.VMEM((width, inner), BF),
            pltpu.VMEM((inner, width), BF),
            pltpu.VMEM((slots, length, width), F32),
            pltpu.VMEM((slots, length, width), F32),
            pltpu.VMEM((slots, length, width), F32),
            pltpu.VMEM((slots, length, 3 * width), BF),
            pltpu.VMEM((width, length), BF),
            pltpu.VMEM((width, length), BF),
            pltpu.VMEM((length, length), F32),
            pltpu.VMEM((slots, length, width), F32),
            pltpu.VMEM((slots, length, inner), BF),
            block(width),
            block(width),
            block(width),
            block(inner),
            block(width),
            block(inner),
            block(width),
            block(3 * width),
            block(width, F32),
            block(width),
            block(length, F32),
            few(width, F32),
            few(width, F32),
            few(width, F32),
            few(width),
            pltpu.VMEM((rows, HEADS, LAT, length), BF),
            few(width, F32),
            few(width),
            few(width),
            few(inner),
            few(inner),
            pltpu.SemaphoreType.DMA((4,)),
            pltpu.SemaphoreType.DMA((9,)),
        ]
        + [pltpu.SemaphoreType.DMA((slots,))] * 4
        + [pltpu.SemaphoreType.DMA((rows,))] * 4,
        compiler_params=pltpu.CompilerParams(
            collective_id=0, has_side_effects=True, vmem_limit_bytes=62 << 20
        ),
    )(emb, cot, seg, tpos, w_qkv, w_out, w_up, w_down, small)


def summed_by_parts(factors, small_grads):
    fa1, fdj, fo, fdhr, fa2, fdu, fg, fdm = factors

    def product(left, right):
        whole = jnp.einsum("ktm,ktn->mn", left, right, preferred_element_type=F32)
        return lax.psum_scatter(whole[None], "dp", scatter_dimension=1, tiled=True)

    small = lax.psum_scatter(
        small_grads.reshape(1, -1), "dp", scatter_dimension=1, tiled=True
    )
    return product(fa1, fdj), product(fo, fdhr), product(fa2, fdu), product(fg, fdm), small


def gradients_kernel(
    sizes,
    plan,
    fa1,
    fdj,
    fo,
    fdhr,
    fa2,
    fdu,
    fg,
    fdm,
    small,
    gqkv,
    gout,
    gup,
    gdown,
    gsmall,
    left,
    right,
    lt,
    gt,
    wa,
    wb,
    ra,
    rb,
    rs,
    xa,
    xb,
    xs,
    ua,
    ub,
    us,
    na,
    nb,
    ns,
    xl,
    ul,
    nl,
    lsem,
    pair_send,
    pair_recv,
    side_send,
    side_recv,
    up_send,
    up_recv,
    down_send,
    down_recv,
):
    width, narrow, depth = sizes
    me = lax.axis_index("dp")
    core = lax.rem(me, 2)
    side = lax.rem(me // 2, 2)
    level = me // 4
    partner = me + 1 - 2 * core
    beside = me + 2 - 4 * side
    above, below = me + 4, me - 4

    def remote(source, target, send, recv, device):
        return pltpu.make_async_remote_copy(
            src_ref=source,
            dst_ref=target,
            send_sem=send,
            recv_sem=recv,
            device_id={"dp": device},
            device_id_type=MESH,
        )

    lefts = {"qkv": fa1, "out": fo, "up": fa2, "down": fg}
    rights = {"qkv": fdj, "out": fdhr, "up": fdu, "down": fdm}
    steps = []
    turned = None
    ahead = 0
    for number, (name, part, _) in enumerate(plan):
        if name == "small":
            continue
        if name == "down":
            while ahead < depth:
                steps.append((number, name, True, ahead, None))
                ahead += 1
            steps += [(number, name, False, block, part) for block in range(depth)]
            continue
        if name != turned:
            steps.append((number, name, True, 0, None))
            turned = name
        steps.append((number, name, False, 0, part))
        for _ in range(2 if number else 1):
            if ahead < depth:
                steps.append((number, "down", True, ahead, None))
                ahead += 1

    def loads(index):
        _, name, turn, block, part = steps[index]
        slot = index % 2
        if turn:
            source = lefts[name].at[:, :, block * width : (block + 1) * width]
            return pltpu.make_async_copy(source, left.at[slot], lsem.at[slot])
        columns = narrow if name == "down" else width
        return pltpu.make_async_copy(
            rights[name].at[:, :, part * columns : (part + 1) * columns],
            right.at[slot, :, :, 0:columns],
            lsem.at[slot],
        )

    def start_loads(index):
        if index < len(steps):
            loads(index).start()

    start_loads(0)

    barrier = pltpu.get_barrier_semaphore()

    def greet(device):
        pl.semaphore_signal(barrier, inc=1, device_id={"dp": device}, device_id_type=MESH)

    greet(partner)
    greet(beside)

    @pl.when(level < 3)
    def _():
        greet(above)

    @pl.when(level > 0)
    def _():
        greet(below)

    pl.semaphore_wait(barrier, 2 + (level + 2) // 3 + (5 - level) // 3)

    views = []
    counts = {"a": 0, "b": 0, "line": 0}
    for number, (name, part, line_first) in enumerate(plan):
        if name == "small":
            views.append((small, rs, xs, us, ns, gsmall))
            continue
        kind = "b" if name == "down" else "a"
        index = counts[kind]
        counts[kind] += 1
        if kind == "a":
            target = {"qkv": gqkv, "out": gout, "up": gup}[name]
            place = target.at[0, :, part * width : (part + 1) * width]
            if line_first:
                along = counts["line"]
                counts["line"] += 1
                further = (xl.at[along], ul.at[along], nl.at[along], place)
            else:
                along = index - counts["line"]
                further = (xa.at[along], ua.at[along], na.at[along], place)
            views.append((wa.at[index % 2], ra.at[index]) + further)
        else:
            place = gdown.at[0, :, part * narrow : (part + 1) * narrow]
            views.append((wb, rb.at[index], xb.at[index], ub.at[index], nb.at[index], place))
    total = len(plan)
    previous = {}
    last_of = {}
    for number, (name, part, _) in enumerate(plan):
        kind = "s" if name == "small" else "b" if name == "down" else "a"
        mine = [n for n in range(number) if ("b" if plan[n][0] == "down" else "a") == kind]
        mine = [n for n in mine if plan[n][0] != "small"]
        back = 1 if kind == "b" else 2
        previous[number] = mine[-back] if kind != "s" and len(mine) >= back else None
        last_of[number] = True
        if previous[number] is not None:
            last_of[previous[number]] = False

    def pair_copy(number):
        w, r = views[number][:2]
        return remote(
            w.at[:, :, 1 - core], r, pair_send.at[number], pair_recv.at[number], partner
        )

    def side_copy(number):
        r, x = views[number][1:3]
        source = r.at[level, 1 - side] if plan[number][2] else r.at[:, 1 - side]
        return remote(source, x, side_send.at[number], side_recv.at[number], beside)

    def along_line(number):
        r, x = views[number][1:3]
        return r if plan[number][2] else x

    def up_copy(number, goal, source=None):
        u = views[number][3]
        return remote(
            u.at[goal - 1] if source is None else source,
            u.at[goal - 1],
            up_send.at[number, goal - 1],
            up_recv.at[number, goal - 1],
            above,
        )

    def down_copy(number, goal, source=None):
        n = views[number][4]
        return remote(
            n.at[goal] if source is None else source,
            n.at[goal],
            down_send.at[number, goal],
            down_recv.at[number, goal],
            below,
        )

    def start_line(number):
        base = along_line(number)

        @pl.when(level == 0)
        def _():
            for goal in (3, 2, 1):
                up_copy(number, goal, base.at[goal]).start()

        @pl.when(level == 3)
        def _():
            for goal in (0, 1, 2):
                down_copy(number, goal, base.at[goal]).start()

    position = {"step": 0}
    slots, length = left.shape[1:3]

    def turn_block(slot, target):
        def body(t, carry):
            tokens = pl.ds(pl.multiple_of(t * length, length), length)
            target[:, tokens] = left[slot, t].T
            return carry

        lax.fori_loop(0, slots, body, 0)

    def right_part(slot, lanes):
        part = right[slot, :, :, lanes]
        return part.reshape(slots * length, part.shape[2])

    def multiply(slot, w):
        def tile(t, carry):
            lanes = pl.ds(pl.multiple_of(t * narrow, narrow), narrow)
            product = dot(lt[...], right_part(slot, lanes))
            w[:, :, :, :, lanes] = product.reshape(w.shape[:4] + (narrow,))
            return carry

        lax.fori_loop(0, width // narrow, tile, 0)


    def produce(number):
        name, part, _ = plan[number]
        if name != "small":
            if previous[number] is not None:
                pair_copy(previous[number]).wait_send()
            w = views[number][0]
            while position["step"] < len(steps) and steps[position["step"]][0] == number:
                index = position["step"]
                position["step"] += 1
                _, source, turn, block, _ = steps[index]
                start_loads(index + 1)
                loads(index).wait()
                if turn:
                    turn_block(index % 2, gt.at[block] if source == "down" else lt)
                elif source == "down":
                    w[block] = dot(gt[block], right_part(index % 2, slice(0, narrow))).reshape(
                        w.shape[1:]
                    )
                else:
                    multiply(index % 2, w)
        pair_copy(number).start()

    def stage_pair(number):
        w, r = views[number][:2]
        pair_copy(number).wait_recv()

        def add(z, carry):
            for s in range(2):
                r[z, s] += w[z, s, core]
            return carry

        lax.fori_loop(0, 4, add, 0)
        if plan[number][2]:
            start_line(number)
        else:
            side_copy(number).start()

    def stage_side(number):
        if plan[number][2]:
            return
        r, x = views[number][1:3]
        side_copy(number).wait_recv()

        def add(z, carry):
            x[z] += r[z, side]
            return carry

        lax.fori_loop(0, 4, add, 0)
        start_line(number)

    def stage_up(number, height):
        u = views[number][3]
        base = along_line(number)

        @pl.when(level == height)
        def _():
            for goal in range(3, height - 1, -1):
                up_copy(number, goal).wait_recv()
                if goal > height:
                    u[goal - 1] += base[goal]
                    up_copy(number, goal).start()

    def stage_down(number, height):
        n = views[number][4]
        base = along_line(number)

        @pl.when(level == height)
        def _():
            for goal in range(0, height + 1):
                down_copy(number, goal).wait_recv()
                if goal < height:
                    n[goal] += base[goal]
                    down_copy(number, goal).start()

    def stage_sum(number):
        u, n, place = views[number][3:]
        base = along_line(number)

        @pl.when(level > 0)
        def _():
            base[level] += u[level - 1]

        @pl.when(level < 3)
        def _():
            base[level] += n[level]

        if plan[number][2]:
            side_copy(number).start()
        else:
            place[...] = base[level]

    def stage_last(number):
        if plan[number][2]:
            r, x = views[number][1:3]
            side_copy(number).wait_recv()
            views[number][5][...] = r[level, side] + x[...]

    def at(stage, number, *more):
        if 0 <= number < total:
            stage(number, *more)

    side_lag, hop = 3, 2
    for moment in range(total + side_lag + 3 * hop + 1):
        at(produce, moment)
        at(stage_pair, moment - 1)
        at(stage_side, moment - side_lag)
        for height in range(4):
            if height > 0:
                at(stage_up, moment - side_lag - hop * height, height)
            if height < 3:
                at(stage_down, moment - side_lag - hop * (3 - height), height)
        at(stage_sum, moment - side_lag - 3 * hop)
        at(stage_last, moment - side_lag - 3 * hop - 1)
    for number in range(total):
        if last_of[number]:
            pair_copy(number).wait_send()
        side_copy(number).wait_send()
        for goal in (1, 2, 3):

            @pl.when(goal > level)
            def _():
                up_copy(number, goal).wait_send()

        for goal in (0, 1, 2):

            @pl.when(goal < level)
            def _():
                down_copy(number, goal).wait_send()


def summed_in_kernel(factors, small_grads):
    fa1, fdj, fo, fdhr, fa2, fdu, fg, fdm = factors
    slots, length, width = fa1.shape
    inner = fg.shape[2]
    owners = 16
    depth = inner // width
    narrow = 256
    a_rows, b_rows = width // owners, inner // owners
    packed = small_grads.size // owners
    lanes = 128
    s_rows = -(-packed // (8 * lanes)) * 8
    small = small_grads.reshape(owners, packed)
    small = jnp.pad(small, ((0, 0), (0, s_rows * lanes - packed)))
    small = small.reshape(4, 2, 2, s_rows, lanes)
    plan = [
        ("qkv", 0, False),
        ("qkv", 1, True),
        ("small", 0, False),
        ("qkv", 2, False),
        ("down", 0, False),
        ("out", 0, True),
        ("down", 1, False),
        ("up", 0, False),
        ("down", 2, False),
        ("up", 1, False),
        ("up", 2, False),
        ("up", 3, False),
    ]
    total = len(plan)
    a_block, b_block, s_block = (a_rows, width), (b_rows, narrow), (s_rows, lanes)
    a_count = total - 1 - width // narrow
    b_count = width // narrow
    line_count = sum(line_first for _, _, line_first in plan)
    vmem = pl.BlockSpec(memory_space=pltpu.VMEM)
    anywhere = pl.BlockSpec(memory_space=pl.ANY)

    def trio(*lead):
        count = a_count if len(lead) == 2 else a_count - line_count
        return [
            pltpu.VMEM((count,) + lead + a_block, F32),
            pltpu.VMEM((b_count,) + lead + b_block, F32),
            pltpu.VMEM(lead + s_block, F32),
        ]

    *grads, small_grad = pl.pallas_call(
        functools.partial(gradients_kernel, (width, narrow, depth), plan),
        out_shape=(
            jax.ShapeDtypeStruct((1, a_rows, 3 * width), F32),
            jax.ShapeDtypeStruct((1, a_rows, width), F32),
            jax.ShapeDtypeStruct((1, a_rows, inner), F32),
            jax.ShapeDtypeStruct((1, b_rows, width), F32),
            jax.ShapeDtypeStruct(s_block, F32),
        ),
        in_specs=[anywhere] * 8 + [vmem],
        out_specs=(vmem,) * 5,
        scratch_shapes=[
            pltpu.VMEM((2, slots, length, width), BF),
            pltpu.VMEM((2, slots, length, width), BF),
            pltpu.VMEM((width, slots * length), BF),
            pltpu.VMEM((depth, width, slots * length), BF),
            pltpu.VMEM((2, 4, 2, 2) + a_block, F32),
            pltpu.VMEM((4, 2, 2) + b_block, F32),
        ]
        + trio(4, 2)
        + trio(4)
        + trio(3)
        + trio(3)
        + [
            pltpu.VMEM((line_count,) + a_block, F32),
            pltpu.VMEM((line_count, 3, 2) + a_block, F32),
            pltpu.VMEM((line_count, 3, 2) + a_block, F32),
        ]
        + [pltpu.SemaphoreType.DMA((2,))]
        + [pltpu.SemaphoreType.DMA((total,))] * 4
        + [pltpu.SemaphoreType.DMA((total, 3))] * 4,
        compiler_params=pltpu.CompilerParams(
            collective_id=1, has_side_effects=True, vmem_limit_bytes=62 << 20
        ),
    )(*factors, small)
    small_grad = small_grad.reshape(1, -1)[:, :packed]
    return tuple(grads) + (small_grad,)


def reduced(factors, small_grads):
    if lax.axis_size("dp") == 16:
        return summed_in_kernel(factors, small_grads)
    return summed_by_parts(factors, small_grads)


def per_device(
    embeddings, cotangent, seg_ids, thought_pos, w_qkv, w_out, w_up, w_down, small_params
):
    section_out, *factors, small_grads = layers(
        embeddings, cotangent, seg_ids, thought_pos, w_qkv, w_out, w_up, w_down, small_params
    )
    return (section_out,) + tuple(reduced(factors, small_grads))


def solution(mesh):
    return jax.shard_map(
        per_device,
        mesh=mesh,
        in_specs=(
            P("dp", None, None),
            P("dp", None, None),
            P("dp", None),
            P("dp", None),
            P("pipe", None, None),
            P("pipe", None, None),
            P("pipe", None, None),
            P("pipe", None, None),
            P("pipe", None),
        ),
        out_specs=(
            P("pipe", "dp", None, None),
            P("pipe", "dp", None),
            P("pipe", "dp", None),
            P("pipe", "dp", None),
            P("pipe", "dp", None),
            P("pipe", "dp"),
        ),
        check_vma=False,
    )
```

```python
import functools

import jax
import jax.numpy as jnp
from jax import lax
from jax.experimental import pallas as pl
from jax.experimental.pallas import tpu as pltpu
from jax.sharding import PartitionSpec as P

HEADS = 12
BF = jnp.bfloat16
F32 = jnp.float32
MESH = pl.DeviceIdType.MESH
EPSILON = 1e-05
MASKED = -1000000000.0
NO_CAP = 3e38
LAT = 16
BLOCK = 128
G1, B1, BQ, BV, BO, G2, B2, BU = 0, 1, 2, 3, 4, 5, 6, 7


def dot(a, b):
    return lax.dot_general(a, b, (((1,), (0,)), ((), ())), preferred_element_type=F32)


def dot_nt(a, b):
    return lax.dot_general(a, b, (((1,), (1,)), ((), ())), preferred_element_type=F32)


def exact_dot(a, b):
    return lax.dot_general(
        a,
        b,
        (((1,), (0,)), ((), ())),
        precision=lax.Precision.HIGHEST,
        preferred_element_type=F32,
    )


def normalized(values):
    centred = values - jnp.mean(values, -1, keepdims=True)
    spread = jnp.mean(centred * centred, -1, keepdims=True)
    scale = lax.rsqrt(spread + EPSILON)
    return centred * scale, scale


def norm_back(hat, scale, grad):
    along = jnp.mean(grad * hat, -1, keepdims=True)
    return scale * (grad - jnp.mean(grad, -1, keepdims=True) - hat * along)


def gelu_both(u):
    c = 0.7978845608028654
    square = u * u
    t = jnp.tanh(c * u * (1.0 + 0.044715 * square))
    half = 0.5 + 0.5 * t
    slope = half + (0.5 * c) * u * (1.0 - t * t) * (1.0 + (3 * 0.044715) * square)
    return u * half, slope


def softmax(scores, axis=-1):
    e = jnp.exp(scores - jnp.max(scores, axis, keepdims=True))
    return e * (1.0 / jnp.sum(e, axis, keepdims=True))


def layers_kernel(
    sizes,
    emb,
    cot,
    seg,
    tpos,
    wqkv_h,
    wout_h,
    wup_h,
    wdown_h,
    small,
    sec,
    fa1,
    fdj,
    fo,
    fdhr,
    fa2,
    fdu,
    fg,
    fdm,
    sg,
    sums,
    joint,
    stat,
    wqkv,
    wout,
    wup,
    wdown,
    xin,
    yb,
    dyb,
    jn,
    ktb,
    dqt,
    capt,
    hm,
    slope,
    a1,
    ob,
    a2,
    gb,
    dm,
    dub,
    dhr,
    djb,
    da,
    dob,
    cap,
    lat,
    thg,
    lx,
    lq,
    lp,
    lh,
    la2,
    lo,
    lg,
    lslope,
    wsem,
    osem,
    ysend,
    yrecv,
    gsend,
    grecv,
    lsend,
    lrecv,
    tsend,
    trecv,
):
    rows, length, width, inner, thoughts = sizes
    blocks = inner // width
    bd = BU + blocks
    pairs = HEADS // 2
    me = lax.axis_index("pipe")
    other = 1 - me

    weights = [
        pltpu.make_async_copy(source.at[0], target, wsem.at[number])
        for number, (source, target) in enumerate(
            ((wqkv_h, wqkv), (wout_h, wout), (wup_h, wup), (wdown_h, wdown))
        )
    ]
    for copy in weights:
        copy.start()
    barrier = pltpu.get_barrier_semaphore()
    pl.semaphore_signal(barrier, inc=1, device_id={"pipe": other}, device_id_type=MESH)
    pl.semaphore_wait(barrier, 1)
    sums[...] = jnp.zeros_like(sums)
    joint[:, 0:width] = small[:, BQ * width : (BQ + 1) * width]
    joint[:, width : 2 * width] = jnp.zeros((1, width), F32)
    joint[:, 2 * width : 3 * width] = small[:, BV * width : (BV + 1) * width]

    def remote(source, target, send, recv):
        return pltpu.make_async_remote_copy(
            src_ref=source,
            dst_ref=target,
            send_sem=send,
            recv_sem=recv,
            device_id={"pipe": other},
            device_id_type=MESH,
        )

    def send_y(k):
        return remote(yb.at[k], xin.at[k], ysend.at[k], yrecv.at[k])

    def send_grad(k):
        return remote(yb.at[k], dyb.at[k], gsend.at[k], grecv.at[k])

    def send_lat(r):
        return remote(lat.at[r], lat.at[r], lsend.at[r], lrecv.at[r])

    def send_thoughts(r):
        return remote(thg.at[r], thg.at[r], tsend.at[r], trecv.at[r])

    def started(source, target, number):
        copy = pltpu.make_async_copy(source, target, osem.at[number])
        copy.start()
        return copy

    def finish(copies):
        for copy in copies:
            copy.wait()

    def each_chunk(step, count):
        def body(i, carry):
            step(pl.ds(pl.multiple_of(i * count, count), count), i * count)
            return carry

        lax.fori_loop(0, length // count, body, 0)

    def loop(count, step):
        def body(i, carry):
            step(i)
            return carry

        lax.fori_loop(0, count, body, 0)

    def add_columns(number, values):
        sums[number] += jnp.sum(values.astype(F32).reshape(-1, 8, width), 0)

    def row(number):
        return small[:, group(number)]

    def group(number):
        return slice(number * width, (number + 1) * width)

    lane = lax.broadcasted_iota(jnp.int32, (1, 128), 1)
    low = lane < 64
    halves = (jnp.where(low, 1.0, 0.0).astype(BF), jnp.where(low, 0.0, 1.0).astype(BF))

    def first_length(r):
        segment = seg[pl.ds(r, 1), :]
        return jnp.sum(jnp.where(segment == 0, 1.0, 0.0), -1, keepdims=True).astype(jnp.int32)

    def set_cap(r):
        first = first_length(r)
        query = lax.broadcasted_iota(jnp.int32, (length, length), 0)
        key = lax.broadcasted_iota(jnp.int32, (length, length), 1)
        lowest = jnp.where(query >= first, first, 0)
        cap[...] = jnp.where((key <= query) & (key >= lowest), NO_CAP, MASKED)

    def set_cap_turned(r):
        first = first_length(r)
        key = lax.broadcasted_iota(jnp.int32, (length, length), 0)
        query = lax.broadcasted_iota(jnp.int32, (length, length), 1)
        lowest = jnp.where(query >= first, first, 0)
        capt[...] = jnp.where((key <= query) & (key >= lowest), NO_CAP, MASKED)

    def positions(r, shift, axis=0):
        shape = (LAT, 1) if axis == 0 else (1, LAT)
        number = lax.broadcasted_iota(jnp.int32, shape, axis)
        result = jnp.full(shape, -1, jnp.int32)
        for j in range(thoughts):
            result = jnp.where(number == j, tpos[r, j] - shift, result)
        return result

    def selector_turned(r, shift):
        place = positions(r, shift, 1)
        return jnp.where(lax.broadcasted_iota(jnp.int32, (length, LAT), 0) == place, 1.0, 0.0)

    def selector(place):
        return jnp.where(lax.broadcasted_iota(jnp.int32, (LAT, length), 1) == place, 1.0, 0.0)

    def unmarked(r, start):
        place = lax.broadcasted_iota(jnp.int32, (32, 1), 0) + start
        keep = jnp.ones((32, 1), F32)
        for j in range(thoughts):
            keep = jnp.where(place == tpos[r, j], 0.0, keep)
        return keep

    def head_lanes(part, hp):
        start = part * width + hp * 128
        if isinstance(hp, int):
            return slice(start, start + 128)
        return pl.ds(pl.multiple_of(start, 128), 128)

    def norm_rows(x, target, k, which, gain, shift, more=None):
        def step(part, _):
            values = x[part, :]
            center = jnp.mean(values, -1, keepdims=True)
            centred = values - center
            scale = lax.rsqrt(jnp.mean(centred * centred, -1, keepdims=True) + EPSILON)
            stat[k, 2 * which, part, :] = center
            stat[k, 2 * which + 1, part, :] = scale
            target[part, :] = (centred * scale * row(gain) + row(shift)).astype(BF)
            if more is not None:
                more(part, values)

        each_chunk(step, 128)

    def norm_rows_back(x, part, k, which, gain, shift):
        scale = stat[k, 2 * which + 1, part, :]
        hat = (x[part, :] - stat[k, 2 * which, part, :]) * scale
        grad = da[part, :]
        add_columns(gain, grad * hat)
        add_columns(shift, grad)
        return norm_back(hat, scale, grad * row(gain))

    def forward(k, x, y, first=None):
        def need(number):
            if first is not None:

                @pl.when(first)
                def _():
                    weights[number].wait()

        norm_rows(x, a1, k, 0, G1, B1)
        copies = [started(a1, fa1.at[k], 0)]
        need(0)

        for part in range(3):
            joined = dot(a1[...], wqkv[:, group(part)]) + joint[:, group(part)]
            jn[k, :, group(part)] = joined.astype(BF)
        for hp in range(pairs):
            q = jn[k, :, head_lanes(0, hp)]
            key = jn[k, :, head_lanes(1, hp)]
            value = jn[k, :, head_lanes(2, hp)]
            out = []
            for h in range(2):
                scores = dot_nt(q * (halves[h] * 0.125), key)
                chance = softmax(jnp.minimum(scores, cap[...])).astype(BF)
                out.append(dot(chance, value))
            ob[:, head_lanes(0, hp)] = jnp.where(low, out[0], out[1]).astype(BF)
        copies.append(started(ob, fo.at[k], 1))
        need(1)
        hm[k] = x[...] + dot(ob[...], wout[...]) + row(BO)

        def begin(part, values):
            y[part, :] = values + row(bd)

        norm_rows(hm.at[k], a2, k, 1, G2, B2, begin)
        copies.append(started(a2, fa2.at[k], 2))
        need(2)
        need(3)

        for c in range(blocks):
            part = group(c)
            g, d = gelu_both(dot(a2[...], wup[:, part]) + row(BU + c))
            gb[:, part] = g.astype(BF)
            slope[k, :, part] = d.astype(BF)
            y[...] += dot(gb[:, part], wdown[part, :])
        copies.append(started(gb, fg.at[k], 3))
        return copies

    def backward(k, x, dy, dx):
        def step(part, _):
            branch = dy[part, :].astype(BF)
            dm[part, :] = branch
            add_columns(bd, branch)

        each_chunk(step, 64)
        copies = [started(dm, fdm.at[k], 4)]
        da[...] = jnp.zeros_like(da)

        for c in range(blocks):
            part = group(c)
            grad = (dot_nt(dm[...], wdown[part, :]) * slope[k, :, part]).astype(BF)
            dub[:, part] = grad
            add_columns(BU + c, grad)
            da[...] += dot_nt(grad, wup[:, part])
        copies.append(started(dub, fdu.at[k], 5))

        def step_two(part, _):
            middle = dy[part, :] + norm_rows_back(hm.at[k], part, k, 1, G2, B2)
            dy[part, :] = middle
            branch = middle.astype(BF)
            dhr[part, :] = branch
            add_columns(BO, branch)

        each_chunk(step_two, 64)
        copies.append(started(dhr, fdhr.at[k], 6))
        dob[...] = dot_nt(dhr[...], wout[...]).astype(BF)
        ktb[...] = jn[k, :, group(1)].T

        def heads(hp):
            q = jn[k, :, head_lanes(0, hp)]
            key = jn[k, :, head_lanes(1, hp)]
            value = jn[k, :, head_lanes(2, hp)]
            grad_out = dob[:, head_lanes(0, hp)]
            dk, dv = [], []
            for h in range(2):
                head = pl.ds(pl.multiple_of(hp * 128 + h * 64, 64), 64)
                dk.append([None] * (length // BLOCK))
                dv.append([None] * (length // BLOCK))
                for start in range(0, length, BLOCK):
                    end = start + BLOCK
                    q_part, grad_part = q[start:end], grad_out[start:end]
                    scores = dot_nt(key[:end], q_part * (halves[h] * 0.125))
                    chance = softmax(jnp.minimum(scores, capt[:end, start:end]), 0)
                    inner_part = chance * dot_nt(value[:end], grad_part * halves[h])
                    total = jnp.sum(inner_part, 0, keepdims=True)
                    grad_scores = (inner_part - chance * total).astype(BF)
                    dqt[head, start:end] = (dot(ktb[head, :end], grad_scores) * 0.125).astype(BF)
                    of_value = dot(chance.astype(BF), grad_part)
                    of_key = dot(grad_scores, q_part)
                    for sums_of, piece in ((dv[h], of_value), (dk[h], of_key)):
                        for number in range(end // BLOCK):
                            block = piece[number * BLOCK : (number + 1) * BLOCK]
                            before = sums_of[number]
                            sums_of[number] = block if before is None else before + block
            for number in range(length // BLOCK):
                place = slice(number * BLOCK, (number + 1) * BLOCK)
                keys = jnp.where(low, dk[0][number], dk[1][number])
                djb[place, head_lanes(1, hp)] = (keys * 0.125).astype(BF)
                values = jnp.where(low, dv[0][number], dv[1][number])
                djb[place, head_lanes(2, hp)] = values.astype(BF)

        loop(pairs, heads)
        djb[:, group(0)] = dqt[...].T
        copies.append(started(djb, fdj.at[k], 7))
        into_input(k, x, dy, dx)
        return copies

    def into_input(k, x, middle, dx):
        da[...] = dot_nt(djb[...], wqkv[...])

        def step(part, _):
            add_columns(BQ, djb[part, group(0)])
            add_columns(BV, djb[part, group(2)])
            dx[part, :] = middle[part, :] + norm_rows_back(x, part, k, 0, G1, B1)

        each_chunk(step, 64)

    def forward_latent(r):
        x = xin.at[r]
        norm_rows(x, a1, r, 0, G1, B1)
        copies = [started(a1, fa1.at[r], 0)]
        jn[r, :, group(1)] = dot(a1[...], wqkv[:, group(1)]).astype(BF)
        jn[r, :, group(2)] = (dot(a1[...], wqkv[:, group(2)]) + row(BV)).astype(BF)
        place = positions(r, 1)
        chosen = exact_dot(selector(place), x[...])
        lx[r] = chosen
        hat, _ = normalized(chosen)
        normed = (hat * row(G1) + row(B1)).astype(BF)
        lq[r] = (dot(normed, wqkv[:, group(0)]) + row(BQ)).astype(BF)
        first = first_length(r)
        key_place = lax.broadcasted_iota(jnp.int32, (LAT, length), 1)
        lowest = jnp.where(place >= first, first, 0)
        limit = jnp.where((key_place <= place) & (key_place >= lowest), NO_CAP, MASKED)

        def heads(hp):
            q = lq[r, :, head_lanes(0, hp)]
            key = jn[r, :, head_lanes(1, hp)]
            value = jn[r, :, head_lanes(2, hp)]
            out = []
            for h in range(2):
                scores = dot_nt(q * (halves[h] * 0.125), key)
                chance = softmax(jnp.minimum(scores, limit)).astype(BF)
                lp[r, 2 * hp + h] = chance
                out.append(dot(chance, value))
            lo[r, :, head_lanes(0, hp)] = jnp.where(low, out[0], out[1]).astype(BF)

        for hp in range(pairs):
            heads(hp)
        middle = chosen + dot(lo[r], wout[...]) + row(BO)
        lh[r] = middle
        hat, _ = normalized(middle)
        la2[r] = (hat * row(G2) + row(B2)).astype(BF)
        lat[r] = middle + row(bd)

        def mlp(c):
            part = group(c)
            u = dot(la2[r], wup[:, part]) + row(BU + c)
            g, d = gelu_both(u)
            lg[r, :, part] = g.astype(BF)
            lslope[r, :, part] = d.astype(BF)
            lat[r] += dot(lg[r, :, part], wdown[part, :])

        for c in range(blocks):
            mlp(c)
        return copies

    def backward_latent(r, dx):
        grad_result = thg[r]
        branch = grad_result.astype(BF)
        top = slice(0, LAT)
        add_columns(bd, branch)
        dm[top, :] = branch
        a2[top, :] = la2[r]
        ob[top, :] = lo[r]
        gb[top, :] = lg[r]
        copies = [
            started(dm, fdm.at[r], 4),
            started(a2, fa2.at[r], 2),
            started(ob, fo.at[r], 1),
            started(gb, fg.at[r], 3),
        ]
        da[top, :] = jnp.zeros((LAT, width), F32)

        def mlp(c):
            part = group(c)
            grad = (dot_nt(dm[top, :], wdown[part, :]) * lslope[r, :, part]).astype(BF)
            dub[top, part] = grad
            add_columns(BU + c, grad)
            da[top, :] += dot_nt(grad, wup[:, part])

        for c in range(blocks):
            mlp(c)
        copies.append(started(dub, fdu.at[r], 5))
        hat, scale = normalized(lh[r])
        grad = da[top, :]
        add_columns(G2, grad * hat)
        add_columns(B2, grad)
        middle = grad_result + norm_back(hat, scale, grad * row(G2))
        rounded = middle.astype(BF)
        dhr[top, :] = rounded
        add_columns(BO, rounded)
        copies.append(started(dhr, fdhr.at[r], 6))
        spread = selector_turned(r, 1)
        dyb[r] = exact_dot(spread, middle)
        place = positions(r, 1, 1)
        first = first_length(r)
        key_place = lax.broadcasted_iota(jnp.int32, (length, LAT), 0)
        lowest = jnp.where(place >= first, first, 0)
        limit = jnp.where((key_place <= place) & (key_place >= lowest), NO_CAP, MASKED)
        dob[top, :] = dot_nt(rounded, wout[...]).astype(BF)

        def heads(hp):
            q = lq[r, :, head_lanes(0, hp)]
            key = jn[r, :, head_lanes(1, hp)]
            value = jn[r, :, head_lanes(2, hp)]
            grad_out = dob[top, head_lanes(0, hp)]
            dq, dk, dv = [], [], []
            for h in range(2):
                grad_masked = grad_out * halves[h]
                chance = lp[r, 2 * hp + h].astype(F32)
                inner_part = chance * dot_nt(grad_masked, value)
                total = jnp.sum(inner_part, -1, keepdims=True)
                dq.append(dot((inner_part - chance * total).astype(BF), key))
                scores = dot_nt(key, q * (halves[h] * 0.125))
                chance = softmax(jnp.minimum(scores, limit), 0)
                inner_part = chance * dot_nt(value, grad_masked)
                total = jnp.sum(inner_part, 0, keepdims=True)
                dk.append(dot((inner_part - chance * total).astype(BF), q))
                dv.append(dot(chance.astype(BF), grad_out))
            grad_q = (jnp.where(low, dq[0], dq[1]) * 0.125).astype(BF)
            djb[:, head_lanes(0, hp)] = dot(spread.astype(BF), grad_q).astype(BF)
            djb[:, head_lanes(1, hp)] = (jnp.where(low, dk[0], dk[1]) * 0.125).astype(BF)
            djb[:, head_lanes(2, hp)] = jnp.where(low, dv[0], dv[1]).astype(BF)

        for hp in range(pairs):
            heads(hp)
        copies.append(started(djb, fdj.at[r], 7))
        into_input(r, xin.at[r], dyb.at[r], dx)
        return copies

    @pl.when(me == 0)
    def _():
        def forward_step(k, carry):
            r = lax.rem(k, rows)
            set_cap(r)

            @pl.when(k < rows)
            def _():
                xin[k] = emb[r].astype(F32)

            @pl.when(k >= rows)
            def _():
                send_lat(r).wait_recv()
                xin[k] = exact_dot(selector_turned(r, 0), lat[r])

                def step(part, start):
                    xin[k, part, :] += emb[r, part, :].astype(F32) * unmarked(r, start)

                each_chunk(step, 32)

            copies = forward(k, xin.at[k], yb.at[k], first=k == 0)
            send_y(k).start()
            finish(copies)
            return carry

        lax.fori_loop(0, 2 * rows, forward_step, 0)

        def backward_step(i, carry):
            k = lax.rem(i + rows, 2 * rows)
            r = lax.rem(i, rows)
            send_y(k).wait_send()
            send_grad(k).wait_recv()
            set_cap_turned(r)
            copies = backward(k, xin.at[k], dyb.at[k], yb.at[k])

            @pl.when(i < rows)
            def _():
                thg[r] = exact_dot(selector(positions(r, 0)), yb[k])
                send_thoughts(r).start()

            @pl.when(i >= rows)
            def _():
                def step(part, start):
                    yb[k, part, :] += yb[rows + r, part, :] * unmarked(r, start)

                each_chunk(step, 32)
                started(yb.at[k], sec.at[0, r], 8).wait()

            finish(copies)
            return carry

        lax.fori_loop(0, 2 * rows, backward_step, 0)

        def drain(r, carry):
            send_thoughts(r).wait_send()
            return carry

        lax.fori_loop(0, rows, drain, 0)

    @pl.when(me == 1)
    def _():
        finish(weights)

        def latent_step(r, carry):
            send_y(r).wait_recv()
            copies = forward_latent(r)
            send_lat(r).start()
            finish(copies)
            return carry

        lax.fori_loop(0, rows, latent_step, 0)

        def language_step(r, carry):
            k = rows + r
            set_cap(r)
            set_cap_turned(r)
            send_y(k).wait_recv()
            copies = forward(k, xin.at[k], dyb.at[k])
            copies.append(started(dyb.at[k], sec.at[0, r], 8))
            dyb[r] = cot[r].astype(F32)
            copies += backward(k, xin.at[k], dyb.at[r], yb.at[k])
            send_grad(k).start()
            finish(copies)
            return carry

        lax.fori_loop(0, rows, language_step, 0)
        for staged in (dm, a2, ob, gb, dub, dhr):
            staged[...] = jnp.zeros_like(staged)

        def latent_back_step(r, carry):
            send_thoughts(r).wait_recv()
            copies = backward_latent(r, yb.at[r])
            send_grad(r).start()
            finish(copies)
            return carry

        lax.fori_loop(0, rows, latent_back_step, 0)

        def drain(r, carry):
            send_lat(r).wait_send()
            send_grad(r).wait_send()
            send_grad(rows + r).wait_send()
            return carry

        lax.fori_loop(0, rows, drain, 0)

    sg[...] = jnp.sum(sums[...], 1)


def layers(emb, cot, seg, tpos, w_qkv, w_out, w_up, w_down, small):
    rows, length, width = emb.shape
    inner = w_up.shape[2]
    thoughts = tpos.shape[1]
    slots = 2 * rows
    packed = small.shape[1] // width
    vmem = pl.BlockSpec(memory_space=pltpu.VMEM)
    anywhere = pl.BlockSpec(memory_space=pl.ANY)
    smem = pl.BlockSpec(memory_space=pltpu.SMEM)

    def factor(columns):
        return jax.ShapeDtypeStruct((slots, length, columns), BF)

    def block(columns, kind=BF):
        return pltpu.VMEM((length, columns), kind)

    def few(columns, kind=BF):
        return pltpu.VMEM((rows, LAT, columns), kind)

    sizes = (rows, length, width, inner, thoughts)
    return pl.pallas_call(
        functools.partial(layers_kernel, sizes),
        out_shape=(
            jax.ShapeDtypeStruct((1, rows, length, width), F32),
            factor(width),
            factor(3 * width),
            factor(width),
            factor(width),
            factor(width),
            factor(inner),
            factor(inner),
            factor(width),
            jax.ShapeDtypeStruct((packed, width), F32),
        ),
        in_specs=[vmem, vmem, vmem, smem] + [anywhere] * 4 + [vmem],
        out_specs=(anywhere,) * 9 + (vmem,),
        scratch_shapes=[
            pltpu.VMEM((packed, 8, width), F32),
            pltpu.VMEM((1, 3 * width), F32),
            pltpu.VMEM((slots, 4, length, 1), F32),
            pltpu.VMEM((width, 3 * width), BF),
            pltpu.VMEM((width, width), BF),
            pltpu.VMEM((width, inner), BF),
            pltpu.VMEM((inner, width), BF),
            pltpu.VMEM((slots, length, width), F32),
            pltpu.VMEM((slots, length, width), F32),
            pltpu.VMEM((slots, length, width), F32),
            pltpu.VMEM((slots, length, 3 * width), BF),
            pltpu.VMEM((width, length), BF),
            pltpu.VMEM((width, length), BF),
            pltpu.VMEM((length, length), F32),
            pltpu.VMEM((slots, length, width), F32),
            pltpu.VMEM((slots, length, inner), BF),
            block(width),
            block(width),
            block(width),
            block(inner),
            block(width),
            block(inner),
            block(width),
            block(3 * width),
            block(width, F32),
            block(width),
            block(length, F32),
            few(width, F32),
            few(width, F32),
            few(width, F32),
            few(width),
            pltpu.VMEM((rows, HEADS, LAT, length), BF),
            few(width, F32),
            few(width),
            few(width),
            few(inner),
            few(inner),
            pltpu.SemaphoreType.DMA((4,)),
            pltpu.SemaphoreType.DMA((9,)),
        ]
        + [pltpu.SemaphoreType.DMA((slots,))] * 4
        + [pltpu.SemaphoreType.DMA((rows,))] * 4,
        compiler_params=pltpu.CompilerParams(
            collective_id=0, has_side_effects=True, vmem_limit_bytes=62 << 20
        ),
    )(emb, cot, seg, tpos, w_qkv, w_out, w_up, w_down, small)


def summed_by_parts(factors, small_grads):
    fa1, fdj, fo, fdhr, fa2, fdu, fg, fdm = factors

    def product(left, right):
        whole = jnp.einsum("ktm,ktn->mn", left, right, preferred_element_type=F32)
        return lax.psum_scatter(whole[None], "dp", scatter_dimension=1, tiled=True)

    small = lax.psum_scatter(
        small_grads.reshape(1, -1), "dp", scatter_dimension=1, tiled=True
    )
    return product(fa1, fdj), product(fo, fdhr), product(fa2, fdu), product(fg, fdm), small


def gradients_kernel(
    sizes,
    plan,
    fa1,
    fdj,
    fo,
    fdhr,
    fa2,
    fdu,
    fg,
    fdm,
    small,
    gqkv,
    gout,
    gup,
    gdown,
    gsmall,
    left,
    right,
    lt,
    gt,
    wa,
    wb,
    ra,
    rb,
    rs,
    xa,
    xb,
    xs,
    ua,
    ub,
    us,
    na,
    nb,
    ns,
    xl,
    ul,
    nl,
    lsem,
    pair_send,
    pair_recv,
    side_send,
    side_recv,
    up_send,
    up_recv,
    down_send,
    down_recv,
):
    width, narrow, depth = sizes
    me = lax.axis_index("dp")
    core = lax.rem(me, 2)
    side = lax.rem(me // 2, 2)
    level = me // 4
    partner = me + 1 - 2 * core
    beside = me + 2 - 4 * side
    above, below = me + 4, me - 4

    def remote(source, target, send, recv, device):
        return pltpu.make_async_remote_copy(
            src_ref=source,
            dst_ref=target,
            send_sem=send,
            recv_sem=recv,
            device_id={"dp": device},
            device_id_type=MESH,
        )

    lefts = {"qkv": fa1, "out": fo, "up": fa2, "down": fg}
    rights = {"qkv": fdj, "out": fdhr, "up": fdu, "down": fdm}
    steps = []
    turned = None
    ahead = 0
    for number, (name, part, _) in enumerate(plan):
        if name == "small":
            continue
        if name == "down":
            while ahead < depth:
                steps.append((number, name, True, ahead, None))
                ahead += 1
            steps += [(number, name, False, block, part) for block in range(depth)]
            continue
        if name != turned:
            steps.append((number, name, True, 0, None))
            turned = name
        steps.append((number, name, False, 0, part))
        for _ in range(2 if number else 1):
            if ahead < depth:
                steps.append((number, "down", True, ahead, None))
                ahead += 1

    def loads(index):
        _, name, turn, block, part = steps[index]
        slot = index % 2
        if turn:
            source = lefts[name].at[:, :, block * width : (block + 1) * width]
            return pltpu.make_async_copy(source, left.at[slot], lsem.at[slot])
        columns = narrow if name == "down" else width
        return pltpu.make_async_copy(
            rights[name].at[:, :, part * columns : (part + 1) * columns],
            right.at[slot, :, :, 0:columns],
            lsem.at[slot],
        )

    def start_loads(index):
        if index < len(steps):
            loads(index).start()

    start_loads(0)

    barrier = pltpu.get_barrier_semaphore()

    def greet(device):
        pl.semaphore_signal(barrier, inc=1, device_id={"dp": device}, device_id_type=MESH)

    greet(partner)
    greet(beside)

    @pl.when(level < 3)
    def _():
        greet(above)

    @pl.when(level > 0)
    def _():
        greet(below)

    pl.semaphore_wait(barrier, 2 + (level + 2) // 3 + (5 - level) // 3)

    views = []
    counts = {"a": 0, "b": 0, "line": 0}
    for number, (name, part, line_first) in enumerate(plan):
        if name == "small":
            views.append((small, rs, xs, us, ns, gsmall))
            continue
        kind = "b" if name == "down" else "a"
        index = counts[kind]
        counts[kind] += 1
        if kind == "a":
            target = {"qkv": gqkv, "out": gout, "up": gup}[name]
            place = target.at[0, :, part * width : (part + 1) * width]
            if line_first:
                along = counts["line"]
                counts["line"] += 1
                further = (xl.at[along], ul.at[along], nl.at[along], place)
            else:
                along = index - counts["line"]
                further = (xa.at[along], ua.at[along], na.at[along], place)
            views.append((wa.at[index % 2], ra.at[index]) + further)
        else:
            place = gdown.at[0, :, part * narrow : (part + 1) * narrow]
            views.append((wb, rb.at[index], xb.at[index], ub.at[index], nb.at[index], place))
    total = len(plan)
    previous = {}
    last_of = {}
    for number, (name, part, _) in enumerate(plan):
        kind = "s" if name == "small" else "b" if name == "down" else "a"
        mine = [n for n in range(number) if ("b" if plan[n][0] == "down" else "a") == kind]
        mine = [n for n in mine if plan[n][0] != "small"]
        back = 1 if kind == "b" else 2
        previous[number] = mine[-back] if kind != "s" and len(mine) >= back else None
        last_of[number] = True
        if previous[number] is not None:
            last_of[previous[number]] = False

    def pair_copy(number):
        w, r = views[number][:2]
        return remote(
            w.at[:, :, 1 - core], r, pair_send.at[number], pair_recv.at[number], partner
        )

    def side_copy(number):
        r, x = views[number][1:3]
        source = r.at[level, 1 - side] if plan[number][2] else r.at[:, 1 - side]
        return remote(source, x, side_send.at[number], side_recv.at[number], beside)

    def along_line(number):
        r, x = views[number][1:3]
        return r if plan[number][2] else x

    def up_copy(number, goal, source=None):
        u = views[number][3]
        return remote(
            u.at[goal - 1] if source is None else source,
            u.at[goal - 1],
            up_send.at[number, goal - 1],
            up_recv.at[number, goal - 1],
            above,
        )

    def down_copy(number, goal, source=None):
        n = views[number][4]
        return remote(
            n.at[goal] if source is None else source,
            n.at[goal],
            down_send.at[number, goal],
            down_recv.at[number, goal],
            below,
        )

    def start_line(number):
        base = along_line(number)

        @pl.when(level == 0)
        def _():
            for goal in (3, 2, 1):
                up_copy(number, goal, base.at[goal]).start()

        @pl.when(level == 3)
        def _():
            for goal in (0, 1, 2):
                down_copy(number, goal, base.at[goal]).start()

    position = {"step": 0}
    slots, length = left.shape[1:3]

    def turn_block(slot, target):
        def body(t, carry):
            tokens = pl.ds(pl.multiple_of(t * length, length), length)
            target[:, tokens] = left[slot, t].T
            return carry

        lax.fori_loop(0, slots, body, 0)

    def right_part(slot, lanes):
        part = right[slot, :, :, lanes]
        return part.reshape(slots * length, part.shape[2])

    def multiply(slot, w):
        def tile(t, carry):
            lanes = pl.ds(pl.multiple_of(t * narrow, narrow), narrow)
            product = dot(lt[...], right_part(slot, lanes))
            w[:, :, :, :, lanes] = product.reshape(w.shape[:4] + (narrow,))
            return carry

        lax.fori_loop(0, width // narrow, tile, 0)


    def produce(number):
        name, part, _ = plan[number]
        if name != "small":
            if previous[number] is not None:
                pair_copy(previous[number]).wait_send()
            w = views[number][0]
            while position["step"] < len(steps) and steps[position["step"]][0] == number:
                index = position["step"]
                position["step"] += 1
                _, source, turn, block, _ = steps[index]
                start_loads(index + 1)
                loads(index).wait()
                if turn:
                    turn_block(index % 2, gt.at[block] if source == "down" else lt)
                elif source == "down":
                    w[block] = dot(gt[block], right_part(index % 2, slice(0, narrow))).reshape(
                        w.shape[1:]
                    )
                else:
                    multiply(index % 2, w)
        pair_copy(number).start()

    def stage_pair(number):
        w, r = views[number][:2]
        pair_copy(number).wait_recv()

        def add(z, carry):
            for s in range(2):
                r[z, s] += w[z, s, core]
            return carry

        lax.fori_loop(0, 4, add, 0)
        if plan[number][2]:
            start_line(number)
        else:
            side_copy(number).start()

    def stage_side(number):
        if plan[number][2]:
            return
        r, x = views[number][1:3]
        side_copy(number).wait_recv()

        def add(z, carry):
            x[z] += r[z, side]
            return carry

        lax.fori_loop(0, 4, add, 0)
        start_line(number)

    def stage_up(number, height):
        u = views[number][3]
        base = along_line(number)

        @pl.when(level == height)
        def _():
            for goal in range(3, height - 1, -1):
                up_copy(number, goal).wait_recv()
                if goal > height:
                    u[goal - 1] += base[goal]
                    up_copy(number, goal).start()

    def stage_down(number, height):
        n = views[number][4]
        base = along_line(number)

        @pl.when(level == height)
        def _():
            for goal in range(0, height + 1):
                down_copy(number, goal).wait_recv()
                if goal < height:
                    n[goal] += base[goal]
                    down_copy(number, goal).start()

    def stage_sum(number):
        u, n, place = views[number][3:]
        base = along_line(number)

        @pl.when(level > 0)
        def _():
            base[level] += u[level - 1]

        @pl.when(level < 3)
        def _():
            base[level] += n[level]

        if plan[number][2]:
            side_copy(number).start()
        else:
            place[...] = base[level]

    def stage_last(number):
        if plan[number][2]:
            r, x = views[number][1:3]
            side_copy(number).wait_recv()
            views[number][5][...] = r[level, side] + x[...]

    def at(stage, number, *more):
        if 0 <= number < total:
            stage(number, *more)

    side_lag, hop = 3, 2
    for moment in range(total + side_lag + 3 * hop + 1):
        at(produce, moment)
        at(stage_pair, moment - 1)
        at(stage_side, moment - side_lag)
        for height in range(4):
            if height > 0:
                at(stage_up, moment - side_lag - hop * height, height)
            if height < 3:
                at(stage_down, moment - side_lag - hop * (3 - height), height)
        at(stage_sum, moment - side_lag - 3 * hop)
        at(stage_last, moment - side_lag - 3 * hop - 1)
    for number in range(total):
        if last_of[number]:
            pair_copy(number).wait_send()
        side_copy(number).wait_send()
        for goal in (1, 2, 3):

            @pl.when(goal > level)
            def _():
                up_copy(number, goal).wait_send()

        for goal in (0, 1, 2):

            @pl.when(goal < level)
            def _():
                down_copy(number, goal).wait_send()


def summed_in_kernel(factors, small_grads):
    fa1, fdj, fo, fdhr, fa2, fdu, fg, fdm = factors
    slots, length, width = fa1.shape
    inner = fg.shape[2]
    owners = 16
    depth = inner // width
    narrow = 256
    a_rows, b_rows = width // owners, inner // owners
    packed = small_grads.size // owners
    lanes = 128
    s_rows = -(-packed // (8 * lanes)) * 8
    small = small_grads.reshape(owners, packed)
    small = jnp.pad(small, ((0, 0), (0, s_rows * lanes - packed)))
    small = small.reshape(4, 2, 2, s_rows, lanes)
    plan = [
        ("qkv", 0, False),
        ("qkv", 1, True),
        ("small", 0, False),
        ("qkv", 2, False),
        ("down", 0, False),
        ("out", 0, True),
        ("down", 1, False),
        ("up", 0, False),
        ("down", 2, False),
        ("up", 1, False),
        ("up", 2, False),
        ("up", 3, False),
    ]
    total = len(plan)
    a_block, b_block, s_block = (a_rows, width), (b_rows, narrow), (s_rows, lanes)
    a_count = total - 1 - width // narrow
    b_count = width // narrow
    line_count = sum(line_first for _, _, line_first in plan)
    vmem = pl.BlockSpec(memory_space=pltpu.VMEM)
    anywhere = pl.BlockSpec(memory_space=pl.ANY)

    def trio(*lead):
        count = a_count if len(lead) == 2 else a_count - line_count
        return [
            pltpu.VMEM((count,) + lead + a_block, F32),
            pltpu.VMEM((b_count,) + lead + b_block, F32),
            pltpu.VMEM(lead + s_block, F32),
        ]

    *grads, small_grad = pl.pallas_call(
        functools.partial(gradients_kernel, (width, narrow, depth), plan),
        out_shape=(
            jax.ShapeDtypeStruct((1, a_rows, 3 * width), F32),
            jax.ShapeDtypeStruct((1, a_rows, width), F32),
            jax.ShapeDtypeStruct((1, a_rows, inner), F32),
            jax.ShapeDtypeStruct((1, b_rows, width), F32),
            jax.ShapeDtypeStruct(s_block, F32),
        ),
        in_specs=[anywhere] * 8 + [vmem],
        out_specs=(vmem,) * 5,
        scratch_shapes=[
            pltpu.VMEM((2, slots, length, width), BF),
            pltpu.VMEM((2, slots, length, width), BF),
            pltpu.VMEM((width, slots * length), BF),
            pltpu.VMEM((depth, width, slots * length), BF),
            pltpu.VMEM((2, 4, 2, 2) + a_block, F32),
            pltpu.VMEM((4, 2, 2) + b_block, F32),
        ]
        + trio(4, 2)
        + trio(4)
        + trio(3)
        + trio(3)
        + [
            pltpu.VMEM((line_count,) + a_block, F32),
            pltpu.VMEM((line_count, 3, 2) + a_block, F32),
            pltpu.VMEM((line_count, 3, 2) + a_block, F32),
        ]
        + [pltpu.SemaphoreType.DMA((2,))]
        + [pltpu.SemaphoreType.DMA((total,))] * 4
        + [pltpu.SemaphoreType.DMA((total, 3))] * 4,
        compiler_params=pltpu.CompilerParams(
            collective_id=1, has_side_effects=True, vmem_limit_bytes=62 << 20
        ),
    )(*factors, small)
    small_grad = small_grad.reshape(1, -1)[:, :packed]
    return tuple(grads) + (small_grad,)


def reduced(factors, small_grads):
    if lax.axis_size("dp") == 16:
        return summed_in_kernel(factors, small_grads)
    return summed_by_parts(factors, small_grads)


def per_device(
    embeddings, cotangent, seg_ids, thought_pos, w_qkv, w_out, w_up, w_down, small_params
):
    section_out, *factors, small_grads = layers(
        embeddings, cotangent, seg_ids, thought_pos, w_qkv, w_out, w_up, w_down, small_params
    )
    return (section_out,) + tuple(reduced(factors, small_grads))


def solution(mesh):
    return jax.shard_map(
        per_device,
        mesh=mesh,
        in_specs=(
            P("dp", None, None),
            P("dp", None, None),
            P("dp", None),
            P("dp", None),
            P("pipe", None, None),
            P("pipe", None, None),
            P("pipe", None, None),
            P("pipe", None, None),
            P("pipe", None),
        ),
        out_specs=(
            P("pipe", "dp", None, None),
            P("pipe", "dp", None),
            P("pipe", "dp", None),
            P("pipe", "dp", None),
            P("pipe", "dp", None),
            P("pipe", "dp"),
        ),
        check_vma=False,
    )
```

```python
import functools

import jax
import jax.numpy as jnp
from jax import lax
from jax.experimental import pallas as pl
from jax.experimental.pallas import tpu as pltpu
from jax.sharding import PartitionSpec as P

HEADS = 12
BF = jnp.bfloat16
F32 = jnp.float32
MESH = pl.DeviceIdType.MESH
EPSILON = 1e-05
MASKED = -1000000000.0
NO_CAP = 3e38
LAT = 16
G1, B1, BQ, BV, BO, G2, B2, BU = 0, 1, 2, 3, 4, 5, 6, 7


def dot(a, b):
    return lax.dot_general(a, b, (((1,), (0,)), ((), ())), preferred_element_type=F32)


def dot_nt(a, b):
    return lax.dot_general(a, b, (((1,), (1,)), ((), ())), preferred_element_type=F32)


def dot_tn(a, b):
    return lax.dot_general(a, b, (((0,), (0,)), ((), ())), preferred_element_type=F32)


def exact_dot(a, b):
    return lax.dot_general(
        a,
        b,
        (((1,), (0,)), ((), ())),
        precision=lax.Precision.HIGHEST,
        preferred_element_type=F32,
    )


def normalized(values):
    centred = values - jnp.mean(values, -1, keepdims=True)
    spread = jnp.mean(centred * centred, -1, keepdims=True)
    scale = lax.rsqrt(spread + EPSILON)
    return centred * scale, scale


def norm_back(hat, scale, grad):
    along = jnp.mean(grad * hat, -1, keepdims=True)
    return scale * (grad - jnp.mean(grad, -1, keepdims=True) - hat * along)


def gelu_both(u):
    c = 0.7978845608028654
    square = u * u
    t = jnp.tanh(c * u * (1.0 + 0.044715 * square))
    half = 0.5 + 0.5 * t
    slope = half + (0.5 * c) * u * (1.0 - t * t) * (1.0 + (3 * 0.044715) * square)
    return u * half, slope


def softmax(scores, axis=-1):
    e = jnp.exp(scores - jnp.max(scores, axis, keepdims=True))
    return e * (1.0 / jnp.sum(e, axis, keepdims=True))


def layers_kernel(
    sizes,
    emb,
    cot,
    seg,
    tpos,
    wqkv_h,
    wout_h,
    wup_h,
    wdown_h,
    small,
    sec,
    fa1,
    fdj,
    fo,
    fdhr,
    fa2,
    fdu,
    fg,
    fdm,
    sg,
    sums,
    joint,
    stat,
    wqkv,
    wout,
    wup,
    wdown,
    xin,
    yb,
    dyb,
    jn,
    pr,
    hm,
    slope,
    a1,
    ob,
    a2,
    gb,
    dm,
    dub,
    dhr,
    djb,
    da,
    dob,
    cap,
    lat,
    thg,
    lx,
    lq,
    lp,
    lh,
    la2,
    lo,
    lg,
    lslope,
    wsem,
    osem,
    ysend,
    yrecv,
    gsend,
    grecv,
    lsend,
    lrecv,
    tsend,
    trecv,
):
    rows, length, width, inner, thoughts = sizes
    blocks = inner // width
    bd = BU + blocks
    pairs = HEADS // 2
    me = lax.axis_index("pipe")
    other = 1 - me

    weights = [
        pltpu.make_async_copy(source.at[0], target, wsem.at[number])
        for number, (source, target) in enumerate(
            ((wqkv_h, wqkv), (wout_h, wout), (wup_h, wup), (wdown_h, wdown))
        )
    ]
    for copy in weights:
        copy.start()
    barrier = pltpu.get_barrier_semaphore()
    pl.semaphore_signal(barrier, inc=1, device_id={"pipe": other}, device_id_type=MESH)
    pl.semaphore_wait(barrier, 1)
    sums[...] = jnp.zeros_like(sums)
    joint[:, 0:width] = small[:, BQ * width : (BQ + 1) * width]
    joint[:, width : 2 * width] = jnp.zeros((1, width), F32)
    joint[:, 2 * width : 3 * width] = small[:, BV * width : (BV + 1) * width]

    def remote(source, target, send, recv):
        return pltpu.make_async_remote_copy(
            src_ref=source,
            dst_ref=target,
            send_sem=send,
            recv_sem=recv,
            device_id={"pipe": other},
            device_id_type=MESH,
        )

    def send_y(k):
        return remote(yb.at[k], xin.at[k], ysend.at[k], yrecv.at[k])

    def send_grad(k):
        return remote(yb.at[k], dyb.at[k], gsend.at[k], grecv.at[k])

    def send_lat(r):
        return remote(lat.at[r], lat.at[r], lsend.at[r], lrecv.at[r])

    def send_thoughts(r):
        return remote(thg.at[r], thg.at[r], tsend.at[r], trecv.at[r])

    def started(source, target, number):
        copy = pltpu.make_async_copy(source, target, osem.at[number])
        copy.start()
        return copy

    def finish(copies):
        for copy in copies:
            copy.wait()

    def each_chunk(step, count):
        def body(i, carry):
            step(pl.ds(pl.multiple_of(i * count, count), count), i * count)
            return carry

        lax.fori_loop(0, length // count, body, 0)

    def loop(count, step):
        def body(i, carry):
            step(i)
            return carry

        lax.fori_loop(0, count, body, 0)

    def add_columns(number, values):
        sums[number] += jnp.sum(values.astype(F32).reshape(-1, 8, width), 0)

    def row(number):
        return small[:, group(number)]

    def group(number):
        return slice(number * width, (number + 1) * width)

    lane = lax.broadcasted_iota(jnp.int32, (1, 128), 1)
    low = lane < 64
    halves = (jnp.where(low, 1.0, 0.0).astype(BF), jnp.where(low, 0.0, 1.0).astype(BF))

    def first_length(r):
        segment = seg[pl.ds(r, 1), :]
        return jnp.sum(jnp.where(segment == 0, 1.0, 0.0), -1, keepdims=True).astype(jnp.int32)

    def set_cap(r):
        first = first_length(r)
        query = lax.broadcasted_iota(jnp.int32, (length, length), 0)
        key = lax.broadcasted_iota(jnp.int32, (length, length), 1)
        lowest = jnp.where(query >= first, first, 0)
        cap[...] = jnp.where((key <= query) & (key >= lowest), NO_CAP, MASKED)

    def positions(r, shift, axis=0):
        shape = (LAT, 1) if axis == 0 else (1, LAT)
        number = lax.broadcasted_iota(jnp.int32, shape, axis)
        result = jnp.full(shape, -1, jnp.int32)
        for j in range(thoughts):
            result = jnp.where(number == j, tpos[r, j] - shift, result)
        return result

    def selector_turned(r, shift):
        place = positions(r, shift, 1)
        return jnp.where(lax.broadcasted_iota(jnp.int32, (length, LAT), 0) == place, 1.0, 0.0)

    def selector(place):
        return jnp.where(lax.broadcasted_iota(jnp.int32, (LAT, length), 1) == place, 1.0, 0.0)

    def unmarked(r, start):
        place = lax.broadcasted_iota(jnp.int32, (32, 1), 0) + start
        keep = jnp.ones((32, 1), F32)
        for j in range(thoughts):
            keep = jnp.where(place == tpos[r, j], 0.0, keep)
        return keep

    def head_lanes(part, hp):
        start = part * width + hp * 128
        if isinstance(hp, int):
            return slice(start, start + 128)
        return pl.ds(pl.multiple_of(start, 128), 128)

    def norm_rows(x, target, k, which, gain, shift, more=None):
        def step(part, _):
            values = x[part, :]
            center = jnp.mean(values, -1, keepdims=True)
            centred = values - center
            scale = lax.rsqrt(jnp.mean(centred * centred, -1, keepdims=True) + EPSILON)
            stat[k, 2 * which, part, :] = center
            stat[k, 2 * which + 1, part, :] = scale
            target[part, :] = (centred * scale * row(gain) + row(shift)).astype(BF)
            if more is not None:
                more(part, values)

        each_chunk(step, 128)

    def norm_rows_back(x, part, k, which, gain, shift):
        scale = stat[k, 2 * which + 1, part, :]
        hat = (x[part, :] - stat[k, 2 * which, part, :]) * scale
        grad = da[part, :]
        add_columns(gain, grad * hat)
        add_columns(shift, grad)
        return norm_back(hat, scale, grad * row(gain))

    def forward(k, x, y, first=None):
        def need(number):
            if first is not None:

                @pl.when(first)
                def _():
                    weights[number].wait()

        norm_rows(x, a1, k, 0, G1, B1)
        copies = [started(a1, fa1.at[k], 0)]
        need(0)

        for part in range(3):
            joined = dot(a1[...], wqkv[:, group(part)]) + joint[:, group(part)]
            jn[k, :, group(part)] = joined.astype(BF)
        for hp in range(pairs):
            q = jn[k, :, head_lanes(0, hp)]
            key = jn[k, :, head_lanes(1, hp)]
            value = jn[k, :, head_lanes(2, hp)]
            out = []
            for h in range(2):
                scores = dot_nt(q * (halves[h] * 0.125), key)
                chance = softmax(jnp.minimum(scores, cap[...])).astype(BF)
                pr[k, 2 * hp + h] = chance
                out.append(dot(chance, value))
            ob[:, head_lanes(0, hp)] = jnp.where(low, out[0], out[1]).astype(BF)
        copies.append(started(ob, fo.at[k], 1))
        need(1)
        hm[k] = x[...] + dot(ob[...], wout[...]) + row(BO)

        def begin(part, values):
            y[part, :] = values + row(bd)

        norm_rows(hm.at[k], a2, k, 1, G2, B2, begin)
        copies.append(started(a2, fa2.at[k], 2))
        need(2)
        need(3)

        for c in range(blocks):
            part = group(c)
            g, d = gelu_both(dot(a2[...], wup[:, part]) + row(BU + c))
            gb[:, part] = g.astype(BF)
            slope[k, :, part] = d.astype(BF)
            y[...] += dot(gb[:, part], wdown[part, :])
        copies.append(started(gb, fg.at[k], 3))
        return copies

    def backward(k, x, dy, dx):
        def step(part, _):
            branch = dy[part, :].astype(BF)
            dm[part, :] = branch
            add_columns(bd, branch)

        each_chunk(step, 64)
        copies = [started(dm, fdm.at[k], 4)]
        da[...] = jnp.zeros_like(da)

        def mlp(c):
            part = pl.ds(pl.multiple_of(c * width, width), width)
            grad = (dot_nt(dm[...], wdown[part, :]) * slope[k, :, part]).astype(BF)
            dub[:, part] = grad
            add_columns(BU + c, grad)
            da[...] += dot_nt(grad, wup[:, part])

        loop(blocks, mlp)
        copies.append(started(dub, fdu.at[k], 5))

        def step_two(part, _):
            middle = dy[part, :] + norm_rows_back(hm.at[k], part, k, 1, G2, B2)
            dy[part, :] = middle
            branch = middle.astype(BF)
            dhr[part, :] = branch
            add_columns(BO, branch)

        each_chunk(step_two, 64)
        copies.append(started(dhr, fdhr.at[k], 6))
        dob[...] = dot_nt(dhr[...], wout[...]).astype(BF)

        def heads(hp):
            q = jn[k, :, head_lanes(0, hp)]
            key = jn[k, :, head_lanes(1, hp)]
            value = jn[k, :, head_lanes(2, hp)]
            grad_out = dob[:, head_lanes(0, hp)]
            dq, dk, dv = [], [], []
            for h in range(2):
                chance = pr[k, 2 * hp + h]
                chance_full = chance.astype(F32)
                inner_part = chance_full * dot_nt(grad_out * halves[h], value)
                total = jnp.sum(inner_part, -1, keepdims=True)
                grad_scores = (inner_part - chance_full * total).astype(BF)
                dq.append(dot(grad_scores, key))
                dk.append(dot_tn(grad_scores, q))
                dv.append(dot_tn(chance, grad_out))
            djb[:, head_lanes(0, hp)] = (jnp.where(low, dq[0], dq[1]) * 0.125).astype(BF)
            djb[:, head_lanes(1, hp)] = (jnp.where(low, dk[0], dk[1]) * 0.125).astype(BF)
            djb[:, head_lanes(2, hp)] = jnp.where(low, dv[0], dv[1]).astype(BF)

        loop(pairs, heads)
        copies.append(started(djb, fdj.at[k], 7))
        into_input(k, x, dy, dx)
        return copies

    def into_input(k, x, middle, dx):
        da[...] = dot_nt(djb[...], wqkv[...])

        def step(part, _):
            add_columns(BQ, djb[part, group(0)])
            add_columns(BV, djb[part, group(2)])
            dx[part, :] = middle[part, :] + norm_rows_back(x, part, k, 0, G1, B1)

        each_chunk(step, 64)

    def forward_latent(r):
        x = xin.at[r]
        norm_rows(x, a1, r, 0, G1, B1)
        copies = [started(a1, fa1.at[r], 0)]
        jn[r, :, group(1)] = dot(a1[...], wqkv[:, group(1)]).astype(BF)
        jn[r, :, group(2)] = (dot(a1[...], wqkv[:, group(2)]) + row(BV)).astype(BF)
        place = positions(r, 1)
        chosen = exact_dot(selector(place), x[...])
        lx[r] = chosen
        hat, _ = normalized(chosen)
        normed = (hat * row(G1) + row(B1)).astype(BF)
        lq[r] = (dot(normed, wqkv[:, group(0)]) + row(BQ)).astype(BF)
        first = first_length(r)
        key_place = lax.broadcasted_iota(jnp.int32, (LAT, length), 1)
        lowest = jnp.where(place >= first, first, 0)
        limit = jnp.where((key_place <= place) & (key_place >= lowest), NO_CAP, MASKED)

        def heads(hp):
            q = lq[r, :, head_lanes(0, hp)]
            key = jn[r, :, head_lanes(1, hp)]
            value = jn[r, :, head_lanes(2, hp)]
            out = []
            for h in range(2):
                scores = dot_nt(q * (halves[h] * 0.125), key)
                chance = softmax(jnp.minimum(scores, limit)).astype(BF)
                lp[r, 2 * hp + h] = chance
                out.append(dot(chance, value))
            lo[r, :, head_lanes(0, hp)] = jnp.where(low, out[0], out[1]).astype(BF)

        for hp in range(pairs):
            heads(hp)
        middle = chosen + dot(lo[r], wout[...]) + row(BO)
        lh[r] = middle
        hat, _ = normalized(middle)
        la2[r] = (hat * row(G2) + row(B2)).astype(BF)
        lat[r] = middle + row(bd)

        def mlp(c):
            part = group(c)
            u = dot(la2[r], wup[:, part]) + row(BU + c)
            g, d = gelu_both(u)
            lg[r, :, part] = g.astype(BF)
            lslope[r, :, part] = d.astype(BF)
            lat[r] += dot(lg[r, :, part], wdown[part, :])

        for c in range(blocks):
            mlp(c)
        return copies

    def backward_latent(r, dx):
        grad_result = thg[r]
        branch = grad_result.astype(BF)
        top = slice(0, LAT)
        add_columns(bd, branch)
        dm[top, :] = branch
        a2[top, :] = la2[r]
        ob[top, :] = lo[r]
        gb[top, :] = lg[r]
        copies = [
            started(dm, fdm.at[r], 4),
            started(a2, fa2.at[r], 2),
            started(ob, fo.at[r], 1),
            started(gb, fg.at[r], 3),
        ]
        da[top, :] = jnp.zeros((LAT, width), F32)

        def mlp(c):
            part = group(c)
            grad = (dot_nt(dm[top, :], wdown[part, :]) * lslope[r, :, part]).astype(BF)
            dub[top, part] = grad
            add_columns(BU + c, grad)
            da[top, :] += dot_nt(grad, wup[:, part])

        for c in range(blocks):
            mlp(c)
        copies.append(started(dub, fdu.at[r], 5))
        hat, scale = normalized(lh[r])
        grad = da[top, :]
        add_columns(G2, grad * hat)
        add_columns(B2, grad)
        middle = grad_result + norm_back(hat, scale, grad * row(G2))
        rounded = middle.astype(BF)
        dhr[top, :] = rounded
        add_columns(BO, rounded)
        copies.append(started(dhr, fdhr.at[r], 6))
        spread = selector_turned(r, 1)
        dyb[r] = exact_dot(spread, middle)
        place = positions(r, 1, 1)
        first = first_length(r)
        key_place = lax.broadcasted_iota(jnp.int32, (length, LAT), 0)
        lowest = jnp.where(place >= first, first, 0)
        limit = jnp.where((key_place <= place) & (key_place >= lowest), NO_CAP, MASKED)
        dob[top, :] = dot_nt(rounded, wout[...]).astype(BF)

        def heads(hp):
            q = lq[r, :, head_lanes(0, hp)]
            key = jn[r, :, head_lanes(1, hp)]
            value = jn[r, :, head_lanes(2, hp)]
            grad_out = dob[top, head_lanes(0, hp)]
            dq, dk, dv = [], [], []
            for h in range(2):
                grad_masked = grad_out * halves[h]
                chance = lp[r, 2 * hp + h].astype(F32)
                inner_part = chance * dot_nt(grad_masked, value)
                total = jnp.sum(inner_part, -1, keepdims=True)
                dq.append(dot((inner_part - chance * total).astype(BF), key))
                scores = dot_nt(key, q * (halves[h] * 0.125))
                chance = softmax(jnp.minimum(scores, limit), 0)
                inner_part = chance * dot_nt(value, grad_masked)
                total = jnp.sum(inner_part, 0, keepdims=True)
                dk.append(dot((inner_part - chance * total).astype(BF), q))
                dv.append(dot(chance.astype(BF), grad_out))
            grad_q = (jnp.where(low, dq[0], dq[1]) * 0.125).astype(BF)
            djb[:, head_lanes(0, hp)] = dot(spread.astype(BF), grad_q).astype(BF)
            djb[:, head_lanes(1, hp)] = (jnp.where(low, dk[0], dk[1]) * 0.125).astype(BF)
            djb[:, head_lanes(2, hp)] = jnp.where(low, dv[0], dv[1]).astype(BF)

        for hp in range(pairs):
            heads(hp)
        copies.append(started(djb, fdj.at[r], 7))
        into_input(r, xin.at[r], dyb.at[r], dx)
        return copies

    @pl.when(me == 0)
    def _():
        def forward_step(k, carry):
            r = lax.rem(k, rows)
            set_cap(r)

            @pl.when(k < rows)
            def _():
                xin[k] = emb[r].astype(F32)

            @pl.when(k >= rows)
            def _():
                send_lat(r).wait_recv()
                xin[k] = exact_dot(selector_turned(r, 0), lat[r])

                def step(part, start):
                    xin[k, part, :] += emb[r, part, :].astype(F32) * unmarked(r, start)

                each_chunk(step, 32)

            copies = forward(k, xin.at[k], yb.at[k], first=k == 0)
            send_y(k).start()
            finish(copies)
            return carry

        lax.fori_loop(0, 2 * rows, forward_step, 0)

        def backward_step(i, carry):
            k = lax.rem(i + rows, 2 * rows)
            r = lax.rem(i, rows)
            send_y(k).wait_send()
            send_grad(k).wait_recv()
            copies = backward(k, xin.at[k], dyb.at[k], yb.at[k])

            @pl.when(i < rows)
            def _():
                thg[r] = exact_dot(selector(positions(r, 0)), yb[k])
                send_thoughts(r).start()

            @pl.when(i >= rows)
            def _():
                def step(part, start):
                    yb[k, part, :] += yb[rows + r, part, :] * unmarked(r, start)

                each_chunk(step, 32)
                started(yb.at[k], sec.at[0, r], 8).wait()

            finish(copies)
            return carry

        lax.fori_loop(0, 2 * rows, backward_step, 0)

        def drain(r, carry):
            send_thoughts(r).wait_send()
            return carry

        lax.fori_loop(0, rows, drain, 0)

    @pl.when(me == 1)
    def _():
        finish(weights)

        def latent_step(r, carry):
            send_y(r).wait_recv()
            copies = forward_latent(r)
            send_lat(r).start()
            finish(copies)
            return carry

        lax.fori_loop(0, rows, latent_step, 0)

        def language_step(r, carry):
            k = rows + r
            set_cap(r)
            send_y(k).wait_recv()
            copies = forward(k, xin.at[k], dyb.at[k])
            copies.append(started(dyb.at[k], sec.at[0, r], 8))
            dyb[r] = cot[r].astype(F32)
            copies += backward(k, xin.at[k], dyb.at[r], yb.at[k])
            send_grad(k).start()
            finish(copies)
            return carry

        lax.fori_loop(0, rows, language_step, 0)
        for staged in (dm, a2, ob, gb, dub, dhr):
            staged[...] = jnp.zeros_like(staged)

        def latent_back_step(r, carry):
            send_thoughts(r).wait_recv()
            copies = backward_latent(r, yb.at[r])
            send_grad(r).start()
            finish(copies)
            return carry

        lax.fori_loop(0, rows, latent_back_step, 0)

        def drain(r, carry):
            send_lat(r).wait_send()
            send_grad(r).wait_send()
            send_grad(rows + r).wait_send()
            return carry

        lax.fori_loop(0, rows, drain, 0)

    sg[...] = jnp.sum(sums[...], 1)


def layers(emb, cot, seg, tpos, w_qkv, w_out, w_up, w_down, small):
    rows, length, width = emb.shape
    inner = w_up.shape[2]
    thoughts = tpos.shape[1]
    slots = 2 * rows
    packed = small.shape[1] // width
    vmem = pl.BlockSpec(memory_space=pltpu.VMEM)
    anywhere = pl.BlockSpec(memory_space=pl.ANY)
    smem = pl.BlockSpec(memory_space=pltpu.SMEM)

    def factor(columns):
        return jax.ShapeDtypeStruct((slots, length, columns), BF)

    def block(columns, kind=BF):
        return pltpu.VMEM((length, columns), kind)

    def few(columns, kind=BF):
        return pltpu.VMEM((rows, LAT, columns), kind)

    sizes = (rows, length, width, inner, thoughts)
    return pl.pallas_call(
        functools.partial(layers_kernel, sizes),
        out_shape=(
            jax.ShapeDtypeStruct((1, rows, length, width), F32),
            factor(width),
            factor(3 * width),
            factor(width),
            factor(width),
            factor(width),
            factor(inner),
            factor(inner),
            factor(width),
            jax.ShapeDtypeStruct((packed, width), F32),
        ),
        in_specs=[vmem, vmem, vmem, smem] + [anywhere] * 4 + [vmem],
        out_specs=(anywhere,) * 9 + (vmem,),
        scratch_shapes=[
            pltpu.VMEM((packed, 8, width), F32),
            pltpu.VMEM((1, 3 * width), F32),
            pltpu.VMEM((slots, 4, length, 1), F32),
            pltpu.VMEM((width, 3 * width), BF),
            pltpu.VMEM((width, width), BF),
            pltpu.VMEM((width, inner), BF),
            pltpu.VMEM((inner, width), BF),
            pltpu.VMEM((slots, length, width), F32),
            pltpu.VMEM((slots, length, width), F32),
            pltpu.VMEM((slots, length, width), F32),
            pltpu.VMEM((slots, length, 3 * width), BF),
            pltpu.VMEM((slots, HEADS, length, length), BF),
            pltpu.VMEM((slots, length, width), F32),
            pltpu.VMEM((slots, length, inner), BF),
            block(width),
            block(width),
            block(width),
            block(inner),
            block(width),
            block(inner),
            block(width),
            block(3 * width),
            block(width, F32),
            block(width),
            block(length, F32),
            few(width, F32),
            few(width, F32),
            few(width, F32),
            few(width),
            pltpu.VMEM((rows, HEADS, LAT, length), BF),
            few(width, F32),
            few(width),
            few(width),
            few(inner),
            few(inner),
            pltpu.SemaphoreType.DMA((4,)),
            pltpu.SemaphoreType.DMA((9,)),
        ]
        + [pltpu.SemaphoreType.DMA((slots,))] * 4
        + [pltpu.SemaphoreType.DMA((rows,))] * 4,
        compiler_params=pltpu.CompilerParams(
            collective_id=0, has_side_effects=True, vmem_limit_bytes=62 << 20
        ),
    )(emb, cot, seg, tpos, w_qkv, w_out, w_up, w_down, small)


def summed_by_parts(factors, small_grads):
    fa1, fdj, fo, fdhr, fa2, fdu, fg, fdm = factors

    def product(left, right):
        whole = jnp.einsum("ktm,ktn->mn", left, right, preferred_element_type=F32)
        return lax.psum_scatter(whole[None], "dp", scatter_dimension=1, tiled=True)

    small = lax.psum_scatter(
        small_grads.reshape(1, -1), "dp", scatter_dimension=1, tiled=True
    )
    return product(fa1, fdj), product(fo, fdhr), product(fa2, fdu), product(fg, fdm), small


def gradients_kernel(
    sizes,
    plan,
    fa1,
    fdj,
    fo,
    fdhr,
    fa2,
    fdu,
    fg,
    fdm,
    small,
    gqkv,
    gout,
    gup,
    gdown,
    gsmall,
    left,
    right,
    lt,
    gt,
    wa,
    wb,
    ra,
    rb,
    rs,
    xa,
    xb,
    xs,
    ua,
    ub,
    us,
    na,
    nb,
    ns,
    xl,
    ul,
    nl,
    lsem,
    pair_send,
    pair_recv,
    side_send,
    side_recv,
    up_send,
    up_recv,
    down_send,
    down_recv,
):
    width, narrow, depth = sizes
    me = lax.axis_index("dp")
    core = lax.rem(me, 2)
    side = lax.rem(me // 2, 2)
    level = me // 4
    partner = me + 1 - 2 * core
    beside = me + 2 - 4 * side
    above, below = me + 4, me - 4

    def remote(source, target, send, recv, device):
        return pltpu.make_async_remote_copy(
            src_ref=source,
            dst_ref=target,
            send_sem=send,
            recv_sem=recv,
            device_id={"dp": device},
            device_id_type=MESH,
        )

    lefts = {"qkv": fa1, "out": fo, "up": fa2, "down": fg}
    rights = {"qkv": fdj, "out": fdhr, "up": fdu, "down": fdm}
    steps = []
    turned = None
    ahead = 0
    for number, (name, part, _) in enumerate(plan):
        if name == "small":
            continue
        if name == "down":
            while ahead < depth:
                steps.append((number, name, True, ahead, None))
                ahead += 1
            steps += [(number, name, False, block, part) for block in range(depth)]
            continue
        if name != turned:
            steps.append((number, name, True, 0, None))
            turned = name
        steps.append((number, name, False, 0, part))
        for _ in range(2 if number else 1):
            if ahead < depth:
                steps.append((number, "down", True, ahead, None))
                ahead += 1

    def loads(index):
        _, name, turn, block, part = steps[index]
        slot = index % 2
        if turn:
            source = lefts[name].at[:, :, block * width : (block + 1) * width]
            return pltpu.make_async_copy(source, left.at[slot], lsem.at[slot])
        columns = narrow if name == "down" else width
        return pltpu.make_async_copy(
            rights[name].at[:, :, part * columns : (part + 1) * columns],
            right.at[slot, :, :, 0:columns],
            lsem.at[slot],
        )

    def start_loads(index):
        if index < len(steps):
            loads(index).start()

    start_loads(0)

    barrier = pltpu.get_barrier_semaphore()

    def greet(device):
        pl.semaphore_signal(barrier, inc=1, device_id={"dp": device}, device_id_type=MESH)

    greet(partner)
    greet(beside)

    @pl.when(level < 3)
    def _():
        greet(above)

    @pl.when(level > 0)
    def _():
        greet(below)

    pl.semaphore_wait(barrier, 2 + (level + 2) // 3 + (5 - level) // 3)

    views = []
    counts = {"a": 0, "b": 0, "line": 0}
    for number, (name, part, line_first) in enumerate(plan):
        if name == "small":
            views.append((small, rs, xs, us, ns, gsmall))
            continue
        kind = "b" if name == "down" else "a"
        index = counts[kind]
        counts[kind] += 1
        if kind == "a":
            target = {"qkv": gqkv, "out": gout, "up": gup}[name]
            place = target.at[0, :, part * width : (part + 1) * width]
            if line_first:
                along = counts["line"]
                counts["line"] += 1
                further = (xl.at[along], ul.at[along], nl.at[along], place)
            else:
                along = index - counts["line"]
                further = (xa.at[along], ua.at[along], na.at[along], place)
            views.append((wa.at[index % 2], ra.at[index]) + further)
        else:
            place = gdown.at[0, :, part * narrow : (part + 1) * narrow]
            views.append((wb, rb.at[index], xb.at[index], ub.at[index], nb.at[index], place))
    total = len(plan)
    previous = {}
    last_of = {}
    for number, (name, part, _) in enumerate(plan):
        kind = "s" if name == "small" else "b" if name == "down" else "a"
        mine = [n for n in range(number) if ("b" if plan[n][0] == "down" else "a") == kind]
        mine = [n for n in mine if plan[n][0] != "small"]
        back = 1 if kind == "b" else 2
        previous[number] = mine[-back] if kind != "s" and len(mine) >= back else None
        last_of[number] = True
        if previous[number] is not None:
            last_of[previous[number]] = False

    def pair_copy(number):
        w, r = views[number][:2]
        return remote(
            w.at[:, :, 1 - core], r, pair_send.at[number], pair_recv.at[number], partner
        )

    def side_copy(number):
        r, x = views[number][1:3]
        source = r.at[level, 1 - side] if plan[number][2] else r.at[:, 1 - side]
        return remote(source, x, side_send.at[number], side_recv.at[number], beside)

    def along_line(number):
        r, x = views[number][1:3]
        return r if plan[number][2] else x

    def up_copy(number, goal, source=None):
        u = views[number][3]
        return remote(
            u.at[goal - 1] if source is None else source,
            u.at[goal - 1],
            up_send.at[number, goal - 1],
            up_recv.at[number, goal - 1],
            above,
        )

    def down_copy(number, goal, source=None):
        n = views[number][4]
        return remote(
            n.at[goal] if source is None else source,
            n.at[goal],
            down_send.at[number, goal],
            down_recv.at[number, goal],
            below,
        )

    def start_line(number):
        base = along_line(number)

        @pl.when(level == 0)
        def _():
            for goal in (3, 2, 1):
                up_copy(number, goal, base.at[goal]).start()

        @pl.when(level == 3)
        def _():
            for goal in (0, 1, 2):
                down_copy(number, goal, base.at[goal]).start()

    position = {"step": 0}
    slots, length = left.shape[1:3]

    def turn_block(slot, target):
        def body(t, carry):
            tokens = pl.ds(pl.multiple_of(t * length, length), length)
            target[:, tokens] = left[slot, t].T
            return carry

        lax.fori_loop(0, slots, body, 0)

    def right_part(slot, lanes):
        part = right[slot, :, :, lanes]
        return part.reshape(slots * length, part.shape[2])

    def multiply(slot, w):
        def tile(t, carry):
            lanes = pl.ds(pl.multiple_of(t * narrow, narrow), narrow)
            product = dot(lt[...], right_part(slot, lanes))
            w[:, :, :, :, lanes] = product.reshape(w.shape[:4] + (narrow,))
            return carry

        lax.fori_loop(0, width // narrow, tile, 0)


    def produce(number):
        name, part, _ = plan[number]
        if name != "small":
            if previous[number] is not None:
                pair_copy(previous[number]).wait_send()
            w = views[number][0]
            while position["step"] < len(steps) and steps[position["step"]][0] == number:
                index = position["step"]
                position["step"] += 1
                _, source, turn, block, _ = steps[index]
                start_loads(index + 1)
                loads(index).wait()
                if turn:
                    turn_block(index % 2, gt.at[block] if source == "down" else lt)
                elif source == "down":
                    w[block] = dot(gt[block], right_part(index % 2, slice(0, narrow))).reshape(
                        w.shape[1:]
                    )
                else:
                    multiply(index % 2, w)
        pair_copy(number).start()

    def stage_pair(number):
        w, r = views[number][:2]
        pair_copy(number).wait_recv()

        def add(z, carry):
            for s in range(2):
                r[z, s] += w[z, s, core]
            return carry

        lax.fori_loop(0, 4, add, 0)
        if plan[number][2]:
            start_line(number)
        else:
            side_copy(number).start()

    def stage_side(number):
        if plan[number][2]:
            return
        r, x = views[number][1:3]
        side_copy(number).wait_recv()

        def add(z, carry):
            x[z] += r[z, side]
            return carry

        lax.fori_loop(0, 4, add, 0)
        start_line(number)

    def stage_up(number, height):
        u = views[number][3]
        base = along_line(number)

        @pl.when(level == height)
        def _():
            for goal in range(3, height - 1, -1):
                up_copy(number, goal).wait_recv()
                if goal > height:
                    u[goal - 1] += base[goal]
                    up_copy(number, goal).start()

    def stage_down(number, height):
        n = views[number][4]
        base = along_line(number)

        @pl.when(level == height)
        def _():
            for goal in range(0, height + 1):
                down_copy(number, goal).wait_recv()
                if goal < height:
                    n[goal] += base[goal]
                    down_copy(number, goal).start()

    def stage_sum(number):
        u, n, place = views[number][3:]
        base = along_line(number)

        @pl.when(level > 0)
        def _():
            base[level] += u[level - 1]

        @pl.when(level < 3)
        def _():
            base[level] += n[level]

        if plan[number][2]:
            side_copy(number).start()
        else:
            place[...] = base[level]

    def stage_last(number):
        if plan[number][2]:
            r, x = views[number][1:3]
            side_copy(number).wait_recv()
            views[number][5][...] = r[level, side] + x[...]

    def at(stage, number, *more):
        if 0 <= number < total:
            stage(number, *more)

    side_lag, hop = 3, 2
    for moment in range(total + side_lag + 3 * hop + 1):
        at(produce, moment)
        at(stage_pair, moment - 1)
        at(stage_side, moment - side_lag)
        for height in range(4):
            if height > 0:
                at(stage_up, moment - side_lag - hop * height, height)
            if height < 3:
                at(stage_down, moment - side_lag - hop * (3 - height), height)
        at(stage_sum, moment - side_lag - 3 * hop)
        at(stage_last, moment - side_lag - 3 * hop - 1)
    for number in range(total):
        if last_of[number]:
            pair_copy(number).wait_send()
        side_copy(number).wait_send()
        for goal in (1, 2, 3):

            @pl.when(goal > level)
            def _():
                up_copy(number, goal).wait_send()

        for goal in (0, 1, 2):

            @pl.when(goal < level)
            def _():
                down_copy(number, goal).wait_send()


def summed_in_kernel(factors, small_grads):
    fa1, fdj, fo, fdhr, fa2, fdu, fg, fdm = factors
    slots, length, width = fa1.shape
    inner = fg.shape[2]
    owners = 16
    depth = inner // width
    narrow = 256
    a_rows, b_rows = width // owners, inner // owners
    packed = small_grads.size // owners
    lanes = 128
    s_rows = -(-packed // (8 * lanes)) * 8
    small = small_grads.reshape(owners, packed)
    small = jnp.pad(small, ((0, 0), (0, s_rows * lanes - packed)))
    small = small.reshape(4, 2, 2, s_rows, lanes)
    plan = [
        ("qkv", 0, False),
        ("qkv", 1, True),
        ("small", 0, False),
        ("qkv", 2, False),
        ("down", 0, False),
        ("out", 0, True),
        ("down", 1, False),
        ("up", 0, False),
        ("down", 2, False),
        ("up", 1, False),
        ("up", 2, False),
        ("up", 3, False),
    ]
    total = len(plan)
    a_block, b_block, s_block = (a_rows, width), (b_rows, narrow), (s_rows, lanes)
    a_count = total - 1 - width // narrow
    b_count = width // narrow
    line_count = sum(line_first for _, _, line_first in plan)
    vmem = pl.BlockSpec(memory_space=pltpu.VMEM)
    anywhere = pl.BlockSpec(memory_space=pl.ANY)

    def trio(*lead):
        count = a_count if len(lead) == 2 else a_count - line_count
        return [
            pltpu.VMEM((count,) + lead + a_block, F32),
            pltpu.VMEM((b_count,) + lead + b_block, F32),
            pltpu.VMEM(lead + s_block, F32),
        ]

    *grads, small_grad = pl.pallas_call(
        functools.partial(gradients_kernel, (width, narrow, depth), plan),
        out_shape=(
            jax.ShapeDtypeStruct((1, a_rows, 3 * width), F32),
            jax.ShapeDtypeStruct((1, a_rows, width), F32),
            jax.ShapeDtypeStruct((1, a_rows, inner), F32),
            jax.ShapeDtypeStruct((1, b_rows, width), F32),
            jax.ShapeDtypeStruct(s_block, F32),
        ),
        in_specs=[anywhere] * 8 + [vmem],
        out_specs=(vmem,) * 5,
        scratch_shapes=[
            pltpu.VMEM((2, slots, length, width), BF),
            pltpu.VMEM((2, slots, length, width), BF),
            pltpu.VMEM((width, slots * length), BF),
            pltpu.VMEM((depth, width, slots * length), BF),
            pltpu.VMEM((2, 4, 2, 2) + a_block, F32),
            pltpu.VMEM((4, 2, 2) + b_block, F32),
        ]
        + trio(4, 2)
        + trio(4)
        + trio(3)
        + trio(3)
        + [
            pltpu.VMEM((line_count,) + a_block, F32),
            pltpu.VMEM((line_count, 3, 2) + a_block, F32),
            pltpu.VMEM((line_count, 3, 2) + a_block, F32),
        ]
        + [pltpu.SemaphoreType.DMA((2,))]
        + [pltpu.SemaphoreType.DMA((total,))] * 4
        + [pltpu.SemaphoreType.DMA((total, 3))] * 4,
        compiler_params=pltpu.CompilerParams(
            collective_id=1, has_side_effects=True, vmem_limit_bytes=62 << 20
        ),
    )(*factors, small)
    small_grad = small_grad.reshape(1, -1)[:, :packed]
    return tuple(grads) + (small_grad,)


def reduced(factors, small_grads):
    if lax.axis_size("dp") == 16:
        return summed_in_kernel(factors, small_grads)
    return summed_by_parts(factors, small_grads)


def per_device(
    embeddings, cotangent, seg_ids, thought_pos, w_qkv, w_out, w_up, w_down, small_params
):
    section_out, *factors, small_grads = layers(
        embeddings, cotangent, seg_ids, thought_pos, w_qkv, w_out, w_up, w_down, small_params
    )
    return (section_out,) + tuple(reduced(factors, small_grads))


def solution(mesh):
    return jax.shard_map(
        per_device,
        mesh=mesh,
        in_specs=(
            P("dp", None, None),
            P("dp", None, None),
            P("dp", None),
            P("dp", None),
            P("pipe", None, None),
            P("pipe", None, None),
            P("pipe", None, None),
            P("pipe", None, None),
            P("pipe", None),
        ),
        out_specs=(
            P("pipe", "dp", None, None),
            P("pipe", "dp", None),
            P("pipe", "dp", None),
            P("pipe", "dp", None),
            P("pipe", "dp", None),
            P("pipe", "dp"),
        ),
        check_vma=False,
    )
```

```python
import functools

import jax
import jax.numpy as jnp
from jax import lax
from jax.experimental import pallas as pl
from jax.experimental.pallas import tpu as pltpu
from jax.sharding import PartitionSpec as P

HEADS = 12
BF = jnp.bfloat16
F32 = jnp.float32
MESH = pl.DeviceIdType.MESH
EPSILON = 1e-05
MASKED = -1000000000.0
NO_CAP = 3e38
LAT = 16
G1, B1, BQ, BV, BO, G2, B2, BU = 0, 1, 2, 3, 4, 5, 6, 7


def dot(a, b):
    return lax.dot_general(a, b, (((1,), (0,)), ((), ())), preferred_element_type=F32)


def dot_nt(a, b):
    return lax.dot_general(a, b, (((1,), (1,)), ((), ())), preferred_element_type=F32)


def dot_tn(a, b):
    return lax.dot_general(a, b, (((0,), (0,)), ((), ())), preferred_element_type=F32)


def exact_dot(a, b):
    return lax.dot_general(
        a,
        b,
        (((1,), (0,)), ((), ())),
        precision=lax.Precision.HIGHEST,
        preferred_element_type=F32,
    )


def normalized(values):
    centred = values - jnp.mean(values, -1, keepdims=True)
    spread = jnp.mean(centred * centred, -1, keepdims=True)
    scale = lax.rsqrt(spread + EPSILON)
    return centred * scale, scale


def norm_back(hat, scale, grad):
    along = jnp.mean(grad * hat, -1, keepdims=True)
    return scale * (grad - jnp.mean(grad, -1, keepdims=True) - hat * along)


def gelu_both(u):
    c = 0.7978845608028654
    square = u * u
    t = jnp.tanh(c * u * (1.0 + 0.044715 * square))
    half = 0.5 + 0.5 * t
    slope = half + (0.5 * c) * u * (1.0 - t * t) * (1.0 + (3 * 0.044715) * square)
    return u * half, slope


def softmax(scores, axis=-1):
    e = jnp.exp(scores - jnp.max(scores, axis, keepdims=True))
    return e * (1.0 / jnp.sum(e, axis, keepdims=True))


def layers_kernel(
    sizes,
    emb,
    cot,
    seg,
    tpos,
    wqkv_h,
    wout_h,
    wup_h,
    wdown_h,
    small,
    sec,
    fa1,
    fdj,
    fo,
    fdhr,
    fa2,
    fdu,
    fg,
    fdm,
    sg,
    sums,
    joint,
    stat,
    wqkv,
    wout,
    wup,
    wdown,
    xin,
    yb,
    dyb,
    jn,
    pr,
    hm,
    slope,
    a1,
    ob,
    a2,
    gb,
    dm,
    dub,
    dhr,
    djb,
    da,
    dob,
    dmt,
    dat,
    djt,
    cap,
    lat,
    thg,
    lx,
    lq,
    lp,
    lh,
    la2,
    lo,
    lg,
    lslope,
    wsem,
    osem,
    ysend,
    yrecv,
    gsend,
    grecv,
    lsend,
    lrecv,
    tsend,
    trecv,
):
    rows, length, width, inner, thoughts = sizes
    blocks = inner // width
    bd = BU + blocks
    pairs = HEADS // 2
    me = lax.axis_index("pipe")
    other = 1 - me

    weights = [
        pltpu.make_async_copy(source.at[0], target, wsem.at[number])
        for number, (source, target) in enumerate(
            ((wqkv_h, wqkv), (wout_h, wout), (wup_h, wup), (wdown_h, wdown))
        )
    ]
    for copy in weights:
        copy.start()
    barrier = pltpu.get_barrier_semaphore()
    pl.semaphore_signal(barrier, inc=1, device_id={"pipe": other}, device_id_type=MESH)
    pl.semaphore_wait(barrier, 1)
    sums[...] = jnp.zeros_like(sums)
    joint[:, 0:width] = small[:, BQ * width : (BQ + 1) * width]
    joint[:, width : 2 * width] = jnp.zeros((1, width), F32)
    joint[:, 2 * width : 3 * width] = small[:, BV * width : (BV + 1) * width]

    def remote(source, target, send, recv):
        return pltpu.make_async_remote_copy(
            src_ref=source,
            dst_ref=target,
            send_sem=send,
            recv_sem=recv,
            device_id={"pipe": other},
            device_id_type=MESH,
        )

    def send_y(k):
        return remote(yb.at[k], xin.at[k], ysend.at[k], yrecv.at[k])

    def send_grad(k):
        return remote(yb.at[k], dyb.at[k], gsend.at[k], grecv.at[k])

    def send_lat(r):
        return remote(lat.at[r], lat.at[r], lsend.at[r], lrecv.at[r])

    def send_thoughts(r):
        return remote(thg.at[r], thg.at[r], tsend.at[r], trecv.at[r])

    def started(source, target, number):
        copy = pltpu.make_async_copy(source, target, osem.at[number])
        copy.start()
        return copy

    def settle(pending, number, source, target):
        @pl.when(pending)
        def _():
            pltpu.make_async_copy(source, target.at[0], osem.at[number]).wait()

    def finish(copies):
        for copy in copies:
            copy.wait()

    def each_chunk(step, count):
        def body(i, carry):
            step(pl.ds(pl.multiple_of(i * count, count), count), i * count)
            return carry

        lax.fori_loop(0, length // count, body, 0)

    def loop(count, step):
        def body(i, carry):
            step(i)
            return carry

        lax.fori_loop(0, count, body, 0)

    def add_columns(number, values):
        sums[number] += jnp.sum(values.astype(F32).reshape(-1, 8, width), 0)

    def row(number):
        return small[:, group(number)]

    def group(number):
        return slice(number * width, (number + 1) * width)

    lane = lax.broadcasted_iota(jnp.int32, (1, 128), 1)
    low = lane < 64
    halves = (jnp.where(low, 1.0, 0.0).astype(BF), jnp.where(low, 0.0, 1.0).astype(BF))

    def first_length(r):
        segment = seg[pl.ds(r, 1), :]
        return jnp.sum(jnp.where(segment == 0, 1.0, 0.0), -1, keepdims=True).astype(jnp.int32)

    def set_cap(r):
        first = first_length(r)
        query = lax.broadcasted_iota(jnp.int32, (length, length), 0)
        key = lax.broadcasted_iota(jnp.int32, (length, length), 1)
        lowest = jnp.where(query >= first, first, 0)
        cap[...] = jnp.where((key <= query) & (key >= lowest), NO_CAP, MASKED)

    def positions(r, shift, axis=0):
        shape = (LAT, 1) if axis == 0 else (1, LAT)
        number = lax.broadcasted_iota(jnp.int32, shape, axis)
        result = jnp.full(shape, -1, jnp.int32)
        for j in range(thoughts):
            result = jnp.where(number == j, tpos[r, j] - shift, result)
        return result

    def selector_turned(r, shift):
        place = positions(r, shift, 1)
        return jnp.where(lax.broadcasted_iota(jnp.int32, (length, LAT), 0) == place, 1.0, 0.0)

    def selector(place):
        return jnp.where(lax.broadcasted_iota(jnp.int32, (LAT, length), 1) == place, 1.0, 0.0)

    def unmarked(r, start):
        place = lax.broadcasted_iota(jnp.int32, (32, 1), 0) + start
        keep = jnp.ones((32, 1), F32)
        for j in range(thoughts):
            keep = jnp.where(place == tpos[r, j], 0.0, keep)
        return keep

    def head_lanes(part, hp):
        start = part * width + hp * 128
        if isinstance(hp, int):
            return slice(start, start + 128)
        return pl.ds(pl.multiple_of(start, 128), 128)

    def norm_rows(x, target, k, which, gain, shift, more=None):
        def step(part, _):
            values = x[part, :]
            center = jnp.mean(values, -1, keepdims=True)
            centred = values - center
            scale = lax.rsqrt(jnp.mean(centred * centred, -1, keepdims=True) + EPSILON)
            stat[k, 2 * which, part, :] = center
            stat[k, 2 * which + 1, part, :] = scale
            target[part, :] = (centred * scale * row(gain) + row(shift)).astype(BF)
            if more is not None:
                more(part, values)

        each_chunk(step, 128)

    def norm_rows_back(x, part, k, which, gain, shift):
        scale = stat[k, 2 * which + 1, part, :]
        hat = (x[part, :] - stat[k, 2 * which, part, :]) * scale
        grad = da[part, :]
        add_columns(gain, grad * hat)
        add_columns(shift, grad)
        return norm_back(hat, scale, grad * row(gain))

    def forward(k, x, y, pending, first=None):
        def need(number):
            if first is not None:

                @pl.when(first)
                def _():
                    weights[number].wait()

        settle(pending, 0, a1, fa1)
        norm_rows(x, a1, k, 0, G1, B1)
        started(a1, fa1.at[k], 0)
        need(0)
        settle(pending, 1, ob, fo)

        for part in range(3):
            joined = dot(a1[...], wqkv[:, group(part)]) + joint[:, group(part)]
            jn[k, :, group(part)] = joined.astype(BF)
        for hp in range(pairs):
            q = jn[k, :, head_lanes(0, hp)]
            key = jn[k, :, head_lanes(1, hp)]
            value = jn[k, :, head_lanes(2, hp)]
            out = []
            for h in range(2):
                scores = dot_nt(q * (halves[h] * 0.125), key)
                chance = softmax(jnp.minimum(scores, cap[...])).astype(BF)
                pr[k, 2 * hp + h] = chance
                out.append(dot(chance, value))
            ob[:, head_lanes(0, hp)] = jnp.where(low, out[0], out[1]).astype(BF)
        started(ob, fo.at[k], 1)
        need(1)
        settle(pending, 2, a2, fa2)
        hm[k] = x[...] + dot(ob[...], wout[...]) + row(BO)

        def begin(part, values):
            y[part, :] = values + row(bd)

        norm_rows(hm.at[k], a2, k, 1, G2, B2, begin)
        started(a2, fa2.at[k], 2)
        need(2)
        need(3)
        settle(pending, 3, gb, fg)

        for c in range(blocks):
            part = group(c)
            g, d = gelu_both(dot(a2[...], wup[:, part]) + row(BU + c))
            gb[:, part] = g.astype(BF)
            slope[k, part, :] = d.astype(BF).T
            y[...] += dot(gb[:, part], wdown[part, :])
        started(gb, fg.at[k], 3)

    def backward(k, x, dy, dx, pending):
        def step(part, _):
            branch = dy[part, :].astype(BF)
            dm[part, :] = branch
            add_columns(bd, branch)

        settle(pending, 4, dm, fdm)
        each_chunk(step, 64)
        started(dm, fdm.at[k], 4)
        dmt[...] = dm[...].T
        dat[...] = jnp.zeros_like(dat)
        settle(pending, 5, dub, fdu)

        def mlp(c):
            part = pl.ds(pl.multiple_of(c * width, width), width)
            grad = (dot(wdown[part, :], dmt[...]) * slope[k, part, :]).astype(BF)
            dat[...] += dot(wup[:, part], grad)
            turned = grad.T
            dub[:, part] = turned
            add_columns(BU + c, turned)

        loop(blocks, mlp)
        da[...] = dat[...].T
        started(dub, fdu.at[k], 5)
        settle(pending, 6, dhr, fdhr)

        def step_two(part, _):
            middle = dy[part, :] + norm_rows_back(hm.at[k], part, k, 1, G2, B2)
            dy[part, :] = middle
            branch = middle.astype(BF)
            dhr[part, :] = branch
            add_columns(BO, branch)

        each_chunk(step_two, 64)
        started(dhr, fdhr.at[k], 6)
        dmt[...] = dhr[...].T
        dob[...] = dot(wout[...], dmt[...]).astype(BF).T
        settle(pending, 7, djb, fdj)

        def heads(hp):
            q = jn[k, :, head_lanes(0, hp)]
            key = jn[k, :, head_lanes(1, hp)]
            value = jn[k, :, head_lanes(2, hp)]
            grad_out = dob[:, head_lanes(0, hp)]
            dq, dk, dv = [], [], []
            for h in range(2):
                chance = pr[k, 2 * hp + h]
                chance_full = chance.astype(F32)
                inner_part = chance_full * dot_nt(grad_out * halves[h], value)
                total = jnp.sum(inner_part, -1, keepdims=True)
                grad_scores = (inner_part - chance_full * total).astype(BF)
                dq.append(dot(grad_scores, key))
                dk.append(dot_tn(grad_scores, q))
                dv.append(dot_tn(chance, grad_out))
            djb[:, head_lanes(0, hp)] = (jnp.where(low, dq[0], dq[1]) * 0.125).astype(BF)
            djb[:, head_lanes(1, hp)] = (jnp.where(low, dk[0], dk[1]) * 0.125).astype(BF)
            djb[:, head_lanes(2, hp)] = jnp.where(low, dv[0], dv[1]).astype(BF)

        loop(pairs, heads)
        started(djb, fdj.at[k], 7)
        into_input(k, x, dy, dx)

    def into_input(k, x, middle, dx):
        djt[...] = djb[...].T
        da[...] = dot(wqkv[...], djt[...]).T

        def step(part, _):
            add_columns(BQ, djb[part, group(0)])
            add_columns(BV, djb[part, group(2)])
            dx[part, :] = middle[part, :] + norm_rows_back(x, part, k, 0, G1, B1)

        each_chunk(step, 64)

    def forward_latent(r):
        x = xin.at[r]
        norm_rows(x, a1, r, 0, G1, B1)
        copies = [started(a1, fa1.at[r], 0)]
        jn[r, :, group(1)] = dot(a1[...], wqkv[:, group(1)]).astype(BF)
        jn[r, :, group(2)] = (dot(a1[...], wqkv[:, group(2)]) + row(BV)).astype(BF)
        place = positions(r, 1)
        chosen = exact_dot(selector(place), x[...])
        lx[r] = chosen
        hat, _ = normalized(chosen)
        normed = (hat * row(G1) + row(B1)).astype(BF)
        lq[r] = (dot(normed, wqkv[:, group(0)]) + row(BQ)).astype(BF)
        first = first_length(r)
        key_place = lax.broadcasted_iota(jnp.int32, (LAT, length), 1)
        lowest = jnp.where(place >= first, first, 0)
        limit = jnp.where((key_place <= place) & (key_place >= lowest), NO_CAP, MASKED)

        def heads(hp):
            q = lq[r, :, head_lanes(0, hp)]
            key = jn[r, :, head_lanes(1, hp)]
            value = jn[r, :, head_lanes(2, hp)]
            out = []
            for h in range(2):
                scores = dot_nt(q * (halves[h] * 0.125), key)
                chance = softmax(jnp.minimum(scores, limit)).astype(BF)
                lp[r, 2 * hp + h] = chance
                out.append(dot(chance, value))
            lo[r, :, head_lanes(0, hp)] = jnp.where(low, out[0], out[1]).astype(BF)

        for hp in range(pairs):
            heads(hp)
        middle = chosen + dot(lo[r], wout[...]) + row(BO)
        lh[r] = middle
        hat, _ = normalized(middle)
        la2[r] = (hat * row(G2) + row(B2)).astype(BF)
        lat[r] = middle + row(bd)

        def mlp(c):
            part = group(c)
            u = dot(la2[r], wup[:, part]) + row(BU + c)
            g, d = gelu_both(u)
            lg[r, :, part] = g.astype(BF)
            lslope[r, :, part] = d.astype(BF)
            lat[r] += dot(lg[r, :, part], wdown[part, :])

        for c in range(blocks):
            mlp(c)
        return copies

    def backward_latent(r, dx):
        grad_result = thg[r]
        branch = grad_result.astype(BF)
        top = slice(0, LAT)
        add_columns(bd, branch)
        dm[top, :] = branch
        a2[top, :] = la2[r]
        ob[top, :] = lo[r]
        gb[top, :] = lg[r]
        copies = [
            started(dm, fdm.at[r], 4),
            started(a2, fa2.at[r], 2),
            started(ob, fo.at[r], 1),
            started(gb, fg.at[r], 3),
        ]
        da[top, :] = jnp.zeros((LAT, width), F32)

        def mlp(c):
            part = group(c)
            grad = (dot_nt(dm[top, :], wdown[part, :]) * lslope[r, :, part]).astype(BF)
            dub[top, part] = grad
            add_columns(BU + c, grad)
            da[top, :] += dot_nt(grad, wup[:, part])

        for c in range(blocks):
            mlp(c)
        copies.append(started(dub, fdu.at[r], 5))
        hat, scale = normalized(lh[r])
        grad = da[top, :]
        add_columns(G2, grad * hat)
        add_columns(B2, grad)
        middle = grad_result + norm_back(hat, scale, grad * row(G2))
        rounded = middle.astype(BF)
        dhr[top, :] = rounded
        add_columns(BO, rounded)
        copies.append(started(dhr, fdhr.at[r], 6))
        spread = selector_turned(r, 1)
        dyb[r] = exact_dot(spread, middle)
        place = positions(r, 1, 1)
        first = first_length(r)
        key_place = lax.broadcasted_iota(jnp.int32, (length, LAT), 0)
        lowest = jnp.where(place >= first, first, 0)
        limit = jnp.where((key_place <= place) & (key_place >= lowest), NO_CAP, MASKED)
        dob[top, :] = dot_nt(rounded, wout[...]).astype(BF)

        def heads(hp):
            q = lq[r, :, head_lanes(0, hp)]
            key = jn[r, :, head_lanes(1, hp)]
            value = jn[r, :, head_lanes(2, hp)]
            grad_out = dob[top, head_lanes(0, hp)]
            dq, dk, dv = [], [], []
            for h in range(2):
                grad_masked = grad_out * halves[h]
                chance = lp[r, 2 * hp + h].astype(F32)
                inner_part = chance * dot_nt(grad_masked, value)
                total = jnp.sum(inner_part, -1, keepdims=True)
                dq.append(dot((inner_part - chance * total).astype(BF), key))
                scores = dot_nt(key, q * (halves[h] * 0.125))
                chance = softmax(jnp.minimum(scores, limit), 0)
                inner_part = chance * dot_nt(value, grad_masked)
                total = jnp.sum(inner_part, 0, keepdims=True)
                dk.append(dot((inner_part - chance * total).astype(BF), q))
                dv.append(dot(chance.astype(BF), grad_out))
            grad_q = (jnp.where(low, dq[0], dq[1]) * 0.125).astype(BF)
            djb[:, head_lanes(0, hp)] = dot(spread.astype(BF), grad_q).astype(BF)
            djb[:, head_lanes(1, hp)] = (jnp.where(low, dk[0], dk[1]) * 0.125).astype(BF)
            djb[:, head_lanes(2, hp)] = jnp.where(low, dv[0], dv[1]).astype(BF)

        for hp in range(pairs):
            heads(hp)
        copies.append(started(djb, fdj.at[r], 7))
        into_input(r, xin.at[r], dyb.at[r], dx)
        return copies

    staged = (
        (a1, fa1), (ob, fo), (a2, fa2), (gb, fg), (dm, fdm), (dub, fdu), (dhr, fdhr), (djb, fdj)
    )

    def settle_all(count, first=0):
        for number in range(first, first + count):
            source, target = staged[number]
            pltpu.make_async_copy(source, target.at[0], osem.at[number]).wait()

    @pl.when(me == 0)
    def _():
        def forward_step(k, carry):
            r = lax.rem(k, rows)
            set_cap(r)

            @pl.when(k < rows)
            def _():
                xin[k] = emb[r].astype(F32)

            @pl.when(k >= rows)
            def _():
                send_lat(r).wait_recv()
                xin[k] = exact_dot(selector_turned(r, 0), lat[r])

                def step(part, start):
                    xin[k, part, :] += emb[r, part, :].astype(F32) * unmarked(r, start)

                each_chunk(step, 32)

            forward(k, xin.at[k], yb.at[k], k > 0, first=k == 0)
            send_y(k).start()
            return carry

        lax.fori_loop(0, 2 * rows, forward_step, 0)
        settle_all(4)

        def backward_step(i, carry):
            k = lax.rem(i + rows, 2 * rows)
            r = lax.rem(i, rows)
            send_y(k).wait_send()
            send_grad(k).wait_recv()
            backward(k, xin.at[k], dyb.at[k], yb.at[k], i > 0)

            @pl.when(i < rows)
            def _():
                thg[r] = exact_dot(selector(positions(r, 0)), yb[k])
                send_thoughts(r).start()

            @pl.when(i >= rows)
            def _():
                def step(part, start):
                    yb[k, part, :] += yb[rows + r, part, :] * unmarked(r, start)

                each_chunk(step, 32)
                started(yb.at[k], sec.at[0, r], 8).wait()

            return carry

        lax.fori_loop(0, 2 * rows, backward_step, 0)
        settle_all(4, 4)

        def drain(r, carry):
            send_thoughts(r).wait_send()
            return carry

        lax.fori_loop(0, rows, drain, 0)

    @pl.when(me == 1)
    def _():
        finish(weights)

        def latent_step(r, carry):
            send_y(r).wait_recv()
            copies = forward_latent(r)
            send_lat(r).start()
            finish(copies)
            return carry

        lax.fori_loop(0, rows, latent_step, 0)

        def language_step(r, carry):
            k = rows + r
            set_cap(r)
            send_y(k).wait_recv()
            forward(k, xin.at[k], dyb.at[k], r > 0)
            result = started(dyb.at[k], sec.at[0, r], 8)
            dyb[r] = cot[r].astype(F32)
            backward(k, xin.at[k], dyb.at[r], yb.at[k], r > 0)
            send_grad(k).start()
            result.wait()
            return carry

        lax.fori_loop(0, rows, language_step, 0)
        settle_all(8)
        for buffer in (dm, a2, ob, gb, dub, dhr):
            buffer[...] = jnp.zeros_like(buffer)

        def latent_back_step(r, carry):
            send_thoughts(r).wait_recv()
            copies = backward_latent(r, yb.at[r])
            send_grad(r).start()
            finish(copies)
            return carry

        lax.fori_loop(0, rows, latent_back_step, 0)

        def drain(r, carry):
            send_lat(r).wait_send()
            send_grad(r).wait_send()
            send_grad(rows + r).wait_send()
            return carry

        lax.fori_loop(0, rows, drain, 0)

    sg[...] = jnp.sum(sums[...], 1)


def layers(emb, cot, seg, tpos, w_qkv, w_out, w_up, w_down, small):
    rows, length, width = emb.shape
    inner = w_up.shape[2]
    thoughts = tpos.shape[1]
    slots = 2 * rows
    packed = small.shape[1] // width
    vmem = pl.BlockSpec(memory_space=pltpu.VMEM)
    anywhere = pl.BlockSpec(memory_space=pl.ANY)
    smem = pl.BlockSpec(memory_space=pltpu.SMEM)

    def factor(columns):
        return jax.ShapeDtypeStruct((slots, length, columns), BF)

    def block(columns, kind=BF):
        return pltpu.VMEM((length, columns), kind)

    def few(columns, kind=BF):
        return pltpu.VMEM((rows, LAT, columns), kind)

    sizes = (rows, length, width, inner, thoughts)
    return pl.pallas_call(
        functools.partial(layers_kernel, sizes),
        out_shape=(
            jax.ShapeDtypeStruct((1, rows, length, width), F32),
            factor(width),
            factor(3 * width),
            factor(width),
            factor(width),
            factor(width),
            factor(inner),
            factor(inner),
            factor(width),
            jax.ShapeDtypeStruct((packed, width), F32),
        ),
        in_specs=[vmem, vmem, vmem, smem] + [anywhere] * 4 + [vmem],
        out_specs=(anywhere,) * 9 + (vmem,),
        scratch_shapes=[
            pltpu.VMEM((packed, 8, width), F32),
            pltpu.VMEM((1, 3 * width), F32),
            pltpu.VMEM((slots, 4, length, 1), F32),
            pltpu.VMEM((width, 3 * width), BF),
            pltpu.VMEM((width, width), BF),
            pltpu.VMEM((width, inner), BF),
            pltpu.VMEM((inner, width), BF),
            pltpu.VMEM((slots, length, width), F32),
            pltpu.VMEM((slots, length, width), F32),
            pltpu.VMEM((slots, length, width), F32),
            pltpu.VMEM((slots, length, 3 * width), BF),
            pltpu.VMEM((slots, HEADS, length, length), BF),
            pltpu.VMEM((slots, length, width), F32),
            pltpu.VMEM((slots, inner, length), BF),
            block(width),
            block(width),
            block(width),
            block(inner),
            block(width),
            block(inner),
            block(width),
            block(3 * width),
            block(width, F32),
            block(width),
            pltpu.VMEM((width, length), BF),
            pltpu.VMEM((width, length), F32),
            pltpu.VMEM((3 * width, length), BF),
            block(length, F32),
            few(width, F32),
            few(width, F32),
            few(width, F32),
            few(width),
            pltpu.VMEM((rows, HEADS, LAT, length), BF),
            few(width, F32),
            few(width),
            few(width),
            few(inner),
            few(inner),
            pltpu.SemaphoreType.DMA((4,)),
            pltpu.SemaphoreType.DMA((9,)),
        ]
        + [pltpu.SemaphoreType.DMA((slots,))] * 4
        + [pltpu.SemaphoreType.DMA((rows,))] * 4,
        compiler_params=pltpu.CompilerParams(
            collective_id=0, has_side_effects=True, vmem_limit_bytes=62 << 20
        ),
    )(emb, cot, seg, tpos, w_qkv, w_out, w_up, w_down, small)


def summed_by_parts(factors, small_grads):
    fa1, fdj, fo, fdhr, fa2, fdu, fg, fdm = factors

    def product(left, right):
        whole = jnp.einsum("ktm,ktn->mn", left, right, preferred_element_type=F32)
        return lax.psum_scatter(whole[None], "dp", scatter_dimension=1, tiled=True)

    small = lax.psum_scatter(
        small_grads.reshape(1, -1), "dp", scatter_dimension=1, tiled=True
    )
    return product(fa1, fdj), product(fo, fdhr), product(fa2, fdu), product(fg, fdm), small


def gradients_kernel(
    sizes,
    plan,
    fa1,
    fdj,
    fo,
    fdhr,
    fa2,
    fdu,
    fg,
    fdm,
    small,
    gqkv,
    gout,
    gup,
    gdown,
    gsmall,
    left,
    right,
    lt,
    gt,
    wa,
    wb,
    ra,
    rb,
    rs,
    xa,
    xb,
    xs,
    ua,
    ub,
    us,
    na,
    nb,
    ns,
    xl,
    ul,
    nl,
    lsem,
    pair_send,
    pair_recv,
    side_send,
    side_recv,
    up_send,
    up_recv,
    down_send,
    down_recv,
):
    width, narrow, depth = sizes
    me = lax.axis_index("dp")
    core = lax.rem(me, 2)
    side = lax.rem(me // 2, 2)
    level = me // 4
    partner = me + 1 - 2 * core
    beside = me + 2 - 4 * side
    above, below = me + 4, me - 4

    def remote(source, target, send, recv, device):
        return pltpu.make_async_remote_copy(
            src_ref=source,
            dst_ref=target,
            send_sem=send,
            recv_sem=recv,
            device_id={"dp": device},
            device_id_type=MESH,
        )

    lefts = {"qkv": fa1, "out": fo, "up": fa2, "down": fg}
    rights = {"qkv": fdj, "out": fdhr, "up": fdu, "down": fdm}
    steps = []
    turned = None
    ahead = 0
    for number, (name, part, _) in enumerate(plan):
        if name == "small":
            continue
        if name == "down":
            while ahead < depth:
                steps.append((number, name, True, ahead, None))
                ahead += 1
            steps += [(number, name, False, block, part) for block in range(depth)]
            continue
        if name != turned:
            steps.append((number, name, True, 0, None))
            turned = name
        steps.append((number, name, False, 0, part))
        for _ in range(2 if number else 1):
            if ahead < depth:
                steps.append((number, "down", True, ahead, None))
                ahead += 1

    def loads(index):
        _, name, turn, block, part = steps[index]
        slot = index % 2
        if turn:
            source = lefts[name].at[:, :, block * width : (block + 1) * width]
            return pltpu.make_async_copy(source, left.at[slot], lsem.at[slot])
        columns = narrow if name == "down" else width
        return pltpu.make_async_copy(
            rights[name].at[:, :, part * columns : (part + 1) * columns],
            right.at[slot, :, :, 0:columns],
            lsem.at[slot],
        )

    def start_loads(index):
        if index < len(steps):
            loads(index).start()

    start_loads(0)

    barrier = pltpu.get_barrier_semaphore()

    def greet(device):
        pl.semaphore_signal(barrier, inc=1, device_id={"dp": device}, device_id_type=MESH)

    greet(partner)
    greet(beside)

    @pl.when(level < 3)
    def _():
        greet(above)

    @pl.when(level > 0)
    def _():
        greet(below)

    pl.semaphore_wait(barrier, 2 + (level + 2) // 3 + (5 - level) // 3)

    views = []
    counts = {"a": 0, "b": 0, "line": 0}
    for number, (name, part, line_first) in enumerate(plan):
        if name == "small":
            views.append((small, rs, xs, us, ns, gsmall))
            continue
        kind = "b" if name == "down" else "a"
        index = counts[kind]
        counts[kind] += 1
        if kind == "a":
            target = {"qkv": gqkv, "out": gout, "up": gup}[name]
            place = target.at[0, :, part * width : (part + 1) * width]
            if line_first:
                along = counts["line"]
                counts["line"] += 1
                further = (xl.at[along], ul.at[along], nl.at[along], place)
            else:
                along = index - counts["line"]
                further = (xa.at[along], ua.at[along], na.at[along], place)
            views.append((wa.at[index % 2], ra.at[index]) + further)
        else:
            place = gdown.at[0, :, part * narrow : (part + 1) * narrow]
            views.append((wb, rb.at[index], xb.at[index], ub.at[index], nb.at[index], place))
    total = len(plan)
    previous = {}
    last_of = {}
    for number, (name, part, _) in enumerate(plan):
        kind = "s" if name == "small" else "b" if name == "down" else "a"
        mine = [n for n in range(number) if ("b" if plan[n][0] == "down" else "a") == kind]
        mine = [n for n in mine if plan[n][0] != "small"]
        back = 1 if kind == "b" else 2
        previous[number] = mine[-back] if kind != "s" and len(mine) >= back else None
        last_of[number] = True
        if previous[number] is not None:
            last_of[previous[number]] = False

    def pair_copy(number):
        w, r = views[number][:2]
        return remote(
            w.at[:, :, 1 - core], r, pair_send.at[number], pair_recv.at[number], partner
        )

    def side_copy(number):
        r, x = views[number][1:3]
        source = r.at[level, 1 - side] if plan[number][2] else r.at[:, 1 - side]
        return remote(source, x, side_send.at[number], side_recv.at[number], beside)

    def along_line(number):
        r, x = views[number][1:3]
        return r if plan[number][2] else x

    def up_copy(number, goal, source=None):
        u = views[number][3]
        return remote(
            u.at[goal - 1] if source is None else source,
            u.at[goal - 1],
            up_send.at[number, goal - 1],
            up_recv.at[number, goal - 1],
            above,
        )

    def down_copy(number, goal, source=None):
        n = views[number][4]
        return remote(
            n.at[goal] if source is None else source,
            n.at[goal],
            down_send.at[number, goal],
            down_recv.at[number, goal],
            below,
        )

    def start_line(number):
        base = along_line(number)

        @pl.when(level == 0)
        def _():
            for goal in (3, 2, 1):
                up_copy(number, goal, base.at[goal]).start()

        @pl.when(level == 3)
        def _():
            for goal in (0, 1, 2):
                down_copy(number, goal, base.at[goal]).start()

    position = {"step": 0}
    slots, length = left.shape[1:3]

    def turn_block(slot, target):
        def body(t, carry):
            tokens = pl.ds(pl.multiple_of(t * length, length), length)
            target[:, tokens] = left[slot, t].T
            return carry

        lax.fori_loop(0, slots, body, 0)

    def right_part(slot, lanes):
        part = right[slot, :, :, lanes]
        return part.reshape(slots * length, part.shape[2])

    def multiply(slot, w):
        def tile(t, carry):
            lanes = pl.ds(pl.multiple_of(t * narrow, narrow), narrow)
            product = dot(lt[...], right_part(slot, lanes))
            w[:, :, :, :, lanes] = product.reshape(w.shape[:4] + (narrow,))
            return carry

        lax.fori_loop(0, width // narrow, tile, 0)


    def produce(number):
        name, part, _ = plan[number]
        if name != "small":
            if previous[number] is not None:
                pair_copy(previous[number]).wait_send()
            w = views[number][0]
            while position["step"] < len(steps) and steps[position["step"]][0] == number:
                index = position["step"]
                position["step"] += 1
                _, source, turn, block, _ = steps[index]
                start_loads(index + 1)
                loads(index).wait()
                if turn:
                    turn_block(index % 2, gt.at[block] if source == "down" else lt)
                elif source == "down":
                    w[block] = dot(gt[block], right_part(index % 2, slice(0, narrow))).reshape(
                        w.shape[1:]
                    )
                else:
                    multiply(index % 2, w)
        pair_copy(number).start()

    def stage_pair(number):
        w, r = views[number][:2]
        pair_copy(number).wait_recv()

        def add(z, carry):
            for s in range(2):
                r[z, s] += w[z, s, core]
            return carry

        lax.fori_loop(0, 4, add, 0)
        if plan[number][2]:
            start_line(number)
        else:
            side_copy(number).start()

    def stage_side(number):
        if plan[number][2]:
            return
        r, x = views[number][1:3]
        side_copy(number).wait_recv()

        def add(z, carry):
            x[z] += r[z, side]
            return carry

        lax.fori_loop(0, 4, add, 0)
        start_line(number)

    def stage_up(number, height):
        u = views[number][3]
        base = along_line(number)

        @pl.when(level == height)
        def _():
            for goal in range(3, height - 1, -1):
                up_copy(number, goal).wait_recv()
                if goal > height:
                    u[goal - 1] += base[goal]
                    up_copy(number, goal).start()

    def stage_down(number, height):
        n = views[number][4]
        base = along_line(number)

        @pl.when(level == height)
        def _():
            for goal in range(0, height + 1):
                down_copy(number, goal).wait_recv()
                if goal < height:
                    n[goal] += base[goal]
                    down_copy(number, goal).start()

    def stage_sum(number):
        u, n, place = views[number][3:]
        base = along_line(number)

        @pl.when(level > 0)
        def _():
            base[level] += u[level - 1]

        @pl.when(level < 3)
        def _():
            base[level] += n[level]

        if plan[number][2]:
            side_copy(number).start()
        else:
            place[...] = base[level]

    def stage_last(number):
        if plan[number][2]:
            r, x = views[number][1:3]
            side_copy(number).wait_recv()
            views[number][5][...] = r[level, side] + x[...]

    def at(stage, number, *more):
        if 0 <= number < total:
            stage(number, *more)

    side_lag, hop = 3, 2
    for moment in range(total + side_lag + 3 * hop + 1):
        at(produce, moment)
        at(stage_pair, moment - 1)
        at(stage_side, moment - side_lag)
        for height in range(4):
            if height > 0:
                at(stage_up, moment - side_lag - hop * height, height)
            if height < 3:
                at(stage_down, moment - side_lag - hop * (3 - height), height)
        at(stage_sum, moment - side_lag - 3 * hop)
        at(stage_last, moment - side_lag - 3 * hop - 1)
    for number in range(total):
        if last_of[number]:
            pair_copy(number).wait_send()
        side_copy(number).wait_send()
        for goal in (1, 2, 3):

            @pl.when(goal > level)
            def _():
                up_copy(number, goal).wait_send()

        for goal in (0, 1, 2):

            @pl.when(goal < level)
            def _():
                down_copy(number, goal).wait_send()


def summed_in_kernel(factors, small_grads):
    fa1, fdj, fo, fdhr, fa2, fdu, fg, fdm = factors
    slots, length, width = fa1.shape
    inner = fg.shape[2]
    owners = 16
    depth = inner // width
    narrow = 256
    a_rows, b_rows = width // owners, inner // owners
    packed = small_grads.size // owners
    lanes = 128
    s_rows = -(-packed // (8 * lanes)) * 8
    small = small_grads.reshape(owners, packed)
    small = jnp.pad(small, ((0, 0), (0, s_rows * lanes - packed)))
    small = small.reshape(4, 2, 2, s_rows, lanes)
    plan = [
        ("qkv", 0, False),
        ("qkv", 1, True),
        ("small", 0, False),
        ("qkv", 2, False),
        ("down", 0, False),
        ("out", 0, True),
        ("down", 1, False),
        ("up", 0, False),
        ("down", 2, False),
        ("up", 1, False),
        ("up", 2, False),
        ("up", 3, False),
    ]
    total = len(plan)
    a_block, b_block, s_block = (a_rows, width), (b_rows, narrow), (s_rows, lanes)
    a_count = total - 1 - width // narrow
    b_count = width // narrow
    line_count = sum(line_first for _, _, line_first in plan)
    vmem = pl.BlockSpec(memory_space=pltpu.VMEM)
    anywhere = pl.BlockSpec(memory_space=pl.ANY)

    def trio(*lead):
        count = a_count if len(lead) == 2 else a_count - line_count
        return [
            pltpu.VMEM((count,) + lead + a_block, F32),
            pltpu.VMEM((b_count,) + lead + b_block, F32),
            pltpu.VMEM(lead + s_block, F32),
        ]

    *grads, small_grad = pl.pallas_call(
        functools.partial(gradients_kernel, (width, narrow, depth), plan),
        out_shape=(
            jax.ShapeDtypeStruct((1, a_rows, 3 * width), F32),
            jax.ShapeDtypeStruct((1, a_rows, width), F32),
            jax.ShapeDtypeStruct((1, a_rows, inner), F32),
            jax.ShapeDtypeStruct((1, b_rows, width), F32),
            jax.ShapeDtypeStruct(s_block, F32),
        ),
        in_specs=[anywhere] * 8 + [vmem],
        out_specs=(vmem,) * 5,
        scratch_shapes=[
            pltpu.VMEM((2, slots, length, width), BF),
            pltpu.VMEM((2, slots, length, width), BF),
            pltpu.VMEM((width, slots * length), BF),
            pltpu.VMEM((depth, width, slots * length), BF),
            pltpu.VMEM((2, 4, 2, 2) + a_block, F32),
            pltpu.VMEM((4, 2, 2) + b_block, F32),
        ]
        + trio(4, 2)
        + trio(4)
        + trio(3)
        + trio(3)
        + [
            pltpu.VMEM((line_count,) + a_block, F32),
            pltpu.VMEM((line_count, 3, 2) + a_block, F32),
            pltpu.VMEM((line_count, 3, 2) + a_block, F32),
        ]
        + [pltpu.SemaphoreType.DMA((2,))]
        + [pltpu.SemaphoreType.DMA((total,))] * 4
        + [pltpu.SemaphoreType.DMA((total, 3))] * 4,
        compiler_params=pltpu.CompilerParams(
            collective_id=1, has_side_effects=True, vmem_limit_bytes=62 << 20
        ),
    )(*factors, small)
    small_grad = small_grad.reshape(1, -1)[:, :packed]
    return tuple(grads) + (small_grad,)


def reduced(factors, small_grads):
    if lax.axis_size("dp") == 16:
        return summed_in_kernel(factors, small_grads)
    return summed_by_parts(factors, small_grads)


def per_device(
    embeddings, cotangent, seg_ids, thought_pos, w_qkv, w_out, w_up, w_down, small_params
):
    section_out, *factors, small_grads = layers(
        embeddings, cotangent, seg_ids, thought_pos, w_qkv, w_out, w_up, w_down, small_params
    )
    return (section_out,) + tuple(reduced(factors, small_grads))


def solution(mesh):
    return jax.shard_map(
        per_device,
        mesh=mesh,
        in_specs=(
            P("dp", None, None),
            P("dp", None, None),
            P("dp", None),
            P("dp", None),
            P("pipe", None, None),
            P("pipe", None, None),
            P("pipe", None, None),
            P("pipe", None, None),
            P("pipe", None),
        ),
        out_specs=(
            P("pipe", "dp", None, None),
            P("pipe", "dp", None),
            P("pipe", "dp", None),
            P("pipe", "dp", None),
            P("pipe", "dp", None),
            P("pipe", "dp"),
        ),
        check_vma=False,
    )
```

```python
import functools

import jax
import jax.numpy as jnp
from jax import lax
from jax.experimental import pallas as pl
from jax.experimental.pallas import tpu as pltpu
from jax.sharding import PartitionSpec as P

HEADS = 12
BF = jnp.bfloat16
F32 = jnp.float32
MESH = pl.DeviceIdType.MESH
EPSILON = 1e-05
MASKED = -1000000000.0
NO_CAP = 3e38
LAT = 16
G1, B1, BQ, BV, BO, G2, B2, BU = 0, 1, 2, 3, 4, 5, 6, 7


def dot(a, b):
    return lax.dot_general(a, b, (((1,), (0,)), ((), ())), preferred_element_type=F32)


def dot_nt(a, b):
    return lax.dot_general(a, b, (((1,), (1,)), ((), ())), preferred_element_type=F32)


def dot_tn(a, b):
    return lax.dot_general(a, b, (((0,), (0,)), ((), ())), preferred_element_type=F32)


def exact_dot(a, b):
    return lax.dot_general(
        a,
        b,
        (((1,), (0,)), ((), ())),
        precision=lax.Precision.HIGHEST,
        preferred_element_type=F32,
    )


def normalized(values):
    centred = values - jnp.mean(values, -1, keepdims=True)
    spread = jnp.mean(centred * centred, -1, keepdims=True)
    scale = lax.rsqrt(spread + EPSILON)
    return centred * scale, scale


def norm_back(hat, scale, grad):
    along = jnp.mean(grad * hat, -1, keepdims=True)
    return scale * (grad - jnp.mean(grad, -1, keepdims=True) - hat * along)


def gelu_both(u):
    c = 0.7978845608028654
    square = u * u
    t = jnp.tanh(c * u * (1.0 + 0.044715 * square))
    half = 0.5 + 0.5 * t
    slope = half + (0.5 * c) * u * (1.0 - t * t) * (1.0 + (3 * 0.044715) * square)
    return u * half, slope


def softmax(scores, axis=-1):
    e = jnp.exp(scores - jnp.max(scores, axis, keepdims=True))
    return e * (1.0 / jnp.sum(e, axis, keepdims=True))


def layers_kernel(
    sizes,
    emb,
    cot,
    seg,
    tpos,
    wqkv_h,
    wout_h,
    wup_h,
    wdown_h,
    small,
    sec,
    fa1,
    fdj,
    fo,
    fdhr,
    fa2,
    fdu,
    fg,
    fdm,
    sg,
    sums,
    joint,
    stat,
    wqkv,
    wout,
    wup,
    wdown,
    xin,
    yb,
    dyb,
    jn,
    pr,
    hm,
    slope,
    a1,
    ob,
    a2,
    gb,
    dm,
    dub,
    dhr,
    djb,
    da,
    dob,
    dmt,
    dat,
    djt,
    cap,
    lat,
    thg,
    lx,
    lq,
    lp,
    lh,
    la2,
    lo,
    lg,
    lslope,
    wsem,
    osem,
    ysend,
    yrecv,
    gsend,
    grecv,
    lsend,
    lrecv,
    tsend,
    trecv,
    follow,
):
    rows, length, width, inner, thoughts = sizes
    blocks = inner // width
    bd = BU + blocks
    pairs = HEADS // 2
    me = lax.axis_index("pipe")
    other = 1 - me

    weights = [
        pltpu.make_async_copy(source.at[0], target, wsem.at[number])
        for number, (source, target) in enumerate(
            ((wqkv_h, wqkv), (wout_h, wout), (wup_h, wup), (wdown_h, wdown))
        )
    ]
    for copy in weights:
        copy.start()
    for buffer in (sums, thg, lx):
        buffer[...] = jnp.zeros_like(buffer)
    replica = lax.axis_index("dp")
    core = lax.rem(replica, 2)
    partner = replica + 1 - 2 * core
    barrier = pltpu.get_barrier_semaphore()
    pl.semaphore_signal(barrier, inc=1, device_id={"pipe": other}, device_id_type=MESH)
    pl.semaphore_signal(barrier, inc=1, device_id={"dp": partner}, device_id_type=MESH)
    pl.semaphore_wait(barrier, 2)
    joint[:, 0:width] = small[:, BQ * width : (BQ + 1) * width]
    joint[:, width : 2 * width] = jnp.zeros((1, width), F32)
    joint[:, 2 * width : 3 * width] = small[:, BV * width : (BV + 1) * width]

    def remote(source, target, send, recv):
        return pltpu.make_async_remote_copy(
            src_ref=source,
            dst_ref=target,
            send_sem=send,
            recv_sem=recv,
            device_id={"pipe": other},
            device_id_type=MESH,
        )

    def send_y(k):
        return remote(yb.at[k], xin.at[k], ysend.at[k], yrecv.at[k])

    def send_grad(k):
        return remote(yb.at[k], dyb.at[k], gsend.at[k], grecv.at[k])

    def send_lat(r):
        return remote(lat.at[r], lat.at[r], lsend.at[r], lrecv.at[r])

    def send_thoughts(r):
        return remote(thg.at[r], thg.at[r], tsend.at[r], trecv.at[r])

    def started(source, target, number):
        copy = pltpu.make_async_copy(source, target, osem.at[number])
        copy.start()
        return copy

    def settle(pending, number, source, target):
        @pl.when(pending)
        def _():
            pltpu.make_async_copy(source, target.at[0], osem.at[number]).wait()

    def finish(copies):
        for copy in copies:
            copy.wait()

    def each_chunk(step, count):
        def body(i, carry):
            step(pl.ds(pl.multiple_of(i * count, count), count), i * count)
            return carry

        lax.fori_loop(0, length // count, body, 0)

    def loop(count, step):
        def body(i, carry):
            step(i)
            return carry

        lax.fori_loop(0, count, body, 0)

    def add_columns(number, values):
        sums[number] += jnp.sum(values.astype(F32).reshape(-1, 8, width), 0)

    def row(number):
        return small[:, group(number)]

    def group(number):
        return slice(number * width, (number + 1) * width)

    lane = lax.broadcasted_iota(jnp.int32, (1, 128), 1)
    low = lane < 64
    halves = (jnp.where(low, 1.0, 0.0).astype(BF), jnp.where(low, 0.0, 1.0).astype(BF))

    def first_length(r):
        segment = seg[pl.ds(r, 1), :]
        return jnp.sum(jnp.where(segment == 0, 1.0, 0.0), -1, keepdims=True).astype(jnp.int32)

    def set_cap(r):
        first = first_length(r)
        query = lax.broadcasted_iota(jnp.int32, (length, length), 0)
        key = lax.broadcasted_iota(jnp.int32, (length, length), 1)
        lowest = jnp.where(query >= first, first, 0)
        cap[...] = jnp.where((key <= query) & (key >= lowest), NO_CAP, MASKED)

    def positions(r, shift, axis=0):
        shape = (LAT, 1) if axis == 0 else (1, LAT)
        number = lax.broadcasted_iota(jnp.int32, shape, axis)
        result = jnp.full(shape, -1, jnp.int32)
        for j in range(thoughts):
            result = jnp.where(number == j, tpos[r, j] - shift, result)
        return result

    def selector_turned(r, shift):
        place = positions(r, shift, 1)
        return jnp.where(lax.broadcasted_iota(jnp.int32, (length, LAT), 0) == place, 1.0, 0.0)

    def unmarked(r, start):
        place = lax.broadcasted_iota(jnp.int32, (32, 1), 0) + start
        keep = jnp.ones((32, 1), F32)
        for j in range(thoughts):
            keep = jnp.where(place == tpos[r, j], 0.0, keep)
        return keep

    def head_lanes(part, hp):
        start = part * width + hp * 128
        if isinstance(hp, int):
            return slice(start, start + 128)
        return pl.ds(pl.multiple_of(start, 128), 128)

    def norm_rows(x, target, k, which, gain, shift, more=None):
        def step(part, _):
            values = x[part, :]
            center = jnp.mean(values, -1, keepdims=True)
            centred = values - center
            scale = lax.rsqrt(jnp.mean(centred * centred, -1, keepdims=True) + EPSILON)
            stat[k, 2 * which, part, :] = center
            stat[k, 2 * which + 1, part, :] = scale
            target[part, :] = (centred * scale * row(gain) + row(shift)).astype(BF)
            if more is not None:
                more(part, values)

        each_chunk(step, 128)

    def norm_rows_back(x, part, k, which, gain, shift):
        scale = stat[k, 2 * which + 1, part, :]
        hat = (x[part, :] - stat[k, 2 * which, part, :]) * scale
        grad = da[part, :]
        add_columns(gain, grad * hat)
        add_columns(shift, grad)
        return norm_back(hat, scale, grad * row(gain))

    def forward(k, x, y, pending, first=None):
        def need(number):
            if first is not None:

                @pl.when(first)
                def _():
                    weights[number].wait()

        settle(pending, 0, a1, fa1)
        norm_rows(x, a1, k, 0, G1, B1)
        started(a1, fa1.at[k], 0)
        need(0)
        settle(pending, 1, ob, fo)

        for part in range(3):
            joined = dot(a1[...], wqkv[:, group(part)]) + joint[:, group(part)]
            jn[k, :, group(part)] = joined.astype(BF)
        if first is not None:

            @pl.when(first & (core == 0))
            def _():
                pl.semaphore_signal(
                    follow, inc=1, device_id={"dp": partner}, device_id_type=MESH
                )

        for hp in range(pairs):
            q = jn[k, :, head_lanes(0, hp)]
            key = jn[k, :, head_lanes(1, hp)]
            value = jn[k, :, head_lanes(2, hp)]
            out = []
            for h in range(2):
                scores = dot_nt(q * (halves[h] * 0.125), key)
                chance = softmax(jnp.minimum(scores, cap[...])).astype(BF)
                pr[k, 2 * hp + h] = chance
                out.append(dot(chance, value))
            ob[:, head_lanes(0, hp)] = jnp.where(low, out[0], out[1]).astype(BF)
        started(ob, fo.at[k], 1)
        need(1)
        settle(pending, 2, a2, fa2)
        hm[k] = x[...] + dot(ob[...], wout[...]) + row(BO)

        def begin(part, values):
            y[part, :] = values + row(bd)

        norm_rows(hm.at[k], a2, k, 1, G2, B2, begin)
        started(a2, fa2.at[k], 2)
        need(2)
        need(3)
        settle(pending, 3, gb, fg)

        for c in range(blocks):
            part = group(c)
            g, d = gelu_both(dot(a2[...], wup[:, part]) + row(BU + c))
            gb[:, part] = g.astype(BF)
            slope[k, part, :] = d.astype(BF).T
            y[...] += dot(gb[:, part], wdown[part, :])
        started(gb, fg.at[k], 3)

    def backward(k, x, dy, dx, pending):
        def step(part, _):
            branch = dy[part, :].astype(BF)
            dm[part, :] = branch
            add_columns(bd, branch)

        settle(pending, 4, dm, fdm)
        each_chunk(step, 64)
        started(dm, fdm.at[k], 4)
        dmt[...] = dm[...].T
        dat[...] = jnp.zeros_like(dat)
        settle(pending, 5, dub, fdu)

        def mlp(c):
            part = pl.ds(pl.multiple_of(c * width, width), width)
            grad = (dot(wdown[part, :], dmt[...]) * slope[k, part, :]).astype(BF)
            dat[...] += dot(wup[:, part], grad)
            turned = grad.T
            dub[:, part] = turned
            add_columns(BU + c, turned)

        loop(blocks, mlp)
        da[...] = dat[...].T
        started(dub, fdu.at[k], 5)
        settle(pending, 6, dhr, fdhr)

        def step_two(part, _):
            middle = dy[part, :] + norm_rows_back(hm.at[k], part, k, 1, G2, B2)
            dy[part, :] = middle
            branch = middle.astype(BF)
            dhr[part, :] = branch
            add_columns(BO, branch)

        each_chunk(step_two, 64)
        started(dhr, fdhr.at[k], 6)
        dmt[...] = dhr[...].T
        dob[...] = dot(wout[...], dmt[...]).astype(BF).T
        settle(pending, 7, djb, fdj)

        def heads(hp):
            q = jn[k, :, head_lanes(0, hp)]
            key = jn[k, :, head_lanes(1, hp)]
            value = jn[k, :, head_lanes(2, hp)]
            grad_out = dob[:, head_lanes(0, hp)]
            dq, dk, dv = [], [], []
            for h in range(2):
                chance = pr[k, 2 * hp + h]
                chance_full = chance.astype(F32)
                inner_part = chance_full * dot_nt(grad_out * halves[h], value)
                total = jnp.sum(inner_part, -1, keepdims=True)
                grad_scores = (inner_part - chance_full * total).astype(BF)
                dq.append(dot(grad_scores, key))
                dk.append(dot_tn(grad_scores, q))
                dv.append(dot_tn(chance, grad_out))
            djb[:, head_lanes(0, hp)] = (jnp.where(low, dq[0], dq[1]) * 0.125).astype(BF)
            djb[:, head_lanes(1, hp)] = (jnp.where(low, dk[0], dk[1]) * 0.125).astype(BF)
            djb[:, head_lanes(2, hp)] = jnp.where(low, dv[0], dv[1]).astype(BF)

        loop(pairs, heads)
        started(djb, fdj.at[k], 7)
        into_input(k, x, dy, dx)

    def into_input(k, x, middle, dx):
        djt[...] = djb[...].T
        da[...] = dot(wqkv[...], djt[...]).T

        def step(part, _):
            add_columns(BQ, djb[part, group(0)])
            add_columns(BV, djb[part, group(2)])
            dx[part, :] = middle[part, :] + norm_rows_back(x, part, k, 0, G1, B1)

        each_chunk(step, 64)

    def forward_latent(r):
        x = xin.at[r]
        norm_rows(x, a1, r, 0, G1, B1)
        copies = [started(a1, fa1.at[r], 0)]
        jn[r, :, group(1)] = dot(a1[...], wqkv[:, group(1)]).astype(BF)
        jn[r, :, group(2)] = (dot(a1[...], wqkv[:, group(2)]) + row(BV)).astype(BF)
        place = positions(r, 1)
        da[...] = x[...]
        for j in range(thoughts):
            lx[r, j : j + 1, :] = da[pl.ds(jnp.maximum(tpos[r, j] - 1, 0), 1), :]
        chosen = lx[r]
        hat, _ = normalized(chosen)
        normed = (hat * row(G1) + row(B1)).astype(BF)
        lq[r] = (dot(normed, wqkv[:, group(0)]) + row(BQ)).astype(BF)
        first = first_length(r)
        key_place = lax.broadcasted_iota(jnp.int32, (LAT, length), 1)
        lowest = jnp.where(place >= first, first, 0)
        limit = jnp.where((key_place <= place) & (key_place >= lowest), NO_CAP, MASKED)

        def heads(hp):
            q = lq[r, :, head_lanes(0, hp)]
            key = jn[r, :, head_lanes(1, hp)]
            value = jn[r, :, head_lanes(2, hp)]
            out = []
            for h in range(2):
                scores = dot_nt(q * (halves[h] * 0.125), key)
                chance = softmax(jnp.minimum(scores, limit)).astype(BF)
                lp[r, 2 * hp + h] = chance
                out.append(dot(chance, value))
            lo[r, :, head_lanes(0, hp)] = jnp.where(low, out[0], out[1]).astype(BF)

        for hp in range(pairs):
            heads(hp)
        middle = chosen + dot(lo[r], wout[...]) + row(BO)
        lh[r] = middle
        hat, _ = normalized(middle)
        la2[r] = (hat * row(G2) + row(B2)).astype(BF)
        lat[r] = middle + row(bd)

        def mlp(c):
            part = group(c)
            u = dot(la2[r], wup[:, part]) + row(BU + c)
            g, d = gelu_both(u)
            lg[r, :, part] = g.astype(BF)
            lslope[r, :, part] = d.astype(BF)
            lat[r] += dot(lg[r, :, part], wdown[part, :])

        for c in range(blocks):
            mlp(c)
        return copies

    def backward_latent(r, dx):
        grad_result = thg[r]
        branch = grad_result.astype(BF)
        top = slice(0, LAT)
        add_columns(bd, branch)
        dm[top, :] = branch
        a2[top, :] = la2[r]
        ob[top, :] = lo[r]
        gb[top, :] = lg[r]
        copies = [
            started(dm, fdm.at[r], 4),
            started(a2, fa2.at[r], 2),
            started(ob, fo.at[r], 1),
            started(gb, fg.at[r], 3),
        ]
        da[top, :] = jnp.zeros((LAT, width), F32)

        def mlp(c):
            part = group(c)
            grad = (dot_nt(dm[top, :], wdown[part, :]) * lslope[r, :, part]).astype(BF)
            dub[top, part] = grad
            add_columns(BU + c, grad)
            da[top, :] += dot_nt(grad, wup[:, part])

        for c in range(blocks):
            mlp(c)
        copies.append(started(dub, fdu.at[r], 5))
        hat, scale = normalized(lh[r])
        grad = da[top, :]
        add_columns(G2, grad * hat)
        add_columns(B2, grad)
        middle = grad_result + norm_back(hat, scale, grad * row(G2))
        rounded = middle.astype(BF)
        dhr[top, :] = rounded
        add_columns(BO, rounded)
        copies.append(started(dhr, fdhr.at[r], 6))
        spread = selector_turned(r, 1)
        dyb[r] = exact_dot(spread, middle)
        place = positions(r, 1, 1)
        first = first_length(r)
        key_place = lax.broadcasted_iota(jnp.int32, (length, LAT), 0)
        lowest = jnp.where(place >= first, first, 0)
        limit = jnp.where((key_place <= place) & (key_place >= lowest), NO_CAP, MASKED)
        dob[top, :] = dot_nt(rounded, wout[...]).astype(BF)

        def heads(hp):
            q = lq[r, :, head_lanes(0, hp)]
            key = jn[r, :, head_lanes(1, hp)]
            value = jn[r, :, head_lanes(2, hp)]
            grad_out = dob[top, head_lanes(0, hp)]
            dq, dk, dv = [], [], []
            for h in range(2):
                grad_masked = grad_out * halves[h]
                chance = lp[r, 2 * hp + h].astype(F32)
                inner_part = chance * dot_nt(grad_masked, value)
                total = jnp.sum(inner_part, -1, keepdims=True)
                dq.append(dot((inner_part - chance * total).astype(BF), key))
                scores = dot_nt(key, q * (halves[h] * 0.125))
                chance = softmax(jnp.minimum(scores, limit), 0)
                inner_part = chance * dot_nt(value, grad_masked)
                total = jnp.sum(inner_part, 0, keepdims=True)
                dk.append(dot((inner_part - chance * total).astype(BF), q))
                dv.append(dot(chance.astype(BF), grad_out))
            grad_q = (jnp.where(low, dq[0], dq[1]) * 0.125).astype(BF)
            djb[:, head_lanes(0, hp)] = dot(spread.astype(BF), grad_q).astype(BF)
            djb[:, head_lanes(1, hp)] = (jnp.where(low, dk[0], dk[1]) * 0.125).astype(BF)
            djb[:, head_lanes(2, hp)] = jnp.where(low, dv[0], dv[1]).astype(BF)

        for hp in range(pairs):
            heads(hp)
        copies.append(started(djb, fdj.at[r], 7))
        into_input(r, xin.at[r], dyb.at[r], dx)
        return copies

    staged = (
        (a1, fa1), (ob, fo), (a2, fa2), (gb, fg), (dm, fdm), (dub, fdu), (dhr, fdhr), (djb, fdj)
    )

    def settle_all(count, first=0):
        for number in range(first, first + count):
            source, target = staged[number]
            pltpu.make_async_copy(source, target.at[0], osem.at[number]).wait()

    @pl.when(me == 0)
    def _():
        def forward_step(k, carry):
            r = lax.rem(k, rows)
            set_cap(r)

            @pl.when((k == 0) & (core == 1))
            def _():
                pl.semaphore_wait(follow, 1)

            @pl.when(k < rows)
            def _():
                xin[k] = emb[r].astype(F32)

            @pl.when(k >= rows)
            def _():
                send_lat(r).wait_recv()
                xin[k] = exact_dot(selector_turned(r, 0), lat[r])

                def step(part, start):
                    xin[k, part, :] += emb[r, part, :].astype(F32) * unmarked(r, start)

                each_chunk(step, 32)

            forward(k, xin.at[k], yb.at[k], k > 0, first=k == 0)

            @pl.when(k > 0)
            def _():
                send_y(k - 1).wait_send()

            send_y(k).start()
            return carry

        lax.fori_loop(0, 2 * rows, forward_step, 0)
        send_y(2 * rows - 1).wait_send()
        settle_all(4)

        def backward_step(i, carry):
            k = lax.rem(i + rows, 2 * rows)
            r = lax.rem(i, rows)
            send_grad(k).wait_recv()
            backward(k, xin.at[k], dyb.at[k], yb.at[k], i > 0)

            @pl.when(i < rows)
            def _():
                for j in range(thoughts):
                    thg[r, j : j + 1, :] = yb[k, pl.ds(tpos[r, j], 1), :]
                send_thoughts(r).start()

            @pl.when(i >= rows)
            def _():
                def step(part, start):
                    yb[k, part, :] += yb[rows + r, part, :] * unmarked(r, start)

                each_chunk(step, 32)
                started(yb.at[k], sec.at[0, r], 8).wait()

            return carry

        lax.fori_loop(0, 2 * rows, backward_step, 0)
        settle_all(4, 4)

        def drain(r, carry):
            send_thoughts(r).wait_send()
            return carry

        lax.fori_loop(0, rows, drain, 0)

    @pl.when(me == 1)
    def _():
        finish(weights)

        def latent_step(r, carry):
            send_y(r).wait_recv()
            copies = forward_latent(r)
            send_lat(r).start()
            finish(copies)
            return carry

        lax.fori_loop(0, rows, latent_step, 0)

        def language_step(r, carry):
            k = rows + r
            set_cap(r)
            send_y(k).wait_recv()
            forward(k, xin.at[k], dyb.at[k], r > 0)
            result = started(dyb.at[k], sec.at[0, r], 8)
            dyb[r] = cot[r].astype(F32)
            backward(k, xin.at[k], dyb.at[r], yb.at[k], r > 0)

            @pl.when(r > 0)
            def _():
                send_grad(k - 1).wait_send()

            send_grad(k).start()
            result.wait()
            return carry

        lax.fori_loop(0, rows, language_step, 0)
        send_grad(2 * rows - 1).wait_send()
        settle_all(8)
        for buffer in (dm, a2, ob, gb, dub, dhr):
            buffer[...] = jnp.zeros_like(buffer)

        def latent_back_step(r, carry):
            send_thoughts(r).wait_recv()
            copies = backward_latent(r, yb.at[r])

            @pl.when(r > 0)
            def _():
                send_grad(r - 1).wait_send()

            send_grad(r).start()
            finish(copies)
            return carry

        lax.fori_loop(0, rows, latent_back_step, 0)

        def drain(r, carry):
            send_lat(r).wait_send()
            return carry

        lax.fori_loop(0, rows, drain, 0)
        send_grad(rows - 1).wait_send()

    sg[...] = jnp.sum(sums[...], 1)


def layers(emb, cot, seg, tpos, w_qkv, w_out, w_up, w_down, small):
    rows, length, width = emb.shape
    inner = w_up.shape[2]
    thoughts = tpos.shape[1]
    slots = 2 * rows
    packed = small.shape[1] // width
    vmem = pl.BlockSpec(memory_space=pltpu.VMEM)
    anywhere = pl.BlockSpec(memory_space=pl.ANY)
    smem = pl.BlockSpec(memory_space=pltpu.SMEM)

    def factor(columns):
        return jax.ShapeDtypeStruct((slots, length, columns), BF)

    def block(columns, kind=BF):
        return pltpu.VMEM((length, columns), kind)

    def few(columns, kind=BF):
        return pltpu.VMEM((rows, LAT, columns), kind)

    sizes = (rows, length, width, inner, thoughts)
    return pl.pallas_call(
        functools.partial(layers_kernel, sizes),
        out_shape=(
            jax.ShapeDtypeStruct((1, rows, length, width), F32),
            factor(width),
            factor(3 * width),
            factor(width),
            factor(width),
            factor(width),
            factor(inner),
            factor(inner),
            factor(width),
            jax.ShapeDtypeStruct((packed, width), F32),
        ),
        in_specs=[vmem, vmem, vmem, smem] + [anywhere] * 4 + [vmem],
        out_specs=(anywhere,) * 9 + (vmem,),
        scratch_shapes=[
            pltpu.VMEM((packed, 8, width), F32),
            pltpu.VMEM((1, 3 * width), F32),
            pltpu.VMEM((slots, 4, length, 1), F32),
            pltpu.VMEM((width, 3 * width), BF),
            pltpu.VMEM((width, width), BF),
            pltpu.VMEM((width, inner), BF),
            pltpu.VMEM((inner, width), BF),
            pltpu.VMEM((slots, length, width), F32),
            pltpu.VMEM((slots, length, width), F32),
            pltpu.VMEM((slots, length, width), F32),
            pltpu.VMEM((slots, length, 3 * width), BF),
            pltpu.VMEM((slots, HEADS, length, length), BF),
            pltpu.VMEM((slots, length, width), F32),
            pltpu.VMEM((slots, inner, length), BF),
            block(width),
            block(width),
            block(width),
            block(inner),
            block(width),
            block(inner),
            block(width),
            block(3 * width),
            block(width, F32),
            block(width),
            pltpu.VMEM((width, length), BF),
            pltpu.VMEM((width, length), F32),
            pltpu.VMEM((3 * width, length), BF),
            block(length, F32),
            few(width, F32),
            few(width, F32),
            few(width, F32),
            few(width),
            pltpu.VMEM((rows, HEADS, LAT, length), BF),
            few(width, F32),
            few(width),
            few(width),
            few(inner),
            few(inner),
            pltpu.SemaphoreType.DMA((4,)),
            pltpu.SemaphoreType.DMA((9,)),
        ]
        + [pltpu.SemaphoreType.DMA((slots,))] * 4
        + [pltpu.SemaphoreType.DMA((rows,))] * 4
        + [pltpu.SemaphoreType.REGULAR],
        compiler_params=pltpu.CompilerParams(
            collective_id=0, has_side_effects=True, vmem_limit_bytes=62 << 20
        ),
    )(emb, cot, seg, tpos, w_qkv, w_out, w_up, w_down, small)


def summed_by_parts(factors, small_grads):
    fa1, fdj, fo, fdhr, fa2, fdu, fg, fdm = factors

    def product(left, right):
        whole = jnp.einsum("ktm,ktn->mn", left, right, preferred_element_type=F32)
        return lax.psum_scatter(whole[None], "dp", scatter_dimension=1, tiled=True)

    small = lax.psum_scatter(
        small_grads.reshape(1, -1), "dp", scatter_dimension=1, tiled=True
    )
    return product(fa1, fdj), product(fo, fdhr), product(fa2, fdu), product(fg, fdm), small


def gradients_kernel(
    sizes,
    plan,
    fa1,
    fdj,
    fo,
    fdhr,
    fa2,
    fdu,
    fg,
    fdm,
    small,
    gqkv,
    gout,
    gup,
    gdown,
    gsmall,
    left,
    right,
    lt,
    gt,
    wa,
    wb,
    ra,
    rb,
    rs,
    xa,
    xb,
    xs,
    ua,
    ub,
    us,
    na,
    nb,
    ns,
    xl,
    ul,
    nl,
    lsem,
    pair_send,
    pair_recv,
    side_send,
    side_recv,
    up_send,
    up_recv,
    down_send,
    down_recv,
):
    width, narrow, depth = sizes
    me = lax.axis_index("dp")
    core = lax.rem(me, 2)
    side = lax.rem(me // 2, 2)
    level = me // 4
    partner = me + 1 - 2 * core
    beside = me + 2 - 4 * side
    above, below = me + 4, me - 4

    def remote(source, target, send, recv, device):
        return pltpu.make_async_remote_copy(
            src_ref=source,
            dst_ref=target,
            send_sem=send,
            recv_sem=recv,
            device_id={"dp": device},
            device_id_type=MESH,
        )

    lefts = {"qkv": fa1, "out": fo, "up": fa2, "down": fg}
    rights = {"qkv": fdj, "out": fdhr, "up": fdu, "down": fdm}
    steps = []
    turned = None
    ahead = 0
    for number, (name, part, _) in enumerate(plan):
        if name == "small":
            continue
        if name == "down":
            while ahead < depth:
                steps.append((number, name, True, ahead, None))
                ahead += 1
            steps += [(number, name, False, block, part) for block in range(depth)]
            continue
        if name != turned:
            steps.append((number, name, True, 0, None))
            turned = name
        steps.append((number, name, False, 0, part))
        for _ in range(2 if number else 1):
            if ahead < depth:
                steps.append((number, "down", True, ahead, None))
                ahead += 1

    def loads(index):
        _, name, turn, block, part = steps[index]
        slot = index % 2
        if turn:
            source = lefts[name].at[:, :, block * width : (block + 1) * width]
            return pltpu.make_async_copy(source, left.at[slot], lsem.at[slot])
        columns = narrow if name == "down" else width
        return pltpu.make_async_copy(
            rights[name].at[:, :, part * columns : (part + 1) * columns],
            right.at[slot, :, :, 0:columns],
            lsem.at[slot],
        )

    def start_loads(index):
        if index < len(steps):
            loads(index).start()

    start_loads(0)

    barrier = pltpu.get_barrier_semaphore()

    def greet(device):
        pl.semaphore_signal(barrier, inc=1, device_id={"dp": device}, device_id_type=MESH)

    greet(partner)
    greet(beside)

    @pl.when(level < 3)
    def _():
        greet(above)

    @pl.when(level > 0)
    def _():
        greet(below)

    pl.semaphore_wait(barrier, 2 + (level + 2) // 3 + (5 - level) // 3)

    views = []
    counts = {"a": 0, "b": 0, "line": 0}
    for number, (name, part, line_first) in enumerate(plan):
        if name == "small":
            views.append((small, rs, xs, us, ns, gsmall))
            continue
        kind = "b" if name == "down" else "a"
        index = counts[kind]
        counts[kind] += 1
        if kind == "a":
            target = {"qkv": gqkv, "out": gout, "up": gup}[name]
            place = target.at[0, :, part * width : (part + 1) * width]
            if line_first:
                along = counts["line"]
                counts["line"] += 1
                further = (xl.at[along], ul.at[along], nl.at[along], place)
            else:
                along = index - counts["line"]
                further = (xa.at[along], ua.at[along], na.at[along], place)
            views.append((wa.at[index % 2], ra.at[index]) + further)
        else:
            place = gdown.at[0, :, part * narrow : (part + 1) * narrow]
            views.append((wb, rb.at[index], xb.at[index], ub.at[index], nb.at[index], place))
    total = len(plan)
    previous = {}
    last_of = {}
    for number, (name, part, _) in enumerate(plan):
        kind = "s" if name == "small" else "b" if name == "down" else "a"
        mine = [n for n in range(number) if ("b" if plan[n][0] == "down" else "a") == kind]
        mine = [n for n in mine if plan[n][0] != "small"]
        back = 1 if kind == "b" else 2
        previous[number] = mine[-back] if kind != "s" and len(mine) >= back else None
        last_of[number] = True
        if previous[number] is not None:
            last_of[previous[number]] = False

    def pair_copy(number):
        w, r = views[number][:2]
        return remote(
            w.at[:, :, 1 - core], r, pair_send.at[number], pair_recv.at[number], partner
        )

    def side_copy(number):
        r, x = views[number][1:3]
        source = r.at[level, 1 - side] if plan[number][2] else r.at[:, 1 - side]
        return remote(source, x, side_send.at[number], side_recv.at[number], beside)

    def along_line(number):
        r, x = views[number][1:3]
        return r if plan[number][2] else x

    def up_copy(number, goal, source=None):
        u = views[number][3]
        return remote(
            u.at[goal - 1] if source is None else source,
            u.at[goal - 1],
            up_send.at[number, goal - 1],
            up_recv.at[number, goal - 1],
            above,
        )

    def down_copy(number, goal, source=None):
        n = views[number][4]
        return remote(
            n.at[goal] if source is None else source,
            n.at[goal],
            down_send.at[number, goal],
            down_recv.at[number, goal],
            below,
        )

    def start_line(number):
        base = along_line(number)

        @pl.when(level == 0)
        def _():
            for goal in (3, 2, 1):
                up_copy(number, goal, base.at[goal]).start()

        @pl.when(level == 3)
        def _():
            for goal in (0, 1, 2):
                down_copy(number, goal, base.at[goal]).start()

    position = {"step": 0}
    slots, length = left.shape[1:3]

    def turn_block(slot, target):
        def body(t, carry):
            tokens = pl.ds(pl.multiple_of(t * length, length), length)
            target[:, tokens] = left[slot, t].T
            return carry

        lax.fori_loop(0, slots, body, 0)

    def right_part(slot, lanes):
        part = right[slot, :, :, lanes]
        return part.reshape(slots * length, part.shape[2])

    def multiply(slot, w):
        def tile(t, carry):
            lanes = pl.ds(pl.multiple_of(t * narrow, narrow), narrow)
            product = dot(lt[...], right_part(slot, lanes))
            w[:, :, :, :, lanes] = product.reshape(w.shape[:4] + (narrow,))
            return carry

        lax.fori_loop(0, width // narrow, tile, 0)


    def produce(number):
        name, part, _ = plan[number]
        if name != "small":
            if previous[number] is not None:
                pair_copy(previous[number]).wait_send()
            w = views[number][0]
            while position["step"] < len(steps) and steps[position["step"]][0] == number:
                index = position["step"]
                position["step"] += 1
                _, source, turn, block, _ = steps[index]
                start_loads(index + 1)
                loads(index).wait()
                if turn:
                    turn_block(index % 2, gt.at[block] if source == "down" else lt)
                elif source == "down":
                    w[block] = dot(gt[block], right_part(index % 2, slice(0, narrow))).reshape(
                        w.shape[1:]
                    )
                else:
                    multiply(index % 2, w)
        pair_copy(number).start()

    def stage_pair(number):
        w, r = views[number][:2]
        pair_copy(number).wait_recv()

        def add(z, carry):
            for s in range(2):
                r[z, s] += w[z, s, core]
            return carry

        lax.fori_loop(0, 4, add, 0)
        if plan[number][2]:
            start_line(number)
        else:
            side_copy(number).start()

    def stage_side(number):
        if plan[number][2]:
            return
        r, x = views[number][1:3]
        side_copy(number).wait_recv()

        def add(z, carry):
            x[z] += r[z, side]
            return carry

        lax.fori_loop(0, 4, add, 0)
        start_line(number)

    def stage_up(number, height):
        u = views[number][3]
        base = along_line(number)

        @pl.when(level == height)
        def _():
            for goal in range(3, height - 1, -1):
                up_copy(number, goal).wait_recv()
                if goal > height:
                    u[goal - 1] += base[goal]
                    up_copy(number, goal).start()

    def stage_down(number, height):
        n = views[number][4]
        base = along_line(number)

        @pl.when(level == height)
        def _():
            for goal in range(0, height + 1):
                down_copy(number, goal).wait_recv()
                if goal < height:
                    n[goal] += base[goal]
                    down_copy(number, goal).start()

    def stage_sum(number):
        u, n, place = views[number][3:]
        base = along_line(number)

        @pl.when(level > 0)
        def _():
            base[level] += u[level - 1]

        @pl.when(level < 3)
        def _():
            base[level] += n[level]

        if plan[number][2]:
            side_copy(number).start()
        else:
            place[...] = base[level]

    def stage_last(number):
        if plan[number][2]:
            r, x = views[number][1:3]
            side_copy(number).wait_recv()
            views[number][5][...] = r[level, side] + x[...]

    def at(stage, number, *more):
        if 0 <= number < total:
            stage(number, *more)

    side_lag, hop = 3, 2
    for moment in range(total + side_lag + 3 * hop + 1):
        at(produce, moment)
        at(stage_pair, moment - 1)
        at(stage_side, moment - side_lag)
        for height in range(4):
            if height > 0:
                at(stage_up, moment - side_lag - hop * height, height)
            if height < 3:
                at(stage_down, moment - side_lag - hop * (3 - height), height)
        at(stage_sum, moment - side_lag - 3 * hop)
        at(stage_last, moment - side_lag - 3 * hop - 1)
    for number in range(total):
        if last_of[number]:
            pair_copy(number).wait_send()
        side_copy(number).wait_send()
        for goal in (1, 2, 3):

            @pl.when(goal > level)
            def _():
                up_copy(number, goal).wait_send()

        for goal in (0, 1, 2):

            @pl.when(goal < level)
            def _():
                down_copy(number, goal).wait_send()


def summed_in_kernel(factors, small_grads):
    fa1, fdj, fo, fdhr, fa2, fdu, fg, fdm = factors
    slots, length, width = fa1.shape
    inner = fg.shape[2]
    owners = 16
    depth = inner // width
    narrow = 256
    a_rows, b_rows = width // owners, inner // owners
    packed = small_grads.size // owners
    lanes = 128
    s_rows = -(-packed // (8 * lanes)) * 8
    small = small_grads.reshape(owners, packed)
    small = jnp.pad(small, ((0, 0), (0, s_rows * lanes - packed)))
    small = small.reshape(4, 2, 2, s_rows, lanes)
    plan = [
        ("qkv", 0, False),
        ("qkv", 1, True),
        ("small", 0, False),
        ("qkv", 2, False),
        ("down", 0, False),
        ("out", 0, True),
        ("down", 1, False),
        ("up", 0, False),
        ("down", 2, False),
        ("up", 1, False),
        ("up", 2, False),
        ("up", 3, False),
    ]
    total = len(plan)
    a_block, b_block, s_block = (a_rows, width), (b_rows, narrow), (s_rows, lanes)
    a_count = total - 1 - width // narrow
    b_count = width // narrow
    line_count = sum(line_first for _, _, line_first in plan)
    vmem = pl.BlockSpec(memory_space=pltpu.VMEM)
    anywhere = pl.BlockSpec(memory_space=pl.ANY)

    def trio(*lead):
        count = a_count if len(lead) == 2 else a_count - line_count
        return [
            pltpu.VMEM((count,) + lead + a_block, F32),
            pltpu.VMEM((b_count,) + lead + b_block, F32),
            pltpu.VMEM(lead + s_block, F32),
        ]

    *grads, small_grad = pl.pallas_call(
        functools.partial(gradients_kernel, (width, narrow, depth), plan),
        out_shape=(
            jax.ShapeDtypeStruct((1, a_rows, 3 * width), F32),
            jax.ShapeDtypeStruct((1, a_rows, width), F32),
            jax.ShapeDtypeStruct((1, a_rows, inner), F32),
            jax.ShapeDtypeStruct((1, b_rows, width), F32),
            jax.ShapeDtypeStruct(s_block, F32),
        ),
        in_specs=[anywhere] * 8 + [vmem],
        out_specs=(vmem,) * 5,
        scratch_shapes=[
            pltpu.VMEM((2, slots, length, width), BF),
            pltpu.VMEM((2, slots, length, width), BF),
            pltpu.VMEM((width, slots * length), BF),
            pltpu.VMEM((depth, width, slots * length), BF),
            pltpu.VMEM((2, 4, 2, 2) + a_block, F32),
            pltpu.VMEM((4, 2, 2) + b_block, F32),
        ]
        + trio(4, 2)
        + trio(4)
        + trio(3)
        + trio(3)
        + [
            pltpu.VMEM((line_count,) + a_block, F32),
            pltpu.VMEM((line_count, 3, 2) + a_block, F32),
            pltpu.VMEM((line_count, 3, 2) + a_block, F32),
        ]
        + [pltpu.SemaphoreType.DMA((2,))]
        + [pltpu.SemaphoreType.DMA((total,))] * 4
        + [pltpu.SemaphoreType.DMA((total, 3))] * 4,
        compiler_params=pltpu.CompilerParams(
            collective_id=1, has_side_effects=True, vmem_limit_bytes=62 << 20
        ),
    )(*factors, small)
    small_grad = small_grad.reshape(1, -1)[:, :packed]
    return tuple(grads) + (small_grad,)


def reduced(factors, small_grads):
    if lax.axis_size("dp") == 16:
        return summed_in_kernel(factors, small_grads)
    return summed_by_parts(factors, small_grads)


def per_device(
    embeddings, cotangent, seg_ids, thought_pos, w_qkv, w_out, w_up, w_down, small_params
):
    section_out, *factors, small_grads = layers(
        embeddings, cotangent, seg_ids, thought_pos, w_qkv, w_out, w_up, w_down, small_params
    )
    return (section_out,) + tuple(reduced(factors, small_grads))


def solution(mesh):
    return jax.shard_map(
        per_device,
        mesh=mesh,
        in_specs=(
            P("dp", None, None),
            P("dp", None, None),
            P("dp", None),
            P("dp", None),
            P("pipe", None, None),
            P("pipe", None, None),
            P("pipe", None, None),
            P("pipe", None, None),
            P("pipe", None),
        ),
        out_specs=(
            P("pipe", "dp", None, None),
            P("pipe", "dp", None),
            P("pipe", "dp", None),
            P("pipe", "dp", None),
            P("pipe", "dp", None),
            P("pipe", "dp"),
        ),
        check_vma=False,
    )
```

```python
import functools

import jax
import jax.numpy as jnp
from jax import lax
from jax.experimental import pallas as pl
from jax.experimental.pallas import tpu as pltpu
from jax.sharding import PartitionSpec as P

HEADS = 12
BF = jnp.bfloat16
F32 = jnp.float32
MESH = pl.DeviceIdType.MESH
EPSILON = 1e-05
MASKED = -1000000000.0
NO_CAP = 3e38
LAT = 16
G1, B1, BQ, BV, BO, G2, B2, BU = 0, 1, 2, 3, 4, 5, 6, 7


def dot(a, b):
    return lax.dot_general(a, b, (((1,), (0,)), ((), ())), preferred_element_type=F32)


def dot_nt(a, b):
    return lax.dot_general(a, b, (((1,), (1,)), ((), ())), preferred_element_type=F32)


def dot_tn(a, b):
    return lax.dot_general(a, b, (((0,), (0,)), ((), ())), preferred_element_type=F32)


def exact_dot(a, b):
    return lax.dot_general(
        a,
        b,
        (((1,), (0,)), ((), ())),
        precision=lax.Precision.HIGHEST,
        preferred_element_type=F32,
    )


def normalized(values):
    centred = values - jnp.mean(values, -1, keepdims=True)
    spread = jnp.mean(centred * centred, -1, keepdims=True)
    scale = lax.rsqrt(spread + EPSILON)
    return centred * scale, scale


def norm_back(hat, scale, grad):
    along = jnp.mean(grad * hat, -1, keepdims=True)
    return scale * (grad - jnp.mean(grad, -1, keepdims=True) - hat * along)


def gelu_both(u):
    c = 0.7978845608028654
    square = u * u
    t = jnp.tanh(c * u * (1.0 + 0.044715 * square))
    half = 0.5 + 0.5 * t
    slope = half + (0.5 * c) * u * (1.0 - t * t) * (1.0 + (3 * 0.044715) * square)
    return u * half, slope


def softmax(scores, axis=-1):
    e = jnp.exp(scores - jnp.max(scores, axis, keepdims=True))
    return e * (1.0 / jnp.sum(e, axis, keepdims=True))


def layers_kernel(
    sizes,
    emb,
    cot,
    seg,
    tpos,
    wqkv_h,
    wout_h,
    wup_h,
    wdown_h,
    small,
    sec,
    fa1,
    fdj,
    fo,
    fdhr,
    fa2,
    fdu,
    fg,
    fdm,
    sg,
    sums,
    joint,
    stat,
    wqkv,
    wout,
    wup,
    wdown,
    xin,
    yb,
    dyb,
    jn,
    pr,
    hm,
    slope,
    bent,
    a1,
    ob,
    a2,
    gb,
    dm,
    dub,
    dhr,
    djb,
    da,
    dob,
    dmt,
    dat,
    djt,
    cap,
    lat,
    thg,
    lx,
    lq,
    lp,
    lh,
    la2,
    lo,
    lg,
    lslope,
    wsem,
    osem,
    ysend,
    yrecv,
    gsend,
    grecv,
    lsend,
    lrecv,
    tsend,
    trecv,
):
    rows, length, width, inner, thoughts = sizes
    blocks = inner // width
    bd = BU + blocks
    pairs = HEADS // 2
    me = lax.axis_index("pipe")
    other = 1 - me

    weights = [
        pltpu.make_async_copy(source.at[0], target, wsem.at[number])
        for number, (source, target) in enumerate(
            ((wqkv_h, wqkv), (wout_h, wout), (wup_h, wup), (wdown_h, wdown))
        )
    ]
    for copy in weights:
        copy.start()
    barrier = pltpu.get_barrier_semaphore()
    pl.semaphore_signal(barrier, inc=1, device_id={"pipe": other}, device_id_type=MESH)
    pl.semaphore_wait(barrier, 1)
    sums[...] = jnp.zeros_like(sums)
    joint[:, 0:width] = small[:, BQ * width : (BQ + 1) * width]
    joint[:, width : 2 * width] = jnp.zeros((1, width), F32)
    joint[:, 2 * width : 3 * width] = small[:, BV * width : (BV + 1) * width]

    def remote(source, target, send, recv):
        return pltpu.make_async_remote_copy(
            src_ref=source,
            dst_ref=target,
            send_sem=send,
            recv_sem=recv,
            device_id={"pipe": other},
            device_id_type=MESH,
        )

    def send_y(k):
        return remote(yb.at[k], xin.at[k], ysend.at[k], yrecv.at[k])

    def send_grad(k):
        return remote(yb.at[k], dyb.at[k], gsend.at[k], grecv.at[k])

    def send_lat(r):
        return remote(lat.at[r], lat.at[r], lsend.at[r], lrecv.at[r])

    def send_thoughts(r):
        return remote(thg.at[r], thg.at[r], tsend.at[r], trecv.at[r])

    def started(source, target, number):
        copy = pltpu.make_async_copy(source, target, osem.at[number])
        copy.start()
        return copy

    def settle(pending, number, source, target):
        @pl.when(pending)
        def _():
            pltpu.make_async_copy(source, target.at[0], osem.at[number]).wait()

    def finish(copies):
        for copy in copies:
            copy.wait()

    def each_chunk(step, count):
        def body(i, carry):
            step(pl.ds(pl.multiple_of(i * count, count), count), i * count)
            return carry

        lax.fori_loop(0, length // count, body, 0)

    def loop(count, step):
        def body(i, carry):
            step(i)
            return carry

        lax.fori_loop(0, count, body, 0)

    def add_columns(number, values):
        sums[number] += jnp.sum(values.astype(F32).reshape(-1, 8, width), 0)

    def row(number):
        return small[:, group(number)]

    def group(number):
        return slice(number * width, (number + 1) * width)

    lane = lax.broadcasted_iota(jnp.int32, (1, 128), 1)
    low = lane < 64
    halves = (jnp.where(low, 1.0, 0.0).astype(BF), jnp.where(low, 0.0, 1.0).astype(BF))

    def first_length(r):
        segment = seg[pl.ds(r, 1), :]
        return jnp.sum(jnp.where(segment == 0, 1.0, 0.0), -1, keepdims=True).astype(jnp.int32)

    def set_cap(r):
        first = first_length(r)
        query = lax.broadcasted_iota(jnp.int32, (length, length), 0)
        key = lax.broadcasted_iota(jnp.int32, (length, length), 1)
        lowest = jnp.where(query >= first, first, 0)
        cap[...] = jnp.where((key <= query) & (key >= lowest), NO_CAP, MASKED)

    def positions(r, shift, axis=0):
        shape = (LAT, 1) if axis == 0 else (1, LAT)
        number = lax.broadcasted_iota(jnp.int32, shape, axis)
        result = jnp.full(shape, -1, jnp.int32)
        for j in range(thoughts):
            result = jnp.where(number == j, tpos[r, j] - shift, result)
        return result

    def selector_turned(r, shift):
        place = positions(r, shift, 1)
        return jnp.where(lax.broadcasted_iota(jnp.int32, (length, LAT), 0) == place, 1.0, 0.0)

    def selector(place):
        return jnp.where(lax.broadcasted_iota(jnp.int32, (LAT, length), 1) == place, 1.0, 0.0)

    def unmarked(r, start):
        place = lax.broadcasted_iota(jnp.int32, (32, 1), 0) + start
        keep = jnp.ones((32, 1), F32)
        for j in range(thoughts):
            keep = jnp.where(place == tpos[r, j], 0.0, keep)
        return keep

    def head_lanes(part, hp):
        start = part * width + hp * 128
        if isinstance(hp, int):
            return slice(start, start + 128)
        return pl.ds(pl.multiple_of(start, 128), 128)

    def norm_rows(x, target, k, which, gain, shift, more=None):
        def step(part, _):
            values = x[part, :]
            center = jnp.mean(values, -1, keepdims=True)
            centred = values - center
            scale = lax.rsqrt(jnp.mean(centred * centred, -1, keepdims=True) + EPSILON)
            stat[k, 2 * which, part, :] = center
            stat[k, 2 * which + 1, part, :] = scale
            target[part, :] = (centred * scale * row(gain) + row(shift)).astype(BF)
            if more is not None:
                more(part, values)

        each_chunk(step, 128)

    def norm_rows_back(x, part, k, which, gain, shift):
        scale = stat[k, 2 * which + 1, part, :]
        hat = (x[part, :] - stat[k, 2 * which, part, :]) * scale
        grad = da[part, :]
        add_columns(gain, grad * hat)
        add_columns(shift, grad)
        return norm_back(hat, scale, grad * row(gain))

    def forward(k, x, y, pending, first=None):
        def need(number):
            if first is not None:

                @pl.when(first)
                def _():
                    weights[number].wait()

        settle(pending, 0, a1, fa1)
        norm_rows(x, a1, k, 0, G1, B1)
        started(a1, fa1.at[k], 0)
        need(0)
        settle(pending, 1, ob, fo)

        for part in range(3):
            joined = dot(a1[...], wqkv[:, group(part)]) + joint[:, group(part)]
            jn[k, :, group(part)] = joined.astype(BF)
        for hp in range(pairs):
            q = jn[k, :, head_lanes(0, hp)]
            key = jn[k, :, head_lanes(1, hp)]
            value = jn[k, :, head_lanes(2, hp)]
            out = []
            for h in range(2):
                scores = dot_nt(q * (halves[h] * 0.125), key)
                chance = softmax(jnp.minimum(scores, cap[...])).astype(BF)
                pr[k, 2 * hp + h] = chance
                out.append(dot(chance, value))
            ob[:, head_lanes(0, hp)] = jnp.where(low, out[0], out[1]).astype(BF)
        started(ob, fo.at[k], 1)
        need(1)
        settle(pending, 2, a2, fa2)
        hm[k] = x[...] + dot(ob[...], wout[...]) + row(BO)

        def begin(part, values):
            y[part, :] = values + row(bd)

        norm_rows(hm.at[k], a2, k, 1, G2, B2, begin)
        started(a2, fa2.at[k], 2)
        need(2)
        need(3)
        settle(pending, 3, gb, fg)

        for c in range(blocks):
            part = group(c)
            g, d = gelu_both(dot(a2[...], wup[:, part]) + row(BU + c))
            gb[:, part] = g.astype(BF)
            bent[:, part] = d.astype(BF)
            y[...] += dot(gb[:, part], wdown[part, :])
        started(gb, fg.at[k], 3)

    def turn_slopes(k):
        for c in range(blocks):
            slope[k, group(c), :] = bent[:, group(c)].T

    def backward(k, x, dy, dx, pending):
        def step(part, _):
            branch = dy[part, :].astype(BF)
            dm[part, :] = branch
            add_columns(bd, branch)

        settle(pending, 4, dm, fdm)
        each_chunk(step, 64)
        started(dm, fdm.at[k], 4)
        dmt[...] = dm[...].T
        dat[...] = jnp.zeros_like(dat)
        settle(pending, 5, dub, fdu)

        def mlp(c):
            part = pl.ds(pl.multiple_of(c * width, width), width)
            grad = (dot(wdown[part, :], dmt[...]) * slope[k, part, :]).astype(BF)
            dat[...] += dot(wup[:, part], grad)
            turned = grad.T
            dub[:, part] = turned
            add_columns(BU + c, turned)

        loop(blocks, mlp)
        da[...] = dat[...].T
        started(dub, fdu.at[k], 5)
        settle(pending, 6, dhr, fdhr)

        def step_two(part, _):
            middle = dy[part, :] + norm_rows_back(hm.at[k], part, k, 1, G2, B2)
            dy[part, :] = middle
            branch = middle.astype(BF)
            dhr[part, :] = branch
            add_columns(BO, branch)

        each_chunk(step_two, 64)
        started(dhr, fdhr.at[k], 6)
        dmt[...] = dhr[...].T
        dob[...] = dot(wout[...], dmt[...]).astype(BF).T
        settle(pending, 7, djb, fdj)

        def heads(hp):
            q = jn[k, :, head_lanes(0, hp)]
            key = jn[k, :, head_lanes(1, hp)]
            value = jn[k, :, head_lanes(2, hp)]
            grad_out = dob[:, head_lanes(0, hp)]
            dq, dk, dv = [], [], []
            for h in range(2):
                chance = pr[k, 2 * hp + h]
                chance_full = chance.astype(F32)
                inner_part = chance_full * dot_nt(grad_out * halves[h], value)
                total = jnp.sum(inner_part, -1, keepdims=True)
                grad_scores = (inner_part - chance_full * total).astype(BF)
                dq.append(dot(grad_scores, key))
                dk.append(dot_tn(grad_scores, q))
                dv.append(dot_tn(chance, grad_out))
            djb[:, head_lanes(0, hp)] = (jnp.where(low, dq[0], dq[1]) * 0.125).astype(BF)
            djb[:, head_lanes(1, hp)] = (jnp.where(low, dk[0], dk[1]) * 0.125).astype(BF)
            djb[:, head_lanes(2, hp)] = jnp.where(low, dv[0], dv[1]).astype(BF)

        loop(pairs, heads)
        started(djb, fdj.at[k], 7)
        into_input(k, x, dy, dx)

    def into_input(k, x, middle, dx):
        djt[...] = djb[...].T
        da[...] = dot(wqkv[...], djt[...]).T

        def step(part, _):
            add_columns(BQ, djb[part, group(0)])
            add_columns(BV, djb[part, group(2)])
            dx[part, :] = middle[part, :] + norm_rows_back(x, part, k, 0, G1, B1)

        each_chunk(step, 64)

    def forward_latent(r):
        x = xin.at[r]
        norm_rows(x, a1, r, 0, G1, B1)
        copies = [started(a1, fa1.at[r], 0)]
        jn[r, :, group(1)] = dot(a1[...], wqkv[:, group(1)]).astype(BF)
        jn[r, :, group(2)] = (dot(a1[...], wqkv[:, group(2)]) + row(BV)).astype(BF)
        place = positions(r, 1)
        chosen = exact_dot(selector(place), x[...])
        lx[r] = chosen
        hat, _ = normalized(chosen)
        normed = (hat * row(G1) + row(B1)).astype(BF)
        lq[r] = (dot(normed, wqkv[:, group(0)]) + row(BQ)).astype(BF)
        first = first_length(r)
        key_place = lax.broadcasted_iota(jnp.int32, (LAT, length), 1)
        lowest = jnp.where(place >= first, first, 0)
        limit = jnp.where((key_place <= place) & (key_place >= lowest), NO_CAP, MASKED)

        def heads(hp):
            q = lq[r, :, head_lanes(0, hp)]
            key = jn[r, :, head_lanes(1, hp)]
            value = jn[r, :, head_lanes(2, hp)]
            out = []
            for h in range(2):
                scores = dot_nt(q * (halves[h] * 0.125), key)
                chance = softmax(jnp.minimum(scores, limit)).astype(BF)
                lp[r, 2 * hp + h] = chance
                out.append(dot(chance, value))
            lo[r, :, head_lanes(0, hp)] = jnp.where(low, out[0], out[1]).astype(BF)

        for hp in range(pairs):
            heads(hp)
        middle = chosen + dot(lo[r], wout[...]) + row(BO)
        lh[r] = middle
        hat, _ = normalized(middle)
        la2[r] = (hat * row(G2) + row(B2)).astype(BF)
        lat[r] = middle + row(bd)

        def mlp(c):
            part = group(c)
            u = dot(la2[r], wup[:, part]) + row(BU + c)
            g, d = gelu_both(u)
            lg[r, :, part] = g.astype(BF)
            lslope[r, :, part] = d.astype(BF)
            lat[r] += dot(lg[r, :, part], wdown[part, :])

        for c in range(blocks):
            mlp(c)
        return copies

    def backward_latent(r, dx):
        grad_result = thg[r]
        branch = grad_result.astype(BF)
        top = slice(0, LAT)
        add_columns(bd, branch)
        dm[top, :] = branch
        a2[top, :] = la2[r]
        ob[top, :] = lo[r]
        gb[top, :] = lg[r]
        copies = [
            started(dm, fdm.at[r], 4),
            started(a2, fa2.at[r], 2),
            started(ob, fo.at[r], 1),
            started(gb, fg.at[r], 3),
        ]
        da[top, :] = jnp.zeros((LAT, width), F32)

        def mlp(c):
            part = group(c)
            grad = (dot_nt(dm[top, :], wdown[part, :]) * lslope[r, :, part]).astype(BF)
            dub[top, part] = grad
            add_columns(BU + c, grad)
            da[top, :] += dot_nt(grad, wup[:, part])

        for c in range(blocks):
            mlp(c)
        copies.append(started(dub, fdu.at[r], 5))
        hat, scale = normalized(lh[r])
        grad = da[top, :]
        add_columns(G2, grad * hat)
        add_columns(B2, grad)
        middle = grad_result + norm_back(hat, scale, grad * row(G2))
        rounded = middle.astype(BF)
        dhr[top, :] = rounded
        add_columns(BO, rounded)
        copies.append(started(dhr, fdhr.at[r], 6))
        spread = selector_turned(r, 1)
        dyb[r] = exact_dot(spread, middle)
        place = positions(r, 1, 1)
        first = first_length(r)
        key_place = lax.broadcasted_iota(jnp.int32, (length, LAT), 0)
        lowest = jnp.where(place >= first, first, 0)
        limit = jnp.where((key_place <= place) & (key_place >= lowest), NO_CAP, MASKED)
        dob[top, :] = dot_nt(rounded, wout[...]).astype(BF)

        def heads(hp):
            q = lq[r, :, head_lanes(0, hp)]
            key = jn[r, :, head_lanes(1, hp)]
            value = jn[r, :, head_lanes(2, hp)]
            grad_out = dob[top, head_lanes(0, hp)]
            dq, dk, dv = [], [], []
            for h in range(2):
                grad_masked = grad_out * halves[h]
                chance = lp[r, 2 * hp + h].astype(F32)
                inner_part = chance * dot_nt(grad_masked, value)
                total = jnp.sum(inner_part, -1, keepdims=True)
                dq.append(dot((inner_part - chance * total).astype(BF), key))
                scores = dot_nt(key, q * (halves[h] * 0.125))
                chance = softmax(jnp.minimum(scores, limit), 0)
                inner_part = chance * dot_nt(value, grad_masked)
                total = jnp.sum(inner_part, 0, keepdims=True)
                dk.append(dot((inner_part - chance * total).astype(BF), q))
                dv.append(dot(chance.astype(BF), grad_out))
            grad_q = (jnp.where(low, dq[0], dq[1]) * 0.125).astype(BF)
            djb[:, head_lanes(0, hp)] = dot(spread.astype(BF), grad_q).astype(BF)
            djb[:, head_lanes(1, hp)] = (jnp.where(low, dk[0], dk[1]) * 0.125).astype(BF)
            djb[:, head_lanes(2, hp)] = jnp.where(low, dv[0], dv[1]).astype(BF)

        for hp in range(pairs):
            heads(hp)
        copies.append(started(djb, fdj.at[r], 7))
        into_input(r, xin.at[r], dyb.at[r], dx)
        return copies

    staged = (
        (a1, fa1), (ob, fo), (a2, fa2), (gb, fg), (dm, fdm), (dub, fdu), (dhr, fdhr), (djb, fdj)
    )

    def settle_all(count, first=0):
        for number in range(first, first + count):
            source, target = staged[number]
            pltpu.make_async_copy(source, target.at[0], osem.at[number]).wait()

    @pl.when(me == 0)
    def _():
        def forward_step(k, carry):
            r = lax.rem(k, rows)
            set_cap(r)

            @pl.when(k < rows)
            def _():
                xin[k] = emb[r].astype(F32)

            @pl.when(k >= rows)
            def _():
                send_lat(r).wait_recv()
                xin[k] = exact_dot(selector_turned(r, 0), lat[r])

                def step(part, start):
                    xin[k, part, :] += emb[r, part, :].astype(F32) * unmarked(r, start)

                each_chunk(step, 32)

            forward(k, xin.at[k], yb.at[k], k > 0, first=k == 0)

            @pl.when(k > 0)
            def _():
                send_y(k - 1).wait_send()

            send_y(k).start()
            turn_slopes(k)
            return carry

        lax.fori_loop(0, 2 * rows, forward_step, 0)
        send_y(2 * rows - 1).wait_send()
        settle_all(4)

        def backward_step(i, carry):
            k = lax.rem(i + rows, 2 * rows)
            r = lax.rem(i, rows)
            send_grad(k).wait_recv()
            backward(k, xin.at[k], dyb.at[k], yb.at[k], i > 0)

            @pl.when(i < rows)
            def _():
                thg[r] = exact_dot(selector(positions(r, 0)), yb[k])
                send_thoughts(r).start()

            @pl.when(i >= rows)
            def _():
                def step(part, start):
                    yb[k, part, :] += yb[rows + r, part, :] * unmarked(r, start)

                each_chunk(step, 32)
                started(yb.at[k], sec.at[0, r], 8).wait()

            return carry

        lax.fori_loop(0, 2 * rows, backward_step, 0)
        settle_all(4, 4)

        def drain(r, carry):
            send_thoughts(r).wait_send()
            return carry

        lax.fori_loop(0, rows, drain, 0)

    @pl.when(me == 1)
    def _():
        finish(weights)

        def latent_step(r, carry):
            send_y(r).wait_recv()
            copies = forward_latent(r)
            send_lat(r).start()
            finish(copies)
            return carry

        lax.fori_loop(0, rows, latent_step, 0)

        def language_step(r, carry):
            k = rows + r
            set_cap(r)
            send_y(k).wait_recv()
            forward(k, xin.at[k], dyb.at[k], r > 0)
            result = started(dyb.at[k], sec.at[0, r], 8)
            turn_slopes(k)
            dyb[r] = cot[r].astype(F32)
            backward(k, xin.at[k], dyb.at[r], yb.at[k], r > 0)
            send_grad(k).start()
            result.wait()
            return carry

        lax.fori_loop(0, rows, language_step, 0)
        settle_all(8)
        for buffer in (dm, a2, ob, gb, dub, dhr):
            buffer[...] = jnp.zeros_like(buffer)

        def latent_back_step(r, carry):
            send_thoughts(r).wait_recv()
            copies = backward_latent(r, yb.at[r])
            send_grad(r).start()
            finish(copies)
            return carry

        lax.fori_loop(0, rows, latent_back_step, 0)

        def drain(r, carry):
            send_lat(r).wait_send()
            send_grad(r).wait_send()
            send_grad(rows + r).wait_send()
            return carry

        lax.fori_loop(0, rows, drain, 0)

    if len(sg.shape) == 2:
        sg[...] = jnp.sum(sums[...], 1)
        return
    packed = sums.shape[0] * width // 16
    totals = [jnp.sum(sums[number], 0, keepdims=True) for number in range(sums.shape[0])]
    flat = jnp.concatenate(totals + [jnp.zeros((1, 128), F32)], 1)
    sg[...] = jnp.zeros_like(sg)
    for owner in range(16):
        z, x, c = owner // 4, owner // 2 % 2, owner % 2
        for line in range(-(-packed // 128)):
            start = owner * packed + line * 128
            sg[z, x, c, line : line + 1, :] = flat[:, start : start + 128]


def layers(emb, cot, seg, tpos, w_qkv, w_out, w_up, w_down, small):
    rows, length, width = emb.shape
    inner = w_up.shape[2]
    thoughts = tpos.shape[1]
    slots = 2 * rows
    packed = small.shape[1] // width
    small_shape = (packed, width)
    if lax.axis_size("dp") == 16:
        small_shape = (4, 2, 2, -(-small.shape[1] // (16 * 8 * 128)) * 8, 128)
    vmem = pl.BlockSpec(memory_space=pltpu.VMEM)
    anywhere = pl.BlockSpec(memory_space=pl.ANY)
    smem = pl.BlockSpec(memory_space=pltpu.SMEM)

    def factor(columns):
        return jax.ShapeDtypeStruct((slots, length, columns), BF)

    def block(columns, kind=BF):
        return pltpu.VMEM((length, columns), kind)

    def few(columns, kind=BF):
        return pltpu.VMEM((rows, LAT, columns), kind)

    sizes = (rows, length, width, inner, thoughts)
    return pl.pallas_call(
        functools.partial(layers_kernel, sizes),
        out_shape=(
            jax.ShapeDtypeStruct((1, rows, length, width), F32),
            factor(width),
            factor(3 * width),
            factor(width),
            factor(width),
            factor(width),
            factor(inner),
            factor(inner),
            factor(width),
            jax.ShapeDtypeStruct(small_shape, F32),
        ),
        in_specs=[vmem, vmem, vmem, smem] + [anywhere] * 4 + [vmem],
        out_specs=(anywhere,) * 9 + (vmem,),
        scratch_shapes=[
            pltpu.VMEM((packed, 8, width), F32),
            pltpu.VMEM((1, 3 * width), F32),
            pltpu.VMEM((slots, 4, length, 1), F32),
            pltpu.VMEM((width, 3 * width), BF),
            pltpu.VMEM((width, width), BF),
            pltpu.VMEM((width, inner), BF),
            pltpu.VMEM((inner, width), BF),
            pltpu.VMEM((slots, length, width), F32),
            pltpu.VMEM((slots, length, width), F32),
            pltpu.VMEM((slots, length, width), F32),
            pltpu.VMEM((slots, length, 3 * width), BF),
            pltpu.VMEM((slots, HEADS, length, length), BF),
            pltpu.VMEM((slots, length, width), F32),
            pltpu.VMEM((slots, inner, length), BF),
            block(inner),
            block(width),
            block(width),
            block(width),
            block(inner),
            block(width),
            block(inner),
            block(width),
            block(3 * width),
            block(width, F32),
            block(width),
            pltpu.VMEM((width, length), BF),
            pltpu.VMEM((width, length), F32),
            pltpu.VMEM((3 * width, length), BF),
            block(length, F32),
            few(width, F32),
            few(width, F32),
            few(width, F32),
            few(width),
            pltpu.VMEM((rows, HEADS, LAT, length), BF),
            few(width, F32),
            few(width),
            few(width),
            few(inner),
            few(inner),
            pltpu.SemaphoreType.DMA((4,)),
            pltpu.SemaphoreType.DMA((9,)),
        ]
        + [pltpu.SemaphoreType.DMA((slots,))] * 4
        + [pltpu.SemaphoreType.DMA((rows,))] * 4,
        compiler_params=pltpu.CompilerParams(
            collective_id=0, has_side_effects=True, vmem_limit_bytes=62 << 20
        ),
    )(emb, cot, seg, tpos, w_qkv, w_out, w_up, w_down, small)


def summed_by_parts(factors, small_grads):
    fa1, fdj, fo, fdhr, fa2, fdu, fg, fdm = factors

    def product(left, right):
        whole = jnp.einsum("ktm,ktn->mn", left, right, preferred_element_type=F32)
        return lax.psum_scatter(whole[None], "dp", scatter_dimension=1, tiled=True)

    small = lax.psum_scatter(
        small_grads.reshape(1, -1), "dp", scatter_dimension=1, tiled=True
    )
    return product(fa1, fdj), product(fo, fdhr), product(fa2, fdu), product(fg, fdm), small


def gradients_kernel(
    sizes,
    plan,
    lags,
    fa1,
    fdj,
    fo,
    fdhr,
    fa2,
    fdu,
    fg,
    fdm,
    small,
    gqkv,
    gout,
    gup,
    gdown,
    gsmall,
    left,
    right,
    lt,
    gt,
    wa,
    ra,
    xa,
    ua,
    na,
    wb,
    rb,
    xb,
    ub,
    nb,
    wc,
    rc,
    xc,
    uc,
    nc,
    rs,
    xs,
    us,
    ns,
    xl,
    ul,
    nl,
    lsem,
    pair_send,
    pair_recv,
    side_send,
    side_recv,
    up_send,
    up_recv,
    down_send,
    down_recv,
):
    width, narrow, depth = sizes
    side_lag, hop, fifo = lags
    me = lax.axis_index("dp")
    core = lax.rem(me, 2)
    side = lax.rem(me // 2, 2)
    level = me // 4
    partner = me + 1 - 2 * core
    beside = me + 2 - 4 * side
    above, below = me + 4, me - 4

    def remote(source, target, send, recv, device):
        return pltpu.make_async_remote_copy(
            src_ref=source,
            dst_ref=target,
            send_sem=send,
            recv_sem=recv,
            device_id={"dp": device},
            device_id_type=MESH,
        )

    buffers = {
        "wide": (wa, ra, xa, ua, na),
        "tall": (wb, rb, xb, ub, nb),
        "part": (wc, rc, xc, uc, nc),
    }
    lefts = {"qkv": fa1, "out": fo, "up": fa2, "down": fg}
    rights = {"qkv": fdj, "out": fdhr, "up": fdu, "down": fdm}
    steps = []
    turned = None
    ahead = 0
    total = len(plan)
    for number, (name, part, _, columns) in enumerate(plan):
        if name == "small":
            continue
        if name == "down":
            while ahead < depth:
                steps.append((number, name, True, ahead, None, 0))
                ahead += 1
            steps += [(number, name, False, block, part, columns) for block in range(depth)]
            continue
        if name != turned:
            steps.append((number, name, True, 0, None, 0))
            turned = name
        steps.append((number, name, False, 0, part, columns))
        for _ in range(2 if number else 1):
            if ahead < depth:
                steps.append((number, "down", True, ahead, None, 0))
                ahead += 1

    def loads(index):
        _, name, turn, block, part, columns = steps[index]
        slot = index % 2
        if turn:
            source = lefts[name].at[:, :, block * width : (block + 1) * width]
            return pltpu.make_async_copy(source, left.at[slot], lsem.at[slot])
        return pltpu.make_async_copy(
            rights[name].at[:, :, part * columns : (part + 1) * columns],
            right.at[slot, :, :, 0:columns],
            lsem.at[slot],
        )

    def start_loads(index):
        if index < len(steps):
            loads(index).start()

    start_loads(0)

    barrier = pltpu.get_barrier_semaphore()

    def greet(device):
        pl.semaphore_signal(barrier, inc=1, device_id={"dp": device}, device_id_type=MESH)

    greet(partner)
    greet(beside)

    @pl.when(level < 3)
    def _():
        greet(above)

    @pl.when(level > 0)
    def _():
        greet(below)

    pl.semaphore_wait(barrier, 2 + (level + 2) // 3 + (5 - level) // 3)

    targets = {"qkv": gqkv, "out": gout, "up": gup, "down": gdown}
    views = []
    previous = {}
    order = {}
    last_of = {number: True for number in range(total)}
    for number, (name, part, line_first, columns) in enumerate(plan):
        kind = kind_of(plan[number])
        if kind == "small":
            views.append((small, rs, xs, us, ns, gsmall))
            previous[number] = None
            continue
        w, r, x, u, n = buffers[kind]
        order.setdefault(kind, []).append(number)
        index = len(order[kind]) - 1
        slots_of = w.shape[0]
        previous[number] = order[kind][index - slots_of] if index >= slots_of else None
        if previous[number] is not None:
            last_of[previous[number]] = False
        place = targets[name].at[0, :, part * columns : (part + 1) * columns]
        along = sum(plan[other][2] for other in order[kind][:index])
        if line_first:
            further = (xl.at[along], ul.at[along], nl.at[along], place)
        else:
            further = (x.at[index - along], u.at[index - along], n.at[index - along], place)
        views.append((w.at[index % slots_of], r.at[index]) + further)

    def pair_copy(number):
        w, r = views[number][:2]
        return remote(
            w.at[:, :, 1 - core], r, pair_send.at[number], pair_recv.at[number], partner
        )

    def side_copy(number):
        r, x = views[number][1:3]
        source = r.at[level, 1 - side] if plan[number][2] else r.at[:, 1 - side]
        return remote(source, x, side_send.at[number], side_recv.at[number], beside)

    def along_line(number):
        r, x = views[number][1:3]
        return r if plan[number][2] else x

    def up_copy(number, goal, source=None):
        u = views[number][3]
        return remote(
            u.at[goal - 1] if source is None else source,
            u.at[goal - 1],
            up_send.at[number, goal - 1],
            up_recv.at[number, goal - 1],
            above,
        )

    def down_copy(number, goal, source=None):
        n = views[number][4]
        return remote(
            n.at[goal] if source is None else source,
            n.at[goal],
            down_send.at[number, goal],
            down_recv.at[number, goal],
            below,
        )

    def start_line(number):
        base = along_line(number)

        @pl.when(level == 0)
        def _():
            for goal in (3, 2, 1):
                up_copy(number, goal, base.at[goal]).start()

        @pl.when(level == 3)
        def _():
            for goal in (0, 1, 2):
                down_copy(number, goal, base.at[goal]).start()

    across = [number for number in range(total) if not plan[number][2]]
    x_before = {number: across[i - 1] if i else None for i, number in enumerate(across)}
    position = {"step": 0}
    slots, length = left.shape[1:3]

    def turn_block(slot, target):
        def body(t, carry):
            tokens = pl.ds(pl.multiple_of(t * length, length), length)
            target[:, tokens] = left[slot, t].T
            return carry

        lax.fori_loop(0, slots, body, 0)

    def right_part(slot, lanes):
        part = right[slot, :, :, lanes]
        return part.reshape(slots * length, part.shape[2])

    def multiply(slot, w, columns):
        def tile(t, carry):
            lanes = pl.ds(pl.multiple_of(t * narrow, narrow), narrow)
            product = dot(lt[...], right_part(slot, lanes))
            w[:, :, :, :, lanes] = product.reshape(w.shape[:4] + (narrow,))
            return carry

        lax.fori_loop(0, columns // narrow, tile, 0)


    def produce(number):
        name = plan[number][0]
        sent = False
        if name != "small":
            if previous[number] is not None:
                pair_copy(previous[number]).wait_send()
            w = views[number][0]
            while position["step"] < len(steps) and steps[position["step"]][0] == number:
                index = position["step"]
                position["step"] += 1
                _, source, turn, block, _, columns = steps[index]
                start_loads(index + 1)
                loads(index).wait()
                if turn:
                    if source == "down" and name != "down" and not sent:
                        pair_copy(number).start()
                        sent = True
                    turn_block(index % 2, gt.at[block] if source == "down" else lt)
                elif source == "down":
                    w[block] = dot(gt[block], right_part(index % 2, slice(0, narrow))).reshape(
                        w.shape[1:]
                    )
                else:
                    multiply(index % 2, w, columns)
        if not sent:
            pair_copy(number).start()

    def stage_pair(number):
        w, r = views[number][:2]
        pair_copy(number).wait_recv()

        def add(z, carry):
            for s in range(2):
                r[z, s] += w[z, s, core]
            return carry

        lax.fori_loop(0, 4, add, 0)
        if plan[number][2]:
            start_line(number)
        else:
            if fifo and x_before[number] is not None:
                side_copy(x_before[number]).wait_send()
            side_copy(number).start()

    def stage_side(number):
        if plan[number][2]:
            return
        r, x = views[number][1:3]
        side_copy(number).wait_recv()

        def add(z, carry):
            x[z] += r[z, side]
            return carry

        lax.fori_loop(0, 4, add, 0)
        start_line(number)

    def stage_up(number, height):
        u = views[number][3]
        base = along_line(number)

        @pl.when(level == height)
        def _():
            for goal in range(3, height - 1, -1):
                up_copy(number, goal).wait_recv()
                if goal > height:
                    u[goal - 1] += base[goal]
                    up_copy(number, goal).start()

    def stage_down(number, height):
        n = views[number][4]
        base = along_line(number)

        @pl.when(level == height)
        def _():
            for goal in range(0, height + 1):
                down_copy(number, goal).wait_recv()
                if goal < height:
                    n[goal] += base[goal]
                    down_copy(number, goal).start()

    def stage_sum(number):
        u, n, place = views[number][3:]
        base = along_line(number)

        @pl.when(level > 0)
        def _():
            base[level] += u[level - 1]

        @pl.when(level < 3)
        def _():
            base[level] += n[level]

        if plan[number][2]:
            side_copy(number).start()
        else:
            place[...] = base[level]

    def stage_last(number):
        if plan[number][2]:
            r, x = views[number][1:3]
            side_copy(number).wait_recv()
            views[number][5][...] = r[level, side] + x[...]

    def at(stage, number, *more):
        if 0 <= number < total:
            stage(number, *more)

    for moment in range(total + side_lag + 3 * hop + 1):
        at(produce, moment)
        at(stage_pair, moment - 1)
        at(stage_side, moment - side_lag)
        for height in range(4):
            if height > 0:
                at(stage_up, moment - side_lag - hop * height, height)
            if height < 3:
                at(stage_down, moment - side_lag - hop * (3 - height), height)
        at(stage_sum, moment - side_lag - 3 * hop)
        at(stage_last, moment - side_lag - 3 * hop - 1)
    for number in range(total):
        if last_of[number]:
            pair_copy(number).wait_send()
        if not fifo or number not in x_before.values():
            side_copy(number).wait_send()
        for goal in (1, 2, 3):

            @pl.when(goal > level)
            def _():
                up_copy(number, goal).wait_send()

        for goal in (0, 1, 2):

            @pl.when(goal < level)
            def _():
                down_copy(number, goal).wait_send()


def kind_of(entry):
    name, _, _, columns = entry
    if name in ("small", "down"):
        return "small" if name == "small" else "tall"
    return "part" if columns == 256 else "wide"


def summed_in_kernel(factors, small, packed):
    fa1, fdj, fo, fdhr, fa2, fdu, fg, fdm = factors
    slots, length, width = fa1.shape
    inner = fg.shape[2]
    owners = 16
    depth = inner // width
    narrow = 256
    a_rows, b_rows = width // owners, inner // owners
    plan = [
        ("qkv", 0, False, width),
        ("qkv", 1, True, width),
        ("down", 0, False, narrow),
        ("small", 0, False, 0),
        ("qkv", 2, False, width),
        ("down", 1, False, narrow),
        ("out", 0, True, width),
        ("up", 0, False, width),
        ("up", 1, False, width),
        ("up", 2, False, width),
        ("up", 9, False, narrow),
        ("up", 10, False, narrow),
        ("up", 11, False, narrow),
        ("down", 2, False, narrow),
    ]
    lags = (3, 2, True)
    total = len(plan)
    s_block = small.shape[3:]
    vmem = pl.BlockSpec(memory_space=pltpu.VMEM)
    anywhere = pl.BlockSpec(memory_space=pl.ANY)

    def of_kind(kind, slots_of, block):
        mine = [entry for entry in plan if kind_of(entry) == kind]
        across = sum(not entry[2] for entry in mine)
        leads = ((slots_of, 4, 2, 2), (len(mine), 4, 2), (across, 4), (across, 3), (across, 3))
        return [pltpu.VMEM(lead + block, F32) for lead in leads]

    line_count = sum(line_first for _, _, line_first, _ in plan)
    a_block = (a_rows, width)
    *grads, small_grad = pl.pallas_call(
        functools.partial(gradients_kernel, (width, narrow, depth), plan, lags),
        out_shape=(
            jax.ShapeDtypeStruct((1, a_rows, 3 * width), F32),
            jax.ShapeDtypeStruct((1, a_rows, width), F32),
            jax.ShapeDtypeStruct((1, a_rows, inner), F32),
            jax.ShapeDtypeStruct((1, b_rows, width), F32),
            jax.ShapeDtypeStruct(s_block, F32),
        ),
        in_specs=[anywhere] * 8 + [vmem],
        out_specs=(vmem,) * 5,
        scratch_shapes=[
            pltpu.VMEM((2, slots, length, width), BF),
            pltpu.VMEM((2, slots, length, width), BF),
            pltpu.VMEM((width, slots * length), BF),
            pltpu.VMEM((depth, width, slots * length), BF),
        ]
        + of_kind("wide", 2, a_block)
        + of_kind("tall", 1, (b_rows, narrow))
        + of_kind("part", 2, (a_rows, narrow))
        + [pltpu.VMEM(lead + s_block, F32) for lead in ((4, 2), (4,), (3,), (3,))]
        + [
            pltpu.VMEM((line_count,) + a_block, F32),
            pltpu.VMEM((line_count, 3, 2) + a_block, F32),
            pltpu.VMEM((line_count, 3, 2) + a_block, F32),
        ]
        + [pltpu.SemaphoreType.DMA((2,))]
        + [pltpu.SemaphoreType.DMA((total,))] * 4
        + [pltpu.SemaphoreType.DMA((total, 3))] * 4,
        compiler_params=pltpu.CompilerParams(
            collective_id=1, has_side_effects=True, vmem_limit_bytes=62 << 20
        ),
    )(*factors, small)
    return tuple(grads) + (small_grad.reshape(1, -1)[:, :packed],)


def reduced(factors, small_grads, size):
    if lax.axis_size("dp") == 16:
        return summed_in_kernel(factors, small_grads, size // 16)
    return summed_by_parts(factors, small_grads)


def per_device(
    embeddings, cotangent, seg_ids, thought_pos, w_qkv, w_out, w_up, w_down, small_params
):
    section_out, *factors, small_grads = layers(
        embeddings, cotangent, seg_ids, thought_pos, w_qkv, w_out, w_up, w_down, small_params
    )
    return (section_out,) + tuple(reduced(factors, small_grads, small_params.size))


def solution(mesh):
    return jax.shard_map(
        per_device,
        mesh=mesh,
        in_specs=(
            P("dp", None, None),
            P("dp", None, None),
            P("dp", None),
            P("dp", None),
            P("pipe", None, None),
            P("pipe", None, None),
            P("pipe", None, None),
            P("pipe", None, None),
            P("pipe", None),
        ),
        out_specs=(
            P("pipe", "dp", None, None),
            P("pipe", "dp", None),
            P("pipe", "dp", None),
            P("pipe", "dp", None),
            P("pipe", "dp", None),
            P("pipe", "dp"),
        ),
        check_vma=False,
    )
```

```python
import functools

import jax
import jax.numpy as jnp
from jax import lax
from jax.experimental import pallas as pl
from jax.experimental.pallas import tpu as pltpu
from jax.sharding import PartitionSpec as P

HEADS = 12
BF = jnp.bfloat16
F32 = jnp.float32
MESH = pl.DeviceIdType.MESH
EPSILON = 1e-05
MASKED = -1000000000.0
NO_CAP = 3e38
LAT = 16
G1, B1, BQ, BV, BO, G2, B2, BU = 0, 1, 2, 3, 4, 5, 6, 7


def dot(a, b):
    return lax.dot_general(a, b, (((1,), (0,)), ((), ())), preferred_element_type=F32)


def dot_nt(a, b):
    return lax.dot_general(a, b, (((1,), (1,)), ((), ())), preferred_element_type=F32)


def dot_tn(a, b):
    return lax.dot_general(a, b, (((0,), (0,)), ((), ())), preferred_element_type=F32)


def exact_dot(a, b):
    return lax.dot_general(
        a,
        b,
        (((1,), (0,)), ((), ())),
        precision=lax.Precision.HIGHEST,
        preferred_element_type=F32,
    )


def normalized(values):
    centred = values - jnp.mean(values, -1, keepdims=True)
    spread = jnp.mean(centred * centred, -1, keepdims=True)
    scale = lax.rsqrt(spread + EPSILON)
    return centred * scale, scale


def norm_back(hat, scale, grad):
    along = jnp.mean(grad * hat, -1, keepdims=True)
    return scale * (grad - jnp.mean(grad, -1, keepdims=True) - hat * along)


def gelu_both(u):
    c = 0.7978845608028654
    square = u * u
    t = jnp.tanh(c * u * (1.0 + 0.044715 * square))
    half = 0.5 + 0.5 * t
    slope = half + (0.5 * c) * u * (1.0 - t * t) * (1.0 + (3 * 0.044715) * square)
    return u * half, slope


def softmax(scores, axis=-1):
    e = jnp.exp(scores - jnp.max(scores, axis, keepdims=True))
    return e * (1.0 / jnp.sum(e, axis, keepdims=True))


def layers_kernel(
    sizes,
    emb,
    cot,
    seg,
    tpos,
    wqkv_h,
    wout_h,
    wup_h,
    wdown_h,
    small,
    sec,
    fa1,
    fdj,
    fo,
    fdhr,
    fa2,
    fdu,
    fg,
    fdm,
    sg,
    sums,
    joint,
    stat,
    wqkv,
    wout,
    wup,
    wdown,
    xin,
    yb,
    dyb,
    jn,
    pr,
    hm,
    slope,
    bent,
    a1,
    ob,
    a2,
    gb,
    dm,
    dub,
    dhr,
    djb,
    da,
    dob,
    dmt,
    dat,
    djt,
    cap,
    lat,
    thg,
    lx,
    lq,
    lp,
    lh,
    la2,
    lo,
    lg,
    lslope,
    wsem,
    osem,
    ysend,
    yrecv,
    gsend,
    grecv,
    lsend,
    lrecv,
    tsend,
    trecv,
):
    rows, length, width, inner, thoughts = sizes
    blocks = inner // width
    bd = BU + blocks
    pairs = HEADS // 2
    me = lax.axis_index("pipe")
    other = 1 - me

    weights = [
        pltpu.make_async_copy(source.at[0], target, wsem.at[number])
        for number, (source, target) in enumerate(
            ((wqkv_h, wqkv), (wout_h, wout), (wup_h, wup), (wdown_h, wdown))
        )
    ]
    for copy in weights:
        copy.start()
    barrier = pltpu.get_barrier_semaphore()
    pl.semaphore_signal(barrier, inc=1, device_id={"pipe": other}, device_id_type=MESH)
    pl.semaphore_wait(barrier, 1)
    sums[...] = jnp.zeros_like(sums)
    joint[:, 0:width] = small[:, BQ * width : (BQ + 1) * width]
    joint[:, width : 2 * width] = jnp.zeros((1, width), F32)
    joint[:, 2 * width : 3 * width] = small[:, BV * width : (BV + 1) * width]

    def remote(source, target, send, recv):
        return pltpu.make_async_remote_copy(
            src_ref=source,
            dst_ref=target,
            send_sem=send,
            recv_sem=recv,
            device_id={"pipe": other},
            device_id_type=MESH,
        )

    def send_y(k):
        return remote(yb.at[k], xin.at[k], ysend.at[k], yrecv.at[k])

    def send_grad(k):
        return remote(yb.at[k], dyb.at[k], gsend.at[k], grecv.at[k])

    def send_lat(r):
        return remote(lat.at[r], lat.at[r], lsend.at[r], lrecv.at[r])

    def send_thoughts(r):
        return remote(thg.at[r], thg.at[r], tsend.at[r], trecv.at[r])

    def started(source, target, number):
        copy = pltpu.make_async_copy(source, target, osem.at[number])
        copy.start()
        return copy

    def settle(pending, number, source, target):
        @pl.when(pending)
        def _():
            pltpu.make_async_copy(source, target.at[0], osem.at[number]).wait()

    def finish(copies):
        for copy in copies:
            copy.wait()

    def each_chunk(step, count):
        def body(i, carry):
            step(pl.ds(pl.multiple_of(i * count, count), count), i * count)
            return carry

        lax.fori_loop(0, length // count, body, 0)

    def loop(count, step):
        def body(i, carry):
            step(i)
            return carry

        lax.fori_loop(0, count, body, 0, unroll=2)

    def add_columns(number, values):
        sums[number] += jnp.sum(values.astype(F32).reshape(-1, 8, width), 0)

    def row(number):
        return small[:, group(number)]

    def group(number):
        return slice(number * width, (number + 1) * width)

    lane = lax.broadcasted_iota(jnp.int32, (1, 128), 1)
    low = lane < 64
    halves = (jnp.where(low, 1.0, 0.0).astype(BF), jnp.where(low, 0.0, 1.0).astype(BF))

    def first_length(r):
        segment = seg[pl.ds(r, 1), :]
        return jnp.sum(jnp.where(segment == 0, 1.0, 0.0), -1, keepdims=True).astype(jnp.int32)

    def set_cap(r):
        first = first_length(r)
        query = lax.broadcasted_iota(jnp.int32, (length, length), 0)
        key = lax.broadcasted_iota(jnp.int32, (length, length), 1)
        lowest = jnp.where(query >= first, first, 0)
        cap[...] = jnp.where((key <= query) & (key >= lowest), NO_CAP, MASKED)

    def positions(r, shift, axis=0):
        shape = (LAT, 1) if axis == 0 else (1, LAT)
        number = lax.broadcasted_iota(jnp.int32, shape, axis)
        result = jnp.full(shape, -1, jnp.int32)
        for j in range(thoughts):
            result = jnp.where(number == j, tpos[r, j] - shift, result)
        return result

    def selector_turned(r, shift):
        place = positions(r, shift, 1)
        return jnp.where(lax.broadcasted_iota(jnp.int32, (length, LAT), 0) == place, 1.0, 0.0)

    def selector(place):
        return jnp.where(lax.broadcasted_iota(jnp.int32, (LAT, length), 1) == place, 1.0, 0.0)

    def unmarked(r, start):
        place = lax.broadcasted_iota(jnp.int32, (32, 1), 0) + start
        keep = jnp.ones((32, 1), F32)
        for j in range(thoughts):
            keep = jnp.where(place == tpos[r, j], 0.0, keep)
        return keep

    def head_lanes(part, hp):
        start = part * width + hp * 128
        if isinstance(hp, int):
            return slice(start, start + 128)
        return pl.ds(pl.multiple_of(start, 128), 128)

    def norm_rows(x, target, k, which, gain, shift, more=None):
        def step(part, _):
            values = x[part, :]
            center = jnp.mean(values, -1, keepdims=True)
            centred = values - center
            scale = lax.rsqrt(jnp.mean(centred * centred, -1, keepdims=True) + EPSILON)
            stat[k, 2 * which, part, :] = center
            stat[k, 2 * which + 1, part, :] = scale
            target[part, :] = (centred * scale * row(gain) + row(shift)).astype(BF)
            if more is not None:
                more(part, values)

        each_chunk(step, 128)

    def norm_rows_back(x, part, k, which, gain, shift):
        scale = stat[k, 2 * which + 1, part, :]
        hat = (x[part, :] - stat[k, 2 * which, part, :]) * scale
        grad = da[part, :]
        add_columns(gain, grad * hat)
        add_columns(shift, grad)
        return norm_back(hat, scale, grad * row(gain))

    def forward(k, x, y, pending, first=None):
        def need(number):
            if first is not None:

                @pl.when(first)
                def _():
                    weights[number].wait()

        settle(pending, 0, a1, fa1)
        norm_rows(x, a1, k, 0, G1, B1)
        started(a1, fa1.at[k], 0)
        need(0)
        settle(pending, 1, ob, fo)

        for part in range(3):
            joined = dot(a1[...], wqkv[:, group(part)]) + joint[:, group(part)]
            jn[k, :, group(part)] = joined.astype(BF)
        for hp in range(pairs):
            q = jn[k, :, head_lanes(0, hp)]
            key = jn[k, :, head_lanes(1, hp)]
            value = jn[k, :, head_lanes(2, hp)]
            out = []
            for h in range(2):
                scores = dot_nt(q * (halves[h] * 0.125), key)
                chance = softmax(jnp.minimum(scores, cap[...])).astype(BF)
                pr[k, 2 * hp + h] = chance
                out.append(dot(chance, value))
            ob[:, head_lanes(0, hp)] = jnp.where(low, out[0], out[1]).astype(BF)
        started(ob, fo.at[k], 1)
        need(1)
        settle(pending, 2, a2, fa2)
        hm[k] = x[...] + dot(ob[...], wout[...]) + row(BO)

        def begin(part, values):
            y[part, :] = values + row(bd)

        norm_rows(hm.at[k], a2, k, 1, G2, B2, begin)
        started(a2, fa2.at[k], 2)
        need(2)
        need(3)
        settle(pending, 3, gb, fg)

        for c in range(blocks):
            part = group(c)
            g, d = gelu_both(dot(a2[...], wup[:, part]) + row(BU + c))
            gb[:, part] = g.astype(BF)
            bent[:, part] = d.astype(BF)
            y[...] += dot(gb[:, part], wdown[part, :])
        started(gb, fg.at[k], 3)

    def turn_slopes(k):
        for c in range(blocks):
            slope[k, group(c), :] = bent[:, group(c)].T

    def backward(k, x, dy, dx, pending):
        def step(part, _):
            branch = dy[part, :].astype(BF)
            dm[part, :] = branch
            add_columns(bd, branch)

        settle(pending, 4, dm, fdm)
        each_chunk(step, 128)
        started(dm, fdm.at[k], 4)
        dmt[...] = dm[...].T
        dat[...] = jnp.zeros_like(dat)
        settle(pending, 5, dub, fdu)

        def mlp(c):
            part = pl.ds(pl.multiple_of(c * width, width), width)
            grad = (dot(wdown[part, :], dmt[...]) * slope[k, part, :]).astype(BF)
            dat[...] += dot(wup[:, part], grad)
            turned = grad.T
            dub[:, part] = turned
            add_columns(BU + c, turned)

        loop(blocks, mlp)
        da[...] = dat[...].T
        started(dub, fdu.at[k], 5)
        settle(pending, 6, dhr, fdhr)

        def step_two(part, _):
            middle = dy[part, :] + norm_rows_back(hm.at[k], part, k, 1, G2, B2)
            dy[part, :] = middle
            branch = middle.astype(BF)
            dhr[part, :] = branch
            add_columns(BO, branch)

        each_chunk(step_two, 128)
        started(dhr, fdhr.at[k], 6)
        dmt[...] = dhr[...].T
        dob[...] = dot(wout[...], dmt[...]).astype(BF).T
        settle(pending, 7, djb, fdj)

        def heads(hp):
            q = jn[k, :, head_lanes(0, hp)]
            key = jn[k, :, head_lanes(1, hp)]
            value = jn[k, :, head_lanes(2, hp)]
            grad_out = dob[:, head_lanes(0, hp)]
            dq, dk, dv = [], [], []
            for h in range(2):
                chance = pr[k, 2 * hp + h]
                chance_full = chance.astype(F32)
                inner_part = chance_full * dot_nt(grad_out * halves[h], value)
                total = jnp.sum(inner_part, -1, keepdims=True)
                grad_scores = (inner_part - chance_full * total).astype(BF)
                dq.append(dot(grad_scores, key))
                dk.append(dot_tn(grad_scores, q))
                dv.append(dot_tn(chance, grad_out))
            djb[:, head_lanes(0, hp)] = (jnp.where(low, dq[0], dq[1]) * 0.125).astype(BF)
            djb[:, head_lanes(1, hp)] = (jnp.where(low, dk[0], dk[1]) * 0.125).astype(BF)
            djb[:, head_lanes(2, hp)] = jnp.where(low, dv[0], dv[1]).astype(BF)

        loop(pairs, heads)
        started(djb, fdj.at[k], 7)
        into_input(k, x, dy, dx)

    def into_input(k, x, middle, dx):
        djt[...] = djb[...].T
        da[...] = dot(wqkv[...], djt[...]).T

        def step(part, _):
            add_columns(BQ, djb[part, group(0)])
            add_columns(BV, djb[part, group(2)])
            dx[part, :] = middle[part, :] + norm_rows_back(x, part, k, 0, G1, B1)

        each_chunk(step, 128)

    def forward_latent(r):
        x = xin.at[r]
        norm_rows(x, a1, r, 0, G1, B1)
        copies = [started(a1, fa1.at[r], 0)]
        jn[r, :, group(1)] = dot(a1[...], wqkv[:, group(1)]).astype(BF)
        jn[r, :, group(2)] = (dot(a1[...], wqkv[:, group(2)]) + row(BV)).astype(BF)
        place = positions(r, 1)
        chosen = exact_dot(selector(place), x[...])
        lx[r] = chosen
        hat, _ = normalized(chosen)
        normed = (hat * row(G1) + row(B1)).astype(BF)
        lq[r] = (dot(normed, wqkv[:, group(0)]) + row(BQ)).astype(BF)
        first = first_length(r)
        key_place = lax.broadcasted_iota(jnp.int32, (LAT, length), 1)
        lowest = jnp.where(place >= first, first, 0)
        limit = jnp.where((key_place <= place) & (key_place >= lowest), NO_CAP, MASKED)

        def heads(hp):
            q = lq[r, :, head_lanes(0, hp)]
            key = jn[r, :, head_lanes(1, hp)]
            value = jn[r, :, head_lanes(2, hp)]
            out = []
            for h in range(2):
                scores = dot_nt(q * (halves[h] * 0.125), key)
                chance = softmax(jnp.minimum(scores, limit)).astype(BF)
                lp[r, 2 * hp + h] = chance
                out.append(dot(chance, value))
            lo[r, :, head_lanes(0, hp)] = jnp.where(low, out[0], out[1]).astype(BF)

        for hp in range(pairs):
            heads(hp)
        middle = chosen + dot(lo[r], wout[...]) + row(BO)
        lh[r] = middle
        hat, _ = normalized(middle)
        la2[r] = (hat * row(G2) + row(B2)).astype(BF)
        lat[r] = middle + row(bd)

        def mlp(c):
            part = group(c)
            u = dot(la2[r], wup[:, part]) + row(BU + c)
            g, d = gelu_both(u)
            lg[r, :, part] = g.astype(BF)
            lslope[r, :, part] = d.astype(BF)
            lat[r] += dot(lg[r, :, part], wdown[part, :])

        for c in range(blocks):
            mlp(c)
        return copies

    def backward_latent(r, dx):
        grad_result = thg[r]
        branch = grad_result.astype(BF)
        top = slice(0, LAT)
        add_columns(bd, branch)
        dm[top, :] = branch
        a2[top, :] = la2[r]
        ob[top, :] = lo[r]
        gb[top, :] = lg[r]
        copies = [
            started(dm, fdm.at[r], 4),
            started(a2, fa2.at[r], 2),
            started(ob, fo.at[r], 1),
            started(gb, fg.at[r], 3),
        ]
        da[top, :] = jnp.zeros((LAT, width), F32)

        def mlp(c):
            part = group(c)
            grad = (dot_nt(dm[top, :], wdown[part, :]) * lslope[r, :, part]).astype(BF)
            dub[top, part] = grad
            add_columns(BU + c, grad)
            da[top, :] += dot_nt(grad, wup[:, part])

        for c in range(blocks):
            mlp(c)
        copies.append(started(dub, fdu.at[r], 5))
        hat, scale = normalized(lh[r])
        grad = da[top, :]
        add_columns(G2, grad * hat)
        add_columns(B2, grad)
        middle = grad_result + norm_back(hat, scale, grad * row(G2))
        rounded = middle.astype(BF)
        dhr[top, :] = rounded
        add_columns(BO, rounded)
        copies.append(started(dhr, fdhr.at[r], 6))
        spread = selector_turned(r, 1)
        dyb[r] = exact_dot(spread, middle)
        place = positions(r, 1, 1)
        first = first_length(r)
        key_place = lax.broadcasted_iota(jnp.int32, (length, LAT), 0)
        lowest = jnp.where(place >= first, first, 0)
        limit = jnp.where((key_place <= place) & (key_place >= lowest), NO_CAP, MASKED)
        dob[top, :] = dot_nt(rounded, wout[...]).astype(BF)

        def heads(hp):
            q = lq[r, :, head_lanes(0, hp)]
            key = jn[r, :, head_lanes(1, hp)]
            value = jn[r, :, head_lanes(2, hp)]
            grad_out = dob[top, head_lanes(0, hp)]
            dq, dk, dv = [], [], []
            for h in range(2):
                grad_masked = grad_out * halves[h]
                chance = lp[r, 2 * hp + h].astype(F32)
                inner_part = chance * dot_nt(grad_masked, value)
                total = jnp.sum(inner_part, -1, keepdims=True)
                dq.append(dot((inner_part - chance * total).astype(BF), key))
                scores = dot_nt(key, q * (halves[h] * 0.125))
                chance = softmax(jnp.minimum(scores, limit), 0)
                inner_part = chance * dot_nt(value, grad_masked)
                total = jnp.sum(inner_part, 0, keepdims=True)
                dk.append(dot((inner_part - chance * total).astype(BF), q))
                dv.append(dot(chance.astype(BF), grad_out))
            grad_q = (jnp.where(low, dq[0], dq[1]) * 0.125).astype(BF)
            djb[:, head_lanes(0, hp)] = dot(spread.astype(BF), grad_q).astype(BF)
            djb[:, head_lanes(1, hp)] = (jnp.where(low, dk[0], dk[1]) * 0.125).astype(BF)
            djb[:, head_lanes(2, hp)] = jnp.where(low, dv[0], dv[1]).astype(BF)

        for hp in range(pairs):
            heads(hp)
        copies.append(started(djb, fdj.at[r], 7))
        into_input(r, xin.at[r], dyb.at[r], dx)
        return copies

    staged = (
        (a1, fa1), (ob, fo), (a2, fa2), (gb, fg), (dm, fdm), (dub, fdu), (dhr, fdhr), (djb, fdj)
    )

    def settle_all(count, first=0):
        for number in range(first, first + count):
            source, target = staged[number]
            pltpu.make_async_copy(source, target.at[0], osem.at[number]).wait()

    @pl.when(me == 0)
    def _():
        def forward_step(k, carry):
            r = lax.rem(k, rows)
            set_cap(r)

            @pl.when(k < rows)
            def _():
                xin[k] = emb[r].astype(F32)

            @pl.when(k >= rows)
            def _():
                send_lat(r).wait_recv()
                xin[k] = exact_dot(selector_turned(r, 0), lat[r])

                def step(part, start):
                    xin[k, part, :] += emb[r, part, :].astype(F32) * unmarked(r, start)

                each_chunk(step, 32)

            forward(k, xin.at[k], yb.at[k], k > 0, first=k == 0)

            @pl.when(k > 0)
            def _():
                send_y(k - 1).wait_send()

            send_y(k).start()
            turn_slopes(k)
            return carry

        lax.fori_loop(0, 2 * rows, forward_step, 0)
        send_y(2 * rows - 1).wait_send()
        settle_all(4)

        def backward_step(i, carry):
            k = lax.rem(i + rows, 2 * rows)
            r = lax.rem(i, rows)
            send_grad(k).wait_recv()
            backward(k, xin.at[k], dyb.at[k], yb.at[k], i > 0)

            @pl.when(i < rows)
            def _():
                thg[r] = exact_dot(selector(positions(r, 0)), yb[k])
                send_thoughts(r).start()

            @pl.when(i >= rows)
            def _():
                def step(part, start):
                    yb[k, part, :] += yb[rows + r, part, :] * unmarked(r, start)

                each_chunk(step, 32)
                started(yb.at[k], sec.at[0, r], 8).wait()

            return carry

        lax.fori_loop(0, 2 * rows, backward_step, 0)
        settle_all(4, 4)

        def drain(r, carry):
            send_thoughts(r).wait_send()
            return carry

        lax.fori_loop(0, rows, drain, 0)

    @pl.when(me == 1)
    def _():
        finish(weights)

        def latent_step(r, carry):
            send_y(r).wait_recv()
            copies = forward_latent(r)
            send_lat(r).start()
            finish(copies)
            return carry

        lax.fori_loop(0, rows, latent_step, 0)

        def language_step(r, carry):
            k = rows + r
            set_cap(r)
            send_y(k).wait_recv()
            forward(k, xin.at[k], dyb.at[k], r > 0)
            result = started(dyb.at[k], sec.at[0, r], 8)
            turn_slopes(k)
            dyb[r] = cot[r].astype(F32)
            backward(k, xin.at[k], dyb.at[r], yb.at[k], r > 0)
            send_grad(k).start()
            result.wait()
            return carry

        lax.fori_loop(0, rows, language_step, 0)
        settle_all(8)
        for buffer in (dm, a2, ob, gb, dub, dhr):
            buffer[...] = jnp.zeros_like(buffer)

        def latent_back_step(r, carry):
            send_thoughts(r).wait_recv()
            copies = backward_latent(r, yb.at[r])
            send_grad(r).start()
            finish(copies)
            return carry

        lax.fori_loop(0, rows, latent_back_step, 0)

        def drain(r, carry):
            send_lat(r).wait_send()
            send_grad(r).wait_send()
            send_grad(rows + r).wait_send()
            return carry

        lax.fori_loop(0, rows, drain, 0)

    sg[...] = jnp.sum(sums[...], 1)


def layers(emb, cot, seg, tpos, w_qkv, w_out, w_up, w_down, small):
    rows, length, width = emb.shape
    inner = w_up.shape[2]
    thoughts = tpos.shape[1]
    slots = 2 * rows
    packed = small.shape[1] // width
    vmem = pl.BlockSpec(memory_space=pltpu.VMEM)
    anywhere = pl.BlockSpec(memory_space=pl.ANY)
    smem = pl.BlockSpec(memory_space=pltpu.SMEM)

    def factor(columns):
        return jax.ShapeDtypeStruct((slots, length, columns), BF)

    def block(columns, kind=BF):
        return pltpu.VMEM((length, columns), kind)

    def few(columns, kind=BF):
        return pltpu.VMEM((rows, LAT, columns), kind)

    sizes = (rows, length, width, inner, thoughts)
    return pl.pallas_call(
        functools.partial(layers_kernel, sizes),
        out_shape=(
            jax.ShapeDtypeStruct((1, rows, length, width), F32),
            factor(width),
            factor(3 * width),
            factor(width),
            factor(width),
            factor(width),
            factor(inner),
            factor(inner),
            factor(width),
            jax.ShapeDtypeStruct((packed, width), F32),
        ),
        in_specs=[vmem, vmem, vmem, smem] + [anywhere] * 4 + [vmem],
        out_specs=(anywhere,) * 9 + (vmem,),
        scratch_shapes=[
            pltpu.VMEM((packed, 8, width), F32),
            pltpu.VMEM((1, 3 * width), F32),
            pltpu.VMEM((slots, 4, length, 1), F32),
            pltpu.VMEM((width, 3 * width), BF),
            pltpu.VMEM((width, width), BF),
            pltpu.VMEM((width, inner), BF),
            pltpu.VMEM((inner, width), BF),
            pltpu.VMEM((slots, length, width), F32),
            pltpu.VMEM((slots, length, width), F32),
            pltpu.VMEM((slots, length, width), F32),
            pltpu.VMEM((slots, length, 3 * width), BF),
            pltpu.VMEM((slots, HEADS, length, length), BF),
            pltpu.VMEM((slots, length, width), F32),
            pltpu.VMEM((slots, inner, length), BF),
            block(inner),
            block(width),
            block(width),
            block(width),
            block(inner),
            block(width),
            block(inner),
            block(width),
            block(3 * width),
            block(width, F32),
            block(width),
            pltpu.VMEM((width, length), BF),
            pltpu.VMEM((width, length), F32),
            pltpu.VMEM((3 * width, length), BF),
            block(length, F32),
            few(width, F32),
            few(width, F32),
            few(width, F32),
            few(width),
            pltpu.VMEM((rows, HEADS, LAT, length), BF),
            few(width, F32),
            few(width),
            few(width),
            few(inner),
            few(inner),
            pltpu.SemaphoreType.DMA((4,)),
            pltpu.SemaphoreType.DMA((9,)),
        ]
        + [pltpu.SemaphoreType.DMA((slots,))] * 4
        + [pltpu.SemaphoreType.DMA((rows,))] * 4,
        compiler_params=pltpu.CompilerParams(
            collective_id=0, has_side_effects=True, vmem_limit_bytes=62 << 20
        ),
    )(emb, cot, seg, tpos, w_qkv, w_out, w_up, w_down, small)


def summed_by_parts(factors, small_grads):
    fa1, fdj, fo, fdhr, fa2, fdu, fg, fdm = factors

    def product(left, right):
        whole = jnp.einsum("ktm,ktn->mn", left, right, preferred_element_type=F32)
        return lax.psum_scatter(whole[None], "dp", scatter_dimension=1, tiled=True)

    small = lax.psum_scatter(
        small_grads.reshape(1, -1), "dp", scatter_dimension=1, tiled=True
    )
    return product(fa1, fdj), product(fo, fdhr), product(fa2, fdu), product(fg, fdm), small


def gradients_kernel(
    sizes,
    plan,
    lags,
    fa1,
    fdj,
    fo,
    fdhr,
    fa2,
    fdu,
    fg,
    fdm,
    small,
    gqkv,
    gout,
    gup,
    gdown,
    gsmall,
    left,
    right,
    lt,
    gt,
    wa,
    ra,
    xa,
    ua,
    na,
    wb,
    rb,
    xb,
    ub,
    nb,
    wc,
    rc,
    xc,
    uc,
    nc,
    rs,
    xs,
    us,
    ns,
    xl,
    ul,
    nl,
    lsem,
    pair_send,
    pair_recv,
    side_send,
    side_recv,
    up_send,
    up_recv,
    down_send,
    down_recv,
):
    width, narrow, depth = sizes
    side_lag, hop, fifo = lags
    me = lax.axis_index("dp")
    core = lax.rem(me, 2)
    side = lax.rem(me // 2, 2)
    level = me // 4
    partner = me + 1 - 2 * core
    beside = me + 2 - 4 * side
    above, below = me + 4, me - 4

    def remote(source, target, send, recv, device):
        return pltpu.make_async_remote_copy(
            src_ref=source,
            dst_ref=target,
            send_sem=send,
            recv_sem=recv,
            device_id={"dp": device},
            device_id_type=MESH,
        )

    buffers = {
        "wide": (wa, ra, xa, ua, na),
        "tall": (wb, rb, xb, ub, nb),
        "part": (wc, rc, xc, uc, nc),
    }
    lefts = {"qkv": fa1, "out": fo, "up": fa2, "down": fg}
    rights = {"qkv": fdj, "out": fdhr, "up": fdu, "down": fdm}
    steps = []
    turned = None
    ahead = 0
    total = len(plan)
    for number, (name, part, _, columns) in enumerate(plan):
        if name == "small":
            continue
        if name == "down":
            while ahead < depth:
                steps.append((number, name, True, ahead, None, 0))
                ahead += 1
            steps += [(number, name, False, block, part, columns) for block in range(depth)]
            continue
        if name != turned:
            steps.append((number, name, True, 0, None, 0))
            turned = name
        steps.append((number, name, False, 0, part, columns))
        for _ in range(2 if number else 1):
            if ahead < depth:
                steps.append((number, "down", True, ahead, None, 0))
                ahead += 1

    def loads(index):
        _, name, turn, block, part, columns = steps[index]
        slot = index % 2
        if turn:
            source = lefts[name].at[:, :, block * width : (block + 1) * width]
            return pltpu.make_async_copy(source, left.at[slot], lsem.at[slot])
        return pltpu.make_async_copy(
            rights[name].at[:, :, part * columns : (part + 1) * columns],
            right.at[slot, :, :, 0:columns],
            lsem.at[slot],
        )

    def start_loads(index):
        if index < len(steps):
            loads(index).start()

    start_loads(0)

    barrier = pltpu.get_barrier_semaphore()

    def greet(device):
        pl.semaphore_signal(barrier, inc=1, device_id={"dp": device}, device_id_type=MESH)

    greet(partner)
    greet(beside)

    @pl.when(level < 3)
    def _():
        greet(above)

    @pl.when(level > 0)
    def _():
        greet(below)

    pl.semaphore_wait(barrier, 2 + (level + 2) // 3 + (5 - level) // 3)

    targets = {"qkv": gqkv, "out": gout, "up": gup, "down": gdown}
    views = []
    previous = {}
    order = {}
    last_of = {number: True for number in range(total)}
    for number, (name, part, line_first, columns) in enumerate(plan):
        kind = kind_of(plan[number])
        if kind == "small":
            views.append((small, rs, xs, us, ns, gsmall))
            previous[number] = None
            continue
        w, r, x, u, n = buffers[kind]
        order.setdefault(kind, []).append(number)
        index = len(order[kind]) - 1
        slots_of = w.shape[0]
        previous[number] = order[kind][index - slots_of] if index >= slots_of else None
        if previous[number] is not None:
            last_of[previous[number]] = False
        place = targets[name].at[0, :, part * columns : (part + 1) * columns]
        along = sum(plan[other][2] for other in order[kind][:index])
        if line_first:
            further = (xl.at[along], ul.at[along], nl.at[along], place)
        else:
            further = (x.at[index - along], u.at[index - along], n.at[index - along], place)
        views.append((w.at[index % slots_of], r.at[index]) + further)

    def pair_copy(number):
        w, r = views[number][:2]
        return remote(
            w.at[:, :, 1 - core], r, pair_send.at[number], pair_recv.at[number], partner
        )

    def side_copy(number):
        r, x = views[number][1:3]
        source = r.at[level, 1 - side] if plan[number][2] else r.at[:, 1 - side]
        return remote(source, x, side_send.at[number], side_recv.at[number], beside)

    def along_line(number):
        r, x = views[number][1:3]
        return r if plan[number][2] else x

    def up_copy(number, goal, source=None):
        u = views[number][3]
        return remote(
            u.at[goal - 1] if source is None else source,
            u.at[goal - 1],
            up_send.at[number, goal - 1],
            up_recv.at[number, goal - 1],
            above,
        )

    def down_copy(number, goal, source=None):
        n = views[number][4]
        return remote(
            n.at[goal] if source is None else source,
            n.at[goal],
            down_send.at[number, goal],
            down_recv.at[number, goal],
            below,
        )

    def start_line(number):
        base = along_line(number)

        @pl.when(level == 0)
        def _():
            for goal in (3, 2, 1):
                up_copy(number, goal, base.at[goal]).start()

        @pl.when(level == 3)
        def _():
            for goal in (0, 1, 2):
                down_copy(number, goal, base.at[goal]).start()

    across = [number for number in range(total) if not plan[number][2]]
    x_before = {number: across[i - 1] if i else None for i, number in enumerate(across)}
    position = {"step": 0}
    slots, length = left.shape[1:3]

    def turn_block(slot, target):
        def body(t, carry):
            tokens = pl.ds(pl.multiple_of(t * length, length), length)
            target[:, tokens] = left[slot, t].T
            return carry

        lax.fori_loop(0, slots, body, 0)

    def right_part(slot, lanes):
        part = right[slot, :, :, lanes]
        return part.reshape(slots * length, part.shape[2])

    def multiply(slot, w, columns):
        def tile(t, carry):
            lanes = pl.ds(pl.multiple_of(t * narrow, narrow), narrow)
            product = dot(lt[...], right_part(slot, lanes))
            w[:, :, :, :, lanes] = product.reshape(w.shape[:4] + (narrow,))
            return carry

        lax.fori_loop(0, columns // narrow, tile, 0)


    def produce(number):
        name = plan[number][0]
        sent = False
        if name != "small":
            if previous[number] is not None:
                pair_copy(previous[number]).wait_send()
            w = views[number][0]
            while position["step"] < len(steps) and steps[position["step"]][0] == number:
                index = position["step"]
                position["step"] += 1
                _, source, turn, block, _, columns = steps[index]
                start_loads(index + 1)
                loads(index).wait()
                if turn:
                    if source == "down" and name != "down" and not sent:
                        pair_copy(number).start()
                        sent = True
                    turn_block(index % 2, gt.at[block] if source == "down" else lt)
                elif source == "down":
                    w[block] = dot(gt[block], right_part(index % 2, slice(0, narrow))).reshape(
                        w.shape[1:]
                    )
                else:
                    multiply(index % 2, w, columns)
        if not sent:
            pair_copy(number).start()

    def stage_pair(number):
        w, r = views[number][:2]
        pair_copy(number).wait_recv()

        def add(z, carry):
            for s in range(2):
                r[z, s] += w[z, s, core]
            return carry

        lax.fori_loop(0, 4, add, 0)
        if plan[number][2]:
            start_line(number)
        else:
            if fifo and x_before[number] is not None:
                side_copy(x_before[number]).wait_send()
            side_copy(number).start()

    def stage_side(number):
        if plan[number][2]:
            return
        r, x = views[number][1:3]
        side_copy(number).wait_recv()

        def add(z, carry):
            x[z] += r[z, side]
            return carry

        lax.fori_loop(0, 4, add, 0)
        start_line(number)

    def stage_up(number, height):
        u = views[number][3]
        base = along_line(number)

        @pl.when(level == height)
        def _():
            for goal in range(3, height - 1, -1):
                up_copy(number, goal).wait_recv()
                if goal > height:
                    u[goal - 1] += base[goal]
                    up_copy(number, goal).start()

    def stage_down(number, height):
        n = views[number][4]
        base = along_line(number)

        @pl.when(level == height)
        def _():
            for goal in range(0, height + 1):
                down_copy(number, goal).wait_recv()
                if goal < height:
                    n[goal] += base[goal]
                    down_copy(number, goal).start()

    def stage_sum(number):
        u, n, place = views[number][3:]
        base = along_line(number)

        @pl.when(level > 0)
        def _():
            base[level] += u[level - 1]

        @pl.when(level < 3)
        def _():
            base[level] += n[level]

        if plan[number][2]:
            side_copy(number).start()
        else:
            place[...] = base[level]

    def stage_last(number):
        if plan[number][2]:
            r, x = views[number][1:3]
            side_copy(number).wait_recv()
            views[number][5][...] = r[level, side] + x[...]

    def at(stage, number, *more):
        if 0 <= number < total:
            stage(number, *more)

    for moment in range(total + side_lag + 3 * hop + 1):
        at(produce, moment)
        at(stage_pair, moment - 1)
        at(stage_side, moment - side_lag)
        for height in range(4):
            if height > 0:
                at(stage_up, moment - side_lag - hop * height, height)
            if height < 3:
                at(stage_down, moment - side_lag - hop * (3 - height), height)
        at(stage_sum, moment - side_lag - 3 * hop)
        at(stage_last, moment - side_lag - 3 * hop - 1)
    for number in range(total):
        if last_of[number]:
            pair_copy(number).wait_send()
        if not fifo or number not in x_before.values():
            side_copy(number).wait_send()
        for goal in (1, 2, 3):

            @pl.when(goal > level)
            def _():
                up_copy(number, goal).wait_send()

        for goal in (0, 1, 2):

            @pl.when(goal < level)
            def _():
                down_copy(number, goal).wait_send()


def kind_of(entry):
    name, _, _, columns = entry
    if name in ("small", "down"):
        return "small" if name == "small" else "tall"
    return "part" if columns == 256 else "wide"


def summed_in_kernel(factors, small_grads):
    fa1, fdj, fo, fdhr, fa2, fdu, fg, fdm = factors
    slots, length, width = fa1.shape
    inner = fg.shape[2]
    owners = 16
    depth = inner // width
    narrow = 256
    a_rows, b_rows = width // owners, inner // owners
    packed = small_grads.size // owners
    lanes = 128
    s_rows = -(-packed // (8 * lanes)) * 8
    small = small_grads.reshape(owners, packed)
    small = jnp.pad(small, ((0, 0), (0, s_rows * lanes - packed)))
    small = small.reshape(4, 2, 2, s_rows, lanes)
    plan = [
        ("qkv", 0, False, width),
        ("qkv", 1, True, width),
        ("down", 0, False, narrow),
        ("small", 0, False, 0),
        ("qkv", 2, False, width),
        ("down", 1, False, narrow),
        ("out", 0, True, width),
        ("up", 0, False, width),
        ("up", 1, False, width),
        ("up", 2, False, width),
        ("up", 9, False, narrow),
        ("up", 10, False, narrow),
        ("up", 11, False, narrow),
        ("down", 2, False, narrow),
    ]
    lags = (3, 2, True)
    total = len(plan)
    s_block = small.shape[3:]
    vmem = pl.BlockSpec(memory_space=pltpu.VMEM)
    anywhere = pl.BlockSpec(memory_space=pl.ANY)

    def of_kind(kind, slots_of, block):
        mine = [entry for entry in plan if kind_of(entry) == kind]
        across = sum(not entry[2] for entry in mine)
        leads = ((slots_of, 4, 2, 2), (len(mine), 4, 2), (across, 4), (across, 3), (across, 3))
        return [pltpu.VMEM(lead + block, F32) for lead in leads]

    line_count = sum(line_first for _, _, line_first, _ in plan)
    a_block = (a_rows, width)
    *grads, small_grad = pl.pallas_call(
        functools.partial(gradients_kernel, (width, narrow, depth), plan, lags),
        out_shape=(
            jax.ShapeDtypeStruct((1, a_rows, 3 * width), F32),
            jax.ShapeDtypeStruct((1, a_rows, width), F32),
            jax.ShapeDtypeStruct((1, a_rows, inner), F32),
            jax.ShapeDtypeStruct((1, b_rows, width), F32),
            jax.ShapeDtypeStruct(s_block, F32),
        ),
        in_specs=[anywhere] * 8 + [vmem],
        out_specs=(vmem,) * 5,
        scratch_shapes=[
            pltpu.VMEM((2, slots, length, width), BF),
            pltpu.VMEM((2, slots, length, width), BF),
            pltpu.VMEM((width, slots * length), BF),
            pltpu.VMEM((depth, width, slots * length), BF),
        ]
        + of_kind("wide", 2, a_block)
        + of_kind("tall", 1, (b_rows, narrow))
        + of_kind("part", 2, (a_rows, narrow))
        + [pltpu.VMEM(lead + s_block, F32) for lead in ((4, 2), (4,), (3,), (3,))]
        + [
            pltpu.VMEM((line_count,) + a_block, F32),
            pltpu.VMEM((line_count, 3, 2) + a_block, F32),
            pltpu.VMEM((line_count, 3, 2) + a_block, F32),
        ]
        + [pltpu.SemaphoreType.DMA((2,))]
        + [pltpu.SemaphoreType.DMA((total,))] * 4
        + [pltpu.SemaphoreType.DMA((total, 3))] * 4,
        compiler_params=pltpu.CompilerParams(
            collective_id=1, has_side_effects=True, vmem_limit_bytes=62 << 20
        ),
    )(*factors, small)
    return tuple(grads) + (small_grad.reshape(1, -1)[:, :packed],)


def reduced(factors, small_grads):
    if lax.axis_size("dp") == 16:
        return summed_in_kernel(factors, small_grads)
    return summed_by_parts(factors, small_grads)


def per_device(
    embeddings, cotangent, seg_ids, thought_pos, w_qkv, w_out, w_up, w_down, small_params
):
    section_out, *factors, small_grads = layers(
        embeddings, cotangent, seg_ids, thought_pos, w_qkv, w_out, w_up, w_down, small_params
    )
    return (section_out,) + tuple(reduced(factors, small_grads))


def solution(mesh):
    return jax.shard_map(
        per_device,
        mesh=mesh,
        in_specs=(
            P("dp", None, None),
            P("dp", None, None),
            P("dp", None),
            P("dp", None),
            P("pipe", None, None),
            P("pipe", None, None),
            P("pipe", None, None),
            P("pipe", None, None),
            P("pipe", None),
        ),
        out_specs=(
            P("pipe", "dp", None, None),
            P("pipe", "dp", None),
            P("pipe", "dp", None),
            P("pipe", "dp", None),
            P("pipe", "dp", None),
            P("pipe", "dp"),
        ),
        check_vma=False,
    )
```

```python
import functools

import jax
import jax.numpy as jnp
from jax import lax
from jax.experimental import pallas as pl
from jax.experimental.pallas import tpu as pltpu
from jax.sharding import PartitionSpec as P

HEADS = 12
BF = jnp.bfloat16
F32 = jnp.float32
MESH = pl.DeviceIdType.MESH
EPSILON = 1e-05
MASKED = -1000000000.0
NO_CAP = 3e38
LAT = 16
G1, B1, BQ, BV, BO, G2, B2, BU = 0, 1, 2, 3, 4, 5, 6, 7


def dot(a, b):
    return lax.dot_general(a, b, (((1,), (0,)), ((), ())), preferred_element_type=F32)


def dot_nt(a, b):
    return lax.dot_general(a, b, (((1,), (1,)), ((), ())), preferred_element_type=F32)


def dot_tn(a, b):
    return lax.dot_general(a, b, (((0,), (0,)), ((), ())), preferred_element_type=F32)


def exact_dot(a, b):
    return lax.dot_general(
        a,
        b,
        (((1,), (0,)), ((), ())),
        precision=lax.Precision.HIGHEST,
        preferred_element_type=F32,
    )


def normalized(values):
    centred = values - jnp.mean(values, -1, keepdims=True)
    spread = jnp.mean(centred * centred, -1, keepdims=True)
    scale = lax.rsqrt(spread + EPSILON)
    return centred * scale, scale


def norm_back(hat, scale, grad):
    along = jnp.mean(grad * hat, -1, keepdims=True)
    return scale * (grad - jnp.mean(grad, -1, keepdims=True) - hat * along)


def gelu_both(u):
    c = 0.7978845608028654
    square = u * u
    t = jnp.tanh(c * u * (1.0 + 0.044715 * square))
    half = 0.5 + 0.5 * t
    slope = half + (0.5 * c) * u * (1.0 - t * t) * (1.0 + (3 * 0.044715) * square)
    return u * half, slope


def softmax(scores, axis=-1):
    e = jnp.exp(scores - jnp.max(scores, axis, keepdims=True))
    return e * (1.0 / jnp.sum(e, axis, keepdims=True))


def layers_kernel(
    sizes,
    emb,
    cot,
    seg,
    tpos,
    wqkv_h,
    wout_h,
    wup_h,
    wdown_h,
    small,
    sec,
    fa1,
    fdj,
    fo,
    fdhr,
    fa2,
    fdu,
    fg,
    fdm,
    sg,
    sums,
    joint,
    stat,
    wqkv,
    wout,
    wup,
    wdown,
    xin,
    yb,
    dyb,
    jn,
    pr,
    hm,
    slope,
    a1,
    ob,
    a2,
    gb,
    dm,
    dub,
    dhr,
    djb,
    da,
    dob,
    dmt,
    dat,
    djt,
    cap,
    lat,
    thg,
    lx,
    lq,
    lp,
    lh,
    la2,
    lo,
    lg,
    lslope,
    wsem,
    osem,
    ysend,
    yrecv,
    gsend,
    grecv,
    lsend,
    lrecv,
    tsend,
    trecv,
):
    rows, length, width, inner, thoughts = sizes
    blocks = inner // width
    bd = BU + blocks
    pairs = HEADS // 2
    me = lax.axis_index("pipe")
    other = 1 - me

    weights = [
        pltpu.make_async_copy(source.at[0], target, wsem.at[number])
        for number, (source, target) in enumerate(
            ((wqkv_h, wqkv), (wout_h, wout), (wup_h, wup), (wdown_h, wdown))
        )
    ]
    for copy in weights:
        copy.start()
    barrier = pltpu.get_barrier_semaphore()
    pl.semaphore_signal(barrier, inc=1, device_id={"pipe": other}, device_id_type=MESH)
    pl.semaphore_wait(barrier, 1)
    sums[...] = jnp.zeros_like(sums)
    joint[:, 0:width] = small[:, BQ * width : (BQ + 1) * width]
    joint[:, width : 2 * width] = jnp.zeros((1, width), F32)
    joint[:, 2 * width : 3 * width] = small[:, BV * width : (BV + 1) * width]

    def remote(source, target, send, recv):
        return pltpu.make_async_remote_copy(
            src_ref=source,
            dst_ref=target,
            send_sem=send,
            recv_sem=recv,
            device_id={"pipe": other},
            device_id_type=MESH,
        )

    class Pieces:
        def __init__(self, source, target, send, recv):
            count = send.shape[0]
            height = length // count
            self.copies = [
                remote(
                    source.at[piece * height : (piece + 1) * height],
                    target.at[piece * height : (piece + 1) * height],
                    send.at[piece],
                    recv.at[piece],
                )
                for piece in range(count)
            ]

        def start(self):
            for copy in self.copies:
                copy.start()

        def wait_send(self):
            for copy in self.copies:
                copy.wait_send()

        def wait_recv(self):
            for copy in self.copies:
                copy.wait_recv()

    def send_y(k):
        return Pieces(yb.at[k], xin.at[k], ysend.at[k], yrecv.at[k])

    def send_grad(k):
        return Pieces(yb.at[k], dyb.at[k], gsend.at[k], grecv.at[k])

    def send_lat(r):
        return remote(lat.at[r], lat.at[r], lsend.at[r], lrecv.at[r])

    def send_thoughts(r):
        return remote(thg.at[r], thg.at[r], tsend.at[r], trecv.at[r])

    def started(source, target, number):
        copy = pltpu.make_async_copy(source, target, osem.at[number])
        copy.start()
        return copy

    def settle(pending, number, source, target):
        @pl.when(pending)
        def _():
            pltpu.make_async_copy(source, target.at[0], osem.at[number]).wait()

    def finish(copies):
        for copy in copies:
            copy.wait()

    def each_chunk(step, count):
        def body(i, carry):
            step(pl.ds(pl.multiple_of(i * count, count), count), i * count)
            return carry

        lax.fori_loop(0, length // count, body, 0)

    def loop(count, step):
        def body(i, carry):
            step(i)
            return carry

        lax.fori_loop(0, count, body, 0)

    def add_columns(number, values):
        sums[number] += jnp.sum(values.astype(F32).reshape(-1, 8, width), 0)

    def row(number):
        return small[:, group(number)]

    def group(number):
        return slice(number * width, (number + 1) * width)

    lane = lax.broadcasted_iota(jnp.int32, (1, 128), 1)
    low = lane < 64
    halves = (jnp.where(low, 1.0, 0.0).astype(BF), jnp.where(low, 0.0, 1.0).astype(BF))

    def first_length(r):
        segment = seg[pl.ds(r, 1), :]
        return jnp.sum(jnp.where(segment == 0, 1.0, 0.0), -1, keepdims=True).astype(jnp.int32)

    def set_cap(r):
        first = first_length(r)
        query = lax.broadcasted_iota(jnp.int32, (length, length), 0)
        key = lax.broadcasted_iota(jnp.int32, (length, length), 1)
        lowest = jnp.where(query >= first, first, 0)
        cap[...] = jnp.where((key <= query) & (key >= lowest), NO_CAP, MASKED)

    def positions(r, shift, axis=0):
        shape = (LAT, 1) if axis == 0 else (1, LAT)
        number = lax.broadcasted_iota(jnp.int32, shape, axis)
        result = jnp.full(shape, -1, jnp.int32)
        for j in range(thoughts):
            result = jnp.where(number == j, tpos[r, j] - shift, result)
        return result

    def selector_turned(r, shift):
        place = positions(r, shift, 1)
        return jnp.where(lax.broadcasted_iota(jnp.int32, (length, LAT), 0) == place, 1.0, 0.0)

    def selector(place):
        return jnp.where(lax.broadcasted_iota(jnp.int32, (LAT, length), 1) == place, 1.0, 0.0)

    def unmarked(r, start):
        place = lax.broadcasted_iota(jnp.int32, (32, 1), 0) + start
        keep = jnp.ones((32, 1), F32)
        for j in range(thoughts):
            keep = jnp.where(place == tpos[r, j], 0.0, keep)
        return keep

    def head_lanes(part, hp):
        start = part * width + hp * 128
        if isinstance(hp, int):
            return slice(start, start + 128)
        return pl.ds(pl.multiple_of(start, 128), 128)

    def norm_rows(x, target, k, which, gain, shift, more=None):
        def step(part, _):
            values = x[part, :]
            center = jnp.mean(values, -1, keepdims=True)
            centred = values - center
            scale = lax.rsqrt(jnp.mean(centred * centred, -1, keepdims=True) + EPSILON)
            stat[k, 2 * which, part, :] = center
            stat[k, 2 * which + 1, part, :] = scale
            target[part, :] = (centred * scale * row(gain) + row(shift)).astype(BF)
            if more is not None:
                more(part, values)

        each_chunk(step, 128)

    def norm_rows_back(x, part, k, which, gain, shift):
        scale = stat[k, 2 * which + 1, part, :]
        hat = (x[part, :] - stat[k, 2 * which, part, :]) * scale
        grad = da[part, :]
        add_columns(gain, grad * hat)
        add_columns(shift, grad)
        return norm_back(hat, scale, grad * row(gain))

    def forward(k, x, y, pending, first=None):
        def need(number):
            if first is not None:

                @pl.when(first)
                def _():
                    weights[number].wait()

        settle(pending, 0, a1, fa1)
        norm_rows(x, a1, k, 0, G1, B1)
        started(a1, fa1.at[k], 0)
        need(0)
        settle(pending, 1, ob, fo)

        for part in range(3):
            joined = dot(a1[...], wqkv[:, group(part)]) + joint[:, group(part)]
            jn[k, :, group(part)] = joined.astype(BF)
        for hp in range(pairs):
            q = jn[k, :, head_lanes(0, hp)]
            key = jn[k, :, head_lanes(1, hp)]
            value = jn[k, :, head_lanes(2, hp)]
            out = []
            for h in range(2):
                scores = dot_nt(q * (halves[h] * 0.125), key)
                chance = softmax(jnp.minimum(scores, cap[...])).astype(BF)
                pr[k, 2 * hp + h] = chance
                out.append(dot(chance, value))
            ob[:, head_lanes(0, hp)] = jnp.where(low, out[0], out[1]).astype(BF)
        started(ob, fo.at[k], 1)
        need(1)
        settle(pending, 2, a2, fa2)
        hm[k] = x[...] + dot(ob[...], wout[...]) + row(BO)

        def begin(part, values):
            y[part, :] = values + row(bd)

        norm_rows(hm.at[k], a2, k, 1, G2, B2, begin)
        started(a2, fa2.at[k], 2)
        need(2)
        need(3)
        settle(pending, 3, gb, fg)

        for c in range(blocks):
            part = group(c)
            g, d = gelu_both(dot(a2[...], wup[:, part]) + row(BU + c))
            gb[:, part] = g.astype(BF)
            slope[k, part, :] = d.astype(BF).T
            y[...] += dot(gb[:, part], wdown[part, :])
        started(gb, fg.at[k], 3)

    def backward(k, x, dy, dx, pending):
        def step(part, _):
            branch = dy[part, :].astype(BF)
            dm[part, :] = branch
            add_columns(bd, branch)

        settle(pending, 4, dm, fdm)
        each_chunk(step, 64)
        started(dm, fdm.at[k], 4)
        dmt[...] = dm[...].T
        dat[...] = jnp.zeros_like(dat)
        settle(pending, 5, dub, fdu)

        def mlp(c):
            part = pl.ds(pl.multiple_of(c * width, width), width)
            grad = (dot(wdown[part, :], dmt[...]) * slope[k, part, :]).astype(BF)
            dat[...] += dot(wup[:, part], grad)
            turned = grad.T
            dub[:, part] = turned
            add_columns(BU + c, turned)

        loop(blocks, mlp)
        da[...] = dat[...].T
        started(dub, fdu.at[k], 5)
        settle(pending, 6, dhr, fdhr)

        def step_two(part, _):
            middle = dy[part, :] + norm_rows_back(hm.at[k], part, k, 1, G2, B2)
            dy[part, :] = middle
            branch = middle.astype(BF)
            dhr[part, :] = branch
            add_columns(BO, branch)

        each_chunk(step_two, 64)
        started(dhr, fdhr.at[k], 6)
        dmt[...] = dhr[...].T
        dob[...] = dot(wout[...], dmt[...]).astype(BF).T
        settle(pending, 7, djb, fdj)

        def heads(hp):
            q = jn[k, :, head_lanes(0, hp)]
            key = jn[k, :, head_lanes(1, hp)]
            value = jn[k, :, head_lanes(2, hp)]
            grad_out = dob[:, head_lanes(0, hp)]
            dq, dk, dv = [], [], []
            for h in range(2):
                chance = pr[k, 2 * hp + h]
                chance_full = chance.astype(F32)
                inner_part = chance_full * dot_nt(grad_out * halves[h], value)
                total = jnp.sum(inner_part, -1, keepdims=True)
                grad_scores = (inner_part - chance_full * total).astype(BF)
                dq.append(dot(grad_scores, key))
                dk.append(dot_tn(grad_scores, q))
                dv.append(dot_tn(chance, grad_out))
            djb[:, head_lanes(0, hp)] = (jnp.where(low, dq[0], dq[1]) * 0.125).astype(BF)
            djb[:, head_lanes(1, hp)] = (jnp.where(low, dk[0], dk[1]) * 0.125).astype(BF)
            djb[:, head_lanes(2, hp)] = jnp.where(low, dv[0], dv[1]).astype(BF)

        loop(pairs, heads)
        started(djb, fdj.at[k], 7)
        into_input(k, x, dy, dx)

    def into_input(k, x, middle, dx):
        djt[...] = djb[...].T
        da[...] = dot(wqkv[...], djt[...]).T

        def step(part, _):
            add_columns(BQ, djb[part, group(0)])
            add_columns(BV, djb[part, group(2)])
            dx[part, :] = middle[part, :] + norm_rows_back(x, part, k, 0, G1, B1)

        each_chunk(step, 64)

    def forward_latent(r):
        x = xin.at[r]
        norm_rows(x, a1, r, 0, G1, B1)
        copies = [started(a1, fa1.at[r], 0)]
        jn[r, :, group(1)] = dot(a1[...], wqkv[:, group(1)]).astype(BF)
        jn[r, :, group(2)] = (dot(a1[...], wqkv[:, group(2)]) + row(BV)).astype(BF)
        place = positions(r, 1)
        chosen = exact_dot(selector(place), x[...])
        lx[r] = chosen
        hat, _ = normalized(chosen)
        normed = (hat * row(G1) + row(B1)).astype(BF)
        lq[r] = (dot(normed, wqkv[:, group(0)]) + row(BQ)).astype(BF)
        first = first_length(r)
        key_place = lax.broadcasted_iota(jnp.int32, (LAT, length), 1)
        lowest = jnp.where(place >= first, first, 0)
        limit = jnp.where((key_place <= place) & (key_place >= lowest), NO_CAP, MASKED)

        def heads(hp):
            q = lq[r, :, head_lanes(0, hp)]
            key = jn[r, :, head_lanes(1, hp)]
            value = jn[r, :, head_lanes(2, hp)]
            out = []
            for h in range(2):
                scores = dot_nt(q * (halves[h] * 0.125), key)
                chance = softmax(jnp.minimum(scores, limit)).astype(BF)
                lp[r, 2 * hp + h] = chance
                out.append(dot(chance, value))
            lo[r, :, head_lanes(0, hp)] = jnp.where(low, out[0], out[1]).astype(BF)

        for hp in range(pairs):
            heads(hp)
        middle = chosen + dot(lo[r], wout[...]) + row(BO)
        lh[r] = middle
        hat, _ = normalized(middle)
        la2[r] = (hat * row(G2) + row(B2)).astype(BF)
        lat[r] = middle + row(bd)

        def mlp(c):
            part = group(c)
            u = dot(la2[r], wup[:, part]) + row(BU + c)
            g, d = gelu_both(u)
            lg[r, :, part] = g.astype(BF)
            lslope[r, :, part] = d.astype(BF)
            lat[r] += dot(lg[r, :, part], wdown[part, :])

        for c in range(blocks):
            mlp(c)
        return copies

    def backward_latent(r, dx):
        grad_result = thg[r]
        branch = grad_result.astype(BF)
        top = slice(0, LAT)
        add_columns(bd, branch)
        dm[top, :] = branch
        a2[top, :] = la2[r]
        ob[top, :] = lo[r]
        gb[top, :] = lg[r]
        copies = [
            started(dm, fdm.at[r], 4),
            started(a2, fa2.at[r], 2),
            started(ob, fo.at[r], 1),
            started(gb, fg.at[r], 3),
        ]
        da[top, :] = jnp.zeros((LAT, width), F32)

        def mlp(c):
            part = group(c)
            grad = (dot_nt(dm[top, :], wdown[part, :]) * lslope[r, :, part]).astype(BF)
            dub[top, part] = grad
            add_columns(BU + c, grad)
            da[top, :] += dot_nt(grad, wup[:, part])

        for c in range(blocks):
            mlp(c)
        copies.append(started(dub, fdu.at[r], 5))
        hat, scale = normalized(lh[r])
        grad = da[top, :]
        add_columns(G2, grad * hat)
        add_columns(B2, grad)
        middle = grad_result + norm_back(hat, scale, grad * row(G2))
        rounded = middle.astype(BF)
        dhr[top, :] = rounded
        add_columns(BO, rounded)
        copies.append(started(dhr, fdhr.at[r], 6))
        spread = selector_turned(r, 1)
        dyb[r] = exact_dot(spread, middle)
        place = positions(r, 1, 1)
        first = first_length(r)
        key_place = lax.broadcasted_iota(jnp.int32, (length, LAT), 0)
        lowest = jnp.where(place >= first, first, 0)
        limit = jnp.where((key_place <= place) & (key_place >= lowest), NO_CAP, MASKED)
        dob[top, :] = dot_nt(rounded, wout[...]).astype(BF)

        def heads(hp):
            q = lq[r, :, head_lanes(0, hp)]
            key = jn[r, :, head_lanes(1, hp)]
            value = jn[r, :, head_lanes(2, hp)]
            grad_out = dob[top, head_lanes(0, hp)]
            dq, dk, dv = [], [], []
            for h in range(2):
                grad_masked = grad_out * halves[h]
                chance = lp[r, 2 * hp + h].astype(F32)
                inner_part = chance * dot_nt(grad_masked, value)
                total = jnp.sum(inner_part, -1, keepdims=True)
                dq.append(dot((inner_part - chance * total).astype(BF), key))
                scores = dot_nt(key, q * (halves[h] * 0.125))
                chance = softmax(jnp.minimum(scores, limit), 0)
                inner_part = chance * dot_nt(value, grad_masked)
                total = jnp.sum(inner_part, 0, keepdims=True)
                dk.append(dot((inner_part - chance * total).astype(BF), q))
                dv.append(dot(chance.astype(BF), grad_out))
            grad_q = (jnp.where(low, dq[0], dq[1]) * 0.125).astype(BF)
            djb[:, head_lanes(0, hp)] = dot(spread.astype(BF), grad_q).astype(BF)
            djb[:, head_lanes(1, hp)] = (jnp.where(low, dk[0], dk[1]) * 0.125).astype(BF)
            djb[:, head_lanes(2, hp)] = jnp.where(low, dv[0], dv[1]).astype(BF)

        for hp in range(pairs):
            heads(hp)
        copies.append(started(djb, fdj.at[r], 7))
        into_input(r, xin.at[r], dyb.at[r], dx)
        return copies

    staged = (
        (a1, fa1), (ob, fo), (a2, fa2), (gb, fg), (dm, fdm), (dub, fdu), (dhr, fdhr), (djb, fdj)
    )

    def settle_all(count, first=0):
        for number in range(first, first + count):
            source, target = staged[number]
            pltpu.make_async_copy(source, target.at[0], osem.at[number]).wait()

    @pl.when(me == 0)
    def _():
        def forward_step(k, carry):
            r = lax.rem(k, rows)
            set_cap(r)

            @pl.when(k < rows)
            def _():
                xin[k] = emb[r].astype(F32)

            @pl.when(k >= rows)
            def _():
                send_lat(r).wait_recv()
                xin[k] = exact_dot(selector_turned(r, 0), lat[r])

                def step(part, start):
                    xin[k, part, :] += emb[r, part, :].astype(F32) * unmarked(r, start)

                each_chunk(step, 32)

            forward(k, xin.at[k], yb.at[k], k > 0, first=k == 0)
            send_y(k).start()
            return carry

        lax.fori_loop(0, 2 * rows, forward_step, 0)
        settle_all(4)

        def backward_step(i, carry):
            k = lax.rem(i + rows, 2 * rows)
            r = lax.rem(i, rows)
            send_y(k).wait_send()
            send_grad(k).wait_recv()
            backward(k, xin.at[k], dyb.at[k], yb.at[k], i > 0)

            @pl.when(i < rows)
            def _():
                thg[r] = exact_dot(selector(positions(r, 0)), yb[k])
                send_thoughts(r).start()

            @pl.when(i >= rows)
            def _():
                def step(part, start):
                    yb[k, part, :] += yb[rows + r, part, :] * unmarked(r, start)

                each_chunk(step, 32)
                started(yb.at[k], sec.at[0, r], 8).wait()

            return carry

        lax.fori_loop(0, 2 * rows, backward_step, 0)
        settle_all(4, 4)

        def drain(r, carry):
            send_thoughts(r).wait_send()
            return carry

        lax.fori_loop(0, rows, drain, 0)

    @pl.when(me == 1)
    def _():
        finish(weights)

        def latent_step(r, carry):
            send_y(r).wait_recv()
            copies = forward_latent(r)
            send_lat(r).start()
            finish(copies)
            return carry

        lax.fori_loop(0, rows, latent_step, 0)

        def language_step(r, carry):
            k = rows + r
            set_cap(r)
            send_y(k).wait_recv()
            forward(k, xin.at[k], dyb.at[k], r > 0)
            result = started(dyb.at[k], sec.at[0, r], 8)
            dyb[r] = cot[r].astype(F32)
            backward(k, xin.at[k], dyb.at[r], yb.at[k], r > 0)
            send_grad(k).start()
            result.wait()
            return carry

        lax.fori_loop(0, rows, language_step, 0)
        settle_all(8)
        for buffer in (dm, a2, ob, gb, dub, dhr):
            buffer[...] = jnp.zeros_like(buffer)

        def latent_back_step(r, carry):
            send_thoughts(r).wait_recv()
            copies = backward_latent(r, yb.at[r])
            send_grad(r).start()
            finish(copies)
            return carry

        lax.fori_loop(0, rows, latent_back_step, 0)

        def drain(r, carry):
            send_lat(r).wait_send()
            send_grad(r).wait_send()
            send_grad(rows + r).wait_send()
            return carry

        lax.fori_loop(0, rows, drain, 0)

    sg[...] = jnp.sum(sums[...], 1)


def layers(emb, cot, seg, tpos, w_qkv, w_out, w_up, w_down, small):
    rows, length, width = emb.shape
    inner = w_up.shape[2]
    thoughts = tpos.shape[1]
    slots = 2 * rows
    packed = small.shape[1] // width
    vmem = pl.BlockSpec(memory_space=pltpu.VMEM)
    anywhere = pl.BlockSpec(memory_space=pl.ANY)
    smem = pl.BlockSpec(memory_space=pltpu.SMEM)

    def factor(columns):
        return jax.ShapeDtypeStruct((slots, length, columns), BF)

    def block(columns, kind=BF):
        return pltpu.VMEM((length, columns), kind)

    def few(columns, kind=BF):
        return pltpu.VMEM((rows, LAT, columns), kind)

    sizes = (rows, length, width, inner, thoughts)
    return pl.pallas_call(
        functools.partial(layers_kernel, sizes),
        out_shape=(
            jax.ShapeDtypeStruct((1, rows, length, width), F32),
            factor(width),
            factor(3 * width),
            factor(width),
            factor(width),
            factor(width),
            factor(inner),
            factor(inner),
            factor(width),
            jax.ShapeDtypeStruct((packed, width), F32),
        ),
        in_specs=[vmem, vmem, vmem, smem] + [anywhere] * 4 + [vmem],
        out_specs=(anywhere,) * 9 + (vmem,),
        scratch_shapes=[
            pltpu.VMEM((packed, 8, width), F32),
            pltpu.VMEM((1, 3 * width), F32),
            pltpu.VMEM((slots, 4, length, 1), F32),
            pltpu.VMEM((width, 3 * width), BF),
            pltpu.VMEM((width, width), BF),
            pltpu.VMEM((width, inner), BF),
            pltpu.VMEM((inner, width), BF),
            pltpu.VMEM((slots, length, width), F32),
            pltpu.VMEM((slots, length, width), F32),
            pltpu.VMEM((slots, length, width), F32),
            pltpu.VMEM((slots, length, 3 * width), BF),
            pltpu.VMEM((slots, HEADS, length, length), BF),
            pltpu.VMEM((slots, length, width), F32),
            pltpu.VMEM((slots, inner, length), BF),
            block(width),
            block(width),
            block(width),
            block(inner),
            block(width),
            block(inner),
            block(width),
            block(3 * width),
            block(width, F32),
            block(width),
            pltpu.VMEM((width, length), BF),
            pltpu.VMEM((width, length), F32),
            pltpu.VMEM((3 * width, length), BF),
            block(length, F32),
            few(width, F32),
            few(width, F32),
            few(width, F32),
            few(width),
            pltpu.VMEM((rows, HEADS, LAT, length), BF),
            few(width, F32),
            few(width),
            few(width),
            few(inner),
            few(inner),
            pltpu.SemaphoreType.DMA((4,)),
            pltpu.SemaphoreType.DMA((9,)),
        ]
        + [pltpu.SemaphoreType.DMA((slots, 4))] * 4
        + [pltpu.SemaphoreType.DMA((rows,))] * 4,
        compiler_params=pltpu.CompilerParams(
            collective_id=0, has_side_effects=True, vmem_limit_bytes=62 << 20
        ),
    )(emb, cot, seg, tpos, w_qkv, w_out, w_up, w_down, small)


def summed_by_parts(factors, small_grads):
    fa1, fdj, fo, fdhr, fa2, fdu, fg, fdm = factors

    def product(left, right):
        whole = jnp.einsum("ktm,ktn->mn", left, right, preferred_element_type=F32)
        return lax.psum_scatter(whole[None], "dp", scatter_dimension=1, tiled=True)

    small = lax.psum_scatter(
        small_grads.reshape(1, -1), "dp", scatter_dimension=1, tiled=True
    )
    return product(fa1, fdj), product(fo, fdhr), product(fa2, fdu), product(fg, fdm), small


def gradients_kernel(
    sizes,
    plan,
    lags,
    fa1,
    fdj,
    fo,
    fdhr,
    fa2,
    fdu,
    fg,
    fdm,
    small,
    gqkv,
    gout,
    gup,
    gdown,
    gsmall,
    left,
    right,
    lt,
    gt,
    wa,
    ra,
    xa,
    ua,
    na,
    wb,
    rb,
    xb,
    ub,
    nb,
    wc,
    rc,
    xc,
    uc,
    nc,
    rs,
    xs,
    us,
    ns,
    xl,
    ul,
    nl,
    lsem,
    pair_send,
    pair_recv,
    side_send,
    side_recv,
    up_send,
    up_recv,
    down_send,
    down_recv,
):
    width, narrow, depth = sizes
    side_lag, hop, fifo = lags
    me = lax.axis_index("dp")
    core = lax.rem(me, 2)
    side = lax.rem(me // 2, 2)
    level = me // 4
    partner = me + 1 - 2 * core
    beside = me + 2 - 4 * side
    above, below = me + 4, me - 4

    def remote(source, target, send, recv, device):
        return pltpu.make_async_remote_copy(
            src_ref=source,
            dst_ref=target,
            send_sem=send,
            recv_sem=recv,
            device_id={"dp": device},
            device_id_type=MESH,
        )

    buffers = {
        "wide": (wa, ra, xa, ua, na),
        "tall": (wb, rb, xb, ub, nb),
        "part": (wc, rc, xc, uc, nc),
    }
    lefts = {"qkv": fa1, "out": fo, "up": fa2, "down": fg}
    rights = {"qkv": fdj, "out": fdhr, "up": fdu, "down": fdm}
    steps = []
    turned = None
    ahead = 0
    total = len(plan)
    for number, (name, part, _, columns) in enumerate(plan):
        if name == "small":
            continue
        if name == "down":
            while ahead < depth:
                steps.append((number, name, True, ahead, None, 0))
                ahead += 1
            steps += [(number, name, False, block, part, columns) for block in range(depth)]
            continue
        if name != turned:
            steps.append((number, name, True, 0, None, 0))
            turned = name
        steps.append((number, name, False, 0, part, columns))
        for _ in range(2 if number else 1):
            if ahead < depth:
                steps.append((number, "down", True, ahead, None, 0))
                ahead += 1

    def loads(index):
        _, name, turn, block, part, columns = steps[index]
        slot = index % 2
        if turn:
            source = lefts[name].at[:, :, block * width : (block + 1) * width]
            return pltpu.make_async_copy(source, left.at[slot], lsem.at[slot])
        return pltpu.make_async_copy(
            rights[name].at[:, :, part * columns : (part + 1) * columns],
            right.at[slot, :, :, 0:columns],
            lsem.at[slot],
        )

    def start_loads(index):
        if index < len(steps):
            loads(index).start()

    start_loads(0)

    barrier = pltpu.get_barrier_semaphore()

    def greet(device):
        pl.semaphore_signal(barrier, inc=1, device_id={"dp": device}, device_id_type=MESH)

    greet(partner)
    greet(beside)

    @pl.when(level < 3)
    def _():
        greet(above)

    @pl.when(level > 0)
    def _():
        greet(below)

    pl.semaphore_wait(barrier, 2 + (level + 2) // 3 + (5 - level) // 3)

    targets = {"qkv": gqkv, "out": gout, "up": gup, "down": gdown}
    views = []
    previous = {}
    order = {}
    last_of = {number: True for number in range(total)}
    for number, (name, part, line_first, columns) in enumerate(plan):
        kind = kind_of(plan[number])
        if kind == "small":
            views.append((small, rs, xs, us, ns, gsmall))
            previous[number] = None
            continue
        w, r, x, u, n = buffers[kind]
        order.setdefault(kind, []).append(number)
        index = len(order[kind]) - 1
        slots_of = w.shape[0]
        previous[number] = order[kind][index - slots_of] if index >= slots_of else None
        if previous[number] is not None:
            last_of[previous[number]] = False
        place = targets[name].at[0, :, part * columns : (part + 1) * columns]
        along = sum(plan[other][2] for other in order[kind][:index])
        if line_first:
            further = (xl.at[along], ul.at[along], nl.at[along], place)
        else:
            further = (x.at[index - along], u.at[index - along], n.at[index - along], place)
        views.append((w.at[index % slots_of], r.at[index]) + further)

    def pair_copy(number):
        w, r = views[number][:2]
        return remote(
            w.at[:, :, 1 - core], r, pair_send.at[number], pair_recv.at[number], partner
        )

    def side_copy(number):
        r, x = views[number][1:3]
        source = r.at[level, 1 - side] if plan[number][2] else r.at[:, 1 - side]
        return remote(source, x, side_send.at[number], side_recv.at[number], beside)

    def along_line(number):
        r, x = views[number][1:3]
        return r if plan[number][2] else x

    def up_copy(number, goal, source=None):
        u = views[number][3]
        return remote(
            u.at[goal - 1] if source is None else source,
            u.at[goal - 1],
            up_send.at[number, goal - 1],
            up_recv.at[number, goal - 1],
            above,
        )

    def down_copy(number, goal, source=None):
        n = views[number][4]
        return remote(
            n.at[goal] if source is None else source,
            n.at[goal],
            down_send.at[number, goal],
            down_recv.at[number, goal],
            below,
        )

    def start_line(number):
        base = along_line(number)

        @pl.when(level == 0)
        def _():
            for goal in (3, 2, 1):
                up_copy(number, goal, base.at[goal]).start()

        @pl.when(level == 3)
        def _():
            for goal in (0, 1, 2):
                down_copy(number, goal, base.at[goal]).start()

    across = [number for number in range(total) if not plan[number][2]]
    x_before = {number: across[i - 1] if i else None for i, number in enumerate(across)}
    position = {"step": 0}
    slots, length = left.shape[1:3]

    def turn_block(slot, target):
        def body(t, carry):
            tokens = pl.ds(pl.multiple_of(t * length, length), length)
            target[:, tokens] = left[slot, t].T
            return carry

        lax.fori_loop(0, slots, body, 0)

    def right_part(slot, lanes):
        part = right[slot, :, :, lanes]
        return part.reshape(slots * length, part.shape[2])

    def multiply(slot, w, columns):
        def tile(t, carry):
            lanes = pl.ds(pl.multiple_of(t * narrow, narrow), narrow)
            product = dot(lt[...], right_part(slot, lanes))
            w[:, :, :, :, lanes] = product.reshape(w.shape[:4] + (narrow,))
            return carry

        lax.fori_loop(0, columns // narrow, tile, 0)


    def produce(number):
        name = plan[number][0]
        sent = False
        if name != "small":
            if previous[number] is not None:
                pair_copy(previous[number]).wait_send()
            w = views[number][0]
            while position["step"] < len(steps) and steps[position["step"]][0] == number:
                index = position["step"]
                position["step"] += 1
                _, source, turn, block, _, columns = steps[index]
                start_loads(index + 1)
                loads(index).wait()
                if turn:
                    if source == "down" and name != "down" and not sent:
                        pair_copy(number).start()
                        sent = True
                    turn_block(index % 2, gt.at[block] if source == "down" else lt)
                elif source == "down":
                    w[block] = dot(gt[block], right_part(index % 2, slice(0, narrow))).reshape(
                        w.shape[1:]
                    )
                else:
                    multiply(index % 2, w, columns)
        if not sent:
            pair_copy(number).start()

    def stage_pair(number):
        w, r = views[number][:2]
        pair_copy(number).wait_recv()

        def add(z, carry):
            for s in range(2):
                r[z, s] += w[z, s, core]
            return carry

        lax.fori_loop(0, 4, add, 0)
        if plan[number][2]:
            start_line(number)
        else:
            if fifo and x_before[number] is not None:
                side_copy(x_before[number]).wait_send()
            side_copy(number).start()

    def stage_side(number):
        if plan[number][2]:
            return
        r, x = views[number][1:3]
        side_copy(number).wait_recv()

        def add(z, carry):
            x[z] += r[z, side]
            return carry

        lax.fori_loop(0, 4, add, 0)
        start_line(number)

    def stage_up(number, height):
        u = views[number][3]
        base = along_line(number)

        @pl.when(level == height)
        def _():
            for goal in range(3, height - 1, -1):
                up_copy(number, goal).wait_recv()
                if goal > height:
                    u[goal - 1] += base[goal]
                    up_copy(number, goal).start()

    def stage_down(number, height):
        n = views[number][4]
        base = along_line(number)

        @pl.when(level == height)
        def _():
            for goal in range(0, height + 1):
                down_copy(number, goal).wait_recv()
                if goal < height:
                    n[goal] += base[goal]
                    down_copy(number, goal).start()

    def stage_sum(number):
        u, n, place = views[number][3:]
        base = along_line(number)

        @pl.when(level > 0)
        def _():
            base[level] += u[level - 1]

        @pl.when(level < 3)
        def _():
            base[level] += n[level]

        if plan[number][2]:
            side_copy(number).start()
        else:
            place[...] = base[level]

    def stage_last(number):
        if plan[number][2]:
            r, x = views[number][1:3]
            side_copy(number).wait_recv()
            views[number][5][...] = r[level, side] + x[...]

    def at(stage, number, *more):
        if 0 <= number < total:
            stage(number, *more)

    for moment in range(total + side_lag + 3 * hop + 1):
        at(produce, moment)
        at(stage_pair, moment - 1)
        at(stage_side, moment - side_lag)
        for height in range(4):
            if height > 0:
                at(stage_up, moment - side_lag - hop * height, height)
            if height < 3:
                at(stage_down, moment - side_lag - hop * (3 - height), height)
        at(stage_sum, moment - side_lag - 3 * hop)
        at(stage_last, moment - side_lag - 3 * hop - 1)
    for number in range(total):
        if last_of[number]:
            pair_copy(number).wait_send()
        if not fifo or number not in x_before.values():
            side_copy(number).wait_send()
        for goal in (1, 2, 3):

            @pl.when(goal > level)
            def _():
                up_copy(number, goal).wait_send()

        for goal in (0, 1, 2):

            @pl.when(goal < level)
            def _():
                down_copy(number, goal).wait_send()


def kind_of(entry):
    name, _, _, columns = entry
    if name in ("small", "down"):
        return "small" if name == "small" else "tall"
    return "part" if columns == 256 else "wide"


def summed_in_kernel(factors, small_grads):
    fa1, fdj, fo, fdhr, fa2, fdu, fg, fdm = factors
    slots, length, width = fa1.shape
    inner = fg.shape[2]
    owners = 16
    depth = inner // width
    narrow = 256
    a_rows, b_rows = width // owners, inner // owners
    packed = small_grads.size // owners
    lanes = 128
    s_rows = -(-packed // (8 * lanes)) * 8
    small = small_grads.reshape(owners, packed)
    small = jnp.pad(small, ((0, 0), (0, s_rows * lanes - packed)))
    small = small.reshape(4, 2, 2, s_rows, lanes)
    plan = [
        ("qkv", 0, False, width),
        ("qkv", 1, True, width),
        ("down", 0, False, narrow),
        ("small", 0, False, 0),
        ("qkv", 2, False, width),
        ("down", 1, False, narrow),
        ("out", 0, True, width),
        ("up", 0, False, width),
        ("up", 1, False, width),
        ("up", 2, False, width),
        ("up", 9, False, narrow),
        ("up", 10, False, narrow),
        ("up", 11, False, narrow),
        ("down", 2, False, narrow),
    ]
    lags = (3, 2, True)
    total = len(plan)
    s_block = small.shape[3:]
    vmem = pl.BlockSpec(memory_space=pltpu.VMEM)
    anywhere = pl.BlockSpec(memory_space=pl.ANY)

    def of_kind(kind, slots_of, block):
        mine = [entry for entry in plan if kind_of(entry) == kind]
        across = sum(not entry[2] for entry in mine)
        leads = ((slots_of, 4, 2, 2), (len(mine), 4, 2), (across, 4), (across, 3), (across, 3))
        return [pltpu.VMEM(lead + block, F32) for lead in leads]

    line_count = sum(line_first for _, _, line_first, _ in plan)
    a_block = (a_rows, width)
    *grads, small_grad = pl.pallas_call(
        functools.partial(gradients_kernel, (width, narrow, depth), plan, lags),
        out_shape=(
            jax.ShapeDtypeStruct((1, a_rows, 3 * width), F32),
            jax.ShapeDtypeStruct((1, a_rows, width), F32),
            jax.ShapeDtypeStruct((1, a_rows, inner), F32),
            jax.ShapeDtypeStruct((1, b_rows, width), F32),
            jax.ShapeDtypeStruct(s_block, F32),
        ),
        in_specs=[anywhere] * 8 + [vmem],
        out_specs=(vmem,) * 5,
        scratch_shapes=[
            pltpu.VMEM((2, slots, length, width), BF),
            pltpu.VMEM((2, slots, length, width), BF),
            pltpu.VMEM((width, slots * length), BF),
            pltpu.VMEM((depth, width, slots * length), BF),
        ]
        + of_kind("wide", 2, a_block)
        + of_kind("tall", 1, (b_rows, narrow))
        + of_kind("part", 2, (a_rows, narrow))
        + [pltpu.VMEM(lead + s_block, F32) for lead in ((4, 2), (4,), (3,), (3,))]
        + [
            pltpu.VMEM((line_count,) + a_block, F32),
            pltpu.VMEM((line_count, 3, 2) + a_block, F32),
            pltpu.VMEM((line_count, 3, 2) + a_block, F32),
        ]
        + [pltpu.SemaphoreType.DMA((2,))]
        + [pltpu.SemaphoreType.DMA((total,))] * 4
        + [pltpu.SemaphoreType.DMA((total, 3))] * 4,
        compiler_params=pltpu.CompilerParams(
            collective_id=1, has_side_effects=True, vmem_limit_bytes=62 << 20
        ),
    )(*factors, small)
    return tuple(grads) + (small_grad.reshape(1, -1)[:, :packed],)


def reduced(factors, small_grads):
    if lax.axis_size("dp") == 16:
        return summed_in_kernel(factors, small_grads)
    return summed_by_parts(factors, small_grads)


def per_device(
    embeddings, cotangent, seg_ids, thought_pos, w_qkv, w_out, w_up, w_down, small_params
):
    section_out, *factors, small_grads = layers(
        embeddings, cotangent, seg_ids, thought_pos, w_qkv, w_out, w_up, w_down, small_params
    )
    return (section_out,) + tuple(reduced(factors, small_grads))


def solution(mesh):
    return jax.shard_map(
        per_device,
        mesh=mesh,
        in_specs=(
            P("dp", None, None),
            P("dp", None, None),
            P("dp", None),
            P("dp", None),
            P("pipe", None, None),
            P("pipe", None, None),
            P("pipe", None, None),
            P("pipe", None, None),
            P("pipe", None),
        ),
        out_specs=(
            P("pipe", "dp", None, None),
            P("pipe", "dp", None),
            P("pipe", "dp", None),
            P("pipe", "dp", None),
            P("pipe", "dp", None),
            P("pipe", "dp"),
        ),
        check_vma=False,
    )
```

```python
import functools

import jax
import jax.numpy as jnp
from jax import lax
from jax.experimental import pallas as pl
from jax.experimental.pallas import tpu as pltpu
from jax.sharding import PartitionSpec as P

HEADS = 12
BF = jnp.bfloat16
F32 = jnp.float32
MESH = pl.DeviceIdType.MESH
EPSILON = 1e-05
MASKED = -1000000000.0
NO_CAP = 3e38
LAT = 16
G1, B1, BQ, BV, BO, G2, B2, BU = 0, 1, 2, 3, 4, 5, 6, 7


def dot(a, b):
    return lax.dot_general(a, b, (((1,), (0,)), ((), ())), preferred_element_type=F32)


def dot_nt(a, b):
    return lax.dot_general(a, b, (((1,), (1,)), ((), ())), preferred_element_type=F32)


def dot_tn(a, b):
    return lax.dot_general(a, b, (((0,), (0,)), ((), ())), preferred_element_type=F32)


def exact_dot(a, b):
    return lax.dot_general(
        a,
        b,
        (((1,), (0,)), ((), ())),
        precision=lax.Precision.HIGHEST,
        preferred_element_type=F32,
    )


def normalized(values):
    centred = values - jnp.mean(values, -1, keepdims=True)
    spread = jnp.mean(centred * centred, -1, keepdims=True)
    scale = lax.rsqrt(spread + EPSILON)
    return centred * scale, scale


def norm_back(hat, scale, grad):
    along = jnp.mean(grad * hat, -1, keepdims=True)
    return scale * (grad - jnp.mean(grad, -1, keepdims=True) - hat * along)


def gelu_both(u):
    c = 0.7978845608028654
    square = u * u
    t = jnp.tanh(c * u * (1.0 + 0.044715 * square))
    half = 0.5 + 0.5 * t
    slope = half + (0.5 * c) * u * (1.0 - t * t) * (1.0 + (3 * 0.044715) * square)
    return u * half, slope


def softmax(scores, axis=-1):
    e = jnp.exp(scores - jnp.max(scores, axis, keepdims=True))
    return e * (1.0 / jnp.sum(e, axis, keepdims=True))


def layers_kernel(
    sizes,
    emb,
    cot,
    seg,
    tpos,
    wqkv_h,
    wout_h,
    wup_h,
    wdown_h,
    small,
    sec,
    fa1,
    fdj,
    fo,
    fdhr,
    fa2,
    fdu,
    fg,
    fdm,
    sg,
    sums,
    joint,
    stat,
    wqkv,
    wout,
    wup,
    wdown,
    xin,
    yb,
    dyb,
    jn,
    pr,
    hm,
    slope,
    a1,
    ob,
    a2,
    gb,
    dm,
    dub,
    dhr,
    djb,
    da,
    dob,
    dmt,
    dat,
    djt,
    cap,
    lat,
    thg,
    lx,
    lq,
    lp,
    lh,
    la2,
    lo,
    lg,
    lslope,
    wsem,
    osem,
    ysend,
    yrecv,
    gsend,
    grecv,
    lsend,
    lrecv,
    tsend,
    trecv,
):
    rows, length, width, inner, thoughts = sizes
    blocks = inner // width
    bd = BU + blocks
    pairs = HEADS // 2
    me = lax.axis_index("pipe")
    other = 1 - me

    weights = [
        pltpu.make_async_copy(source.at[0], target, wsem.at[number])
        for number, (source, target) in enumerate(
            ((wqkv_h, wqkv), (wout_h, wout), (wup_h, wup), (wdown_h, wdown))
        )
    ]
    for copy in weights:
        copy.start()
    barrier = pltpu.get_barrier_semaphore()
    pl.semaphore_signal(barrier, inc=1, device_id={"pipe": other}, device_id_type=MESH)
    pl.semaphore_wait(barrier, 1)
    sums[...] = jnp.zeros_like(sums)
    joint[:, 0:width] = small[:, BQ * width : (BQ + 1) * width]
    joint[:, width : 2 * width] = jnp.zeros((1, width), F32)
    joint[:, 2 * width : 3 * width] = small[:, BV * width : (BV + 1) * width]

    def remote(source, target, send, recv):
        return pltpu.make_async_remote_copy(
            src_ref=source,
            dst_ref=target,
            send_sem=send,
            recv_sem=recv,
            device_id={"pipe": other},
            device_id_type=MESH,
        )

    def send_y(k):
        return remote(yb.at[k], xin.at[k], ysend.at[k], yrecv.at[k])

    def send_grad(k):
        return remote(yb.at[k], dyb.at[k], gsend.at[k], grecv.at[k])

    def send_lat(r):
        return remote(lat.at[r], lat.at[r], lsend.at[r], lrecv.at[r])

    def send_thoughts(r):
        return remote(thg.at[r], thg.at[r], tsend.at[r], trecv.at[r])

    def started(source, target, number):
        copy = pltpu.make_async_copy(source, target, osem.at[number])
        copy.start()
        return copy

    def settle(pending, number, source, target):
        @pl.when(pending)
        def _():
            pltpu.make_async_copy(source, target.at[0], osem.at[number]).wait()

    def finish(copies):
        for copy in copies:
            copy.wait()

    def each_chunk(step, count):
        def body(i, carry):
            step(pl.ds(pl.multiple_of(i * count, count), count), i * count)
            return carry

        lax.fori_loop(0, length // count, body, 0)

    def loop(count, step):
        def body(i, carry):
            step(i)
            return carry

        lax.fori_loop(0, count, body, 0)

    def add_columns(number, values):
        sums[number] += jnp.sum(values.astype(F32).reshape(-1, 8, width), 0)

    def row(number):
        return small[:, group(number)]

    def group(number):
        return slice(number * width, (number + 1) * width)

    lane = lax.broadcasted_iota(jnp.int32, (1, 128), 1)
    low = lane < 64
    halves = (jnp.where(low, 1.0, 0.0).astype(BF), jnp.where(low, 0.0, 1.0).astype(BF))

    def first_length(r):
        segment = seg[pl.ds(r, 1), :]
        return jnp.sum(jnp.where(segment == 0, 1.0, 0.0), -1, keepdims=True).astype(jnp.int32)

    def set_cap(r):
        first = first_length(r)
        query = lax.broadcasted_iota(jnp.int32, (length, length), 0)
        key = lax.broadcasted_iota(jnp.int32, (length, length), 1)
        lowest = jnp.where(query >= first, first, 0)
        cap[...] = jnp.where((key <= query) & (key >= lowest), NO_CAP, MASKED)

    def positions(r, shift, axis=0):
        shape = (LAT, 1) if axis == 0 else (1, LAT)
        number = lax.broadcasted_iota(jnp.int32, shape, axis)
        result = jnp.full(shape, -1, jnp.int32)
        for j in range(thoughts):
            result = jnp.where(number == j, tpos[r, j] - shift, result)
        return result

    def selector_turned(r, shift):
        place = positions(r, shift, 1)
        return jnp.where(lax.broadcasted_iota(jnp.int32, (length, LAT), 0) == place, 1.0, 0.0)

    def selector(place):
        return jnp.where(lax.broadcasted_iota(jnp.int32, (LAT, length), 1) == place, 1.0, 0.0)

    def unmarked(r, start):
        place = lax.broadcasted_iota(jnp.int32, (32, 1), 0) + start
        keep = jnp.ones((32, 1), F32)
        for j in range(thoughts):
            keep = jnp.where(place == tpos[r, j], 0.0, keep)
        return keep

    def head_lanes(part, hp):
        start = part * width + hp * 128
        if isinstance(hp, int):
            return slice(start, start + 128)
        return pl.ds(pl.multiple_of(start, 128), 128)

    def norm_rows(x, target, k, which, gain, shift, more=None):
        def step(part, _):
            values = x[part, :]
            center = jnp.mean(values, -1, keepdims=True)
            centred = values - center
            scale = lax.rsqrt(jnp.mean(centred * centred, -1, keepdims=True) + EPSILON)
            stat[k, 2 * which, part, :] = center
            stat[k, 2 * which + 1, part, :] = scale
            target[part, :] = (centred * scale * row(gain) + row(shift)).astype(BF)
            if more is not None:
                more(part, values)

        each_chunk(step, 128)

    def norm_rows_back(x, part, k, which, gain, shift):
        scale = stat[k, 2 * which + 1, part, :]
        hat = (x[part, :] - stat[k, 2 * which, part, :]) * scale
        grad = da[part, :]
        add_columns(gain, grad * hat)
        add_columns(shift, grad)
        return norm_back(hat, scale, grad * row(gain))

    def forward(k, x, y, pending, first=None):
        def need(number):
            if first is not None:

                @pl.when(first)
                def _():
                    weights[number].wait()

        settle(pending, 0, a1, fa1)
        norm_rows(x, a1, k, 0, G1, B1)
        started(a1, fa1.at[k], 0)
        need(0)
        settle(pending, 1, ob, fo)

        for part in range(3):
            joined = dot(a1[...], wqkv[:, group(part)]) + joint[:, group(part)]
            jn[k, :, group(part)] = joined.astype(BF)
        for hp in range(pairs):
            q = jn[k, :, head_lanes(0, hp)]
            key = jn[k, :, head_lanes(1, hp)]
            value = jn[k, :, head_lanes(2, hp)]
            out = []
            for h in range(2):
                scores = dot_nt(q * (halves[h] * 0.125), key)
                chance = softmax(jnp.minimum(scores, cap[...])).astype(BF)
                pr[k, 2 * hp + h] = chance
                out.append(dot(chance, value))
            ob[:, head_lanes(0, hp)] = jnp.where(low, out[0], out[1]).astype(BF)
        started(ob, fo.at[k], 1)
        need(1)
        settle(pending, 2, a2, fa2)
        hm[k] = x[...] + dot(ob[...], wout[...]) + row(BO)

        def begin(part, values):
            y[part, :] = values + row(bd)

        norm_rows(hm.at[k], a2, k, 1, G2, B2, begin)
        started(a2, fa2.at[k], 2)
        need(2)
        need(3)
        settle(pending, 3, gb, fg)

        for c in range(blocks):
            part = group(c)
            g, d = gelu_both(dot(a2[...], wup[:, part]) + row(BU + c))
            gb[:, part] = g.astype(BF)
            slope[k, part, :] = d.astype(BF).T
            y[...] += dot(gb[:, part], wdown[part, :])
        started(gb, fg.at[k], 3)

    def backward(k, x, dy, dx, pending):
        def step(part, _):
            branch = dy[part, :].astype(BF)
            dm[part, :] = branch
            add_columns(bd, branch)

        settle(pending, 4, dm, fdm)
        each_chunk(step, 64)
        started(dm, fdm.at[k], 4)
        dmt[...] = dm[...].T
        dat[...] = jnp.zeros_like(dat)
        settle(pending, 5, dub, fdu)

        def mlp(c):
            part = pl.ds(pl.multiple_of(c * width, width), width)
            grad = (dot(wdown[part, :], dmt[...]) * slope[k, part, :]).astype(BF)
            dat[...] += dot(wup[:, part], grad)
            turned = grad.T
            dub[:, part] = turned
            add_columns(BU + c, turned)

        loop(blocks, mlp)
        da[...] = dat[...].T
        started(dub, fdu.at[k], 5)
        settle(pending, 6, dhr, fdhr)

        def step_two(part, _):
            middle = dy[part, :] + norm_rows_back(hm.at[k], part, k, 1, G2, B2)
            dy[part, :] = middle
            branch = middle.astype(BF)
            dhr[part, :] = branch
            add_columns(BO, branch)

        each_chunk(step_two, 64)
        started(dhr, fdhr.at[k], 6)
        dmt[...] = dhr[...].T
        dob[...] = dot(wout[...], dmt[...]).astype(BF).T
        settle(pending, 7, djb, fdj)

        def heads(hp):
            q = jn[k, :, head_lanes(0, hp)]
            key = jn[k, :, head_lanes(1, hp)]
            value = jn[k, :, head_lanes(2, hp)]
            grad_out = dob[:, head_lanes(0, hp)]
            dq, dk, dv = [], [], []
            for h in range(2):
                chance = pr[k, 2 * hp + h]
                chance_full = chance.astype(F32)
                inner_part = chance_full * dot_nt(grad_out * halves[h], value)
                total = jnp.sum(inner_part, -1, keepdims=True)
                grad_scores = (inner_part - chance_full * total).astype(BF)
                dq.append(dot(grad_scores, key))
                dk.append(dot_tn(grad_scores, q))
                dv.append(dot_tn(chance, grad_out))
            djb[:, head_lanes(0, hp)] = (jnp.where(low, dq[0], dq[1]) * 0.125).astype(BF)
            djb[:, head_lanes(1, hp)] = (jnp.where(low, dk[0], dk[1]) * 0.125).astype(BF)
            djb[:, head_lanes(2, hp)] = jnp.where(low, dv[0], dv[1]).astype(BF)

        loop(pairs, heads)
        started(djb, fdj.at[k], 7)
        into_input(k, x, dy, dx)

    def into_input(k, x, middle, dx):
        djt[...] = djb[...].T
        da[...] = dot(wqkv[...], djt[...]).T

        def step(part, _):
            add_columns(BQ, djb[part, group(0)])
            add_columns(BV, djb[part, group(2)])
            dx[part, :] = middle[part, :] + norm_rows_back(x, part, k, 0, G1, B1)

        each_chunk(step, 64)

    def forward_latent(r):
        x = xin.at[r]
        norm_rows(x, a1, r, 0, G1, B1)
        copies = [started(a1, fa1.at[r], 0)]
        jn[r, :, group(1)] = dot(a1[...], wqkv[:, group(1)]).astype(BF)
        jn[r, :, group(2)] = (dot(a1[...], wqkv[:, group(2)]) + row(BV)).astype(BF)
        place = positions(r, 1)
        chosen = exact_dot(selector(place), x[...])
        lx[r] = chosen
        hat, _ = normalized(chosen)
        normed = (hat * row(G1) + row(B1)).astype(BF)
        lq[r] = (dot(normed, wqkv[:, group(0)]) + row(BQ)).astype(BF)
        first = first_length(r)
        key_place = lax.broadcasted_iota(jnp.int32, (LAT, length), 1)
        lowest = jnp.where(place >= first, first, 0)
        limit = jnp.where((key_place <= place) & (key_place >= lowest), NO_CAP, MASKED)

        def heads(hp):
            q = lq[r, :, head_lanes(0, hp)]
            key = jn[r, :, head_lanes(1, hp)]
            value = jn[r, :, head_lanes(2, hp)]
            out = []
            for h in range(2):
                scores = dot_nt(q * (halves[h] * 0.125), key)
                chance = softmax(jnp.minimum(scores, limit)).astype(BF)
                lp[r, 2 * hp + h] = chance
                out.append(dot(chance, value))
            lo[r, :, head_lanes(0, hp)] = jnp.where(low, out[0], out[1]).astype(BF)

        for hp in range(pairs):
            heads(hp)
        middle = chosen + dot(lo[r], wout[...]) + row(BO)
        lh[r] = middle
        hat, _ = normalized(middle)
        la2[r] = (hat * row(G2) + row(B2)).astype(BF)
        lat[r] = middle + row(bd)

        def mlp(c):
            part = group(c)
            u = dot(la2[r], wup[:, part]) + row(BU + c)
            g, d = gelu_both(u)
            lg[r, :, part] = g.astype(BF)
            lslope[r, :, part] = d.astype(BF)
            lat[r] += dot(lg[r, :, part], wdown[part, :])

        for c in range(blocks):
            mlp(c)
        return copies

    def backward_latent(r, dx):
        grad_result = thg[r]
        branch = grad_result.astype(BF)
        top = slice(0, LAT)
        add_columns(bd, branch)
        dm[top, :] = branch
        a2[top, :] = la2[r]
        ob[top, :] = lo[r]
        gb[top, :] = lg[r]
        copies = [
            started(dm, fdm.at[r], 4),
            started(a2, fa2.at[r], 2),
            started(ob, fo.at[r], 1),
            started(gb, fg.at[r], 3),
        ]
        da[top, :] = jnp.zeros((LAT, width), F32)

        def mlp(c):
            part = group(c)
            grad = (dot_nt(dm[top, :], wdown[part, :]) * lslope[r, :, part]).astype(BF)
            dub[top, part] = grad
            add_columns(BU + c, grad)
            da[top, :] += dot_nt(grad, wup[:, part])

        for c in range(blocks):
            mlp(c)
        copies.append(started(dub, fdu.at[r], 5))
        hat, scale = normalized(lh[r])
        grad = da[top, :]
        add_columns(G2, grad * hat)
        add_columns(B2, grad)
        middle = grad_result + norm_back(hat, scale, grad * row(G2))
        rounded = middle.astype(BF)
        dhr[top, :] = rounded
        add_columns(BO, rounded)
        copies.append(started(dhr, fdhr.at[r], 6))
        spread = selector_turned(r, 1)
        dyb[r] = exact_dot(spread, middle)
        place = positions(r, 1, 1)
        first = first_length(r)
        key_place = lax.broadcasted_iota(jnp.int32, (length, LAT), 0)
        lowest = jnp.where(place >= first, first, 0)
        limit = jnp.where((key_place <= place) & (key_place >= lowest), NO_CAP, MASKED)
        dob[top, :] = dot_nt(rounded, wout[...]).astype(BF)

        def heads(hp):
            q = lq[r, :, head_lanes(0, hp)]
            key = jn[r, :, head_lanes(1, hp)]
            value = jn[r, :, head_lanes(2, hp)]
            grad_out = dob[top, head_lanes(0, hp)]
            dq, dk, dv = [], [], []
            for h in range(2):
                grad_masked = grad_out * halves[h]
                chance = lp[r, 2 * hp + h].astype(F32)
                inner_part = chance * dot_nt(grad_masked, value)
                total = jnp.sum(inner_part, -1, keepdims=True)
                dq.append(dot((inner_part - chance * total).astype(BF), key))
                scores = dot_nt(key, q * (halves[h] * 0.125))
                chance = softmax(jnp.minimum(scores, limit), 0)
                inner_part = chance * dot_nt(value, grad_masked)
                total = jnp.sum(inner_part, 0, keepdims=True)
                dk.append(dot((inner_part - chance * total).astype(BF), q))
                dv.append(dot(chance.astype(BF), grad_out))
            grad_q = (jnp.where(low, dq[0], dq[1]) * 0.125).astype(BF)
            djb[:, head_lanes(0, hp)] = dot(spread.astype(BF), grad_q).astype(BF)
            djb[:, head_lanes(1, hp)] = (jnp.where(low, dk[0], dk[1]) * 0.125).astype(BF)
            djb[:, head_lanes(2, hp)] = jnp.where(low, dv[0], dv[1]).astype(BF)

        for hp in range(pairs):
            heads(hp)
        copies.append(started(djb, fdj.at[r], 7))
        into_input(r, xin.at[r], dyb.at[r], dx)
        return copies

    staged = (
        (a1, fa1), (ob, fo), (a2, fa2), (gb, fg), (dm, fdm), (dub, fdu), (dhr, fdhr), (djb, fdj)
    )

    def settle_all(count, first=0):
        for number in range(first, first + count):
            source, target = staged[number]
            pltpu.make_async_copy(source, target.at[0], osem.at[number]).wait()

    @pl.when(me == 0)
    def _():
        def forward_step(k, carry):
            r = lax.rem(k, rows)
            set_cap(r)

            @pl.when(k < rows)
            def _():
                xin[k] = emb[r].astype(F32)

            @pl.when(k >= rows)
            def _():
                send_lat(r).wait_recv()
                xin[k] = exact_dot(selector_turned(r, 0), lat[r])

                def step(part, start):
                    xin[k, part, :] += emb[r, part, :].astype(F32) * unmarked(r, start)

                each_chunk(step, 32)

            forward(k, xin.at[k], yb.at[k], k > 0, first=k == 0)
            send_y(k).start()
            return carry

        lax.fori_loop(0, 2 * rows, forward_step, 0)
        settle_all(4)

        def backward_step(i, carry):
            k = lax.rem(i + rows, 2 * rows)
            r = lax.rem(i, rows)
            send_y(k).wait_send()
            send_grad(k).wait_recv()
            backward(k, xin.at[k], dyb.at[k], yb.at[k], i > 0)

            @pl.when(i < rows)
            def _():
                thg[r] = exact_dot(selector(positions(r, 0)), yb[k])
                send_thoughts(r).start()

            @pl.when(i >= rows)
            def _():
                def step(part, start):
                    yb[k, part, :] += yb[rows + r, part, :] * unmarked(r, start)

                each_chunk(step, 32)
                started(yb.at[k], sec.at[0, r], 8).wait()

            return carry

        lax.fori_loop(0, 2 * rows, backward_step, 0)
        settle_all(4, 4)

        def drain(r, carry):
            send_thoughts(r).wait_send()
            return carry

        lax.fori_loop(0, rows, drain, 0)

    @pl.when(me == 1)
    def _():
        finish(weights)

        def latent_step(r, carry):
            send_y(r).wait_recv()
            copies = forward_latent(r)
            send_lat(r).start()
            finish(copies)
            return carry

        lax.fori_loop(0, rows, latent_step, 0)

        def language_step(r, carry):
            k = rows + r
            set_cap(r)
            send_y(k).wait_recv()
            forward(k, xin.at[k], dyb.at[k], r > 0)
            result = started(dyb.at[k], sec.at[0, r], 8)
            dyb[r] = cot[r].astype(F32)
            backward(k, xin.at[k], dyb.at[r], yb.at[k], r > 0)
            send_grad(k).start()
            result.wait()
            return carry

        lax.fori_loop(0, rows, language_step, 0)
        settle_all(8)
        for buffer in (dm, a2, ob, gb, dub, dhr):
            buffer[...] = jnp.zeros_like(buffer)

        def latent_back_step(r, carry):
            send_thoughts(r).wait_recv()
            copies = backward_latent(r, yb.at[r])
            send_grad(r).start()
            finish(copies)
            return carry

        lax.fori_loop(0, rows, latent_back_step, 0)

        def drain(r, carry):
            send_lat(r).wait_send()
            send_grad(r).wait_send()
            send_grad(rows + r).wait_send()
            return carry

        lax.fori_loop(0, rows, drain, 0)

    sg[...] = jnp.sum(sums[...], 1)


def layers(emb, cot, seg, tpos, w_qkv, w_out, w_up, w_down, small):
    rows, length, width = emb.shape
    inner = w_up.shape[2]
    thoughts = tpos.shape[1]
    slots = 2 * rows
    packed = small.shape[1] // width
    vmem = pl.BlockSpec(memory_space=pltpu.VMEM)
    anywhere = pl.BlockSpec(memory_space=pl.ANY)
    smem = pl.BlockSpec(memory_space=pltpu.SMEM)

    def factor(columns):
        return jax.ShapeDtypeStruct((slots, length, columns), BF)

    def block(columns, kind=BF):
        return pltpu.VMEM((length, columns), kind)

    def few(columns, kind=BF):
        return pltpu.VMEM((rows, LAT, columns), kind)

    sizes = (rows, length, width, inner, thoughts)
    return pl.pallas_call(
        functools.partial(layers_kernel, sizes),
        out_shape=(
            jax.ShapeDtypeStruct((1, rows, length, width), F32),
            factor(width),
            factor(3 * width),
            factor(width),
            factor(width),
            factor(width),
            factor(inner),
            factor(inner),
            factor(width),
            jax.ShapeDtypeStruct((packed, width), F32),
        ),
        in_specs=[vmem, vmem, vmem, smem] + [anywhere] * 4 + [vmem],
        out_specs=(anywhere,) * 9 + (vmem,),
        scratch_shapes=[
            pltpu.VMEM((packed, 8, width), F32),
            pltpu.VMEM((1, 3 * width), F32),
            pltpu.VMEM((slots, 4, length, 1), F32),
            pltpu.VMEM((width, 3 * width), BF),
            pltpu.VMEM((width, width), BF),
            pltpu.VMEM((width, inner), BF),
            pltpu.VMEM((inner, width), BF),
            pltpu.VMEM((slots, length, width), F32),
            pltpu.VMEM((slots, length, width), F32),
            pltpu.VMEM((slots, length, width), F32),
            pltpu.VMEM((slots, length, 3 * width), BF),
            pltpu.VMEM((slots, HEADS, length, length), BF),
            pltpu.VMEM((slots, length, width), F32),
            pltpu.VMEM((slots, inner, length), BF),
            block(width),
            block(width),
            block(width),
            block(inner),
            block(width),
            block(inner),
            block(width),
            block(3 * width),
            block(width, F32),
            block(width),
            pltpu.VMEM((width, length), BF),
            pltpu.VMEM((width, length), F32),
            pltpu.VMEM((3 * width, length), BF),
            block(length, F32),
            few(width, F32),
            few(width, F32),
            few(width, F32),
            few(width),
            pltpu.VMEM((rows, HEADS, LAT, length), BF),
            few(width, F32),
            few(width),
            few(width),
            few(inner),
            few(inner),
            pltpu.SemaphoreType.DMA((4,)),
            pltpu.SemaphoreType.DMA((9,)),
        ]
        + [pltpu.SemaphoreType.DMA((slots,))] * 4
        + [pltpu.SemaphoreType.DMA((rows,))] * 4,
        compiler_params=pltpu.CompilerParams(
            collective_id=0, has_side_effects=True, vmem_limit_bytes=62 << 20
        ),
    )(emb, cot, seg, tpos, w_qkv, w_out, w_up, w_down, small)


def summed_by_parts(factors, small_grads):
    fa1, fdj, fo, fdhr, fa2, fdu, fg, fdm = factors

    def product(left, right):
        whole = jnp.einsum("ktm,ktn->mn", left, right, preferred_element_type=F32)
        return lax.psum_scatter(whole[None], "dp", scatter_dimension=1, tiled=True)

    small = lax.psum_scatter(
        small_grads.reshape(1, -1), "dp", scatter_dimension=1, tiled=True
    )
    return product(fa1, fdj), product(fo, fdhr), product(fa2, fdu), product(fg, fdm), small


def gradients_kernel(
    sizes,
    plan,
    lags,
    fa1,
    fdj,
    fo,
    fdhr,
    fa2,
    fdu,
    fg,
    fdm,
    small,
    gqkv,
    gout,
    gup,
    gdown,
    gsmall,
    left,
    right,
    lt,
    lt_down,
    wa,
    ra,
    xa,
    ua,
    na,
    wb,
    rb,
    xb,
    ub,
    nb,
    rs,
    xs,
    us,
    ns,
    xl,
    ul,
    nl,
    kept,
    lsem,
    pair_send,
    pair_recv,
    side_send,
    side_recv,
    up_send,
    up_recv,
    down_send,
    down_recv,
    over_send,
    over_recv,
):
    width, narrow, depth = sizes
    side_lag, hop = lags
    me = lax.axis_index("dp")
    core = lax.rem(me, 2)
    side = lax.rem(me // 2, 2)
    level = me // 4
    partner = me + 1 - 2 * core
    beside = me + 2 - 4 * side
    above, below = me + 4, me - 4
    plane = lax.axis_index("pipe")

    def remote(source, target, send, recv, device):
        return pltpu.make_async_remote_copy(
            src_ref=source,
            dst_ref=target,
            send_sem=send,
            recv_sem=recv,
            device_id={"dp": device},
            device_id_type=MESH,
        )

    buffers = {"wide": (wa, ra, xa, ua, na), "tall": (wb, rb, xb, ub, nb)}
    lefts = {"qkv": fa1, "out": fo, "up": fa2, "down": fg}
    rights = {"qkv": fdj, "out": fdhr, "up": fdu, "down": fdm}
    total = len(plan)
    names = [entry[0] for entry in plan]
    guest = names.index("guest")
    exported = 0
    steps = []
    turned = None
    for number, (name, part, _, columns) in enumerate(plan):
        if name in ("small", "guest"):
            continue
        if name == "down":
            for block in range(depth):
                steps.append((number, name, True, block, None, 0))
                steps.append((number, name, False, block, part, columns))
            continue
        if name != turned:
            steps.append((number, name, True, 0, None, 0))
            turned = name
        steps.append((number, name, False, 0, part, columns))

    def loads(index):
        _, name, turn, block, part, columns = steps[index]
        slot = index % 2
        if turn:
            source = lefts[name].at[:, :, block * width : (block + 1) * width]
            return pltpu.make_async_copy(source, left.at[slot], lsem.at[slot])
        return pltpu.make_async_copy(
            rights[name].at[:, :, part * columns : (part + 1) * columns],
            right.at[slot, :, :, 0:columns],
            lsem.at[slot],
        )

    def start_loads(index):
        if index < len(steps):
            loads(index).start()

    start_loads(0)

    barrier = pltpu.get_barrier_semaphore()

    def greet(device):
        pl.semaphore_signal(barrier, inc=1, device_id={"dp": device}, device_id_type=MESH)

    greet(partner)
    greet(beside)

    @pl.when(level < 3)
    def _():
        greet(above)

    @pl.when(level > 0)
    def _():
        greet(below)

    @pl.when(plane == 1)
    def _():
        pl.semaphore_signal(barrier, inc=1, device_id={"pipe": 0}, device_id_type=MESH)

    pl.semaphore_wait(barrier, 2 + (level + 2) // 3 + (5 - level) // 3 + 1 - plane)

    targets = {"qkv": gqkv, "out": gout, "up": gup, "down": gdown}
    views = []
    previous = {}
    order = {}
    made = {}
    last_of = {number: True for number in range(total)}
    for number, (name, part, line_first, columns) in enumerate(plan):
        kind = kind_of(plan[number])
        if kind == "small":
            views.append((small, rs, xs, us, ns, gsmall))
            previous[number] = None
            continue
        w, r, x, u, n = buffers[kind]
        order.setdefault(kind, []).append(number)
        index = len(order[kind]) - 1
        along = sum(plan[other][2] for other in order[kind][:index])
        if name == "guest":
            views.append(
                (None, r.at[index], x.at[index - along], u.at[index - along], n.at[index - along], kept)
            )
            continue
        made.setdefault(kind, []).append(number)
        turn = len(made[kind]) - 1
        slots_of = w.shape[0]
        previous[number] = made[kind][turn - slots_of] if turn >= slots_of else None
        if previous[number] is not None:
            last_of[previous[number]] = False
        place = targets[name].at[0, :, part * columns : (part + 1) * columns]
        if line_first:
            further = (xl.at[along], ul.at[along], nl.at[along], place)
        else:
            further = (x.at[index - along], u.at[index - along], n.at[index - along], place)
        views.append((w.at[turn % slots_of], r.at[index]) + further)

    def over(source, target, number):
        return pltpu.make_async_remote_copy(
            src_ref=source,
            dst_ref=target,
            send_sem=over_send.at[number],
            recv_sem=over_recv.at[number],
            device_id={"pipe": 1 - plane},
            device_id_type=MESH,
        )

    def hand_over():
        return over(views[exported][1], views[guest][1], 0)

    def hand_back():
        return over(kept, views[exported][5], 1)

    def where(number, condition=None):
        if number in (exported, guest):
            condition = plane == 1 if condition is None else condition & (plane == 1)
        if condition is None:
            return lambda body: body()
        return pl.when(condition)

    def pair_copy(number):
        w, r = views[number][:2]
        return remote(
            w.at[:, :, 1 - core], r, pair_send.at[number], pair_recv.at[number], partner
        )

    def side_copy(number):
        r, x = views[number][1:3]
        source = r.at[level, 1 - side] if plan[number][2] else r.at[:, 1 - side]
        return remote(source, x, side_send.at[number], side_recv.at[number], beside)

    def along_line(number):
        r, x = views[number][1:3]
        return r if plan[number][2] else x

    def up_copy(number, goal, source=None):
        u = views[number][3]
        return remote(
            u.at[goal - 1] if source is None else source,
            u.at[goal - 1],
            up_send.at[number, goal - 1],
            up_recv.at[number, goal - 1],
            above,
        )

    def down_copy(number, goal, source=None):
        n = views[number][4]
        return remote(
            n.at[goal] if source is None else source,
            n.at[goal],
            down_send.at[number, goal],
            down_recv.at[number, goal],
            below,
        )

    def start_line(number):
        base = along_line(number)

        @pl.when(level == 0)
        def _():
            for goal in (3, 2, 1):
                up_copy(number, goal, base.at[goal]).start()

        @pl.when(level == 3)
        def _():
            for goal in (0, 1, 2):
                down_copy(number, goal, base.at[goal]).start()

    position = {"step": 0}
    slots, length = left.shape[1:3]

    def turn_block(slot, target):
        def body(t, carry):
            tokens = pl.ds(pl.multiple_of(t * length, length), length)
            target[:, tokens] = left[slot, t].T
            return carry

        lax.fori_loop(0, slots, body, 0)

    def right_part(slot, lanes):
        part = right[slot, :, :, lanes]
        return part.reshape(slots * length, part.shape[2])

    def multiply(slot, w, columns):
        def tile(t, carry):
            lanes = pl.ds(pl.multiple_of(t * narrow, narrow), narrow)
            product = dot(lt[...], right_part(slot, lanes))
            w[:, :, :, :, lanes] = product.reshape(w.shape[:4] + (narrow,))
            return carry

        lax.fori_loop(0, columns // narrow, tile, 0)


    def produce(number):
        name = plan[number][0]
        if name == "guest":
            return
        if name != "small":
            if previous[number] is not None:
                pair_copy(previous[number]).wait_send()
            w = views[number][0]
            while position["step"] < len(steps) and steps[position["step"]][0] == number:
                index = position["step"]
                position["step"] += 1
                _, source, turn, block, _, columns = steps[index]
                start_loads(index + 1)
                loads(index).wait()
                if turn:
                    turn_block(index % 2, lt_down if source == "down" else lt)
                elif source == "down":
                    part = right_part(index % 2, slice(0, narrow))
                    w[block] = dot(lt_down[...], part).reshape(w.shape[1:])
                else:
                    multiply(index % 2, w, columns)
        pair_copy(number).start()

    def stage_pair(number):
        if number == guest:

            @pl.when(plane == 1)
            def _():
                hand_over().wait_recv()
                side_copy(number).start()

            return
        w, r = views[number][:2]
        pair_copy(number).wait_recv()

        def add(z, carry):
            for s in range(2):
                r[z, s] += w[z, s, core]
            return carry

        lax.fori_loop(0, 4, add, 0)
        if plan[number][2]:
            start_line(number)
            return

        @where(number)
        def _():
            side_copy(number).start()

        if number == exported:

            @pl.when(plane == 0)
            def _():
                hand_over().start()

    def stage_side(number):
        if plan[number][2]:
            return

        @where(number)
        def _():
            r, x = views[number][1:3]
            side_copy(number).wait_recv()

            def add(z, carry):
                x[z] += r[z, side]
                return carry

            lax.fori_loop(0, 4, add, 0)
            start_line(number)

    def stage_up(number, height):
        u = views[number][3]
        base = along_line(number)

        @where(number, level == height)
        def _():
            for goal in range(3, height - 1, -1):
                up_copy(number, goal).wait_recv()
                if goal > height:
                    u[goal - 1] += base[goal]
                    up_copy(number, goal).start()

    def stage_down(number, height):
        n = views[number][4]
        base = along_line(number)

        @where(number, level == height)
        def _():
            for goal in range(0, height + 1):
                down_copy(number, goal).wait_recv()
                if goal < height:
                    n[goal] += base[goal]
                    down_copy(number, goal).start()

    def stage_sum(number):
        u, n, place = views[number][3:]
        base = along_line(number)

        @where(number, level > 0)
        def _():
            base[level] += u[level - 1]

        @where(number, level < 3)
        def _():
            base[level] += n[level]

        if plan[number][2]:
            side_copy(number).start()
            return

        @where(number)
        def _():
            place[...] = base[level]
            if number == guest:
                hand_back().start()

    def stage_last(number):
        if plan[number][2]:
            r, x = views[number][1:3]
            side_copy(number).wait_recv()
            views[number][5][...] = r[level, side] + x[...]

    def at(stage, number, *more):
        if 0 <= number < total:
            stage(number, *more)

    for moment in range(total + side_lag + 3 * hop + 1):
        at(produce, moment)
        at(stage_pair, moment - 1)
        at(stage_side, moment - side_lag)
        for height in range(4):
            if height > 0:
                at(stage_up, moment - side_lag - hop * height, height)
            if height < 3:
                at(stage_down, moment - side_lag - hop * (3 - height), height)
        at(stage_sum, moment - side_lag - 3 * hop)
        at(stage_last, moment - side_lag - 3 * hop - 1)
    for number in range(total):
        if last_of[number] and number != guest:
            pair_copy(number).wait_send()

        @where(number)
        def _():
            side_copy(number).wait_send()

        for goal in (1, 2, 3):

            @where(number, goal > level)
            def _():
                up_copy(number, goal).wait_send()

        for goal in (0, 1, 2):

            @where(number, goal < level)
            def _():
                down_copy(number, goal).wait_send()

    @pl.when(plane == 0)
    def _():
        hand_over().wait_send()
        hand_back().wait_recv()

    @pl.when(plane == 1)
    def _():
        hand_back().wait_send()


def kind_of(entry):
    return {"small": "small", "down": "tall"}.get(entry[0], "wide")


def summed_in_kernel(factors, small_grads):
    fa1, fdj, fo, fdhr, fa2, fdu, fg, fdm = factors
    slots, length, width = fa1.shape
    inner = fg.shape[2]
    owners = 16
    depth = inner // width
    narrow = 256
    a_rows, b_rows = width // owners, inner // owners
    packed = small_grads.size // owners
    lanes = 128
    s_rows = -(-packed // (8 * lanes)) * 8
    small = small_grads.reshape(owners, packed)
    small = jnp.pad(small, ((0, 0), (0, s_rows * lanes - packed)))
    small = small.reshape(4, 2, 2, s_rows, lanes)
    plan = [
        ("qkv", 0, False, width),
        ("qkv", 1, True, width),
        ("qkv", 2, False, width),
        ("small", 0, False, 0),
        ("out", 0, False, width),
        ("up", 0, False, width),
        ("down", 0, False, narrow),
        ("up", 1, True, width),
        ("down", 1, False, narrow),
        ("guest", 0, False, width),
        ("up", 2, False, width),
        ("up", 3, False, width),
        ("down", 2, False, narrow),
    ]
    lags = (3, 3)
    total = len(plan)
    s_block = small.shape[3:]
    vmem = pl.BlockSpec(memory_space=pltpu.VMEM)
    anywhere = pl.BlockSpec(memory_space=pl.ANY)

    def of_kind(kind, slots_of, block):
        mine = [entry for entry in plan if kind_of(entry) == kind]
        across = sum(not entry[2] for entry in mine)
        leads = ((slots_of, 4, 2, 2), (len(mine), 4, 2), (across, 4), (across, 3), (across, 3))
        return [pltpu.VMEM(lead + block, F32) for lead in leads]

    line_count = sum(line_first for _, _, line_first, _ in plan)
    a_block = (a_rows, width)
    *grads, small_grad = pl.pallas_call(
        functools.partial(gradients_kernel, (width, narrow, depth), plan, lags),
        out_shape=(
            jax.ShapeDtypeStruct((1, a_rows, 3 * width), F32),
            jax.ShapeDtypeStruct((1, a_rows, width), F32),
            jax.ShapeDtypeStruct((1, a_rows, inner), F32),
            jax.ShapeDtypeStruct((1, b_rows, width), F32),
            jax.ShapeDtypeStruct(s_block, F32),
        ),
        in_specs=[anywhere] * 8 + [vmem],
        out_specs=(vmem,) * 5,
        scratch_shapes=[
            pltpu.VMEM((2, slots, length, width), BF),
            pltpu.VMEM((2, slots, length, width), BF),
            pltpu.VMEM((width, slots * length), BF),
            pltpu.VMEM((width, slots * length), BF),
        ]
        + of_kind("wide", 2, a_block)
        + of_kind("tall", 1, (b_rows, narrow))
        + [pltpu.VMEM(lead + s_block, F32) for lead in ((4, 2), (4,), (3,), (3,))]
        + [
            pltpu.VMEM((line_count,) + a_block, F32),
            pltpu.VMEM((line_count, 3, 2) + a_block, F32),
            pltpu.VMEM((line_count, 3, 2) + a_block, F32),
            pltpu.VMEM(a_block, F32),
        ]
        + [pltpu.SemaphoreType.DMA((2,))]
        + [pltpu.SemaphoreType.DMA((total,))] * 4
        + [pltpu.SemaphoreType.DMA((total, 3))] * 4
        + [pltpu.SemaphoreType.DMA((2,))] * 2,
        compiler_params=pltpu.CompilerParams(
            collective_id=1, has_side_effects=True, vmem_limit_bytes=62 << 20
        ),
    )(*factors, small)
    return tuple(grads) + (small_grad.reshape(1, -1)[:, :packed],)


def reduced(factors, small_grads):
    if lax.axis_size("dp") == 16:
        return summed_in_kernel(factors, small_grads)
    return summed_by_parts(factors, small_grads)


def per_device(
    embeddings, cotangent, seg_ids, thought_pos, w_qkv, w_out, w_up, w_down, small_params
):
    section_out, *factors, small_grads = layers(
        embeddings, cotangent, seg_ids, thought_pos, w_qkv, w_out, w_up, w_down, small_params
    )
    return (section_out,) + tuple(reduced(factors, small_grads))


def solution(mesh):
    return jax.shard_map(
        per_device,
        mesh=mesh,
        in_specs=(
            P("dp", None, None),
            P("dp", None, None),
            P("dp", None),
            P("dp", None),
            P("pipe", None, None),
            P("pipe", None, None),
            P("pipe", None, None),
            P("pipe", None, None),
            P("pipe", None),
        ),
        out_specs=(
            P("pipe", "dp", None, None),
            P("pipe", "dp", None),
            P("pipe", "dp", None),
            P("pipe", "dp", None),
            P("pipe", "dp", None),
            P("pipe", "dp"),
        ),
        check_vma=False,
    )
```

```python
import functools

import jax
import jax.numpy as jnp
from jax import lax
from jax.experimental import pallas as pl
from jax.experimental.pallas import tpu as pltpu
from jax.sharding import PartitionSpec as P

HEADS = 12
BF = jnp.bfloat16
F32 = jnp.float32
MESH = pl.DeviceIdType.MESH
EPSILON = 1e-05
MASKED = -1000000000.0
NO_CAP = 3e38
LAT = 16
G1, B1, BQ, BV, BO, G2, B2, BU = 0, 1, 2, 3, 4, 5, 6, 7


def dot(a, b):
    return lax.dot_general(a, b, (((1,), (0,)), ((), ())), preferred_element_type=F32)


def dot_nt(a, b):
    return lax.dot_general(a, b, (((1,), (1,)), ((), ())), preferred_element_type=F32)


def dot_tn(a, b):
    return lax.dot_general(a, b, (((0,), (0,)), ((), ())), preferred_element_type=F32)


def exact_dot(a, b):
    return lax.dot_general(
        a,
        b,
        (((1,), (0,)), ((), ())),
        precision=lax.Precision.HIGHEST,
        preferred_element_type=F32,
    )


def normalized(values):
    centred = values - jnp.mean(values, -1, keepdims=True)
    spread = jnp.mean(centred * centred, -1, keepdims=True)
    scale = lax.rsqrt(spread + EPSILON)
    return centred * scale, scale


def norm_back(hat, scale, grad):
    along = jnp.mean(grad * hat, -1, keepdims=True)
    return scale * (grad - jnp.mean(grad, -1, keepdims=True) - hat * along)


def gelu_both(u):
    c = 0.7978845608028654
    square = u * u
    t = jnp.tanh(c * u * (1.0 + 0.044715 * square))
    half = 0.5 + 0.5 * t
    slope = half + (0.5 * c) * u * (1.0 - t * t) * (1.0 + (3 * 0.044715) * square)
    return u * half, slope


def softmax(scores, axis=-1):
    e = jnp.exp(scores - jnp.max(scores, axis, keepdims=True))
    return e * (1.0 / jnp.sum(e, axis, keepdims=True))


def layers_kernel(
    sizes,
    emb,
    cot,
    seg,
    tpos,
    wqkv_h,
    wout_h,
    wup_h,
    wdown_h,
    small,
    sec,
    fa1,
    fdj,
    fo,
    fdhr,
    fa2,
    fdu,
    fg,
    fdm,
    sg,
    sums,
    joint,
    stat,
    wqkv,
    wout,
    wup,
    wdown,
    xin,
    yb,
    dyb,
    jn,
    pr,
    hm,
    slope,
    a1,
    ob,
    a2,
    gb,
    dm,
    dub,
    dhr,
    djb,
    da,
    dob,
    dmt,
    dat,
    djt,
    cap,
    lat,
    thg,
    lx,
    lq,
    lp,
    lh,
    la2,
    lo,
    lg,
    lslope,
    wsem,
    osem,
    ysend,
    yrecv,
    gsend,
    grecv,
    lsend,
    lrecv,
    tsend,
    trecv,
):
    rows, length, width, inner, thoughts = sizes
    blocks = inner // width
    bd = BU + blocks
    pairs = HEADS // 2
    me = lax.axis_index("pipe")
    other = 1 - me

    weights = [
        pltpu.make_async_copy(source.at[0], target, wsem.at[number])
        for number, (source, target) in enumerate(
            ((wqkv_h, wqkv), (wout_h, wout), (wup_h, wup), (wdown_h, wdown))
        )
    ]
    for copy in weights:
        copy.start()
    barrier = pltpu.get_barrier_semaphore()
    pl.semaphore_signal(barrier, inc=1, device_id={"pipe": other}, device_id_type=MESH)
    pl.semaphore_wait(barrier, 1)
    sums[...] = jnp.zeros_like(sums)
    joint[:, 0:width] = small[:, BQ * width : (BQ + 1) * width]
    joint[:, width : 2 * width] = jnp.zeros((1, width), F32)
    joint[:, 2 * width : 3 * width] = small[:, BV * width : (BV + 1) * width]

    def remote(source, target, send, recv):
        return pltpu.make_async_remote_copy(
            src_ref=source,
            dst_ref=target,
            send_sem=send,
            recv_sem=recv,
            device_id={"pipe": other},
            device_id_type=MESH,
        )

    def send_y(k):
        return remote(yb.at[k], xin.at[k], ysend.at[k], yrecv.at[k])

    def send_grad(k):
        return remote(yb.at[k], dyb.at[k], gsend.at[k], grecv.at[k])

    def send_lat(r):
        return remote(lat.at[r], lat.at[r], lsend.at[r], lrecv.at[r])

    def send_thoughts(r):
        return remote(thg.at[r], thg.at[r], tsend.at[r], trecv.at[r])

    def started(source, target, number):
        copy = pltpu.make_async_copy(source, target, osem.at[number])
        copy.start()
        return copy

    def settle(pending, number, source, target):
        @pl.when(pending)
        def _():
            pltpu.make_async_copy(source, target.at[0], osem.at[number]).wait()

    def finish(copies):
        for copy in copies:
            copy.wait()

    def each_chunk(step, count):
        def body(i, carry):
            step(pl.ds(pl.multiple_of(i * count, count), count), i * count)
            return carry

        lax.fori_loop(0, length // count, body, 0)

    def loop(count, step):
        def body(i, carry):
            step(i)
            return carry

        lax.fori_loop(0, count, body, 0)

    def add_columns(number, values):
        sums[number] += jnp.sum(values.astype(F32).reshape(-1, 8, width), 0)

    def row(number):
        return small[:, group(number)]

    def group(number):
        return slice(number * width, (number + 1) * width)

    lane = lax.broadcasted_iota(jnp.int32, (1, 128), 1)
    low = lane < 64
    halves = (jnp.where(low, 1.0, 0.0).astype(BF), jnp.where(low, 0.0, 1.0).astype(BF))

    def first_length(r):
        segment = seg[pl.ds(r, 1), :]
        return jnp.sum(jnp.where(segment == 0, 1.0, 0.0), -1, keepdims=True).astype(jnp.int32)

    def set_cap(r):
        first = first_length(r)
        query = lax.broadcasted_iota(jnp.int32, (length, length), 0)
        key = lax.broadcasted_iota(jnp.int32, (length, length), 1)
        lowest = jnp.where(query >= first, first, 0)
        cap[...] = jnp.where((key <= query) & (key >= lowest), NO_CAP, MASKED)

    def positions(r, shift, axis=0):
        shape = (LAT, 1) if axis == 0 else (1, LAT)
        number = lax.broadcasted_iota(jnp.int32, shape, axis)
        result = jnp.full(shape, -1, jnp.int32)
        for j in range(thoughts):
            result = jnp.where(number == j, tpos[r, j] - shift, result)
        return result

    def selector_turned(r, shift):
        place = positions(r, shift, 1)
        return jnp.where(lax.broadcasted_iota(jnp.int32, (length, LAT), 0) == place, 1.0, 0.0)

    def selector(place):
        return jnp.where(lax.broadcasted_iota(jnp.int32, (LAT, length), 1) == place, 1.0, 0.0)

    def unmarked(r, start):
        place = lax.broadcasted_iota(jnp.int32, (32, 1), 0) + start
        keep = jnp.ones((32, 1), F32)
        for j in range(thoughts):
            keep = jnp.where(place == tpos[r, j], 0.0, keep)
        return keep

    def head_lanes(part, hp):
        start = part * width + hp * 128
        if isinstance(hp, int):
            return slice(start, start + 128)
        return pl.ds(pl.multiple_of(start, 128), 128)

    def norm_rows(x, target, k, which, gain, shift, more=None):
        def step(part, _):
            values = x[part, :]
            center = jnp.mean(values, -1, keepdims=True)
            centred = values - center
            scale = lax.rsqrt(jnp.mean(centred * centred, -1, keepdims=True) + EPSILON)
            stat[k, 2 * which, part, :] = center
            stat[k, 2 * which + 1, part, :] = scale
            target[part, :] = (centred * scale * row(gain) + row(shift)).astype(BF)
            if more is not None:
                more(part, values)

        each_chunk(step, 128)

    def norm_rows_back(x, part, k, which, gain, shift):
        scale = stat[k, 2 * which + 1, part, :]
        hat = (x[part, :] - stat[k, 2 * which, part, :]) * scale
        grad = da[part, :]
        add_columns(gain, grad * hat)
        add_columns(shift, grad)
        return norm_back(hat, scale, grad * row(gain))

    def forward(k, x, y, pending, first=None):
        def need(number):
            if first is not None:

                @pl.when(first)
                def _():
                    weights[number].wait()

        settle(pending, 0, a1, fa1)
        norm_rows(x, a1, k, 0, G1, B1)
        started(a1, fa1.at[k], 0)
        need(0)
        settle(pending, 1, ob, fo)

        for part in range(3):
            joined = dot(a1[...], wqkv[:, group(part)]) + joint[:, group(part)]
            jn[k, :, group(part)] = joined.astype(BF)
        for hp in range(pairs):
            q = jn[k, :, head_lanes(0, hp)]
            key = jn[k, :, head_lanes(1, hp)]
            value = jn[k, :, head_lanes(2, hp)]
            out = []
            for h in range(2):
                scores = dot_nt(q * (halves[h] * 0.125), key)
                chance = softmax(jnp.minimum(scores, cap[...])).astype(BF)
                pr[k, 2 * hp + h] = chance
                out.append(dot(chance, value))
            ob[:, head_lanes(0, hp)] = jnp.where(low, out[0], out[1]).astype(BF)
        started(ob, fo.at[k], 1)
        need(1)
        settle(pending, 2, a2, fa2)
        hm[k] = x[...] + dot(ob[...], wout[...]) + row(BO)

        def begin(part, values):
            y[part, :] = values + row(bd)

        norm_rows(hm.at[k], a2, k, 1, G2, B2, begin)
        started(a2, fa2.at[k], 2)
        need(2)
        need(3)
        settle(pending, 3, gb, fg)

        for c in range(blocks):
            part = group(c)
            g, d = gelu_both(dot(a2[...], wup[:, part]) + row(BU + c))
            gb[:, part] = g.astype(BF)
            slope[k, part, :] = d.astype(BF).T
            y[...] += dot(gb[:, part], wdown[part, :])
        started(gb, fg.at[k], 3)

    def backward(k, x, dy, dx, pending):
        def step(part, _):
            branch = dy[part, :].astype(BF)
            dm[part, :] = branch
            add_columns(bd, branch)

        settle(pending, 4, dm, fdm)
        each_chunk(step, 64)
        started(dm, fdm.at[k], 4)
        dmt[...] = dm[...].T
        dat[...] = jnp.zeros_like(dat)
        settle(pending, 5, dub, fdu)

        def mlp(c):
            part = pl.ds(pl.multiple_of(c * width, width), width)
            grad = (dot(wdown[part, :], dmt[...]) * slope[k, part, :]).astype(BF)
            dat[...] += dot(wup[:, part], grad)
            turned = grad.T
            dub[:, part] = turned
            add_columns(BU + c, turned)

        loop(blocks, mlp)
        da[...] = dat[...].T
        started(dub, fdu.at[k], 5)
        settle(pending, 6, dhr, fdhr)

        def step_two(part, _):
            middle = dy[part, :] + norm_rows_back(hm.at[k], part, k, 1, G2, B2)
            dy[part, :] = middle
            branch = middle.astype(BF)
            dhr[part, :] = branch
            add_columns(BO, branch)

        each_chunk(step_two, 64)
        started(dhr, fdhr.at[k], 6)
        dmt[...] = dhr[...].T
        dob[...] = dot(wout[...], dmt[...]).astype(BF).T
        settle(pending, 7, djb, fdj)

        def heads(hp):
            q = jn[k, :, head_lanes(0, hp)]
            key = jn[k, :, head_lanes(1, hp)]
            value = jn[k, :, head_lanes(2, hp)]
            grad_out = dob[:, head_lanes(0, hp)]
            dq, dk, dv = [], [], []
            for h in range(2):
                chance = pr[k, 2 * hp + h]
                chance_full = chance.astype(F32)
                inner_part = chance_full * dot_nt(grad_out * halves[h], value)
                total = jnp.sum(inner_part, -1, keepdims=True)
                grad_scores = (inner_part - chance_full * total).astype(BF)
                dq.append(dot(grad_scores, key))
                dk.append(dot_tn(grad_scores, q))
                dv.append(dot_tn(chance, grad_out))
            djb[:, head_lanes(0, hp)] = (jnp.where(low, dq[0], dq[1]) * 0.125).astype(BF)
            djb[:, head_lanes(1, hp)] = (jnp.where(low, dk[0], dk[1]) * 0.125).astype(BF)
            djb[:, head_lanes(2, hp)] = jnp.where(low, dv[0], dv[1]).astype(BF)

        loop(pairs, heads)
        started(djb, fdj.at[k], 7)
        into_input(k, x, dy, dx)

    def into_input(k, x, middle, dx):
        djt[...] = djb[...].T
        da[...] = dot(wqkv[...], djt[...]).T

        def step(part, _):
            add_columns(BQ, djb[part, group(0)])
            add_columns(BV, djb[part, group(2)])
            dx[part, :] = middle[part, :] + norm_rows_back(x, part, k, 0, G1, B1)

        each_chunk(step, 64)

    def forward_latent(r):
        x = xin.at[r]
        norm_rows(x, a1, r, 0, G1, B1)
        copies = [started(a1, fa1.at[r], 0)]
        jn[r, :, group(1)] = dot(a1[...], wqkv[:, group(1)]).astype(BF)
        jn[r, :, group(2)] = (dot(a1[...], wqkv[:, group(2)]) + row(BV)).astype(BF)
        place = positions(r, 1)
        chosen = exact_dot(selector(place), x[...])
        lx[r] = chosen
        hat, _ = normalized(chosen)
        normed = (hat * row(G1) + row(B1)).astype(BF)
        lq[r] = (dot(normed, wqkv[:, group(0)]) + row(BQ)).astype(BF)
        first = first_length(r)
        key_place = lax.broadcasted_iota(jnp.int32, (LAT, length), 1)
        lowest = jnp.where(place >= first, first, 0)
        limit = jnp.where((key_place <= place) & (key_place >= lowest), NO_CAP, MASKED)

        def heads(hp):
            q = lq[r, :, head_lanes(0, hp)]
            key = jn[r, :, head_lanes(1, hp)]
            value = jn[r, :, head_lanes(2, hp)]
            out = []
            for h in range(2):
                scores = dot_nt(q * (halves[h] * 0.125), key)
                chance = softmax(jnp.minimum(scores, limit)).astype(BF)
                lp[r, 2 * hp + h] = chance
                out.append(dot(chance, value))
            lo[r, :, head_lanes(0, hp)] = jnp.where(low, out[0], out[1]).astype(BF)

        for hp in range(pairs):
            heads(hp)
        middle = chosen + dot(lo[r], wout[...]) + row(BO)
        lh[r] = middle
        hat, _ = normalized(middle)
        la2[r] = (hat * row(G2) + row(B2)).astype(BF)
        lat[r] = middle + row(bd)

        def mlp(c):
            part = group(c)
            u = dot(la2[r], wup[:, part]) + row(BU + c)
            g, d = gelu_both(u)
            lg[r, :, part] = g.astype(BF)
            lslope[r, :, part] = d.astype(BF)
            lat[r] += dot(lg[r, :, part], wdown[part, :])

        for c in range(blocks):
            mlp(c)
        return copies

    def backward_latent(r, dx):
        grad_result = thg[r]
        branch = grad_result.astype(BF)
        top = slice(0, LAT)
        add_columns(bd, branch)
        dm[top, :] = branch
        a2[top, :] = la2[r]
        ob[top, :] = lo[r]
        gb[top, :] = lg[r]
        copies = [
            started(dm, fdm.at[r], 4),
            started(a2, fa2.at[r], 2),
            started(ob, fo.at[r], 1),
            started(gb, fg.at[r], 3),
        ]
        da[top, :] = jnp.zeros((LAT, width), F32)

        def mlp(c):
            part = group(c)
            grad = (dot_nt(dm[top, :], wdown[part, :]) * lslope[r, :, part]).astype(BF)
            dub[top, part] = grad
            add_columns(BU + c, grad)
            da[top, :] += dot_nt(grad, wup[:, part])

        for c in range(blocks):
            mlp(c)
        copies.append(started(dub, fdu.at[r], 5))
        hat, scale = normalized(lh[r])
        grad = da[top, :]
        add_columns(G2, grad * hat)
        add_columns(B2, grad)
        middle = grad_result + norm_back(hat, scale, grad * row(G2))
        rounded = middle.astype(BF)
        dhr[top, :] = rounded
        add_columns(BO, rounded)
        copies.append(started(dhr, fdhr.at[r], 6))
        spread = selector_turned(r, 1)
        dyb[r] = exact_dot(spread, middle)
        place = positions(r, 1, 1)
        first = first_length(r)
        key_place = lax.broadcasted_iota(jnp.int32, (length, LAT), 0)
        lowest = jnp.where(place >= first, first, 0)
        limit = jnp.where((key_place <= place) & (key_place >= lowest), NO_CAP, MASKED)
        dob[top, :] = dot_nt(rounded, wout[...]).astype(BF)

        def heads(hp):
            q = lq[r, :, head_lanes(0, hp)]
            key = jn[r, :, head_lanes(1, hp)]
            value = jn[r, :, head_lanes(2, hp)]
            grad_out = dob[top, head_lanes(0, hp)]
            dq, dk, dv = [], [], []
            for h in range(2):
                grad_masked = grad_out * halves[h]
                chance = lp[r, 2 * hp + h].astype(F32)
                inner_part = chance * dot_nt(grad_masked, value)
                total = jnp.sum(inner_part, -1, keepdims=True)
                dq.append(dot((inner_part - chance * total).astype(BF), key))
                scores = dot_nt(key, q * (halves[h] * 0.125))
                chance = softmax(jnp.minimum(scores, limit), 0)
                inner_part = chance * dot_nt(value, grad_masked)
                total = jnp.sum(inner_part, 0, keepdims=True)
                dk.append(dot((inner_part - chance * total).astype(BF), q))
                dv.append(dot(chance.astype(BF), grad_out))
            grad_q = (jnp.where(low, dq[0], dq[1]) * 0.125).astype(BF)
            djb[:, head_lanes(0, hp)] = dot(spread.astype(BF), grad_q).astype(BF)
            djb[:, head_lanes(1, hp)] = (jnp.where(low, dk[0], dk[1]) * 0.125).astype(BF)
            djb[:, head_lanes(2, hp)] = jnp.where(low, dv[0], dv[1]).astype(BF)

        for hp in range(pairs):
            heads(hp)
        copies.append(started(djb, fdj.at[r], 7))
        into_input(r, xin.at[r], dyb.at[r], dx)
        return copies

    staged = (
        (a1, fa1), (ob, fo), (a2, fa2), (gb, fg), (dm, fdm), (dub, fdu), (dhr, fdhr), (djb, fdj)
    )

    def settle_all(count, first=0):
        for number in range(first, first + count):
            source, target = staged[number]
            pltpu.make_async_copy(source, target.at[0], osem.at[number]).wait()

    @pl.when(me == 0)
    def _():
        def forward_step(k, carry):
            r = lax.rem(k, rows)
            set_cap(r)

            @pl.when(k < rows)
            def _():
                xin[k] = emb[r].astype(F32)

            @pl.when(k >= rows)
            def _():
                send_lat(r).wait_recv()
                xin[k] = exact_dot(selector_turned(r, 0), lat[r])

                def step(part, start):
                    xin[k, part, :] += emb[r, part, :].astype(F32) * unmarked(r, start)

                each_chunk(step, 32)

            forward(k, xin.at[k], yb.at[k], k > 0, first=k == 0)
            send_y(k).start()
            return carry

        lax.fori_loop(0, 2 * rows, forward_step, 0)
        settle_all(4)

        def backward_step(i, carry):
            k = lax.rem(i + rows, 2 * rows)
            r = lax.rem(i, rows)
            send_y(k).wait_send()
            send_grad(k).wait_recv()
            backward(k, xin.at[k], dyb.at[k], yb.at[k], i > 0)

            @pl.when(i < rows)
            def _():
                thg[r] = exact_dot(selector(positions(r, 0)), yb[k])
                send_thoughts(r).start()

            @pl.when(i >= rows)
            def _():
                def step(part, start):
                    yb[k, part, :] += yb[rows + r, part, :] * unmarked(r, start)

                each_chunk(step, 32)
                started(yb.at[k], sec.at[0, r], 8).wait()

            return carry

        lax.fori_loop(0, 2 * rows, backward_step, 0)
        settle_all(4, 4)

        def drain(r, carry):
            send_thoughts(r).wait_send()
            return carry

        lax.fori_loop(0, rows, drain, 0)

    @pl.when(me == 1)
    def _():
        finish(weights)

        def latent_step(r, carry):
            send_y(r).wait_recv()
            copies = forward_latent(r)
            send_lat(r).start()
            finish(copies)
            return carry

        lax.fori_loop(0, rows, latent_step, 0)

        def language_step(r, carry):
            k = rows + r
            set_cap(r)
            send_y(k).wait_recv()
            forward(k, xin.at[k], dyb.at[k], r > 0)
            result = started(dyb.at[k], sec.at[0, r], 8)
            dyb[r] = cot[r].astype(F32)
            backward(k, xin.at[k], dyb.at[r], yb.at[k], r > 0)
            send_grad(k).start()
            result.wait()
            return carry

        lax.fori_loop(0, rows, language_step, 0)
        settle_all(8)
        for buffer in (dm, a2, ob, gb, dub, dhr):
            buffer[...] = jnp.zeros_like(buffer)

        def latent_back_step(r, carry):
            send_thoughts(r).wait_recv()
            copies = backward_latent(r, yb.at[r])
            send_grad(r).start()
            finish(copies)
            return carry

        lax.fori_loop(0, rows, latent_back_step, 0)

        def drain(r, carry):
            send_lat(r).wait_send()
            send_grad(r).wait_send()
            send_grad(rows + r).wait_send()
            return carry

        lax.fori_loop(0, rows, drain, 0)

    sg[...] = jnp.sum(sums[...], 1)


def layers(emb, cot, seg, tpos, w_qkv, w_out, w_up, w_down, small):
    rows, length, width = emb.shape
    inner = w_up.shape[2]
    thoughts = tpos.shape[1]
    slots = 2 * rows
    packed = small.shape[1] // width
    vmem = pl.BlockSpec(memory_space=pltpu.VMEM)
    anywhere = pl.BlockSpec(memory_space=pl.ANY)
    smem = pl.BlockSpec(memory_space=pltpu.SMEM)

    def factor(columns):
        return jax.ShapeDtypeStruct((slots, length, columns), BF)

    def block(columns, kind=BF):
        return pltpu.VMEM((length, columns), kind)

    def few(columns, kind=BF):
        return pltpu.VMEM((rows, LAT, columns), kind)

    sizes = (rows, length, width, inner, thoughts)
    return pl.pallas_call(
        functools.partial(layers_kernel, sizes),
        out_shape=(
            jax.ShapeDtypeStruct((1, rows, length, width), F32),
            factor(width),
            factor(3 * width),
            factor(width),
            factor(width),
            factor(width),
            factor(inner),
            factor(inner),
            factor(width),
            jax.ShapeDtypeStruct((packed, width), F32),
        ),
        in_specs=[vmem, vmem, vmem, smem] + [anywhere] * 4 + [vmem],
        out_specs=(anywhere,) * 9 + (vmem,),
        scratch_shapes=[
            pltpu.VMEM((packed, 8, width), F32),
            pltpu.VMEM((1, 3 * width), F32),
            pltpu.VMEM((slots, 4, length, 1), F32),
            pltpu.VMEM((width, 3 * width), BF),
            pltpu.VMEM((width, width), BF),
            pltpu.VMEM((width, inner), BF),
            pltpu.VMEM((inner, width), BF),
            pltpu.VMEM((slots, length, width), F32),
            pltpu.VMEM((slots, length, width), F32),
            pltpu.VMEM((slots, length, width), F32),
            pltpu.VMEM((slots, length, 3 * width), BF),
            pltpu.VMEM((slots, HEADS, length, length), BF),
            pltpu.VMEM((slots, length, width), F32),
            pltpu.VMEM((slots, inner, length), BF),
            block(width),
            block(width),
            block(width),
            block(inner),
            block(width),
            block(inner),
            block(width),
            block(3 * width),
            block(width, F32),
            block(width),
            pltpu.VMEM((width, length), BF),
            pltpu.VMEM((width, length), F32),
            pltpu.VMEM((3 * width, length), BF),
            block(length, F32),
            few(width, F32),
            few(width, F32),
            few(width, F32),
            few(width),
            pltpu.VMEM((rows, HEADS, LAT, length), BF),
            few(width, F32),
            few(width),
            few(width),
            few(inner),
            few(inner),
            pltpu.SemaphoreType.DMA((4,)),
            pltpu.SemaphoreType.DMA((9,)),
        ]
        + [pltpu.SemaphoreType.DMA((slots,))] * 4
        + [pltpu.SemaphoreType.DMA((rows,))] * 4,
        compiler_params=pltpu.CompilerParams(
            collective_id=0, has_side_effects=True, vmem_limit_bytes=62 << 20
        ),
    )(emb, cot, seg, tpos, w_qkv, w_out, w_up, w_down, small)


def summed_by_parts(factors, small_grads):
    fa1, fdj, fo, fdhr, fa2, fdu, fg, fdm = factors

    def product(left, right):
        whole = jnp.einsum("ktm,ktn->mn", left, right, preferred_element_type=F32)
        return lax.psum_scatter(whole[None], "dp", scatter_dimension=1, tiled=True)

    small = lax.psum_scatter(
        small_grads.reshape(1, -1), "dp", scatter_dimension=1, tiled=True
    )
    return product(fa1, fdj), product(fo, fdhr), product(fa2, fdu), product(fg, fdm), small


def gradients_kernel(
    sizes,
    plan,
    lags,
    fa1,
    fdj,
    fo,
    fdhr,
    fa2,
    fdu,
    fg,
    fdm,
    small,
    gqkv,
    gout,
    gup,
    gdown,
    gsmall,
    left,
    right,
    lt,
    lt_down,
    wa,
    ra,
    xa,
    ua,
    na,
    wb,
    rb,
    xb,
    ub,
    nb,
    rs,
    xs,
    us,
    ns,
    xl,
    ul,
    nl,
    kept,
    lsem,
    pair_send,
    pair_recv,
    side_send,
    side_recv,
    up_send,
    up_recv,
    down_send,
    down_recv,
    over_send,
    over_recv,
):
    width, narrow, depth = sizes
    side_lag, hop = lags
    me = lax.axis_index("dp")
    core = lax.rem(me, 2)
    side = lax.rem(me // 2, 2)
    level = me // 4
    partner = me + 1 - 2 * core
    beside = me + 2 - 4 * side
    above, below = me + 4, me - 4
    plane = lax.axis_index("pipe")

    def remote(source, target, send, recv, device):
        return pltpu.make_async_remote_copy(
            src_ref=source,
            dst_ref=target,
            send_sem=send,
            recv_sem=recv,
            device_id={"dp": device},
            device_id_type=MESH,
        )

    buffers = {"wide": (wa, ra, xa, ua, na), "tall": (wb, rb, xb, ub, nb)}
    lefts = {"qkv": fa1, "out": fo, "up": fa2, "down": fg}
    rights = {"qkv": fdj, "out": fdhr, "up": fdu, "down": fdm}
    total = len(plan)
    names = [entry[0] for entry in plan]
    guest = names.index("guest")
    exported = 0
    steps = []
    turned = None
    for number, (name, part, _, columns) in enumerate(plan):
        if name in ("small", "guest"):
            continue
        if name == "down":
            for block in range(depth):
                steps.append((number, name, True, block, None, 0))
                steps.append((number, name, False, block, part, columns))
            continue
        if name != turned:
            steps.append((number, name, True, 0, None, 0))
            turned = name
        steps.append((number, name, False, 0, part, columns))

    def loads(index):
        _, name, turn, block, part, columns = steps[index]
        slot = index % 2
        if turn:
            source = lefts[name].at[:, :, block * width : (block + 1) * width]
            return pltpu.make_async_copy(source, left.at[slot], lsem.at[slot])
        return pltpu.make_async_copy(
            rights[name].at[:, :, part * columns : (part + 1) * columns],
            right.at[slot, :, :, 0:columns],
            lsem.at[slot],
        )

    def start_loads(index):
        if index < len(steps):
            loads(index).start()

    start_loads(0)

    barrier = pltpu.get_barrier_semaphore()

    def greet(device):
        pl.semaphore_signal(barrier, inc=1, device_id={"dp": device}, device_id_type=MESH)

    greet(partner)
    greet(beside)

    @pl.when(level < 3)
    def _():
        greet(above)

    @pl.when(level > 0)
    def _():
        greet(below)

    @pl.when(plane == 1)
    def _():
        pl.semaphore_signal(barrier, inc=1, device_id={"pipe": 0}, device_id_type=MESH)

    pl.semaphore_wait(barrier, 2 + (level + 2) // 3 + (5 - level) // 3 + 1 - plane)

    targets = {"qkv": gqkv, "out": gout, "up": gup, "down": gdown}
    views = []
    previous = {}
    order = {}
    made = {}
    last_of = {number: True for number in range(total)}
    for number, (name, part, line_first, columns) in enumerate(plan):
        kind = kind_of(plan[number])
        if kind == "small":
            views.append((small, rs, xs, us, ns, gsmall))
            previous[number] = None
            continue
        w, r, x, u, n = buffers[kind]
        order.setdefault(kind, []).append(number)
        index = len(order[kind]) - 1
        along = sum(plan[other][2] for other in order[kind][:index])
        if name == "guest":
            views.append(
                (None, r.at[index], x.at[index - along], u.at[index - along], n.at[index - along], kept)
            )
            continue
        made.setdefault(kind, []).append(number)
        turn = len(made[kind]) - 1
        slots_of = w.shape[0]
        previous[number] = made[kind][turn - slots_of] if turn >= slots_of else None
        if previous[number] is not None:
            last_of[previous[number]] = False
        place = targets[name].at[0, :, part * columns : (part + 1) * columns]
        if line_first:
            further = (xl.at[along], ul.at[along], nl.at[along], place)
        else:
            further = (x.at[index - along], u.at[index - along], n.at[index - along], place)
        views.append((w.at[turn % slots_of], r.at[index]) + further)

    def over(source, target, number):
        return pltpu.make_async_remote_copy(
            src_ref=source,
            dst_ref=target,
            send_sem=over_send.at[number],
            recv_sem=over_recv.at[number],
            device_id={"pipe": 1 - plane},
            device_id_type=MESH,
        )

    def hand_over():
        return over(views[exported][1], views[guest][1], 0)

    def hand_back():
        return over(kept, views[exported][5], 1)

    def where(number, condition=None):
        if number in (exported, guest):
            condition = plane == 1 if condition is None else condition & (plane == 1)
        if condition is None:
            return lambda body: body()
        return pl.when(condition)

    def pair_copy(number):
        w, r = views[number][:2]
        return remote(
            w.at[:, :, 1 - core], r, pair_send.at[number], pair_recv.at[number], partner
        )

    def side_copy(number):
        r, x = views[number][1:3]
        source = r.at[level, 1 - side] if plan[number][2] else r.at[:, 1 - side]
        return remote(source, x, side_send.at[number], side_recv.at[number], beside)

    def along_line(number):
        r, x = views[number][1:3]
        return r if plan[number][2] else x

    def up_copy(number, goal, source=None):
        u = views[number][3]
        return remote(
            u.at[goal - 1] if source is None else source,
            u.at[goal - 1],
            up_send.at[number, goal - 1],
            up_recv.at[number, goal - 1],
            above,
        )

    def down_copy(number, goal, source=None):
        n = views[number][4]
        return remote(
            n.at[goal] if source is None else source,
            n.at[goal],
            down_send.at[number, goal],
            down_recv.at[number, goal],
            below,
        )

    def start_line(number):
        base = along_line(number)

        @pl.when(level == 0)
        def _():
            for goal in (3, 2, 1):
                up_copy(number, goal, base.at[goal]).start()

        @pl.when(level == 3)
        def _():
            for goal in (0, 1, 2):
                down_copy(number, goal, base.at[goal]).start()

    position = {"step": 0}
    slots, length = left.shape[1:3]

    def turn_block(slot, target):
        def body(t, carry):
            tokens = pl.ds(pl.multiple_of(t * length, length), length)
            target[:, tokens] = left[slot, t].T
            return carry

        lax.fori_loop(0, slots, body, 0)

    def right_part(slot, lanes):
        part = right[slot, :, :, lanes]
        return part.reshape(slots * length, part.shape[2])

    def multiply(slot, w, columns):
        def tile(t, carry):
            lanes = pl.ds(pl.multiple_of(t * narrow, narrow), narrow)
            product = dot(lt[...], right_part(slot, lanes))
            w[:, :, :, :, lanes] = product.reshape(w.shape[:4] + (narrow,))
            return carry

        lax.fori_loop(0, columns // narrow, tile, 0)


    def produce(number):
        name = plan[number][0]
        if name == "guest":
            return
        if name != "small":
            if previous[number] is not None:
                pair_copy(previous[number]).wait_send()
            w = views[number][0]
            while position["step"] < len(steps) and steps[position["step"]][0] == number:
                index = position["step"]
                position["step"] += 1
                _, source, turn, block, _, columns = steps[index]
                start_loads(index + 1)
                loads(index).wait()
                if turn:
                    turn_block(index % 2, lt_down if source == "down" else lt)
                elif source == "down":
                    part = right_part(index % 2, slice(0, narrow))
                    w[block] = dot(lt_down[...], part).reshape(w.shape[1:])
                else:
                    multiply(index % 2, w, columns)
        pair_copy(number).start()

    def stage_pair(number):
        if number == guest:

            @pl.when(plane == 1)
            def _():
                hand_over().wait_recv()
                side_copy(number).start()

            return
        w, r = views[number][:2]
        pair_copy(number).wait_recv()

        def add(z, carry):
            for s in range(2):
                r[z, s] += w[z, s, core]
            return carry

        lax.fori_loop(0, 4, add, 0)
        if plan[number][2]:
            start_line(number)
            return

        @where(number)
        def _():
            side_copy(number).start()

        if number == exported:

            @pl.when(plane == 0)
            def _():
                hand_over().start()

    def stage_side(number):
        if plan[number][2]:
            return

        @where(number)
        def _():
            r, x = views[number][1:3]
            side_copy(number).wait_recv()

            def add(z, carry):
                x[z] += r[z, side]
                return carry

            lax.fori_loop(0, 4, add, 0)
            start_line(number)

    def stage_up(number, height):
        u = views[number][3]
        base = along_line(number)

        @where(number, level == height)
        def _():
            for goal in range(3, height - 1, -1):
                up_copy(number, goal).wait_recv()
                if goal > height:
                    u[goal - 1] += base[goal]
                    up_copy(number, goal).start()

    def stage_down(number, height):
        n = views[number][4]
        base = along_line(number)

        @where(number, level == height)
        def _():
            for goal in range(0, height + 1):
                down_copy(number, goal).wait_recv()
                if goal < height:
                    n[goal] += base[goal]
                    down_copy(number, goal).start()

    def stage_sum(number):
        u, n, place = views[number][3:]
        base = along_line(number)

        @where(number, level > 0)
        def _():
            base[level] += u[level - 1]

        @where(number, level < 3)
        def _():
            base[level] += n[level]

        if plan[number][2]:
            side_copy(number).start()
            return

        @where(number)
        def _():
            place[...] = base[level]
            if number == guest:
                hand_back().start()

    def stage_last(number):
        if plan[number][2]:
            r, x = views[number][1:3]
            side_copy(number).wait_recv()
            views[number][5][...] = r[level, side] + x[...]

    def at(stage, number, *more):
        if 0 <= number < total:
            stage(number, *more)

    for moment in range(total + side_lag + 3 * hop + 1):
        at(produce, moment)
        at(stage_pair, moment - 1)
        at(stage_side, moment - side_lag)
        for height in range(4):
            if height > 0:
                at(stage_up, moment - side_lag - hop * height, height)
            if height < 3:
                at(stage_down, moment - side_lag - hop * (3 - height), height)
        at(stage_sum, moment - side_lag - 3 * hop)
        at(stage_last, moment - side_lag - 3 * hop - 1)
    for number in range(total):
        if last_of[number] and number != guest:
            pair_copy(number).wait_send()

        @where(number)
        def _():
            side_copy(number).wait_send()

        for goal in (1, 2, 3):

            @where(number, goal > level)
            def _():
                up_copy(number, goal).wait_send()

        for goal in (0, 1, 2):

            @where(number, goal < level)
            def _():
                down_copy(number, goal).wait_send()

    @pl.when(plane == 0)
    def _():
        hand_over().wait_send()
        hand_back().wait_recv()

    @pl.when(plane == 1)
    def _():
        hand_back().wait_send()


def kind_of(entry):
    return {"small": "small", "down": "tall"}.get(entry[0], "wide")


def summed_in_kernel(factors, small_grads):
    fa1, fdj, fo, fdhr, fa2, fdu, fg, fdm = factors
    slots, length, width = fa1.shape
    inner = fg.shape[2]
    owners = 16
    depth = inner // width
    narrow = 256
    a_rows, b_rows = width // owners, inner // owners
    packed = small_grads.size // owners
    lanes = 128
    s_rows = -(-packed // (8 * lanes)) * 8
    small = small_grads.reshape(owners, packed)
    small = jnp.pad(small, ((0, 0), (0, s_rows * lanes - packed)))
    small = small.reshape(4, 2, 2, s_rows, lanes)
    plan = [
        ("qkv", 0, False, width),
        ("qkv", 1, True, width),
        ("qkv", 2, False, width),
        ("small", 0, False, 0),
        ("out", 0, False, width),
        ("up", 0, False, width),
        ("down", 0, False, narrow),
        ("up", 1, True, width),
        ("down", 1, False, narrow),
        ("guest", 0, False, width),
        ("up", 2, False, width),
        ("up", 3, False, width),
        ("down", 2, False, narrow),
    ]
    lags = (3, 2)
    total = len(plan)
    s_block = small.shape[3:]
    vmem = pl.BlockSpec(memory_space=pltpu.VMEM)
    anywhere = pl.BlockSpec(memory_space=pl.ANY)

    def of_kind(kind, slots_of, block):
        mine = [entry for entry in plan if kind_of(entry) == kind]
        across = sum(not entry[2] for entry in mine)
        leads = ((slots_of, 4, 2, 2), (len(mine), 4, 2), (across, 4), (across, 3), (across, 3))
        return [pltpu.VMEM(lead + block, F32) for lead in leads]

    line_count = sum(line_first for _, _, line_first, _ in plan)
    a_block = (a_rows, width)
    *grads, small_grad = pl.pallas_call(
        functools.partial(gradients_kernel, (width, narrow, depth), plan, lags),
        out_shape=(
            jax.ShapeDtypeStruct((1, a_rows, 3 * width), F32),
            jax.ShapeDtypeStruct((1, a_rows, width), F32),
            jax.ShapeDtypeStruct((1, a_rows, inner), F32),
            jax.ShapeDtypeStruct((1, b_rows, width), F32),
            jax.ShapeDtypeStruct(s_block, F32),
        ),
        in_specs=[anywhere] * 8 + [vmem],
        out_specs=(vmem,) * 5,
        scratch_shapes=[
            pltpu.VMEM((2, slots, length, width), BF),
            pltpu.VMEM((2, slots, length, width), BF),
            pltpu.VMEM((width, slots * length), BF),
            pltpu.VMEM((width, slots * length), BF),
        ]
        + of_kind("wide", 2, a_block)
        + of_kind("tall", 1, (b_rows, narrow))
        + [pltpu.VMEM(lead + s_block, F32) for lead in ((4, 2), (4,), (3,), (3,))]
        + [
            pltpu.VMEM((line_count,) + a_block, F32),
            pltpu.VMEM((line_count, 3, 2) + a_block, F32),
            pltpu.VMEM((line_count, 3, 2) + a_block, F32),
            pltpu.VMEM(a_block, F32),
        ]
        + [pltpu.SemaphoreType.DMA((2,))]
        + [pltpu.SemaphoreType.DMA((total,))] * 4
        + [pltpu.SemaphoreType.DMA((total, 3))] * 4
        + [pltpu.SemaphoreType.DMA((2,))] * 2,
        compiler_params=pltpu.CompilerParams(
            collective_id=1, has_side_effects=True, vmem_limit_bytes=62 << 20
        ),
    )(*factors, small)
    return tuple(grads) + (small_grad,)


def results_kernel(count, *refs):
    sources, small = refs[:count], refs[count]
    targets, packed = refs[count + 1 : 2 * count + 1], refs[2 * count + 1]
    held, load_sem, store_sem = refs[2 * count + 2 : -2], refs[-2], refs[-1]
    loads = [
        pltpu.make_async_copy(sources[i], held[i], load_sem.at[i]) for i in range(count)
    ]
    stores = [
        pltpu.make_async_copy(held[i], targets[i], store_sem.at[i]) for i in range(count)
    ]
    for load in loads:
        load.start()
    lines = [small[line : line + 1, :] for line in range(small.shape[0])]
    packed[...] = jnp.concatenate(lines, 1)[:, : packed.shape[1]]
    for load, store in zip(loads, stores):
        load.wait()
        store.start()
    for store in stores:
        store.wait()


def copied_out(large, small, packed):
    count = len(large)
    vmem = pl.BlockSpec(memory_space=pltpu.VMEM)
    anywhere = pl.BlockSpec(memory_space=pl.ANY)
    shapes = [jax.ShapeDtypeStruct(array.shape, array.dtype) for array in large]
    return pl.pallas_call(
        functools.partial(results_kernel, count),
        out_shape=tuple(shapes) + (jax.ShapeDtypeStruct((1, packed), F32),),
        in_specs=[anywhere] * count + [vmem],
        out_specs=(anywhere,) * count + (vmem,),
        scratch_shapes=[pltpu.VMEM(array.shape, array.dtype) for array in large]
        + [pltpu.SemaphoreType.DMA((count,))] * 2,
        compiler_params=pltpu.CompilerParams(vmem_limit_bytes=16 << 20),
    )(*large, small)


def reduced(section_out, factors, small_grads):
    if lax.axis_size("dp") == 16:
        *grads, small_grad = summed_in_kernel(factors, small_grads)
        return copied_out([section_out] + grads, small_grad, small_grads.size // 16)
    return (section_out,) + tuple(summed_by_parts(factors, small_grads))


def per_device(
    embeddings, cotangent, seg_ids, thought_pos, w_qkv, w_out, w_up, w_down, small_params
):
    section_out, *factors, small_grads = layers(
        embeddings, cotangent, seg_ids, thought_pos, w_qkv, w_out, w_up, w_down, small_params
    )
    return tuple(reduced(section_out, factors, small_grads))


def solution(mesh):
    return jax.shard_map(
        per_device,
        mesh=mesh,
        in_specs=(
            P("dp", None, None),
            P("dp", None, None),
            P("dp", None),
            P("dp", None),
            P("pipe", None, None),
            P("pipe", None, None),
            P("pipe", None, None),
            P("pipe", None, None),
            P("pipe", None),
        ),
        out_specs=(
            P("pipe", "dp", None, None),
            P("pipe", "dp", None),
            P("pipe", "dp", None),
            P("pipe", "dp", None),
            P("pipe", "dp", None),
            P("pipe", "dp"),
        ),
        check_vma=False,
    )
```

```python
import functools

import jax
import jax.numpy as jnp
from jax import lax
from jax.experimental import pallas as pl
from jax.experimental.pallas import tpu as pltpu
from jax.sharding import PartitionSpec as P

HEADS = 12
BF = jnp.bfloat16
F32 = jnp.float32
MESH = pl.DeviceIdType.MESH
EPSILON = 1e-05
MASKED = -1000000000.0
NO_CAP = 3e38
LAT = 16
G1, B1, BQ, BV, BO, G2, B2, BU = 0, 1, 2, 3, 4, 5, 6, 7


def dot(a, b):
    return lax.dot_general(a, b, (((1,), (0,)), ((), ())), preferred_element_type=F32)


def dot_nt(a, b):
    return lax.dot_general(a, b, (((1,), (1,)), ((), ())), preferred_element_type=F32)


def dot_tn(a, b):
    return lax.dot_general(a, b, (((0,), (0,)), ((), ())), preferred_element_type=F32)


def exact_dot(a, b):
    return lax.dot_general(
        a,
        b,
        (((1,), (0,)), ((), ())),
        precision=lax.Precision.HIGHEST,
        preferred_element_type=F32,
    )


def normalized(values):
    centred = values - jnp.mean(values, -1, keepdims=True)
    spread = jnp.mean(centred * centred, -1, keepdims=True)
    scale = lax.rsqrt(spread + EPSILON)
    return centred * scale, scale


def norm_back(hat, scale, grad):
    along = jnp.mean(grad * hat, -1, keepdims=True)
    return scale * (grad - jnp.mean(grad, -1, keepdims=True) - hat * along)


def gelu_both(u):
    c = 0.7978845608028654
    square = u * u
    t = jnp.tanh(c * u * (1.0 + 0.044715 * square))
    half = 0.5 + 0.5 * t
    slope = half + (0.5 * c) * u * (1.0 - t * t) * (1.0 + (3 * 0.044715) * square)
    return u * half, slope


def softmax(scores, axis=-1):
    e = jnp.exp(scores - jnp.max(scores, axis, keepdims=True))
    return e * (1.0 / jnp.sum(e, axis, keepdims=True))


def layers_kernel(
    sizes,
    emb,
    cot,
    seg,
    tpos,
    wqkv_h,
    wout_h,
    wup_h,
    wdown_h,
    small,
    sec,
    fa1,
    fdj,
    fo,
    fdhr,
    fa2,
    fdu,
    fg,
    fdm,
    sg,
    sums,
    joint,
    stat,
    wqkv,
    wout,
    wup,
    wdown,
    xin,
    yb,
    dyb,
    jn,
    pr,
    hm,
    slope,
    a1,
    ob,
    a2,
    gb,
    dm,
    dub,
    dhr,
    djb,
    da,
    dob,
    dmt,
    dat,
    djt,
    cap,
    lat,
    thg,
    lx,
    lq,
    lp,
    lh,
    la2,
    lo,
    lg,
    lslope,
    wsem,
    osem,
    ysend,
    yrecv,
    gsend,
    grecv,
    lsend,
    lrecv,
    tsend,
    trecv,
    heard,
):
    rows, length, width, inner, thoughts = sizes
    blocks = inner // width
    bd = BU + blocks
    pairs = HEADS // 2
    me = lax.axis_index("pipe")
    other = 1 - me

    weights = [
        pltpu.make_async_copy(source.at[0], target, wsem.at[number])
        for number, (source, target) in enumerate(
            ((wqkv_h, wqkv), (wout_h, wout), (wup_h, wup), (wdown_h, wdown))
        )
    ]
    for copy in weights:
        copy.start()
    barrier = pltpu.get_barrier_semaphore()
    pl.semaphore_signal(barrier, inc=1, device_id={"pipe": other}, device_id_type=MESH)
    pl.semaphore_wait(barrier, 1)
    sums[...] = jnp.zeros_like(sums)
    joint[:, 0:width] = small[:, BQ * width : (BQ + 1) * width]
    joint[:, width : 2 * width] = jnp.zeros((1, width), F32)
    joint[:, 2 * width : 3 * width] = small[:, BV * width : (BV + 1) * width]

    def remote(source, target, send, recv):
        return pltpu.make_async_remote_copy(
            src_ref=source,
            dst_ref=target,
            send_sem=send,
            recv_sem=recv,
            device_id={"pipe": other},
            device_id_type=MESH,
        )

    def send_y(k):
        return remote(yb.at[k], xin.at[k], ysend.at[k], yrecv.at[k])

    def send_grad(k):
        return remote(yb.at[k], dyb.at[k], gsend.at[k], grecv.at[k])

    def send_lat(r):
        return remote(lat.at[r], lat.at[r], lsend.at[r], lrecv.at[r])

    def send_thoughts(r):
        return remote(thg.at[r], thg.at[r], tsend.at[r], trecv.at[r])

    def started(source, target, number):
        copy = pltpu.make_async_copy(source, target, osem.at[number])
        copy.start()
        return copy

    def settle(pending, number, source, target):
        @pl.when(pending)
        def _():
            pltpu.make_async_copy(source, target.at[0], osem.at[number]).wait()

    def finish(copies):
        for copy in copies:
            copy.wait()

    def each_chunk(step, count):
        def body(i, carry):
            step(pl.ds(pl.multiple_of(i * count, count), count), i * count)
            return carry

        lax.fori_loop(0, length // count, body, 0)

    def loop(count, step):
        def body(i, carry):
            step(i)
            return carry

        lax.fori_loop(0, count, body, 0)

    def add_columns(number, values):
        sums[number] += jnp.sum(values.astype(F32).reshape(-1, 8, width), 0)

    def row(number):
        return small[:, group(number)]

    def group(number):
        return slice(number * width, (number + 1) * width)

    lane = lax.broadcasted_iota(jnp.int32, (1, 128), 1)
    low = lane < 64
    halves = (jnp.where(low, 1.0, 0.0).astype(BF), jnp.where(low, 0.0, 1.0).astype(BF))

    def first_length(r):
        segment = seg[pl.ds(r, 1), :]
        return jnp.sum(jnp.where(segment == 0, 1.0, 0.0), -1, keepdims=True).astype(jnp.int32)

    def set_cap(r):
        first = first_length(r)
        query = lax.broadcasted_iota(jnp.int32, (length, length), 0)
        key = lax.broadcasted_iota(jnp.int32, (length, length), 1)
        lowest = jnp.where(query >= first, first, 0)
        cap[...] = jnp.where((key <= query) & (key >= lowest), NO_CAP, MASKED)

    def positions(r, shift, axis=0):
        shape = (LAT, 1) if axis == 0 else (1, LAT)
        number = lax.broadcasted_iota(jnp.int32, shape, axis)
        result = jnp.full(shape, -1, jnp.int32)
        for j in range(thoughts):
            result = jnp.where(number == j, tpos[r, j] - shift, result)
        return result

    def selector_turned(r, shift):
        place = positions(r, shift, 1)
        return jnp.where(lax.broadcasted_iota(jnp.int32, (length, LAT), 0) == place, 1.0, 0.0)

    def selector(place):
        return jnp.where(lax.broadcasted_iota(jnp.int32, (LAT, length), 1) == place, 1.0, 0.0)

    def unmarked(r, start):
        place = lax.broadcasted_iota(jnp.int32, (32, 1), 0) + start
        keep = jnp.ones((32, 1), F32)
        for j in range(thoughts):
            keep = jnp.where(place == tpos[r, j], 0.0, keep)
        return keep

    def head_lanes(part, hp):
        start = part * width + hp * 128
        if isinstance(hp, int):
            return slice(start, start + 128)
        return pl.ds(pl.multiple_of(start, 128), 128)

    def norm_rows(x, target, k, which, gain, shift, more=None):
        def step(part, _):
            values = x[part, :]
            center = jnp.mean(values, -1, keepdims=True)
            centred = values - center
            scale = lax.rsqrt(jnp.mean(centred * centred, -1, keepdims=True) + EPSILON)
            stat[k, 2 * which, part, :] = center
            stat[k, 2 * which + 1, part, :] = scale
            target[part, :] = (centred * scale * row(gain) + row(shift)).astype(BF)
            if more is not None:
                more(part, values)

        each_chunk(step, 128)

    def norm_rows_back(x, part, k, which, gain, shift):
        scale = stat[k, 2 * which + 1, part, :]
        hat = (x[part, :] - stat[k, 2 * which, part, :]) * scale
        grad = da[part, :]
        add_columns(gain, grad * hat)
        add_columns(shift, grad)
        return norm_back(hat, scale, grad * row(gain))

    def forward(k, x, y, pending, first=None):
        def need(number):
            if first is not None:

                @pl.when(first)
                def _():
                    weights[number].wait()

        settle(pending, 0, a1, fa1)
        norm_rows(x, a1, k, 0, G1, B1)
        started(a1, fa1.at[k], 0)
        need(0)
        settle(pending, 1, ob, fo)

        for part in range(3):
            joined = dot(a1[...], wqkv[:, group(part)]) + joint[:, group(part)]
            jn[k, :, group(part)] = joined.astype(BF)
        for hp in range(pairs):
            q = jn[k, :, head_lanes(0, hp)]
            key = jn[k, :, head_lanes(1, hp)]
            value = jn[k, :, head_lanes(2, hp)]
            out = []
            for h in range(2):
                scores = dot_nt(q * (halves[h] * 0.125), key)
                chance = softmax(jnp.minimum(scores, cap[...])).astype(BF)
                pr[k, 2 * hp + h] = chance
                out.append(dot(chance, value))
            ob[:, head_lanes(0, hp)] = jnp.where(low, out[0], out[1]).astype(BF)
        started(ob, fo.at[k], 1)
        need(1)
        settle(pending, 2, a2, fa2)
        hm[k] = x[...] + dot(ob[...], wout[...]) + row(BO)

        def begin(part, values):
            y[part, :] = values + row(bd)

        norm_rows(hm.at[k], a2, k, 1, G2, B2, begin)
        started(a2, fa2.at[k], 2)
        need(2)
        need(3)
        settle(pending, 3, gb, fg)

        for c in range(blocks):
            part = group(c)
            g, d = gelu_both(dot(a2[...], wup[:, part]) + row(BU + c))
            gb[:, part] = g.astype(BF)
            slope[k, part, :] = d.astype(BF).T
            y[...] += dot(gb[:, part], wdown[part, :])
        started(gb, fg.at[k], 3)

    def backward(k, x, dy, dx, pending):
        def step(part, _):
            branch = dy[part, :].astype(BF)
            dm[part, :] = branch
            add_columns(bd, branch)

        settle(pending, 4, dm, fdm)
        each_chunk(step, 64)
        started(dm, fdm.at[k], 4)
        dmt[...] = dm[...].T
        dat[...] = jnp.zeros_like(dat)
        settle(pending, 5, dub, fdu)

        def mlp(c):
            part = pl.ds(pl.multiple_of(c * width, width), width)
            grad = (dot(wdown[part, :], dmt[...]) * slope[k, part, :]).astype(BF)
            dat[...] += dot(wup[:, part], grad)
            turned = grad.T
            dub[:, part] = turned
            add_columns(BU + c, turned)

        loop(blocks, mlp)
        da[...] = dat[...].T
        started(dub, fdu.at[k], 5)
        settle(pending, 6, dhr, fdhr)

        def step_two(part, _):
            middle = dy[part, :] + norm_rows_back(hm.at[k], part, k, 1, G2, B2)
            dy[part, :] = middle
            branch = middle.astype(BF)
            dhr[part, :] = branch
            add_columns(BO, branch)

        each_chunk(step_two, 64)
        started(dhr, fdhr.at[k], 6)
        dmt[...] = dhr[...].T
        dob[...] = dot(wout[...], dmt[...]).astype(BF).T
        settle(pending, 7, djb, fdj)

        def heads(hp):
            q = jn[k, :, head_lanes(0, hp)]
            key = jn[k, :, head_lanes(1, hp)]
            value = jn[k, :, head_lanes(2, hp)]
            grad_out = dob[:, head_lanes(0, hp)]
            dq, dk, dv = [], [], []
            for h in range(2):
                chance = pr[k, 2 * hp + h]
                chance_full = chance.astype(F32)
                inner_part = chance_full * dot_nt(grad_out * halves[h], value)
                total = jnp.sum(inner_part, -1, keepdims=True)
                grad_scores = (inner_part - chance_full * total).astype(BF)
                dq.append(dot(grad_scores, key))
                dk.append(dot_tn(grad_scores, q))
                dv.append(dot_tn(chance, grad_out))
            djb[:, head_lanes(0, hp)] = (jnp.where(low, dq[0], dq[1]) * 0.125).astype(BF)
            djb[:, head_lanes(1, hp)] = (jnp.where(low, dk[0], dk[1]) * 0.125).astype(BF)
            djb[:, head_lanes(2, hp)] = jnp.where(low, dv[0], dv[1]).astype(BF)

        loop(pairs, heads)
        started(djb, fdj.at[k], 7)
        into_input(k, x, dy, dx)

    def into_input(k, x, middle, dx):
        djt[...] = djb[...].T
        da[...] = dot(wqkv[...], djt[...]).T

        def step(part, _):
            add_columns(BQ, djb[part, group(0)])
            add_columns(BV, djb[part, group(2)])
            dx[part, :] = middle[part, :] + norm_rows_back(x, part, k, 0, G1, B1)

        each_chunk(step, 64)

    def forward_latent(r):
        x = xin.at[r]
        norm_rows(x, a1, r, 0, G1, B1)
        copies = [started(a1, fa1.at[r], 0)]
        jn[r, :, group(1)] = dot(a1[...], wqkv[:, group(1)]).astype(BF)
        jn[r, :, group(2)] = (dot(a1[...], wqkv[:, group(2)]) + row(BV)).astype(BF)
        place = positions(r, 1)
        chosen = exact_dot(selector(place), x[...])
        lx[r] = chosen
        hat, _ = normalized(chosen)
        normed = (hat * row(G1) + row(B1)).astype(BF)
        lq[r] = (dot(normed, wqkv[:, group(0)]) + row(BQ)).astype(BF)
        first = first_length(r)
        key_place = lax.broadcasted_iota(jnp.int32, (LAT, length), 1)
        lowest = jnp.where(place >= first, first, 0)
        limit = jnp.where((key_place <= place) & (key_place >= lowest), NO_CAP, MASKED)

        def heads(hp):
            q = lq[r, :, head_lanes(0, hp)]
            key = jn[r, :, head_lanes(1, hp)]
            value = jn[r, :, head_lanes(2, hp)]
            out = []
            for h in range(2):
                scores = dot_nt(q * (halves[h] * 0.125), key)
                chance = softmax(jnp.minimum(scores, limit)).astype(BF)
                lp[r, 2 * hp + h] = chance
                out.append(dot(chance, value))
            lo[r, :, head_lanes(0, hp)] = jnp.where(low, out[0], out[1]).astype(BF)

        for hp in range(pairs):
            heads(hp)
        middle = chosen + dot(lo[r], wout[...]) + row(BO)
        lh[r] = middle
        hat, _ = normalized(middle)
        la2[r] = (hat * row(G2) + row(B2)).astype(BF)
        lat[r] = middle + row(bd)

        def mlp(c):
            part = group(c)
            u = dot(la2[r], wup[:, part]) + row(BU + c)
            g, d = gelu_both(u)
            lg[r, :, part] = g.astype(BF)
            lslope[r, :, part] = d.astype(BF)
            lat[r] += dot(lg[r, :, part], wdown[part, :])

        for c in range(blocks):
            mlp(c)
        return copies

    def backward_latent(r, dx):
        grad_result = thg[r]
        branch = grad_result.astype(BF)
        top = slice(0, LAT)
        add_columns(bd, branch)
        dm[top, :] = branch
        a2[top, :] = la2[r]
        ob[top, :] = lo[r]
        gb[top, :] = lg[r]
        copies = [
            started(dm, fdm.at[r], 4),
            started(a2, fa2.at[r], 2),
            started(ob, fo.at[r], 1),
            started(gb, fg.at[r], 3),
        ]
        da[top, :] = jnp.zeros((LAT, width), F32)

        def mlp(c):
            part = group(c)
            grad = (dot_nt(dm[top, :], wdown[part, :]) * lslope[r, :, part]).astype(BF)
            dub[top, part] = grad
            add_columns(BU + c, grad)
            da[top, :] += dot_nt(grad, wup[:, part])

        for c in range(blocks):
            mlp(c)
        copies.append(started(dub, fdu.at[r], 5))
        hat, scale = normalized(lh[r])
        grad = da[top, :]
        add_columns(G2, grad * hat)
        add_columns(B2, grad)
        middle = grad_result + norm_back(hat, scale, grad * row(G2))
        rounded = middle.astype(BF)
        dhr[top, :] = rounded
        add_columns(BO, rounded)
        copies.append(started(dhr, fdhr.at[r], 6))
        spread = selector_turned(r, 1)
        dyb[r] = exact_dot(spread, middle)
        place = positions(r, 1, 1)
        first = first_length(r)
        key_place = lax.broadcasted_iota(jnp.int32, (length, LAT), 0)
        lowest = jnp.where(place >= first, first, 0)
        limit = jnp.where((key_place <= place) & (key_place >= lowest), NO_CAP, MASKED)
        dob[top, :] = dot_nt(rounded, wout[...]).astype(BF)

        def heads(hp):
            q = lq[r, :, head_lanes(0, hp)]
            key = jn[r, :, head_lanes(1, hp)]
            value = jn[r, :, head_lanes(2, hp)]
            grad_out = dob[top, head_lanes(0, hp)]
            dq, dk, dv = [], [], []
            for h in range(2):
                grad_masked = grad_out * halves[h]
                chance = lp[r, 2 * hp + h].astype(F32)
                inner_part = chance * dot_nt(grad_masked, value)
                total = jnp.sum(inner_part, -1, keepdims=True)
                dq.append(dot((inner_part - chance * total).astype(BF), key))
                scores = dot_nt(key, q * (halves[h] * 0.125))
                chance = softmax(jnp.minimum(scores, limit), 0)
                inner_part = chance * dot_nt(value, grad_masked)
                total = jnp.sum(inner_part, 0, keepdims=True)
                dk.append(dot((inner_part - chance * total).astype(BF), q))
                dv.append(dot(chance.astype(BF), grad_out))
            grad_q = (jnp.where(low, dq[0], dq[1]) * 0.125).astype(BF)
            djb[:, head_lanes(0, hp)] = dot(spread.astype(BF), grad_q).astype(BF)
            djb[:, head_lanes(1, hp)] = (jnp.where(low, dk[0], dk[1]) * 0.125).astype(BF)
            djb[:, head_lanes(2, hp)] = jnp.where(low, dv[0], dv[1]).astype(BF)

        for hp in range(pairs):
            heads(hp)
        copies.append(started(djb, fdj.at[r], 7))
        into_input(r, xin.at[r], dyb.at[r], dx)
        return copies

    staged = (
        (a1, fa1), (ob, fo), (a2, fa2), (gb, fg), (dm, fdm), (dub, fdu), (dhr, fdhr), (djb, fdj)
    )

    def settle_all(count, first=0):
        for number in range(first, first + count):
            source, target = staged[number]
            pltpu.make_async_copy(source, target.at[0], osem.at[number]).wait()

    @pl.when(me == 0)
    def _():
        def forward_step(k, carry):
            r = lax.rem(k, rows)
            set_cap(r)

            @pl.when(k < rows)
            def _():
                xin[k] = emb[r].astype(F32)

            @pl.when(k >= rows)
            def _():
                send_lat(r).wait_recv()
                xin[k] = exact_dot(selector_turned(r, 0), lat[r])

                def step(part, start):
                    xin[k, part, :] += emb[r, part, :].astype(F32) * unmarked(r, start)

                each_chunk(step, 32)

            forward(k, xin.at[k], yb.at[k], k > 0, first=k == 0)
            send_y(k).start()
            return carry

        lax.fori_loop(0, 2 * rows, forward_step, 0)
        settle_all(4)

        def backward_step(i, carry):
            k = lax.rem(i + rows, 2 * rows)
            r = lax.rem(i, rows)
            send_y(k).wait_send()
            send_grad(k).wait_recv()

            @pl.when(i == 2 * rows - 1)
            def _():
                pl.semaphore_signal(
                    heard, inc=1, device_id={"pipe": other}, device_id_type=MESH
                )

            backward(k, xin.at[k], dyb.at[k], yb.at[k], i > 0)

            @pl.when(i < rows)
            def _():
                thg[r] = exact_dot(selector(positions(r, 0)), yb[k])
                send_thoughts(r).start()

            @pl.when(i >= rows)
            def _():
                def step(part, start):
                    yb[k, part, :] += yb[rows + r, part, :] * unmarked(r, start)

                each_chunk(step, 32)
                started(yb.at[k], sec.at[0, r], 8).wait()

            return carry

        lax.fori_loop(0, 2 * rows, backward_step, 0)
        settle_all(4, 4)

        def drain(r, carry):
            send_thoughts(r).wait_send()
            return carry

        lax.fori_loop(0, rows, drain, 0)

    @pl.when(me == 1)
    def _():
        finish(weights)

        def latent_step(r, carry):
            send_y(r).wait_recv()
            copies = forward_latent(r)
            send_lat(r).start()
            finish(copies)
            return carry

        lax.fori_loop(0, rows, latent_step, 0)

        def language_step(r, carry):
            k = rows + r
            set_cap(r)
            send_y(k).wait_recv()
            forward(k, xin.at[k], dyb.at[k], r > 0)
            result = started(dyb.at[k], sec.at[0, r], 8)
            dyb[r] = cot[r].astype(F32)
            backward(k, xin.at[k], dyb.at[r], yb.at[k], r > 0)
            send_grad(k).start()
            result.wait()
            return carry

        lax.fori_loop(0, rows, language_step, 0)
        settle_all(8)
        for buffer in (dm, a2, ob, gb, dub, dhr):
            buffer[...] = jnp.zeros_like(buffer)

        def latent_back_step(r, carry):
            send_thoughts(r).wait_recv()
            copies = backward_latent(r, yb.at[r])
            send_grad(r).start()
            finish(copies)
            return carry

        lax.fori_loop(0, rows, latent_back_step, 0)

        def drain(r, carry):
            send_lat(r).wait_send()
            send_grad(r).wait_send()
            send_grad(rows + r).wait_send()
            return carry

        lax.fori_loop(0, rows, drain, 0)
        pl.semaphore_wait(heard, 1)

    sg[...] = jnp.sum(sums[...], 1)


def layers(emb, cot, seg, tpos, w_qkv, w_out, w_up, w_down, small):
    rows, length, width = emb.shape
    inner = w_up.shape[2]
    thoughts = tpos.shape[1]
    slots = 2 * rows
    packed = small.shape[1] // width
    vmem = pl.BlockSpec(memory_space=pltpu.VMEM)
    anywhere = pl.BlockSpec(memory_space=pl.ANY)
    smem = pl.BlockSpec(memory_space=pltpu.SMEM)

    def factor(columns):
        return jax.ShapeDtypeStruct((slots, length, columns), BF)

    def block(columns, kind=BF):
        return pltpu.VMEM((length, columns), kind)

    def few(columns, kind=BF):
        return pltpu.VMEM((rows, LAT, columns), kind)

    sizes = (rows, length, width, inner, thoughts)
    return pl.pallas_call(
        functools.partial(layers_kernel, sizes),
        out_shape=(
            jax.ShapeDtypeStruct((1, rows, length, width), F32),
            factor(width),
            factor(3 * width),
            factor(width),
            factor(width),
            factor(width),
            factor(inner),
            factor(inner),
            factor(width),
            jax.ShapeDtypeStruct((packed, width), F32),
        ),
        in_specs=[vmem, vmem, vmem, smem] + [anywhere] * 4 + [vmem],
        out_specs=(anywhere,) * 9 + (vmem,),
        scratch_shapes=[
            pltpu.VMEM((packed, 8, width), F32),
            pltpu.VMEM((1, 3 * width), F32),
            pltpu.VMEM((slots, 4, length, 1), F32),
            pltpu.VMEM((width, 3 * width), BF),
            pltpu.VMEM((width, width), BF),
            pltpu.VMEM((width, inner), BF),
            pltpu.VMEM((inner, width), BF),
            pltpu.VMEM((slots, length, width), F32),
            pltpu.VMEM((slots, length, width), F32),
            pltpu.VMEM((slots, length, width), F32),
            pltpu.VMEM((slots, length, 3 * width), BF),
            pltpu.VMEM((slots, HEADS, length, length), BF),
            pltpu.VMEM((slots, length, width), F32),
            pltpu.VMEM((slots, inner, length), BF),
            block(width),
            block(width),
            block(width),
            block(inner),
            block(width),
            block(inner),
            block(width),
            block(3 * width),
            block(width, F32),
            block(width),
            pltpu.VMEM((width, length), BF),
            pltpu.VMEM((width, length), F32),
            pltpu.VMEM((3 * width, length), BF),
            block(length, F32),
            few(width, F32),
            few(width, F32),
            few(width, F32),
            few(width),
            pltpu.VMEM((rows, HEADS, LAT, length), BF),
            few(width, F32),
            few(width),
            few(width),
            few(inner),
            few(inner),
            pltpu.SemaphoreType.DMA((4,)),
            pltpu.SemaphoreType.DMA((9,)),
        ]
        + [pltpu.SemaphoreType.DMA((slots,))] * 4
        + [pltpu.SemaphoreType.DMA((rows,))] * 4
        + [pltpu.SemaphoreType.REGULAR],
        compiler_params=pltpu.CompilerParams(
            collective_id=0, has_side_effects=True, vmem_limit_bytes=62 << 20
        ),
    )(emb, cot, seg, tpos, w_qkv, w_out, w_up, w_down, small)


def summed_by_parts(factors, small_grads):
    fa1, fdj, fo, fdhr, fa2, fdu, fg, fdm = factors

    def product(left, right):
        whole = jnp.einsum("ktm,ktn->mn", left, right, preferred_element_type=F32)
        return lax.psum_scatter(whole[None], "dp", scatter_dimension=1, tiled=True)

    small = lax.psum_scatter(
        small_grads.reshape(1, -1), "dp", scatter_dimension=1, tiled=True
    )
    return product(fa1, fdj), product(fo, fdhr), product(fa2, fdu), product(fg, fdm), small


def gradients_kernel(
    sizes,
    plan,
    lags,
    fa1,
    fdj,
    fo,
    fdhr,
    fa2,
    fdu,
    fg,
    fdm,
    small,
    gqkv,
    gout,
    gup,
    gdown,
    gsmall,
    left,
    right,
    lt,
    lt_down,
    wa,
    ra,
    xa,
    ua,
    na,
    wb,
    rb,
    xb,
    ub,
    nb,
    rs,
    xs,
    us,
    ns,
    xl,
    ul,
    nl,
    kept,
    lsem,
    pair_send,
    pair_recv,
    side_send,
    side_recv,
    up_send,
    up_recv,
    down_send,
    down_recv,
    over_send,
    over_recv,
):
    width, narrow, depth = sizes
    side_lag, hop = lags
    me = lax.axis_index("dp")
    core = lax.rem(me, 2)
    side = lax.rem(me // 2, 2)
    level = me // 4
    partner = me + 1 - 2 * core
    beside = me + 2 - 4 * side
    above, below = me + 4, me - 4
    plane = lax.axis_index("pipe")

    def remote(source, target, send, recv, device):
        return pltpu.make_async_remote_copy(
            src_ref=source,
            dst_ref=target,
            send_sem=send,
            recv_sem=recv,
            device_id={"dp": device},
            device_id_type=MESH,
        )

    buffers = {"wide": (wa, ra, xa, ua, na), "tall": (wb, rb, xb, ub, nb)}
    lefts = {"qkv": fa1, "out": fo, "up": fa2, "down": fg}
    rights = {"qkv": fdj, "out": fdhr, "up": fdu, "down": fdm}
    total = len(plan)
    names = [entry[0] for entry in plan]
    guest = names.index("guest")
    exported = 0
    steps = []
    turned = None
    for number, (name, part, _, columns) in enumerate(plan):
        if name in ("small", "guest"):
            continue
        if name == "down":
            for block in range(depth):
                steps.append((number, name, True, block, None, 0))
                steps.append((number, name, False, block, part, columns))
            continue
        if name != turned:
            steps.append((number, name, True, 0, None, 0))
            turned = name
        steps.append((number, name, False, 0, part, columns))

    def loads(index):
        _, name, turn, block, part, columns = steps[index]
        slot = index % 2
        if turn:
            source = lefts[name].at[:, :, block * width : (block + 1) * width]
            return pltpu.make_async_copy(source, left.at[slot], lsem.at[slot])
        return pltpu.make_async_copy(
            rights[name].at[:, :, part * columns : (part + 1) * columns],
            right.at[slot, :, :, 0:columns],
            lsem.at[slot],
        )

    def start_loads(index):
        if index < len(steps):
            loads(index).start()

    start_loads(0)

    barrier = pltpu.get_barrier_semaphore()

    def greet(device):
        pl.semaphore_signal(barrier, inc=1, device_id={"dp": device}, device_id_type=MESH)

    greet(partner)
    greet(beside)

    @pl.when(level < 3)
    def _():
        greet(above)

    @pl.when(level > 0)
    def _():
        greet(below)

    @pl.when(plane == 1)
    def _():
        pl.semaphore_signal(barrier, inc=1, device_id={"pipe": 0}, device_id_type=MESH)

    pl.semaphore_wait(barrier, 2 + (level + 2) // 3 + (5 - level) // 3 + 1 - plane)

    targets = {"qkv": gqkv, "out": gout, "up": gup, "down": gdown}
    views = []
    previous = {}
    order = {}
    made = {}
    last_of = {number: True for number in range(total)}
    for number, (name, part, line_first, columns) in enumerate(plan):
        kind = kind_of(plan[number])
        if kind == "small":
            views.append((small, rs, xs, us, ns, gsmall))
            previous[number] = None
            continue
        w, r, x, u, n = buffers[kind]
        order.setdefault(kind, []).append(number)
        index = len(order[kind]) - 1
        along = sum(plan[other][2] for other in order[kind][:index])
        if name == "guest":
            views.append(
                (None, r.at[index], x.at[index - along], u.at[index - along], n.at[index - along], kept)
            )
            continue
        made.setdefault(kind, []).append(number)
        turn = len(made[kind]) - 1
        slots_of = w.shape[0]
        previous[number] = made[kind][turn - slots_of] if turn >= slots_of else None
        if previous[number] is not None:
            last_of[previous[number]] = False
        place = targets[name].at[0, :, part * columns : (part + 1) * columns]
        if line_first:
            further = (xl.at[along], ul.at[along], nl.at[along], place)
        else:
            further = (x.at[index - along], u.at[index - along], n.at[index - along], place)
        views.append((w.at[turn % slots_of], r.at[index]) + further)

    def over(source, target, number):
        return pltpu.make_async_remote_copy(
            src_ref=source,
            dst_ref=target,
            send_sem=over_send.at[number],
            recv_sem=over_recv.at[number],
            device_id={"pipe": 1 - plane},
            device_id_type=MESH,
        )

    def hand_over():
        return over(views[exported][1], views[guest][1], 0)

    def hand_back():
        return over(kept, views[exported][5], 1)

    def where(number, condition=None):
        if number in (exported, guest):
            condition = plane == 1 if condition is None else condition & (plane == 1)
        if condition is None:
            return lambda body: body()
        return pl.when(condition)

    def pair_copy(number):
        w, r = views[number][:2]
        return remote(
            w.at[:, :, 1 - core], r, pair_send.at[number], pair_recv.at[number], partner
        )

    def side_copy(number):
        r, x = views[number][1:3]
        source = r.at[level, 1 - side] if plan[number][2] else r.at[:, 1 - side]
        return remote(source, x, side_send.at[number], side_recv.at[number], beside)

    def along_line(number):
        r, x = views[number][1:3]
        return r if plan[number][2] else x

    def up_copy(number, goal, source=None):
        u = views[number][3]
        return remote(
            u.at[goal - 1] if source is None else source,
            u.at[goal - 1],
            up_send.at[number, goal - 1],
            up_recv.at[number, goal - 1],
            above,
        )

    def down_copy(number, goal, source=None):
        n = views[number][4]
        return remote(
            n.at[goal] if source is None else source,
            n.at[goal],
            down_send.at[number, goal],
            down_recv.at[number, goal],
            below,
        )

    def start_line(number):
        base = along_line(number)

        @pl.when(level == 0)
        def _():
            for goal in (3, 2, 1):
                up_copy(number, goal, base.at[goal]).start()

        @pl.when(level == 3)
        def _():
            for goal in (0, 1, 2):
                down_copy(number, goal, base.at[goal]).start()

    position = {"step": 0}
    slots, length = left.shape[1:3]

    def turn_block(slot, target):
        def body(t, carry):
            tokens = pl.ds(pl.multiple_of(t * length, length), length)
            target[:, tokens] = left[slot, t].T
            return carry

        lax.fori_loop(0, slots, body, 0)

    def right_part(slot, lanes):
        part = right[slot, :, :, lanes]
        return part.reshape(slots * length, part.shape[2])

    def multiply(slot, w, columns):
        def tile(t, carry):
            lanes = pl.ds(pl.multiple_of(t * narrow, narrow), narrow)
            product = dot(lt[...], right_part(slot, lanes))
            w[:, :, :, :, lanes] = product.reshape(w.shape[:4] + (narrow,))
            return carry

        lax.fori_loop(0, columns // narrow, tile, 0)


    def produce(number):
        name = plan[number][0]
        if name == "guest":
            return
        if name != "small":
            if previous[number] is not None:
                pair_copy(previous[number]).wait_send()
            w = views[number][0]
            while position["step"] < len(steps) and steps[position["step"]][0] == number:
                index = position["step"]
                position["step"] += 1
                _, source, turn, block, _, columns = steps[index]
                start_loads(index + 1)
                loads(index).wait()
                if turn:
                    turn_block(index % 2, lt_down if source == "down" else lt)
                elif source == "down":
                    part = right_part(index % 2, slice(0, narrow))
                    w[block] = dot(lt_down[...], part).reshape(w.shape[1:])
                else:
                    multiply(index % 2, w, columns)
        pair_copy(number).start()

    def stage_pair(number):
        if number == guest:

            @pl.when(plane == 1)
            def _():
                hand_over().wait_recv()
                side_copy(number).start()

            return
        w, r = views[number][:2]
        pair_copy(number).wait_recv()

        def add(z, carry):
            for s in range(2):
                r[z, s] += w[z, s, core]
            return carry

        lax.fori_loop(0, 4, add, 0)
        if plan[number][2]:
            start_line(number)
            return

        @where(number)
        def _():
            side_copy(number).start()

        if number == exported:

            @pl.when(plane == 0)
            def _():
                hand_over().start()

    def stage_side(number):
        if plan[number][2]:
            return

        @where(number)
        def _():
            r, x = views[number][1:3]
            side_copy(number).wait_recv()

            def add(z, carry):
                x[z] += r[z, side]
                return carry

            lax.fori_loop(0, 4, add, 0)
            start_line(number)

    def stage_up(number, height):
        u = views[number][3]
        base = along_line(number)

        @where(number, level == height)
        def _():
            for goal in range(3, height - 1, -1):
                up_copy(number, goal).wait_recv()
                if goal > height:
                    u[goal - 1] += base[goal]
                    up_copy(number, goal).start()

    def stage_down(number, height):
        n = views[number][4]
        base = along_line(number)

        @where(number, level == height)
        def _():
            for goal in range(0, height + 1):
                down_copy(number, goal).wait_recv()
                if goal < height:
                    n[goal] += base[goal]
                    down_copy(number, goal).start()

    def stage_sum(number):
        u, n, place = views[number][3:]
        base = along_line(number)

        @where(number, level > 0)
        def _():
            base[level] += u[level - 1]

        @where(number, level < 3)
        def _():
            base[level] += n[level]

        if plan[number][2]:
            side_copy(number).start()
            return

        @where(number)
        def _():
            place[...] = base[level]
            if number == guest:
                hand_back().start()

    def stage_last(number):
        if plan[number][2]:
            r, x = views[number][1:3]
            side_copy(number).wait_recv()
            views[number][5][...] = r[level, side] + x[...]

    def at(stage, number, *more):
        if 0 <= number < total:
            stage(number, *more)

    for moment in range(total + side_lag + 3 * hop + 1):
        at(produce, moment)
        at(stage_pair, moment - 1)
        at(stage_side, moment - side_lag)
        for height in range(4):
            if height > 0:
                at(stage_up, moment - side_lag - hop * height, height)
            if height < 3:
                at(stage_down, moment - side_lag - hop * (3 - height), height)
        at(stage_sum, moment - side_lag - 3 * hop)
        at(stage_last, moment - side_lag - 3 * hop - 1)
    for number in range(total):
        if last_of[number] and number != guest:
            pair_copy(number).wait_send()

        @where(number)
        def _():
            side_copy(number).wait_send()

        for goal in (1, 2, 3):

            @where(number, goal > level)
            def _():
                up_copy(number, goal).wait_send()

        for goal in (0, 1, 2):

            @where(number, goal < level)
            def _():
                down_copy(number, goal).wait_send()

    @pl.when(plane == 0)
    def _():
        hand_over().wait_send()
        hand_back().wait_recv()

    @pl.when(plane == 1)
    def _():
        hand_back().wait_send()


def kind_of(entry):
    return {"small": "small", "down": "tall"}.get(entry[0], "wide")


def summed_in_kernel(factors, small_grads):
    fa1, fdj, fo, fdhr, fa2, fdu, fg, fdm = factors
    slots, length, width = fa1.shape
    inner = fg.shape[2]
    owners = 16
    depth = inner // width
    narrow = 256
    a_rows, b_rows = width // owners, inner // owners
    packed = small_grads.size // owners
    lanes = 128
    s_rows = -(-packed // (8 * lanes)) * 8
    small = small_grads.reshape(owners, packed)
    small = jnp.pad(small, ((0, 0), (0, s_rows * lanes - packed)))
    small = small.reshape(4, 2, 2, s_rows, lanes)
    plan = [
        ("qkv", 0, False, width),
        ("qkv", 1, True, width),
        ("qkv", 2, False, width),
        ("small", 0, False, 0),
        ("out", 0, False, width),
        ("up", 0, False, width),
        ("down", 0, False, narrow),
        ("up", 1, True, width),
        ("down", 1, False, narrow),
        ("guest", 0, False, width),
        ("up", 2, False, width),
        ("up", 3, False, width),
        ("down", 2, False, narrow),
    ]
    lags = (3, 2)
    total = len(plan)
    s_block = small.shape[3:]
    vmem = pl.BlockSpec(memory_space=pltpu.VMEM)
    anywhere = pl.BlockSpec(memory_space=pl.ANY)

    def of_kind(kind, slots_of, block):
        mine = [entry for entry in plan if kind_of(entry) == kind]
        across = sum(not entry[2] for entry in mine)
        leads = ((slots_of, 4, 2, 2), (len(mine), 4, 2), (across, 4), (across, 3), (across, 3))
        return [pltpu.VMEM(lead + block, F32) for lead in leads]

    line_count = sum(line_first for _, _, line_first, _ in plan)
    a_block = (a_rows, width)
    *grads, small_grad = pl.pallas_call(
        functools.partial(gradients_kernel, (width, narrow, depth), plan, lags),
        out_shape=(
            jax.ShapeDtypeStruct((1, a_rows, 3 * width), F32),
            jax.ShapeDtypeStruct((1, a_rows, width), F32),
            jax.ShapeDtypeStruct((1, a_rows, inner), F32),
            jax.ShapeDtypeStruct((1, b_rows, width), F32),
            jax.ShapeDtypeStruct(s_block, F32),
        ),
        in_specs=[anywhere] * 8 + [vmem],
        out_specs=(vmem,) * 5,
        scratch_shapes=[
            pltpu.VMEM((2, slots, length, width), BF),
            pltpu.VMEM((2, slots, length, width), BF),
            pltpu.VMEM((width, slots * length), BF),
            pltpu.VMEM((width, slots * length), BF),
        ]
        + of_kind("wide", 2, a_block)
        + of_kind("tall", 1, (b_rows, narrow))
        + [pltpu.VMEM(lead + s_block, F32) for lead in ((4, 2), (4,), (3,), (3,))]
        + [
            pltpu.VMEM((line_count,) + a_block, F32),
            pltpu.VMEM((line_count, 3, 2) + a_block, F32),
            pltpu.VMEM((line_count, 3, 2) + a_block, F32),
            pltpu.VMEM(a_block, F32),
        ]
        + [pltpu.SemaphoreType.DMA((2,))]
        + [pltpu.SemaphoreType.DMA((total,))] * 4
        + [pltpu.SemaphoreType.DMA((total, 3))] * 4
        + [pltpu.SemaphoreType.DMA((2,))] * 2,
        compiler_params=pltpu.CompilerParams(
            collective_id=1, has_side_effects=True, vmem_limit_bytes=62 << 20
        ),
    )(*factors, small)
    return tuple(grads) + (small_grad,)


def results_kernel(count, *refs):
    sources, small = refs[:count], refs[count]
    targets, packed = refs[count + 1 : 2 * count + 1], refs[2 * count + 1]
    held, load_sem, store_sem = refs[2 * count + 2 : -2], refs[-2], refs[-1]
    loads = [
        pltpu.make_async_copy(sources[i], held[i], load_sem.at[i]) for i in range(count)
    ]
    stores = [
        pltpu.make_async_copy(held[i], targets[i], store_sem.at[i]) for i in range(count)
    ]
    for load in loads:
        load.start()
    lines = [small[line : line + 1, :] for line in range(small.shape[0])]
    packed[...] = jnp.concatenate(lines, 1)[:, : packed.shape[1]]
    for load, store in zip(loads, stores):
        load.wait()
        store.start()
    for store in stores:
        store.wait()


def copied_out(large, small, packed):
    count = len(large)
    vmem = pl.BlockSpec(memory_space=pltpu.VMEM)
    anywhere = pl.BlockSpec(memory_space=pl.ANY)
    shapes = [jax.ShapeDtypeStruct(array.shape, array.dtype) for array in large]
    return pl.pallas_call(
        functools.partial(results_kernel, count),
        out_shape=tuple(shapes) + (jax.ShapeDtypeStruct((1, packed), F32),),
        in_specs=[anywhere] * count + [vmem],
        out_specs=(anywhere,) * count + (vmem,),
        scratch_shapes=[pltpu.VMEM(array.shape, array.dtype) for array in large]
        + [pltpu.SemaphoreType.DMA((count,))] * 2,
        compiler_params=pltpu.CompilerParams(vmem_limit_bytes=62 << 20),
    )(*large, small)


def reduced(section_out, factors, small_grads):
    if lax.axis_size("dp") == 16:
        *grads, small_grad = summed_in_kernel(factors, small_grads)
        return copied_out([section_out] + grads, small_grad, small_grads.size // 16)
    return (section_out,) + tuple(summed_by_parts(factors, small_grads))


def per_device(
    embeddings, cotangent, seg_ids, thought_pos, w_qkv, w_out, w_up, w_down, small_params
):
    section_out, *factors, small_grads = layers(
        embeddings, cotangent, seg_ids, thought_pos, w_qkv, w_out, w_up, w_down, small_params
    )
    return tuple(reduced(section_out, factors, small_grads))


def solution(mesh):
    return jax.shard_map(
        per_device,
        mesh=mesh,
        in_specs=(
            P("dp", None, None),
            P("dp", None, None),
            P("dp", None),
            P("dp", None),
            P("pipe", None, None),
            P("pipe", None, None),
            P("pipe", None, None),
            P("pipe", None, None),
            P("pipe", None),
        ),
        out_specs=(
            P("pipe", "dp", None, None),
            P("pipe", "dp", None),
            P("pipe", "dp", None),
            P("pipe", "dp", None),
            P("pipe", "dp", None),
            P("pipe", "dp"),
        ),
        check_vma=False,
    )
```

```python
import functools

import jax
import jax.numpy as jnp
from jax import lax
from jax.experimental import pallas as pl
from jax.experimental.pallas import tpu as pltpu
from jax.sharding import PartitionSpec as P

HEADS = 12
BF = jnp.bfloat16
F32 = jnp.float32
MESH = pl.DeviceIdType.MESH
EPSILON = 1e-05
MASKED = -1000000000.0
NO_CAP = 3e38
LAT = 16
G1, B1, BQ, BV, BO, G2, B2, BU = 0, 1, 2, 3, 4, 5, 6, 7


def dot(a, b):
    return lax.dot_general(a, b, (((1,), (0,)), ((), ())), preferred_element_type=F32)


def dot_nt(a, b):
    return lax.dot_general(a, b, (((1,), (1,)), ((), ())), preferred_element_type=F32)


def dot_tn(a, b):
    return lax.dot_general(a, b, (((0,), (0,)), ((), ())), preferred_element_type=F32)


def exact_dot(a, b):
    return lax.dot_general(
        a,
        b,
        (((1,), (0,)), ((), ())),
        precision=lax.Precision.HIGHEST,
        preferred_element_type=F32,
    )


def normalized(values):
    centred = values - jnp.mean(values, -1, keepdims=True)
    spread = jnp.mean(centred * centred, -1, keepdims=True)
    scale = lax.rsqrt(spread + EPSILON)
    return centred * scale, scale


def norm_back(hat, scale, grad):
    along = jnp.mean(grad * hat, -1, keepdims=True)
    return scale * (grad - jnp.mean(grad, -1, keepdims=True) - hat * along)


def gelu_both(u):
    c = 0.7978845608028654
    square = u * u
    t = jnp.tanh(c * u * (1.0 + 0.044715 * square))
    half = 0.5 + 0.5 * t
    slope = half + (0.5 * c) * u * (1.0 - t * t) * (1.0 + (3 * 0.044715) * square)
    return u * half, slope


def softmax(scores, axis=-1):
    e = jnp.exp(scores - jnp.max(scores, axis, keepdims=True))
    return e * (1.0 / jnp.sum(e, axis, keepdims=True))


def layers_kernel(
    sizes,
    emb,
    cot,
    seg,
    tpos,
    wqkv_h,
    wout_h,
    wup_h,
    wdown_h,
    small,
    sec,
    fa1,
    fdj,
    fo,
    fdhr,
    fa2,
    fdu,
    fg,
    fdm,
    sg,
    sums,
    joint,
    stat,
    wqkv,
    wout,
    wup,
    wdown,
    xin,
    yb,
    dyb,
    jn,
    pr,
    hm,
    slope,
    a1,
    ob,
    a2,
    gb,
    dm,
    dub,
    dhr,
    djb,
    da,
    dob,
    dmt,
    dat,
    djt,
    cap,
    lat,
    thg,
    lx,
    lq,
    lp,
    lh,
    la2,
    lo,
    lg,
    lslope,
    wsem,
    osem,
    ysend,
    yrecv,
    gsend,
    grecv,
    lsend,
    lrecv,
    tsend,
    trecv,
    heard,
):
    rows, length, width, inner, thoughts = sizes
    blocks = inner // width
    bd = BU + blocks
    pairs = HEADS // 2
    me = lax.axis_index("pipe")
    other = 1 - me

    weights = [
        pltpu.make_async_copy(source.at[0], target, wsem.at[number])
        for number, (source, target) in enumerate(
            ((wqkv_h, wqkv), (wout_h, wout), (wup_h, wup), (wdown_h, wdown))
        )
    ]
    for copy in weights:
        copy.start()
    barrier = pltpu.get_barrier_semaphore()
    pl.semaphore_signal(barrier, inc=1, device_id={"pipe": other}, device_id_type=MESH)
    pl.semaphore_wait(barrier, 1)
    sums[...] = jnp.zeros_like(sums)
    joint[:, 0:width] = small[:, BQ * width : (BQ + 1) * width]
    joint[:, width : 2 * width] = jnp.zeros((1, width), F32)
    joint[:, 2 * width : 3 * width] = small[:, BV * width : (BV + 1) * width]

    def remote(source, target, send, recv):
        return pltpu.make_async_remote_copy(
            src_ref=source,
            dst_ref=target,
            send_sem=send,
            recv_sem=recv,
            device_id={"pipe": other},
            device_id_type=MESH,
        )

    def send_y(k):
        return remote(yb.at[k], xin.at[k], ysend.at[k], yrecv.at[k])

    def send_grad(k):
        return remote(yb.at[k], dyb.at[k], gsend.at[k], grecv.at[k])

    def send_lat(r):
        return remote(lat.at[r], lat.at[r], lsend.at[r], lrecv.at[r])

    def send_thoughts(r):
        return remote(thg.at[r], thg.at[r], tsend.at[r], trecv.at[r])

    def started(source, target, number):
        copy = pltpu.make_async_copy(source, target, osem.at[number])
        copy.start()
        return copy

    def settle(pending, number, source, target):
        @pl.when(pending)
        def _():
            pltpu.make_async_copy(source, target.at[0], osem.at[number]).wait()

    def finish(copies):
        for copy in copies:
            copy.wait()

    def each_chunk(step, count):
        def body(i, carry):
            step(pl.ds(pl.multiple_of(i * count, count), count), i * count)
            return carry

        lax.fori_loop(0, length // count, body, 0)

    def loop(count, step):
        def body(i, carry):
            step(i)
            return carry

        lax.fori_loop(0, count, body, 0)

    def add_columns(number, values):
        sums[number] += jnp.sum(values.astype(F32).reshape(-1, 8, width), 0)

    def row(number):
        return small[:, group(number)]

    def group(number):
        return slice(number * width, (number + 1) * width)

    lane = lax.broadcasted_iota(jnp.int32, (1, 128), 1)
    low = lane < 64
    halves = (jnp.where(low, 1.0, 0.0).astype(BF), jnp.where(low, 0.0, 1.0).astype(BF))

    def first_length(r):
        segment = seg[pl.ds(r, 1), :]
        return jnp.sum(jnp.where(segment == 0, 1.0, 0.0), -1, keepdims=True).astype(jnp.int32)

    def set_cap(r):
        first = first_length(r)
        query = lax.broadcasted_iota(jnp.int32, (length, length), 0)
        key = lax.broadcasted_iota(jnp.int32, (length, length), 1)
        lowest = jnp.where(query >= first, first, 0)
        cap[...] = jnp.where((key <= query) & (key >= lowest), NO_CAP, MASKED)

    def positions(r, shift, axis=0):
        shape = (LAT, 1) if axis == 0 else (1, LAT)
        number = lax.broadcasted_iota(jnp.int32, shape, axis)
        result = jnp.full(shape, -1, jnp.int32)
        for j in range(thoughts):
            result = jnp.where(number == j, tpos[r, j] - shift, result)
        return result

    def selector_turned(r, shift):
        place = positions(r, shift, 1)
        return jnp.where(lax.broadcasted_iota(jnp.int32, (length, LAT), 0) == place, 1.0, 0.0)

    def selector(place):
        return jnp.where(lax.broadcasted_iota(jnp.int32, (LAT, length), 1) == place, 1.0, 0.0)

    def unmarked(r, start):
        place = lax.broadcasted_iota(jnp.int32, (32, 1), 0) + start
        keep = jnp.ones((32, 1), F32)
        for j in range(thoughts):
            keep = jnp.where(place == tpos[r, j], 0.0, keep)
        return keep

    def head_lanes(part, hp):
        start = part * width + hp * 128
        if isinstance(hp, int):
            return slice(start, start + 128)
        return pl.ds(pl.multiple_of(start, 128), 128)

    def norm_rows(x, target, k, which, gain, shift, more=None):
        def step(part, _):
            values = x[part, :]
            center = jnp.mean(values, -1, keepdims=True)
            centred = values - center
            scale = lax.rsqrt(jnp.mean(centred * centred, -1, keepdims=True) + EPSILON)
            stat[k, 2 * which, part, :] = center
            stat[k, 2 * which + 1, part, :] = scale
            target[part, :] = (centred * scale * row(gain) + row(shift)).astype(BF)
            if more is not None:
                more(part, values)

        each_chunk(step, 128)

    def norm_rows_back(x, part, k, which, gain, shift):
        scale = stat[k, 2 * which + 1, part, :]
        hat = (x[part, :] - stat[k, 2 * which, part, :]) * scale
        grad = da[part, :]
        add_columns(gain, grad * hat)
        add_columns(shift, grad)
        return norm_back(hat, scale, grad * row(gain))

    def forward(k, x, y, pending, first=None):
        def need(number):
            if first is not None:

                @pl.when(first)
                def _():
                    weights[number].wait()

        settle(pending, 0, a1, fa1)
        norm_rows(x, a1, k, 0, G1, B1)
        started(a1, fa1.at[k], 0)
        need(0)
        settle(pending, 1, ob, fo)

        for part in range(3):
            joined = dot(a1[...], wqkv[:, group(part)]) + joint[:, group(part)]
            jn[k, :, group(part)] = joined.astype(BF)
        for hp in range(pairs):
            q = jn[k, :, head_lanes(0, hp)]
            key = jn[k, :, head_lanes(1, hp)]
            value = jn[k, :, head_lanes(2, hp)]
            out = []
            for h in range(2):
                scores = dot_nt(q * (halves[h] * 0.125), key)
                chance = softmax(jnp.minimum(scores, cap[...])).astype(BF)
                pr[k, 2 * hp + h] = chance
                out.append(dot(chance, value))
            ob[:, head_lanes(0, hp)] = jnp.where(low, out[0], out[1]).astype(BF)
        started(ob, fo.at[k], 1)
        need(1)
        settle(pending, 2, a2, fa2)
        hm[k] = x[...] + dot(ob[...], wout[...]) + row(BO)

        def begin(part, values):
            y[part, :] = values + row(bd)

        norm_rows(hm.at[k], a2, k, 1, G2, B2, begin)
        started(a2, fa2.at[k], 2)
        need(2)
        need(3)
        settle(pending, 3, gb, fg)

        for c in range(blocks):
            part = group(c)
            g, d = gelu_both(dot(a2[...], wup[:, part]) + row(BU + c))
            gb[:, part] = g.astype(BF)
            slope[k, part, :] = d.astype(BF).T
            y[...] += dot(gb[:, part], wdown[part, :])
        started(gb, fg.at[k], 3)

    def backward(k, x, dy, dx, pending):
        def step(part, _):
            branch = dy[part, :].astype(BF)
            dm[part, :] = branch
            add_columns(bd, branch)

        settle(pending, 4, dm, fdm)
        each_chunk(step, 64)
        started(dm, fdm.at[k], 4)
        dmt[...] = dm[...].T
        dat[...] = jnp.zeros_like(dat)
        settle(pending, 5, dub, fdu)

        def mlp(c):
            part = pl.ds(pl.multiple_of(c * width, width), width)
            grad = (dot(wdown[part, :], dmt[...]) * slope[k, part, :]).astype(BF)
            dat[...] += dot(wup[:, part], grad)
            turned = grad.T
            dub[:, part] = turned
            add_columns(BU + c, turned)

        loop(blocks, mlp)
        da[...] = dat[...].T
        started(dub, fdu.at[k], 5)
        settle(pending, 6, dhr, fdhr)

        def step_two(part, _):
            middle = dy[part, :] + norm_rows_back(hm.at[k], part, k, 1, G2, B2)
            dy[part, :] = middle
            branch = middle.astype(BF)
            dhr[part, :] = branch
            add_columns(BO, branch)

        each_chunk(step_two, 64)
        started(dhr, fdhr.at[k], 6)
        dmt[...] = dhr[...].T
        dob[...] = dot(wout[...], dmt[...]).astype(BF).T
        settle(pending, 7, djb, fdj)

        def heads(hp):
            q = jn[k, :, head_lanes(0, hp)]
            key = jn[k, :, head_lanes(1, hp)]
            value = jn[k, :, head_lanes(2, hp)]
            grad_out = dob[:, head_lanes(0, hp)]
            dq, dk, dv = [], [], []
            for h in range(2):
                chance = pr[k, 2 * hp + h]
                chance_full = chance.astype(F32)
                inner_part = chance_full * dot_nt(grad_out * halves[h], value)
                total = jnp.sum(inner_part, -1, keepdims=True)
                grad_scores = (inner_part - chance_full * total).astype(BF)
                dq.append(dot(grad_scores, key))
                dk.append(dot_tn(grad_scores, q))
                dv.append(dot_tn(chance, grad_out))
            djb[:, head_lanes(0, hp)] = (jnp.where(low, dq[0], dq[1]) * 0.125).astype(BF)
            djb[:, head_lanes(1, hp)] = (jnp.where(low, dk[0], dk[1]) * 0.125).astype(BF)
            djb[:, head_lanes(2, hp)] = jnp.where(low, dv[0], dv[1]).astype(BF)

        loop(pairs, heads)
        started(djb, fdj.at[k], 7)
        into_input(k, x, dy, dx)

    def into_input(k, x, middle, dx):
        djt[...] = djb[...].T
        da[...] = dot(wqkv[...], djt[...]).T

        def step(part, _):
            add_columns(BQ, djb[part, group(0)])
            add_columns(BV, djb[part, group(2)])
            dx[part, :] = middle[part, :] + norm_rows_back(x, part, k, 0, G1, B1)

        each_chunk(step, 64)

    def forward_latent(r):
        x = xin.at[r]
        norm_rows(x, a1, r, 0, G1, B1)
        copies = [started(a1, fa1.at[r], 0)]
        jn[r, :, group(1)] = dot(a1[...], wqkv[:, group(1)]).astype(BF)
        jn[r, :, group(2)] = (dot(a1[...], wqkv[:, group(2)]) + row(BV)).astype(BF)
        place = positions(r, 1)
        chosen = exact_dot(selector(place), x[...])
        lx[r] = chosen
        hat, _ = normalized(chosen)
        normed = (hat * row(G1) + row(B1)).astype(BF)
        lq[r] = (dot(normed, wqkv[:, group(0)]) + row(BQ)).astype(BF)
        first = first_length(r)
        key_place = lax.broadcasted_iota(jnp.int32, (LAT, length), 1)
        lowest = jnp.where(place >= first, first, 0)
        limit = jnp.where((key_place <= place) & (key_place >= lowest), NO_CAP, MASKED)

        def heads(hp):
            q = lq[r, :, head_lanes(0, hp)]
            key = jn[r, :, head_lanes(1, hp)]
            value = jn[r, :, head_lanes(2, hp)]
            out = []
            for h in range(2):
                scores = dot_nt(q * (halves[h] * 0.125), key)
                chance = softmax(jnp.minimum(scores, limit)).astype(BF)
                lp[r, 2 * hp + h] = chance
                out.append(dot(chance, value))
            lo[r, :, head_lanes(0, hp)] = jnp.where(low, out[0], out[1]).astype(BF)

        for hp in range(pairs):
            heads(hp)
        middle = chosen + dot(lo[r], wout[...]) + row(BO)
        lh[r] = middle
        hat, _ = normalized(middle)
        la2[r] = (hat * row(G2) + row(B2)).astype(BF)
        lat[r] = middle + row(bd)

        def mlp(c):
            part = group(c)
            u = dot(la2[r], wup[:, part]) + row(BU + c)
            g, d = gelu_both(u)
            lg[r, :, part] = g.astype(BF)
            lslope[r, :, part] = d.astype(BF)
            lat[r] += dot(lg[r, :, part], wdown[part, :])

        for c in range(blocks):
            mlp(c)
        return copies

    def backward_latent(r, dx):
        grad_result = thg[r]
        branch = grad_result.astype(BF)
        top = slice(0, LAT)
        add_columns(bd, branch)
        dm[top, :] = branch
        a2[top, :] = la2[r]
        ob[top, :] = lo[r]
        gb[top, :] = lg[r]
        copies = [
            started(dm, fdm.at[r], 4),
            started(a2, fa2.at[r], 2),
            started(ob, fo.at[r], 1),
            started(gb, fg.at[r], 3),
        ]
        da[top, :] = jnp.zeros((LAT, width), F32)

        def mlp(c):
            part = group(c)
            grad = (dot_nt(dm[top, :], wdown[part, :]) * lslope[r, :, part]).astype(BF)
            dub[top, part] = grad
            add_columns(BU + c, grad)
            da[top, :] += dot_nt(grad, wup[:, part])

        for c in range(blocks):
            mlp(c)
        copies.append(started(dub, fdu.at[r], 5))
        hat, scale = normalized(lh[r])
        grad = da[top, :]
        add_columns(G2, grad * hat)
        add_columns(B2, grad)
        middle = grad_result + norm_back(hat, scale, grad * row(G2))
        rounded = middle.astype(BF)
        dhr[top, :] = rounded
        add_columns(BO, rounded)
        copies.append(started(dhr, fdhr.at[r], 6))
        spread = selector_turned(r, 1)
        dyb[r] = exact_dot(spread, middle)
        place = positions(r, 1, 1)
        first = first_length(r)
        key_place = lax.broadcasted_iota(jnp.int32, (length, LAT), 0)
        lowest = jnp.where(place >= first, first, 0)
        limit = jnp.where((key_place <= place) & (key_place >= lowest), NO_CAP, MASKED)
        dob[top, :] = dot_nt(rounded, wout[...]).astype(BF)

        def heads(hp):
            q = lq[r, :, head_lanes(0, hp)]
            key = jn[r, :, head_lanes(1, hp)]
            value = jn[r, :, head_lanes(2, hp)]
            grad_out = dob[top, head_lanes(0, hp)]
            dq, dk, dv = [], [], []
            for h in range(2):
                grad_masked = grad_out * halves[h]
                chance = lp[r, 2 * hp + h].astype(F32)
                inner_part = chance * dot_nt(grad_masked, value)
                total = jnp.sum(inner_part, -1, keepdims=True)
                dq.append(dot((inner_part - chance * total).astype(BF), key))
                scores = dot_nt(key, q * (halves[h] * 0.125))
                chance = softmax(jnp.minimum(scores, limit), 0)
                inner_part = chance * dot_nt(value, grad_masked)
                total = jnp.sum(inner_part, 0, keepdims=True)
                dk.append(dot((inner_part - chance * total).astype(BF), q))
                dv.append(dot(chance.astype(BF), grad_out))
            grad_q = (jnp.where(low, dq[0], dq[1]) * 0.125).astype(BF)
            djb[:, head_lanes(0, hp)] = dot(spread.astype(BF), grad_q).astype(BF)
            djb[:, head_lanes(1, hp)] = (jnp.where(low, dk[0], dk[1]) * 0.125).astype(BF)
            djb[:, head_lanes(2, hp)] = jnp.where(low, dv[0], dv[1]).astype(BF)

        for hp in range(pairs):
            heads(hp)
        copies.append(started(djb, fdj.at[r], 7))
        into_input(r, xin.at[r], dyb.at[r], dx)
        return copies

    staged = (
        (a1, fa1), (ob, fo), (a2, fa2), (gb, fg), (dm, fdm), (dub, fdu), (dhr, fdhr), (djb, fdj)
    )

    def settle_all(count, first=0):
        for number in range(first, first + count):
            source, target = staged[number]
            pltpu.make_async_copy(source, target.at[0], osem.at[number]).wait()

    @pl.when(me == 0)
    def _():
        def forward_step(k, carry):
            r = lax.rem(k, rows)
            set_cap(r)

            @pl.when(k < rows)
            def _():
                xin[k] = emb[r].astype(F32)

            @pl.when(k >= rows)
            def _():
                send_lat(r).wait_recv()
                xin[k] = exact_dot(selector_turned(r, 0), lat[r])

                def step(part, start):
                    xin[k, part, :] += emb[r, part, :].astype(F32) * unmarked(r, start)

                each_chunk(step, 32)

            forward(k, xin.at[k], yb.at[k], k > 0, first=k == 0)
            send_y(k).start()
            return carry

        lax.fori_loop(0, 2 * rows, forward_step, 0)
        settle_all(4)

        def backward_step(i, carry):
            k = lax.rem(i + rows, 2 * rows)
            r = lax.rem(i, rows)
            send_y(k).wait_send()
            send_grad(k).wait_recv()

            @pl.when(i == 2 * rows - 1)
            def _():
                pl.semaphore_signal(
                    heard, inc=1, device_id={"pipe": other}, device_id_type=MESH
                )

            backward(k, xin.at[k], dyb.at[k], yb.at[k], i > 0)

            @pl.when(i < rows)
            def _():
                thg[r] = exact_dot(selector(positions(r, 0)), yb[k])
                send_thoughts(r).start()

            @pl.when(i >= rows)
            def _():
                def step(part, start):
                    yb[k, part, :] += yb[rows + r, part, :] * unmarked(r, start)

                each_chunk(step, 32)
                started(yb.at[k], sec.at[0, r], 8).wait()

            return carry

        lax.fori_loop(0, 2 * rows, backward_step, 0)
        settle_all(4, 4)

        def drain(r, carry):
            send_thoughts(r).wait_send()
            return carry

        lax.fori_loop(0, rows, drain, 0)

    @pl.when(me == 1)
    def _():
        finish(weights)

        def latent_step(r, carry):
            send_y(r).wait_recv()
            copies = forward_latent(r)
            send_lat(r).start()
            finish(copies)
            return carry

        lax.fori_loop(0, rows, latent_step, 0)

        def language_step(r, carry):
            k = rows + r
            set_cap(r)
            send_y(k).wait_recv()
            forward(k, xin.at[k], dyb.at[k], r > 0)
            result = started(dyb.at[k], sec.at[0, r], 8)
            dyb[r] = cot[r].astype(F32)
            backward(k, xin.at[k], dyb.at[r], yb.at[k], r > 0)
            send_grad(k).start()
            result.wait()
            return carry

        lax.fori_loop(0, rows, language_step, 0)
        settle_all(8)
        for buffer in (dm, a2, ob, gb, dub, dhr):
            buffer[...] = jnp.zeros_like(buffer)

        def latent_back_step(r, carry):
            send_thoughts(r).wait_recv()
            copies = backward_latent(r, yb.at[r])
            send_grad(r).start()
            finish(copies)
            return carry

        lax.fori_loop(0, rows, latent_back_step, 0)

        def drain(r, carry):
            send_lat(r).wait_send()
            send_grad(r).wait_send()
            send_grad(rows + r).wait_send()
            return carry

        lax.fori_loop(0, rows, drain, 0)
        pl.semaphore_wait(heard, 1)

    sg[...] = jnp.sum(sums[...], 1)


def layers(emb, cot, seg, tpos, w_qkv, w_out, w_up, w_down, small):
    rows, length, width = emb.shape
    inner = w_up.shape[2]
    thoughts = tpos.shape[1]
    slots = 2 * rows
    packed = small.shape[1] // width
    vmem = pl.BlockSpec(memory_space=pltpu.VMEM)
    anywhere = pl.BlockSpec(memory_space=pl.ANY)
    smem = pl.BlockSpec(memory_space=pltpu.SMEM)

    def factor(columns):
        return jax.ShapeDtypeStruct((slots, length, columns), BF)

    def block(columns, kind=BF):
        return pltpu.VMEM((length, columns), kind)

    def few(columns, kind=BF):
        return pltpu.VMEM((rows, LAT, columns), kind)

    sizes = (rows, length, width, inner, thoughts)
    return pl.pallas_call(
        functools.partial(layers_kernel, sizes),
        out_shape=(
            jax.ShapeDtypeStruct((1, rows, length, width), F32),
            factor(width),
            factor(3 * width),
            factor(width),
            factor(width),
            factor(width),
            factor(inner),
            factor(inner),
            factor(width),
            jax.ShapeDtypeStruct((packed, width), F32),
        ),
        in_specs=[vmem, vmem, vmem, smem] + [anywhere] * 4 + [vmem],
        out_specs=(anywhere,) * 9 + (vmem,),
        scratch_shapes=[
            pltpu.VMEM((packed, 8, width), F32),
            pltpu.VMEM((1, 3 * width), F32),
            pltpu.VMEM((slots, 4, length, 1), F32),
            pltpu.VMEM((width, 3 * width), BF),
            pltpu.VMEM((width, width), BF),
            pltpu.VMEM((width, inner), BF),
            pltpu.VMEM((inner, width), BF),
            pltpu.VMEM((slots, length, width), F32),
            pltpu.VMEM((slots, length, width), F32),
            pltpu.VMEM((slots, length, width), F32),
            pltpu.VMEM((slots, length, 3 * width), BF),
            pltpu.VMEM((slots, HEADS, length, length), BF),
            pltpu.VMEM((slots, length, width), F32),
            pltpu.VMEM((slots, inner, length), BF),
            block(width),
            block(width),
            block(width),
            block(inner),
            block(width),
            block(inner),
            block(width),
            block(3 * width),
            block(width, F32),
            block(width),
            pltpu.VMEM((width, length), BF),
            pltpu.VMEM((width, length), F32),
            pltpu.VMEM((3 * width, length), BF),
            block(length, F32),
            few(width, F32),
            few(width, F32),
            few(width, F32),
            few(width),
            pltpu.VMEM((rows, HEADS, LAT, length), BF),
            few(width, F32),
            few(width),
            few(width),
            few(inner),
            few(inner),
            pltpu.SemaphoreType.DMA((4,)),
            pltpu.SemaphoreType.DMA((9,)),
        ]
        + [pltpu.SemaphoreType.DMA((slots,))] * 4
        + [pltpu.SemaphoreType.DMA((rows,))] * 4
        + [pltpu.SemaphoreType.REGULAR],
        compiler_params=pltpu.CompilerParams(
            collective_id=0, has_side_effects=True, vmem_limit_bytes=62 << 20
        ),
    )(emb, cot, seg, tpos, w_qkv, w_out, w_up, w_down, small)


def summed_by_parts(factors, small_grads):
    fa1, fdj, fo, fdhr, fa2, fdu, fg, fdm = factors

    def product(left, right):
        whole = jnp.einsum("ktm,ktn->mn", left, right, preferred_element_type=F32)
        return lax.psum_scatter(whole[None], "dp", scatter_dimension=1, tiled=True)

    small = lax.psum_scatter(
        small_grads.reshape(1, -1), "dp", scatter_dimension=1, tiled=True
    )
    return product(fa1, fdj), product(fo, fdhr), product(fa2, fdu), product(fg, fdm), small


def gradients_kernel(
    sizes,
    plan,
    lags,
    fa1,
    fdj,
    fo,
    fdhr,
    fa2,
    fdu,
    fg,
    fdm,
    small,
    gqkv,
    gout,
    gup,
    gdown,
    gsmall,
    left,
    right,
    lt,
    lt_down,
    left_down,
    right_down,
    wa,
    ra,
    xa,
    ua,
    na,
    wb,
    rb,
    xb,
    ub,
    nb,
    rs,
    xs,
    us,
    ns,
    xl,
    ul,
    nl,
    kept,
    lsem,
    pair_send,
    pair_recv,
    side_send,
    side_recv,
    up_send,
    up_recv,
    down_send,
    down_recv,
    over_send,
    over_recv,
):
    width, narrow, depth = sizes
    side_lag, hop = lags
    me = lax.axis_index("dp")
    core = lax.rem(me, 2)
    side = lax.rem(me // 2, 2)
    level = me // 4
    partner = me + 1 - 2 * core
    beside = me + 2 - 4 * side
    above, below = me + 4, me - 4
    plane = lax.axis_index("pipe")

    def remote(source, target, send, recv, device):
        return pltpu.make_async_remote_copy(
            src_ref=source,
            dst_ref=target,
            send_sem=send,
            recv_sem=recv,
            device_id={"dp": device},
            device_id_type=MESH,
        )

    buffers = {"wide": (wa, ra, xa, ua, na), "tall": (wb, rb, xb, ub, nb)}
    lefts = {"qkv": fa1, "out": fo, "up": fa2, "down": fg}
    rights = {"qkv": fdj, "out": fdhr, "up": fdu, "down": fdm}
    total = len(plan)
    names = [entry[0] for entry in plan]
    guest = names.index("guest")
    exported = 0
    steps = []
    turned = None
    for number, (name, part, _, columns) in enumerate(plan):
        if name in ("small", "guest", "down"):
            continue
        if name != turned:
            steps.append((number, name, True, 0, None, 0))
            turned = name
        steps.append((number, name, False, 0, part, columns))

    def loads(index):
        _, name, turn, block, part, columns = steps[index]
        slot = index % 2
        if turn:
            source = lefts[name].at[:, :, block * width : (block + 1) * width]
            return pltpu.make_async_copy(source, left.at[slot], lsem.at[slot])
        return pltpu.make_async_copy(
            rights[name].at[:, :, part * columns : (part + 1) * columns],
            right.at[slot, :, :, 0:columns],
            lsem.at[slot],
        )

    def start_loads(index):
        if index < len(steps):
            loads(index).start()

    start_loads(0)

    barrier = pltpu.get_barrier_semaphore()

    def greet(device):
        pl.semaphore_signal(barrier, inc=1, device_id={"dp": device}, device_id_type=MESH)

    greet(partner)
    greet(beside)

    @pl.when(level < 3)
    def _():
        greet(above)

    @pl.when(level > 0)
    def _():
        greet(below)

    @pl.when(plane == 1)
    def _():
        pl.semaphore_signal(barrier, inc=1, device_id={"pipe": 0}, device_id_type=MESH)

    pl.semaphore_wait(barrier, 2 + (level + 2) // 3 + (5 - level) // 3 + 1 - plane)

    targets = {"qkv": gqkv, "out": gout, "up": gup, "down": gdown}
    views = []
    previous = {}
    order = {}
    made = {}
    last_of = {number: True for number in range(total)}
    for number, (name, part, line_first, columns) in enumerate(plan):
        kind = kind_of(plan[number])
        if kind == "small":
            views.append((small, rs, xs, us, ns, gsmall))
            previous[number] = None
            continue
        w, r, x, u, n = buffers[kind]
        order.setdefault(kind, []).append(number)
        index = len(order[kind]) - 1
        along = sum(plan[other][2] for other in order[kind][:index])
        if name == "guest":
            views.append(
                (None, r.at[index], x.at[index - along], u.at[index - along], n.at[index - along], kept)
            )
            continue
        made.setdefault(kind, []).append(number)
        turn = len(made[kind]) - 1
        slots_of = w.shape[0]
        previous[number] = made[kind][turn - slots_of] if turn >= slots_of else None
        if previous[number] is not None:
            last_of[previous[number]] = False
        place = targets[name].at[0, :, part * columns : (part + 1) * columns]
        if line_first:
            further = (xl.at[along], ul.at[along], nl.at[along], place)
        else:
            further = (x.at[index - along], u.at[index - along], n.at[index - along], place)
        views.append((w.at[turn % slots_of], r.at[index]) + further)

    def over(source, target, number):
        return pltpu.make_async_remote_copy(
            src_ref=source,
            dst_ref=target,
            send_sem=over_send.at[number],
            recv_sem=over_recv.at[number],
            device_id={"pipe": 1 - plane},
            device_id_type=MESH,
        )

    def hand_over():
        return over(views[exported][1], views[guest][1], 0)

    def hand_back():
        return over(kept, views[exported][5], 1)

    def where(number, condition=None):
        if number in (exported, guest):
            condition = plane == 1 if condition is None else condition & (plane == 1)
        if condition is None:
            return lambda body: body()
        return pl.when(condition)

    def pair_copy(number):
        w, r = views[number][:2]
        return remote(
            w.at[:, :, 1 - core], r, pair_send.at[number], pair_recv.at[number], partner
        )

    def side_copy(number):
        r, x = views[number][1:3]
        source = r.at[level, 1 - side] if plan[number][2] else r.at[:, 1 - side]
        return remote(source, x, side_send.at[number], side_recv.at[number], beside)

    def along_line(number):
        r, x = views[number][1:3]
        return r if plan[number][2] else x

    def up_copy(number, goal, source=None):
        u = views[number][3]
        return remote(
            u.at[goal - 1] if source is None else source,
            u.at[goal - 1],
            up_send.at[number, goal - 1],
            up_recv.at[number, goal - 1],
            above,
        )

    def down_copy(number, goal, source=None):
        n = views[number][4]
        return remote(
            n.at[goal] if source is None else source,
            n.at[goal],
            down_send.at[number, goal],
            down_recv.at[number, goal],
            below,
        )

    def start_line(number):
        base = along_line(number)

        @pl.when(level == 0)
        def _():
            for goal in (3, 2, 1):
                up_copy(number, goal, base.at[goal]).start()

        @pl.when(level == 3)
        def _():
            for goal in (0, 1, 2):
                down_copy(number, goal, base.at[goal]).start()

    position = {"step": 0}
    slots, length = left.shape[1:3]

    def turn_block(source, target):
        def body(t, carry):
            tokens = pl.ds(pl.multiple_of(t * length, length), length)
            target[:, tokens] = source[t].T
            return carry

        lax.fori_loop(0, slots, body, 0)

    def right_part(slot, lanes):
        part = right[slot, :, :, lanes]
        return part.reshape(slots * length, part.shape[2])

    def produce_down(entry, w):
        part, columns = entry[1], entry[3]
        columns = slice(part * columns, (part + 1) * columns)
        copy = pltpu.make_async_copy(
            rights["down"].at[:, :, columns], right_down, lsem.at[2]
        )
        copy.start()
        copy.wait()

        def body(block, carry):
            rows_of = pl.ds(pl.multiple_of(block * width, width), width)
            copy = pltpu.make_async_copy(
                lefts["down"].at[:, :, rows_of], left_down, lsem.at[2]
            )
            copy.start()
            copy.wait()
            turn_block(left_down, lt_down)
            factor = right_down[...].reshape(slots * length, narrow)
            w[block] = dot(lt_down[...], factor).reshape(w.shape[1:])
            return carry

        lax.fori_loop(0, depth, body, 0)

    def multiply(slot, w, columns):
        def tile(t, carry):
            lanes = pl.ds(pl.multiple_of(t * narrow, narrow), narrow)
            product = dot(lt[...], right_part(slot, lanes))
            w[:, :, :, :, lanes] = product.reshape(w.shape[:4] + (narrow,))
            return carry

        lax.fori_loop(0, columns // narrow, tile, 0)


    def produce(number):
        name = plan[number][0]
        if name == "guest":
            return
        if name != "small":
            if previous[number] is not None:
                pair_copy(previous[number]).wait_send()
            w = views[number][0]
            if name == "down":
                produce_down(plan[number], w)
            while position["step"] < len(steps) and steps[position["step"]][0] == number:
                index = position["step"]
                position["step"] += 1
                _, source, turn, block, _, columns = steps[index]
                start_loads(index + 1)
                loads(index).wait()
                if turn:
                    turn_block(left.at[index % 2], lt)
                else:
                    multiply(index % 2, w, columns)
        pair_copy(number).start()

    def stage_pair(number):
        if number == guest:

            @pl.when(plane == 1)
            def _():
                hand_over().wait_recv()
                side_copy(number).start()

            return
        w, r = views[number][:2]
        pair_copy(number).wait_recv()

        def add(z, carry):
            for s in range(2):
                r[z, s] += w[z, s, core]
            return carry

        lax.fori_loop(0, 4, add, 0)
        if plan[number][2]:
            start_line(number)
            return

        @where(number)
        def _():
            side_copy(number).start()

        if number == exported:

            @pl.when(plane == 0)
            def _():
                hand_over().start()

    def stage_side(number):
        if plan[number][2]:
            return

        @where(number)
        def _():
            r, x = views[number][1:3]
            side_copy(number).wait_recv()

            def add(z, carry):
                x[z] += r[z, side]
                return carry

            lax.fori_loop(0, 4, add, 0)
            start_line(number)

    def stage_up(number, height):
        u = views[number][3]
        base = along_line(number)

        @where(number, level == height)
        def _():
            for goal in range(3, height - 1, -1):
                up_copy(number, goal).wait_recv()
                if goal > height:
                    u[goal - 1] += base[goal]
                    up_copy(number, goal).start()

    def stage_down(number, height):
        n = views[number][4]
        base = along_line(number)

        @where(number, level == height)
        def _():
            for goal in range(0, height + 1):
                down_copy(number, goal).wait_recv()
                if goal < height:
                    n[goal] += base[goal]
                    down_copy(number, goal).start()

    def stage_sum(number):
        u, n, place = views[number][3:]
        base = along_line(number)

        @where(number, level > 0)
        def _():
            base[level] += u[level - 1]

        @where(number, level < 3)
        def _():
            base[level] += n[level]

        if plan[number][2]:
            side_copy(number).start()
            return

        @where(number)
        def _():
            place[...] = base[level]
            if number == guest:
                hand_back().start()

    def stage_last(number):
        if plan[number][2]:
            r, x = views[number][1:3]
            side_copy(number).wait_recv()
            views[number][5][...] = r[level, side] + x[...]

    def at(stage, number, *more):
        if 0 <= number < total:
            stage(number, *more)

    for moment in range(total + side_lag + 3 * hop + 1):
        at(produce, moment)
        at(stage_pair, moment - 1)
        at(stage_side, moment - side_lag)
        for height in range(4):
            if height > 0:
                at(stage_up, moment - side_lag - hop * height, height)
            if height < 3:
                at(stage_down, moment - side_lag - hop * (3 - height), height)
        at(stage_sum, moment - side_lag - 3 * hop)
        at(stage_last, moment - side_lag - 3 * hop - 1)
    for number in range(total):
        if last_of[number] and number != guest:
            pair_copy(number).wait_send()

        @where(number)
        def _():
            side_copy(number).wait_send()

        for goal in (1, 2, 3):

            @where(number, goal > level)
            def _():
                up_copy(number, goal).wait_send()

        for goal in (0, 1, 2):

            @where(number, goal < level)
            def _():
                down_copy(number, goal).wait_send()

    @pl.when(plane == 0)
    def _():
        hand_over().wait_send()
        hand_back().wait_recv()

    @pl.when(plane == 1)
    def _():
        hand_back().wait_send()


def kind_of(entry):
    return {"small": "small", "down": "tall"}.get(entry[0], "wide")


def summed_in_kernel(factors, small_grads):
    fa1, fdj, fo, fdhr, fa2, fdu, fg, fdm = factors
    slots, length, width = fa1.shape
    inner = fg.shape[2]
    owners = 16
    depth = inner // width
    narrow = 256
    a_rows, b_rows = width // owners, inner // owners
    packed = small_grads.size // owners
    lanes = 128
    s_rows = -(-packed // (8 * lanes)) * 8
    small = small_grads.reshape(owners, packed)
    small = jnp.pad(small, ((0, 0), (0, s_rows * lanes - packed)))
    small = small.reshape(4, 2, 2, s_rows, lanes)
    plan = [
        ("qkv", 0, False, width),
        ("qkv", 1, True, width),
        ("qkv", 2, False, width),
        ("small", 0, False, 0),
        ("out", 0, False, width),
        ("up", 0, False, width),
        ("down", 0, False, narrow),
        ("up", 1, True, width),
        ("down", 1, False, narrow),
        ("guest", 0, False, width),
        ("up", 2, False, width),
        ("up", 3, False, width),
        ("down", 2, False, narrow),
    ]
    lags = (3, 2)
    total = len(plan)
    s_block = small.shape[3:]
    vmem = pl.BlockSpec(memory_space=pltpu.VMEM)
    anywhere = pl.BlockSpec(memory_space=pl.ANY)

    def of_kind(kind, slots_of, block):
        mine = [entry for entry in plan if kind_of(entry) == kind]
        across = sum(not entry[2] for entry in mine)
        leads = ((slots_of, 4, 2, 2), (len(mine), 4, 2), (across, 4), (across, 3), (across, 3))
        return [pltpu.VMEM(lead + block, F32) for lead in leads]

    line_count = sum(line_first for _, _, line_first, _ in plan)
    a_block = (a_rows, width)
    *grads, small_grad = pl.pallas_call(
        functools.partial(gradients_kernel, (width, narrow, depth), plan, lags),
        out_shape=(
            jax.ShapeDtypeStruct((1, a_rows, 3 * width), F32),
            jax.ShapeDtypeStruct((1, a_rows, width), F32),
            jax.ShapeDtypeStruct((1, a_rows, inner), F32),
            jax.ShapeDtypeStruct((1, b_rows, width), F32),
            jax.ShapeDtypeStruct(s_block, F32),
        ),
        in_specs=[anywhere] * 8 + [vmem],
        out_specs=(vmem,) * 5,
        scratch_shapes=[
            pltpu.VMEM((2, slots, length, width), BF),
            pltpu.VMEM((2, slots, length, width), BF),
            pltpu.VMEM((width, slots * length), BF),
            pltpu.VMEM((width, slots * length), BF),
            pltpu.VMEM((slots, length, width), BF),
            pltpu.VMEM((slots, length, narrow), BF),
        ]
        + of_kind("wide", 2, a_block)
        + of_kind("tall", 1, (b_rows, narrow))
        + [pltpu.VMEM(lead + s_block, F32) for lead in ((4, 2), (4,), (3,), (3,))]
        + [
            pltpu.VMEM((line_count,) + a_block, F32),
            pltpu.VMEM((line_count, 3, 2) + a_block, F32),
            pltpu.VMEM((line_count, 3, 2) + a_block, F32),
            pltpu.VMEM(a_block, F32),
        ]
        + [pltpu.SemaphoreType.DMA((3,))]
        + [pltpu.SemaphoreType.DMA((total,))] * 4
        + [pltpu.SemaphoreType.DMA((total, 3))] * 4
        + [pltpu.SemaphoreType.DMA((2,))] * 2,
        compiler_params=pltpu.CompilerParams(
            collective_id=1, has_side_effects=True, vmem_limit_bytes=62 << 20
        ),
    )(*factors, small)
    return tuple(grads) + (small_grad,)


def results_kernel(count, *refs):
    sources, small = refs[:count], refs[count]
    targets, packed = refs[count + 1 : 2 * count + 1], refs[2 * count + 1]
    held, load_sem, store_sem = refs[2 * count + 2 : -2], refs[-2], refs[-1]
    loads = [
        pltpu.make_async_copy(sources[i], held[i], load_sem.at[i]) for i in range(count)
    ]
    stores = [
        pltpu.make_async_copy(held[i], targets[i], store_sem.at[i]) for i in range(count)
    ]
    for load in loads:
        load.start()
    lines = [small[line : line + 1, :] for line in range(small.shape[0])]
    packed[...] = jnp.concatenate(lines, 1)[:, : packed.shape[1]]
    for load, store in zip(loads, stores):
        load.wait()
        store.start()
    for store in stores:
        store.wait()


def copied_out(large, small, packed):
    count = len(large)
    vmem = pl.BlockSpec(memory_space=pltpu.VMEM)
    anywhere = pl.BlockSpec(memory_space=pl.ANY)
    shapes = [jax.ShapeDtypeStruct(array.shape, array.dtype) for array in large]
    return pl.pallas_call(
        functools.partial(results_kernel, count),
        out_shape=tuple(shapes) + (jax.ShapeDtypeStruct((1, packed), F32),),
        in_specs=[anywhere] * count + [vmem],
        out_specs=(anywhere,) * count + (vmem,),
        scratch_shapes=[pltpu.VMEM(array.shape, array.dtype) for array in large]
        + [pltpu.SemaphoreType.DMA((count,))] * 2,
        compiler_params=pltpu.CompilerParams(vmem_limit_bytes=62 << 20),
    )(*large, small)


def reduced(section_out, factors, small_grads):
    if lax.axis_size("dp") == 16:
        *grads, small_grad = summed_in_kernel(factors, small_grads)
        return copied_out([section_out] + grads, small_grad, small_grads.size // 16)
    return (section_out,) + tuple(summed_by_parts(factors, small_grads))


def per_device(
    embeddings, cotangent, seg_ids, thought_pos, w_qkv, w_out, w_up, w_down, small_params
):
    section_out, *factors, small_grads = layers(
        embeddings, cotangent, seg_ids, thought_pos, w_qkv, w_out, w_up, w_down, small_params
    )
    return tuple(reduced(section_out, factors, small_grads))


def solution(mesh):
    return jax.shard_map(
        per_device,
        mesh=mesh,
        in_specs=(
            P("dp", None, None),
            P("dp", None, None),
            P("dp", None),
            P("dp", None),
            P("pipe", None, None),
            P("pipe", None, None),
            P("pipe", None, None),
            P("pipe", None, None),
            P("pipe", None),
        ),
        out_specs=(
            P("pipe", "dp", None, None),
            P("pipe", "dp", None),
            P("pipe", "dp", None),
            P("pipe", "dp", None),
            P("pipe", "dp", None),
            P("pipe", "dp"),
        ),
        check_vma=False,
    )
```
